32 devices in a mesh: dp: 16 (over z, y, x), mp: 2 (over core).
Axes of the slice: x: 2, y: 2, z: 4, core: 2. Of those that a mesh axis runs over, the one named last changes fastest.
Arguments:
- pixels: bfloat16 [256, 196, 768], P('dp'), may hold values from -6 to 6
- labels: int32 [256], replicated, may hold values from 0 to 999, as said below
- teacher: int32 [256], P('dp'), may hold values from 0 to 999, as said below
- partner: int32 [256], P('dp'), may hold values from 0 to 255, as said below
- mix_weight: float32 [256], P('dp'), may hold values from 0.2 to 0.8
- class_weight: float32 [1000], replicated, may hold values from 0.7 to 15
- tables: float32 [2966, 384], P(None, ('dp', 'mp'))
- tables_first: float32 [2966, 384], P(None, ('dp', 'mp'))
- tables_second: float32 [2966, 384], P(None, ('dp', 'mp'))
- vectors: float32 [14, 384], P(None, ('dp', 'mp'))
- vectors_first: float32 [14, 384], P(None, ('dp', 'mp'))
- vectors_second: float32 [14, 384], P(None, ('dp', 'mp'))
- attention: float32 [2, 384, 1536], P(None, 'dp', 'mp')
- attention_first: float32 [2, 384, 1536], P(None, 'dp', 'mp')
- attention_second: float32 [2, 384, 1536], P(None, 'dp', 'mp')
- feedforward: float32 [2, 384, 2, 1536], P(None, 'dp', None, 'mp'), may hold values from -0.3125 to 0.3125
- feedforward_first: float32 [2, 384, 2, 1536], P(None, 'dp', None, 'mp')
- feedforward_second: float32 [2, 384, 2, 1536], P(None, 'dp', None, 'mp')
- split_bias: float32 [2, 2304], P(None, 'mp'), may hold values from -1.2 to 1.2
- split_bias_first: float32 [2, 2304], P(None, 'mp')
- split_bias_second: float32 [2, 2304], P(None, 'mp')
- head_bias: float32 [2000], replicated, may hold values from -3 to 3
- head_bias_first: float32 [2000], replicated
- head_bias_second: float32 [2000], replicated
Outputs:
- loss_sum: float32 [], replicated
- weight_sum: float32 [], replicated
- grad_norm: float32 [], replicated
- tables_out: float32 [2966, 384], P(None, ('dp', 'mp'))
- tables_first_out: float32 [2966, 384], P(None, ('dp', 'mp'))
- tables_second_out: float32 [2966, 384], P(None, ('dp', 'mp'))
- tables_copy: bfloat16 [2966, 384], P(None, ('dp', 'mp'))
- vectors_out: float32 [14, 384], P(None, ('dp', 'mp'))
- vectors_first_out: float32 [14, 384], P(None, ('dp', 'mp'))
- vectors_second_out: float32 [14, 384], P(None, ('dp', 'mp'))
- attention_out: float32 [2, 384, 1536], P(None, 'dp', 'mp')
- attention_first_out: float32 [2, 384, 1536], P(None, 'dp', 'mp')
- attention_second_out: float32 [2, 384, 1536], P(None, 'dp', 'mp')
- attention_copy: bfloat16 [2, 384, 1536], P(None, 'dp', 'mp')
- feedforward_out: float32 [2, 384, 2, 1536], P(None, 'dp', None, 'mp')
- feedforward_first_out: float32 [2, 384, 2, 1536], P(None, 'dp', None, 'mp')
- feedforward_second_out: float32 [2, 384, 2, 1536], P(None, 'dp', None, 'mp')
- feedforward_copy: bfloat16 [2, 384, 2, 1536], P(None, 'dp', None, 'mp')
- split_bias_out: float32 [2, 2304], P(None, 'mp')
- split_bias_first_out: float32 [2, 2304], P(None, 'mp')
- split_bias_second_out: float32 [2, 2304], P(None, 'mp')
- head_bias_out: float32 [2000], replicated
- head_bias_first_out: float32 [2000], replicated
- head_bias_second_out: float32 [2000], replicated
The draws below stay inside these ranges and needn't reach their ends.
Inputs may be any that keep to these rules, and one draw needn't show every extreme that they name: partner[i] is an image of the block of 16 images numbered (i // 16 + 16 // 2) mod 16; within each block the partners form a permutation of the partner block. labels[i] lies between i * 1000 // 256 and that plus max(125, 2) - 1, capped at 999; labels[0] is 0. teacher[i] lies between i * 1000 // 256 and that plus max(125, 2) - 1, capped at 999; teacher[0] is 0.
All inputs are finite; a program needn't handle non-finite values.
Results may differ from the reference program's by a relative error of at most 0.012.
Values may be sent and summed in bfloat16 or wider, within the bound.
A program may use at most 320 MiB of HBM per device.

```python
import math
import jax
import jax.numpy as jnp
from jax import lax

D = 384
HEADS = 6
HD = 64
FF = 1536
CLS = 1000
PD = 768
PATCHES = 196
IMG_DEV = 16
LAYERS = 2
STEP = 10
TOK = 198
IMAGES = 256
ER = 2966
NV = 14
PARAMS = 4689872
N_MP = 2


clip_limit = 0.02


def entry_size(boost):
    return boost * clip_limit / math.sqrt(PARAMS)


def first_moment(key, shape, boost):
    return jax.random.normal(key, shape, jnp.float32) * (0.111 * entry_size(boost))


def second_moment(key, shape, boost):
    factor = jnp.exp(jax.random.uniform(key, shape, jnp.float32, 0.0, math.log(4.0)))
    return factor * (0.001 * entry_size(boost) ** 2)


def rising_classes(key):
    spread_width = max(CLS // 8, 2)
    order = jnp.arange(IMAGES, dtype=jnp.int32)
    base = order * CLS // IMAGES
    offset = jax.random.randint(key, (IMAGES,), 0, spread_width, dtype=jnp.int32) * (order > 0).astype(jnp.int32)
    return jnp.minimum(base + offset, CLS - 1).astype(jnp.int32)


def draw_labels(key, part):
    key = jax.random.fold_in(key, 41)
    return rising_classes(key)


def draw_teacher(key, part):
    key = jax.random.fold_in(key, 42)
    return rising_classes(key)


def draw_class_weight(key, part):
    key = jax.random.fold_in(key, 43)
    position = jnp.arange(CLS, dtype=jnp.float32) / max(CLS - 1, 1)
    slope = math.log(6.0)
    jitter = jax.random.uniform(key, (CLS,), jnp.float32, 0.7, 1.3)
    return jnp.exp(slope * position) * jitter


def draw_partner(key, part):
    key = jax.random.fold_in(key, 11)
    blocks = IMAGES // IMG_DEV
    keys = jax.random.split(key, blocks)
    inner = jax.vmap(lambda item: jax.random.permutation(item, IMG_DEV))(keys)
    home = (jnp.arange(blocks, dtype=jnp.int32) + blocks // 2) % blocks
    return (home[:, None] * IMG_DEV + inner.astype(jnp.int32)).reshape(IMAGES).astype(jnp.int32)


def draw_tables(key, part):
    key = jax.random.fold_in(key, 1)
    rows = jnp.arange(ER, dtype=jnp.int32)[:, None]
    base = jax.random.normal(key, (ER, D), jnp.float32)
    scale = jnp.where(rows < PD, PD ** (-0.5), jnp.where(rows < PD + TOK, 0.5, 2.0 * D ** (-0.5)))
    return base * scale


def draw_vectors(key, part):
    key = jax.random.fold_in(key, 2)
    gain_key, bias_key = jax.random.split(key)
    rows = jnp.arange(NV, dtype=jnp.int32)[:, None]
    columns = jnp.arange(D, dtype=jnp.float32)[None, :]
    rising = jnp.exp(math.log(3.0) * (columns / D - 0.5)) * jax.random.uniform(gain_key, (NV, D), jnp.float32, 0.85, 1.15)
    shifts = 0.2 * jax.random.normal(bias_key, (NV, D), jnp.float32)
    is_gain = ((rows % 6 == 0) | (rows % 6 == 2)) & (rows < 6 * LAYERS) | (rows == 6 * LAYERS)
    return jnp.where(is_gain, rising, shifts)


def draw_attention(key, part):
    key = jax.random.fold_in(key, 3)
    columns = jnp.arange(4 * D, dtype=jnp.int32)[None, None, :]
    base = jax.random.normal(key, (LAYERS, D, 4 * D), jnp.float32) * D ** (-0.5)
    return base * jnp.where(columns // HD % 4 == 3, 6.0, 1.0)


def draw_tables_first(key, part):
    key = jax.random.fold_in(key, 21)
    return first_moment(key, (ER, D), 1.0)


def draw_tables_second(key, part):
    key = jax.random.fold_in(key, 22)
    return second_moment(key, (ER, D), 1.0)


def draw_vectors_first(key, part):
    key = jax.random.fold_in(key, 23)
    return first_moment(key, (NV, D), 4.0)


def draw_vectors_second(key, part):
    key = jax.random.fold_in(key, 24)
    return second_moment(key, (NV, D), 4.0)


def draw_attention_first(key, part):
    key = jax.random.fold_in(key, 25)
    return first_moment(key, (LAYERS, D, 4 * D), 1.0)


def draw_attention_second(key, part):
    key = jax.random.fold_in(key, 26)
    return second_moment(key, (LAYERS, D, 4 * D), 1.0)


def draw_feedforward_first(key, part):
    key = jax.random.fold_in(key, 27)
    return first_moment(key, (LAYERS, D, 2, FF), 1.0)


def draw_feedforward_second(key, part):
    key = jax.random.fold_in(key, 28)
    return second_moment(key, (LAYERS, D, 2, FF), 1.0)


def draw_split_bias_first(key, part):
    key = jax.random.fold_in(key, 29)
    return first_moment(key, (LAYERS, 2 * D + FF), 2.0)


def draw_split_bias_second(key, part):
    key = jax.random.fold_in(key, 30)
    return second_moment(key, (LAYERS, 2 * D + FF), 2.0)


def draw_head_bias_first(key, part):
    key = jax.random.fold_in(key, 31)
    return first_moment(key, (2 * CLS,), 2.0)


def draw_head_bias_second(key, part):
    key = jax.random.fold_in(key, 32)
    return second_moment(key, (2 * CLS,), 2.0)


def steps_of(stream_key, shape, cuts, low, top_value):
    level, own = 1.0, jax.random.fold_in(stream_key, 6)
    for dim, shards_of in cuts:
        draws = jnp.exp(jax.random.uniform(jax.random.fold_in(own, dim), (shards_of,), jnp.float32, low / len(cuts), top_value / len(cuts)))
        level = level * jnp.repeat(draws, shape[dim] // shards_of).reshape([-1 if axis == dim else 1 for axis in range(len(shape))])
    return level


def noise(stream_key, dims, scale, reach, cuts=(), kind=jnp.bfloat16):
    gain = steps_of(stream_key, dims, cuts, -0.22, 0.18) if cuts else 1.0
    values = jax.random.normal(stream_key, dims, jnp.float32) * scale * gain
    return jnp.minimum(jnp.maximum(values, -reach), reach).astype(kind)


def setup_inputs(seed: int = 0) -> dict:
    splits = jax.random.split(jax.random.key(seed), 25)
    return {
        "pixels": noise(splits[0], (IMAGES, PATCHES, PD), 1.0, 6.0, ((0, 16),)),
        "labels": draw_labels(jax.random.fold_in(splits[24], 71), 0),
        "teacher": draw_teacher(jax.random.fold_in(splits[24], 71), 0),
        "partner": draw_partner(jax.random.fold_in(splits[24], 71), 0),
        "mix_weight": jnp.clip(0.2 + 0.6 * jax.random.uniform(splits[4], (IMAGES,), jnp.float32) ** steps_of(splits[4], (IMAGES,), ((0, 16),), -0.2, 0.2), 0.2, 0.8),
        "class_weight": draw_class_weight(jax.random.fold_in(splits[24], 71), 0),
        "tables": draw_tables(jax.random.fold_in(splits[24], 71), 0),
        "tables_first": draw_tables_first(jax.random.fold_in(splits[24], 71), 0),
        "tables_second": draw_tables_second(jax.random.fold_in(splits[24], 71), 0),
        "vectors": draw_vectors(jax.random.fold_in(splits[24], 71), 0),
        "vectors_first": draw_vectors_first(jax.random.fold_in(splits[24], 71), 0),
        "vectors_second": draw_vectors_second(jax.random.fold_in(splits[24], 71), 0),
        "attention": draw_attention(jax.random.fold_in(splits[24], 71), 0),
        "attention_first": draw_attention_first(jax.random.fold_in(splits[24], 71), 0),
        "attention_second": draw_attention_second(jax.random.fold_in(splits[24], 71), 0),
        "feedforward": noise(splits[15], (LAYERS, D, 2, FF), D ** -0.5, 0.3125, ((1, 16), (3, 2)), jnp.float32),
        "feedforward_first": draw_feedforward_first(jax.random.fold_in(splits[24], 71), 0),
        "feedforward_second": draw_feedforward_second(jax.random.fold_in(splits[24], 71), 0),
        "split_bias": noise(splits[18], (LAYERS, 2 * D + FF), 0.2, 1.2, ((1, 2),), jnp.float32),
        "split_bias_first": draw_split_bias_first(jax.random.fold_in(splits[24], 71), 0),
        "split_bias_second": draw_split_bias_second(jax.random.fold_in(splits[24], 71), 0),
        "head_bias": noise(splits[21], (2 * CLS,), 0.5, 3.0, (), jnp.float32),
        "head_bias_first": draw_head_bias_first(jax.random.fold_in(splits[24], 71), 0),
        "head_bias_second": draw_head_bias_second(jax.random.fold_in(splits[24], 71), 0),
    }


@jax.custom_vjp
def low(v):
    return lax.optimization_barrier(v.astype(jnp.bfloat16)).astype(jnp.float32)

@jax.custom_vjp
def low_back(v):
    return v

def low_keep(v):
    return (low(v), None)

def low_pass(kept, grad):
    return (grad,)

def back_keep(v):
    return (v, None)

def back_low(kept, grad):
    return (low(grad),)
low.defvjp(low_keep, low_pass)
low_back.defvjp(back_keep, back_low)
norm_eps = 1e-06
clip_limit = 0.02
beta_one = 0.9
beta_two = 0.999
adam_eps = 1e-08
matrix_rate = 0.08
vector_rate = 0.5
matrix_decay = 0.05
highest_precision = lax.Precision.HIGHEST

def both_ways(values):
    return low(low_back(values))

def layer_norm(values, gain_row, shift_row):
    average = lax.optimization_barrier(jnp.mean(values, -1, keepdims=True))
    centered = values - average
    variance = lax.optimization_barrier(jnp.mean(centered * centered, -1, keepdims=True))
    return centered * lax.rsqrt(variance + norm_eps) * gain_row + shift_row

def block(stream, rows_six, in_heads, ffw_now, qv_bias, up_bias):
    normed = low(layer_norm(stream, rows_six[0], rows_six[1]))
    projected = jnp.einsum('bsd,dhcf->bshcf', normed, in_heads[:, :, :3], precision=highest_precision)
    queries = both_ways(projected[:, :, :, 0] + qv_bias[:, 0])
    key_rows = both_ways(projected[:, :, :, 1])
    values = both_ways(projected[:, :, :, 2] + qv_bias[:, 1])
    scores = low_back(jnp.einsum('bshf,bthf->bhst', queries, key_rows, precision=highest_precision) * 0.125)
    highest = lax.optimization_barrier(jnp.max(scores, -1, keepdims=True))
    exponent = jnp.exp(scores - highest)
    attn_probs = both_ways(exponent / lax.optimization_barrier(jnp.sum(exponent, -1, keepdims=True)))
    heads_out = both_ways(jnp.einsum('bhst,bthf->bshf', attn_probs, values, precision=highest_precision))
    attended = low_back(jnp.einsum('bshf,ehf->bse', heads_out, in_heads[:, :, 3], precision=highest_precision))
    middle = stream + attended + rows_six[4]
    normed_two = low(layer_norm(middle, rows_six[2], rows_six[3]))
    upward = low_back(jnp.einsum('bsd,df->bsf', normed_two, ffw_now[:, 0], precision=highest_precision) + up_bias)
    hidden = both_ways(jax.nn.gelu(upward, approximate=False))
    output = low_back(jnp.einsum('bsf,df->bsd', hidden, ffw_now[:, 1], precision=highest_precision))
    return middle + output + rows_six[5]

def model(params, mixed, loss_coef):
    tables, vectors, attention, feedforward, split_bias, head_bias = [low(item) for item in params]
    count = mixed.shape[0]
    patch_proj = tables[:PD]
    token_table = tables[PD:PD + TOK]
    head_rows = tables[PD + TOK:].reshape(2, CLS, D)
    embedded = low_back(jnp.einsum('bpi,id->bpd', mixed, patch_proj, precision=highest_precision))
    stream = jnp.concatenate([jnp.zeros((count, 2, D), jnp.float32), embedded], 1) + token_table
    for layer_index in range(LAYERS):
        rows_six = vectors[6 * layer_index:6 * layer_index + 6]
        in_heads = attention[layer_index].reshape(D, HEADS, 4, HD)
        pieces = split_bias[layer_index].reshape(N_MP, -1)
        qv_bias = pieces[:, :2 * D // N_MP].reshape(HEADS, 2, HD)
        up_bias = pieces[:, 2 * D // N_MP:].reshape(FF)
        stream = block(stream, rows_six, in_heads, feedforward[layer_index], qv_bias, up_bias)
    final = low(layer_norm(stream[:, :2], vectors[6 * LAYERS], vectors[6 * LAYERS + 1]))
    logits = low_back(jnp.einsum('btd,tcd->btc', final, head_rows, precision=highest_precision)) + head_bias.reshape(2, CLS)
    highest = lax.optimization_barrier(jnp.max(logits, -1, keepdims=True))
    log_total = highest + jnp.log(lax.optimization_barrier(jnp.sum(jnp.exp(logits - highest), -1, keepdims=True)))
    return jnp.sum(loss_coef * (log_total - logits))

def adamw(master, first, second, gradient, rate, decay):
    first = beta_one * first + (1.0 - beta_one) * gradient
    second = beta_two * second + (1.0 - beta_two) * gradient * gradient
    first_hat = first / (1.0 - beta_one ** STEP)
    second_hat = second / (1.0 - beta_two ** STEP)
    master = master - rate * (first_hat / (jnp.sqrt(second_hat) + adam_eps) + decay * master)
    return (master, first, second)

def reference(pixels, labels, teacher, partner, mix_weight, class_weight, tables, tables_first, tables_second, vectors, vectors_first, vectors_second, attention, attention_first, attention_second, feedforward, feedforward_first, feedforward_second, split_bias, split_bias_first, split_bias_second, head_bias, head_bias_first, head_bias_second):
    params = (tables, vectors, attention, feedforward, split_bias, head_bias)
    firsts = (tables_first, vectors_first, attention_first, feedforward_first, split_bias_first, head_bias_first)
    seconds = (tables_second, vectors_second, attention_second, feedforward_second, split_bias_second, head_bias_second)
    classes = jnp.arange(CLS, dtype=jnp.int32)
    partner_labels = jnp.take(labels, partner, axis=0)
    own_weight = mix_weight * jnp.take(class_weight, labels)
    other_weight = (1.0 - mix_weight) * jnp.take(class_weight, partner_labels)
    coef_cls = own_weight[:, None] * (classes[None, :] == labels[:, None]) + other_weight[:, None] * (classes[None, :] == partner_labels[:, None])
    coef_dist = jnp.take(class_weight, teacher)[:, None] * (classes[None, :] == teacher[:, None])
    coef_all = jnp.stack([coef_cls, coef_dist], 1)
    weight_sum = jnp.sum(coef_all)

    def per_group(carry, group_index):
        start = group_index * IMG_DEV
        own = lax.dynamic_slice_in_dim(pixels, start, IMG_DEV, 0).astype(jnp.float32)
        chosen = lax.dynamic_slice_in_dim(partner, start, IMG_DEV, 0)
        other = jnp.take(pixels, chosen, axis=0).astype(jnp.float32)
        mixing = lax.dynamic_slice_in_dim(mix_weight, start, IMG_DEV, 0)[:, None, None]
        mixed = low(mixing * own + (1.0 - mixing) * other)
        loss_coef = lax.dynamic_slice_in_dim(coef_all, start, IMG_DEV, 0)
        loss_part, pull = jax.vjp(lambda items: model(items, mixed, loss_coef), params)
        grads = pull(jnp.ones((), jnp.float32))[0]
        running, sums = carry
        return ((running + loss_part, jax.tree.map(jnp.add, sums, grads)), None)
    start_state = (jnp.zeros((), jnp.float32), jax.tree.map(jnp.zeros_like, params))
    (loss_sum, grads), unused = lax.scan(per_group, start_state, jnp.arange(IMAGES // IMG_DEV, dtype=jnp.int32))
    squares = jnp.zeros((), jnp.float32)
    for item in grads:
        squares = squares + jnp.sum(item * item)
    grad_norm = jnp.sqrt(squares) / weight_sum
    factor = jnp.minimum(1.0, clip_limit / grad_norm) / weight_sum
    rates = (matrix_rate, vector_rate, matrix_rate, matrix_rate, vector_rate, vector_rate)
    decays = (matrix_decay, 0.0, matrix_decay, matrix_decay, 0.0, 0.0)
    updated = [adamw(params[k], firsts[k], seconds[k], grads[k] * factor, rates[k], decays[k]) for k in range(6)]
    (t_new, t_one, t_two), (v_new, v_one, v_two), (a_new, a_one, a_two), (f_new, f_one, f_two), (s_new, s_one, s_two), (h_new, h_one, h_two) = updated
    return (loss_sum, weight_sum, grad_norm, t_new, t_one, t_two, t_new.astype(jnp.bfloat16), v_new, v_one, v_two, a_new, a_one, a_two, a_new.astype(jnp.bfloat16), f_new, f_one, f_two, f_new.astype(jnp.bfloat16), s_new, s_one, s_two, h_new, h_one, h_two)
```

```python
import functools

import jax
import jax.numpy as jnp
from jax import lax
from jax.experimental import pallas as pl
from jax.experimental.pallas import tpu as pltpu
from jax.sharding import PartitionSpec as P

D = 384
HEADS = 6
HD = 64
FF = 1536
CLS = 1000
PD = 768
PATCHES = 196
LAYERS = 2
STEP = 10
TOK = 198
TP = 208
GRP = 2
ROWS = GRP * TP
HALF = FF // 2
COLS = 6144
T_COLS = 1536
MIB = 1 << 20

norm_eps = 1e-06
clip_limit = 0.02
beta_one = 0.9
beta_two = 0.999
adam_eps = 1e-08
matrix_rate = 0.08
vector_rate = 0.5
matrix_decay = 0.05

f32 = jnp.float32
bf16 = jnp.bfloat16
MESH = pl.DeviceIdType.MESH
AB = ((1,), (0,))
ABT = ((1,), (1,))
ATB = ((0,), (0,))


def mm(left, right, dims=AB):
    return lax.dot_general(left, right, (dims, ((), ())), preferred_element_type=f32)


def full_spec(shape):
    return pl.BlockSpec(shape, lambda *_: (0,) * len(shape), pipeline_mode=pl.Buffered(1))


def row_loop(total, chunk, body):
    def step(index, carry):
        body(pl.ds(pl.multiple_of(index * chunk, chunk), chunk))
        return carry

    lax.fori_loop(0, total // chunk, step, 0, unroll=2)


def center(x):
    mean = jnp.mean(x, -1, keepdims=True)
    xc = x - mean
    scale = lax.rsqrt(jnp.mean(xc * xc, -1, keepdims=True) + norm_eps)
    return xc * scale, scale


def gelu_pair(x):
    z = x * 0.7071067811865476
    e = jnp.exp(-(z * z))
    den = 1.0 + 0.3275911 * jnp.abs(z)
    r = pl.reciprocal(den, approx=True)
    r = r * (2.0 - den * r)
    poly = r * (
        0.127414796
        + r * (-0.142248368 + r * (0.7107068705 + r * (-0.7265760135 + r * 0.5307027145)))
    )
    tail = poly * e
    cdf = jnp.where(x > 0.0, 1.0 - tail, tail)
    return x * cdf, cdf + x * (e * 0.3989422804014327)


def embed_kernel(inv_ref, base_ref, pix_ref, w_ref, own_ref, send_ref, flat):
    rows = pix_ref.shape[0]
    count = rows // PATCHES
    chunk = rows // 7
    for c in range(7):
        pix = pix_ref[c * chunk : (c + 1) * chunk]
        out = mm(pix[:, :D], w_ref[0, :, :D], ABT) + mm(pix[:, D:], w_ref[1, :, :D], ABT)
        for j in range(3):
            flat[j, c * chunk : (c + 1) * chunk] = out[:, 128 * j : 128 * (j + 1)]
    for k in range(own_ref.shape[0]):
        for j in range(3):
            cols = slice(128 * j, 128 * (j + 1))
            own_ref[k, :, cols] = flat[j, pl.ds(inv_ref[k], PATCHES, stride=count), :]
            send_ref[k, :, cols] = flat[j, pl.ds(base_ref[0] + k, PATCHES, stride=count), :].astype(
                bf16
            )


def embed(inv, base, pix, weights, count):
    return pl.pallas_call(
        embed_kernel,
        grid=(1,),
        in_specs=[
            pl.BlockSpec(memory_space=pltpu.SMEM),
            pl.BlockSpec(memory_space=pltpu.SMEM),
            full_spec(pix.shape),
            pl.BlockSpec((2, D, 512), lambda i: (0, 0, 0), pipeline_mode=pl.Buffered(1)),
        ],
        out_specs=[full_spec((count, PATCHES, D)), full_spec((count, PATCHES, D))],
        out_shape=[
            jax.ShapeDtypeStruct((count, PATCHES, D), f32),
            jax.ShapeDtypeStruct((count, PATCHES, D), bf16),
        ],
        scratch_shapes=[pltpu.VMEM((3, pix.shape[0], 128), f32)],
        compiler_params=pltpu.CompilerParams(vmem_limit_bytes=48 * MIB),
        name="embed_images",
    )(inv, base, pix, weights)


def attn_tiles(w_ref, layer, qkv_w, out_w):
    base = T_COLS + 768 * layer
    for t in range(4):
        cols = base + 128 * t
        pieces = [w_ref[0, :, cols : cols + 128], w_ref[1, :, cols : cols + 128]]
        third = base + 512 + 64 * t
        tile = base + 512 + 128 * (t // 2)
        lane = third - tile
        pieces.append(
            jnp.concatenate(
                [w_ref[m, :, tile : tile + 128][:, lane : lane + 64] for m in range(2)], 1
            )
        )
        for j in range(3):
            if t < 3:
                at = D * t + 128 * j
                qkv_w[:, at : at + 128] = pieces[j]
            else:
                out_w[:, 128 * j : 128 * (j + 1)] = pieces[j]


def split_tokens(w_ref, col):
    seg = jnp.concatenate([w_ref[0, :, col : col + 128], w_ref[1, :, col : col + 128]], 1)
    return jnp.transpose(seg.astype(f32), (1, 0))


def attend(g, qkv_ref, p_ref, ho_ref):
    rows = slice(g * TP, (g + 1) * TP)
    lane = lax.broadcasted_iota(jnp.int32, (TP, 128), 1)
    key_mask = jnp.where(lax.broadcasted_iota(jnp.int32, (1, TP), 1) < TOK, 0.0, -1e30).astype(f32)
    for j in range(3):
        q = qkv_ref[rows, 128 * j : 128 * (j + 1)]
        k = qkv_ref[rows, D + 128 * j : D + 128 * (j + 1)]
        v = qkv_ref[rows, 2 * D + 128 * j : 2 * D + 128 * (j + 1)]
        outs = []
        for s in range(2):
            mine = (lane < 64) if s == 0 else (lane >= 64)
            scores = mm(jnp.where(mine, q, jnp.zeros_like(q)), k, ABT) + key_mask
            exps = jnp.exp(scores - jnp.max(scores, -1, keepdims=True))
            probs = (exps * (1.0 / jnp.sum(exps, -1, keepdims=True))).astype(bf16)
            p_ref[6 * g + 2 * j + s] = probs
            outs.append(mm(probs, v))
        ho_ref[rows, 128 * j : 128 * (j + 1)] = jnp.where(lane < 64, outs[0], outs[1]).astype(bf16)


def forward_kernel(mix_ref, own_ref, far_ref, w_ref, bias_ref, ub_ref, *refs):
    kept = refs[: 7 * LAYERS]
    tail_ref, tok_ref = refs[7 * LAYERS : 7 * LAYERS + 2]
    qkv_w, out_w, nbuf, up_s, last = refs[7 * LAYERS + 2 :]
    step = pl.program_id(0)

    @pl.when(step == 0)
    def _():
        tok_ref[...] = split_tokens(w_ref, D)
        for layer in range(LAYERS):
            attn_tiles(w_ref, layer, qkv_w.at[layer], out_w.at[layer])

    for g in range(GRP):
        w = mix_ref[step * GRP + g]
        x_ref = kept[0]
        x_ref[g * TP : g * TP + PATCHES] = (
            w * own_ref[g] + (1.0 - w) * far_ref[g].astype(f32) + tok_ref[:PATCHES]
        )
        x_ref[g * TP + PATCHES : (g + 1) * TP] = tok_ref[PATCHES:TP]
    for layer in range(LAYERS):
        x_ref, mid_ref, qkv_ref, p_ref, ho_ref, hid_ref, gp_ref = kept[7 * layer : 7 * layer + 7]
        v0 = TP + 6 * layer
        row = [tok_ref[v0 + i : v0 + i + 1] for i in range(6)]

        def norm(src, gain, shift):
            def body(rs):
                nbuf[rs] = (center(src[rs])[0] * gain + shift).astype(bf16)

            row_loop(ROWS, 16, body)

        norm(x_ref, row[0], row[1])
        n = nbuf[...]
        q = mm(n, qkv_w[layer, :, :D]) + bias_ref[layer : layer + 1, :D]
        qkv_ref[:, :D] = (q.astype(bf16).astype(f32) * 0.125).astype(bf16)
        qkv_ref[:, D : 2 * D] = mm(n, qkv_w[layer, :, D : 2 * D]).astype(bf16)
        v = mm(n, qkv_w[layer, :, 2 * D :]) + bias_ref[layer : layer + 1, D : 2 * D]
        qkv_ref[:, 2 * D :] = v.astype(bf16)
        for g in range(GRP):
            attend(g, qkv_ref, p_ref, ho_ref)
        mid_ref[...] = x_ref[...] + mm(ho_ref[...], out_w[layer], ABT) + row[4]
        norm(mid_ref, row[2], row[3])
        f0 = T_COLS + 768 * LAYERS + 1536 * layer
        for m in range(2):
            cols = slice(HALF * m, HALF * (m + 1))
            up_s[...] = (
                mm(nbuf[...], w_ref[m, :, f0 : f0 + HALF]) + ub_ref[layer : layer + 1, cols]
            )

            def body(rs):
                hid, gp = gelu_pair(up_s[rs])
                hid_ref[rs, cols] = hid.astype(bf16)
                gp_ref[rs, cols] = gp.astype(bf16)

            row_loop(ROWS, 16, body)
        out = mid_ref[...] + row[5]
        for m in range(2):
            cols = slice(HALF * m, HALF * (m + 1))
            out = out + mm(hid_ref[:, cols], w_ref[m, :, f0 + HALF : f0 + FF], ABT)
        if layer + 1 < LAYERS:
            kept[7 * (layer + 1)][...] = out
        else:
            last[...] = out
            for g in range(GRP):
                tail_ref[16 * g : 16 * (g + 1)] = last[g * TP + 192 : (g + 1) * TP]


def kept_shapes(count):
    n = count * TP
    return [
        ((n, D), f32),
        ((n, D), f32),
        ((n, 3 * D), bf16),
        ((count * HEADS, TP, TP), bf16),
        ((n, D), bf16),
        ((n, FF), bf16),
        ((n, FF), bf16),
    ]


def block_of(shape, steps):
    block = (shape[0] // steps,) + tuple(shape[1:])
    return pl.BlockSpec(block, lambda i: (i,) + (0,) * (len(block) - 1))


def forward(mix, own, far, weights, bias, ub):
    count = own.shape[0]
    steps = count // GRP
    outs = kept_shapes(count) * LAYERS + [((count * 16, D), f32)]
    shapes = [jax.ShapeDtypeStruct(s, t) for s, t in outs] + [jax.ShapeDtypeStruct((256, D), f32)]
    specs = [block_of(s, steps) for s, _ in outs] + [full_spec((256, D))]
    return pl.pallas_call(
        forward_kernel,
        grid=(steps,),
        in_specs=[
            pl.BlockSpec(memory_space=pltpu.SMEM),
            block_of(own.shape, steps),
            block_of(far.shape, steps),
            full_spec(weights.shape),
            full_spec(bias.shape),
            full_spec(ub.shape),
        ],
        out_specs=specs,
        out_shape=shapes,
        scratch_shapes=[
            pltpu.VMEM((LAYERS, D, 3 * D), bf16),
            pltpu.VMEM((LAYERS, D, D), bf16),
            pltpu.VMEM((ROWS, D), bf16),
            pltpu.VMEM((ROWS, HALF), f32),
            pltpu.VMEM((ROWS, D), f32),
        ],
        compiler_params=pltpu.CompilerParams(vmem_limit_bytes=60 * MIB),
        name="forward_layers",
    )(mix, own, far, weights, bias, ub)


def norm_back(dy, xhat, scale, gain):
    dyg = dy * gain
    c1 = jnp.mean(dyg, -1, keepdims=True)
    c2 = jnp.mean(dyg * xhat, -1, keepdims=True)
    return scale * (dyg - c1 - xhat * c2)


def head_kernel(
    rows_ref, w_ref, hb_ref, lab_ref, lw_ref, vec_ref, dh_ref, dx_ref, dv_ref, dhb_ref, stat_ref
):
    gain, shift = vec_ref[0:1], vec_ref[1:2]
    loss = jnp.zeros((1, 1), f32)
    weight = jnp.zeros((1, 1), f32)
    dgain = jnp.zeros((1, D), f32)
    dshift = jnp.zeros((1, D), f32)
    count = rows_ref.shape[1]
    for h in range(2):
        xhat, scale = center(rows_ref[h])
        final = (xhat * gain + shift).astype(bf16)
        halves = []
        for m in range(2):
            wh = w_ref[m, :, 512 * h : 512 * (h + 1)]
            at = 1024 * h + 512 * m
            logits = mm(final, wh) + hb_ref[0:1, at : at + 512]
            ids = lax.broadcasted_iota(jnp.int32, (count, 512), 1) + 512 * m
            coef = jnp.where(ids == lab_ref[:, 2 * h : 2 * h + 1], lw_ref[:, 2 * h : 2 * h + 1], 0.0)
            if h == 0:
                coef = coef + jnp.where(ids == lab_ref[:, 1:2], lw_ref[:, 1:2], 0.0)
            halves.append((wh, logits, coef))
        top = jnp.maximum(*[jnp.max(x[1], -1, keepdims=True) for x in halves])
        exps = [jnp.exp(x[1] - top) for x in halves]
        total = sum(jnp.sum(x, -1, keepdims=True) for x in exps)
        lse = top + jnp.log(total)
        csum = sum(jnp.sum(x[2], -1, keepdims=True) for x in halves)
        dfinal = jnp.zeros((count, D), f32)
        for m in range(2):
            wh, logits, coef = halves[m]
            loss = loss + jnp.sum(jnp.sum(coef * (lse - logits), -1, keepdims=True), 0, keepdims=True)
            dl = csum * (exps[m] / total) - coef
            at = 1024 * h + 512 * m
            dhb_ref[0:1, at : at + 512] = jnp.sum(dl, 0, keepdims=True)
            low = dl.astype(bf16)
            dh_ref[m, :, 512 * h : 512 * (h + 1)] = mm(final, low, ATB)
            dfinal = dfinal + mm(low, wh, ABT)
        weight = weight + jnp.sum(csum, 0, keepdims=True)
        dx_ref[h] = norm_back(dfinal, xhat, scale, gain)
        dgain = dgain + jnp.sum(dfinal * xhat, 0, keepdims=True)
        dshift = dshift + jnp.sum(dfinal, 0, keepdims=True)
    dv_ref[...] = jnp.zeros_like(dv_ref)
    dv_ref[0:1] = dgain
    dv_ref[1:2] = dshift
    which = lax.broadcasted_iota(jnp.int32, stat_ref.shape, 1)
    stat_ref[...] = jnp.where(which == 0, loss, jnp.where(which == 1, weight, 0.0))


def head(rows, weights, hb, labs, lws, vec):
    count = rows.shape[1]
    shapes = [(2, D, 1024), (2, count, D), (8, D), (8, 2048), (8, 128)]
    return pl.pallas_call(
        head_kernel,
        grid=(1,),
        in_specs=[
            full_spec(rows.shape),
            pl.BlockSpec((2, D, 1024), lambda i: (0, 0, 0), pipeline_mode=pl.Buffered(1)),
            full_spec(hb.shape),
            full_spec(labs.shape),
            full_spec(lws.shape),
            full_spec(vec.shape),
        ],
        out_specs=[full_spec(s) for s in shapes],
        out_shape=[jax.ShapeDtypeStruct(s, f32) for s in shapes],
        compiler_params=pltpu.CompilerParams(vmem_limit_bytes=48 * MIB),
        name="loss_heads",
    )(rows, weights, hb, labs, lws, vec)


def attend_back(g, dho, qkv_ref, p_ref, dproj):
    rows = slice(g * TP, (g + 1) * TP)
    lane = lax.broadcasted_iota(jnp.int32, (TP, 128), 1)
    for j in range(3):
        q = qkv_ref[rows, 128 * j : 128 * (j + 1)]
        k = qkv_ref[rows, D + 128 * j : D + 128 * (j + 1)]
        v = qkv_ref[rows, 2 * D + 128 * j : 2 * D + 128 * (j + 1)]
        do = dho[rows, 128 * j : 128 * (j + 1)]
        qt, kt, dot_ = (jnp.transpose(a, (1, 0)) for a in (q, k, do))
        for s in range(2):
            mine = (lane < 64) if s == 0 else (lane >= 64)
            sub = slice(64 * s, 64 * (s + 1))
            at = 128 * j + 64 * s
            probs = p_ref[6 * g + 2 * j + s]
            dproj[g, 2 * D + at : 2 * D + at + 64] = mm(dot_[sub], probs).astype(bf16)
            dprob = mm(jnp.where(mine, do, jnp.zeros_like(do)), v, ABT)
            p32 = probs.astype(f32)
            delta = jnp.sum(dprob * p32, -1, keepdims=True)
            ds = (p32 * (dprob - delta)).astype(bf16)
            dproj[g, at : at + 64] = (mm(kt[sub], ds, ABT) * 0.125).astype(bf16)
            dproj[g, D + at : D + at + 64] = mm(qt[sub], ds).astype(bf16)


def backward_kernel(
    dz_ref,
    x_ref,
    mid_ref,
    qkv_ref,
    p_ref,
    ho_ref,
    hid_ref,
    gp_ref,
    wa_ref,
    wf_ref,
    vec_ref,
    dzo_ref,
    ga_ref,
    gf_ref,
    gv_ref,
    gb_ref,
    gu_ref,
    qkv_w,
    out_w,
    dqkv,
    dout,
    nbuf,
    dz,
    dn,
    du,
    dproj,
):
    step = pl.program_id(0)
    gain1, shift1, gain2, shift2 = (vec_ref[i : i + 1] for i in range(4))

    @pl.when(step == 0)
    def _():
        gf_ref[...] = jnp.zeros_like(gf_ref)
        gv_ref[...] = jnp.zeros_like(gv_ref)
        gu_ref[...] = jnp.zeros_like(gu_ref)
        dqkv[...] = jnp.zeros_like(dqkv)
        dout[...] = jnp.zeros_like(dout)
        attn_tiles_local(wa_ref, qkv_w, out_w)

    def norm(src, gain, shift):
        def body(rs):
            nbuf[rs] = (center(src[rs])[0] * gain + shift).astype(bf16)

        row_loop(ROWS, 16, body)

    norm(mid_ref, gain2, shift2)
    gv_ref[5:6] += jnp.sum(dz_ref[...], 0, keepdims=True)
    rz = dz_ref[...].astype(bf16)
    rzt = jnp.transpose(rz, (1, 0))
    nt = jnp.transpose(nbuf[...], (1, 0))
    for m in range(2):
        cols = slice(HALF * m, HALF * (m + 1))
        dh = mm(rz, wf_ref[m, :, HALF:])
        du_val = dh.astype(bf16).astype(f32) * gp_ref[:, cols].astype(f32)
        du[...] = du_val.astype(bf16)
        gu_ref[0:1, cols] += jnp.sum(du[...].astype(f32), 0, keepdims=True)
        gf_ref[m, :, HALF:] += mm(rzt, hid_ref[:, cols])
        gf_ref[m, :, :HALF] += mm(nt, du[...])
        part = mm(du[...], wf_ref[m, :, :HALF], ABT)
        dn[...] = part if m == 0 else dn[...] + part

    def pull(src, gain, dz_in, dz_out, at):
        def body(rs, carry):
            dg, db, total = carry
            rs = pl.ds(pl.multiple_of(rs * 16, 16), 16)
            xhat, scale = center(src[rs])
            dy = dn[rs]
            new = dz_in[rs] + norm_back(dy, xhat, scale, gain)
            dz_out[rs] = new
            return dg + dy * xhat, db + dy, total + new

        zero = jnp.zeros((16, D), f32)
        dg, db, total = lax.fori_loop(0, ROWS // 16, body, (zero, zero, zero))
        gv_ref[at : at + 1] += jnp.sum(dg, 0, keepdims=True)
        gv_ref[at + 1 : at + 2] += jnp.sum(db, 0, keepdims=True)
        return total

    total = pull(mid_ref, gain2, dz_ref, dz, 2)
    gv_ref[4:5] += jnp.sum(total, 0, keepdims=True)
    rz2 = dz[...].astype(bf16)
    dout[...] += mm(jnp.transpose(rz2, (1, 0)), ho_ref[...])
    dho = mm(rz2, out_w[...]).astype(bf16)
    norm(x_ref, gain1, shift1)
    ones = jnp.ones((TP, 128), bf16)
    for g in range(GRP):
        rows = slice(g * TP, (g + 1) * TP)
        attend_back(g, dho, qkv_ref, p_ref, dproj)
        dqkv[:, :D] += mm(dproj[g], nbuf[rows])
        dqkv[:, D:] += mm(dproj[g], ones)
        dn[rows] = jnp.transpose(mm(qkv_w[...], dproj[g]), (1, 0))
    pull(x_ref, gain1, dz, dzo_ref, 0)

    @pl.when(step == pl.num_programs(0) - 1)
    def _():
        for t in range(4):
            for j in range(3):
                at = D * t + 128 * j
                tile = (
                    jnp.transpose(dqkv[at : at + 128, :D], (1, 0))
                    if t < 3
                    else dout[:, 128 * j : 128 * (j + 1)]
                )
                if j < 2:
                    ga_ref[j, :, 128 * t : 128 * (t + 1)] = tile
                else:
                    for m in range(2):
                        lo = 512 + 64 * t
                        ga_ref[m, :, lo : lo + 64] = tile[:, 64 * m : 64 * (m + 1)]
        gb_ref[...] = jnp.transpose(dqkv[:, D:], (1, 0))[0:8]


def attn_tiles_local(w_ref, qkv_w, out_w):
    for t in range(4):
        cols = 128 * t
        pieces = [w_ref[0, :, cols : cols + 128], w_ref[1, :, cols : cols + 128]]
        tile = 512 + 128 * (t // 2)
        lane = 64 * (t % 2)
        pieces.append(
            jnp.concatenate(
                [w_ref[m, :, tile : tile + 128][:, lane : lane + 64] for m in range(2)], 1
            )
        )
        for j in range(3):
            if t < 3:
                at = D * t + 128 * j
                qkv_w[:, at : at + 128] = pieces[j]
            else:
                out_w[:, 128 * j : 128 * (j + 1)] = pieces[j]


def backward(layer, dz, kept, weights, vec):
    steps = dz.shape[0] // ROWS
    a_block = T_COLS // 768 + layer
    f_block = (T_COLS + 768 * LAYERS) // 1536 + layer
    shapes = [(2, D, 768), (2, D, 1536), (8, D), (8, 3 * D), (8, FF)]
    return pl.pallas_call(
        backward_kernel,
        grid=(steps,),
        in_specs=[block_of(a.shape, steps) for a in (dz,) + tuple(kept)]
        + [
            pl.BlockSpec((2, D, 768), lambda i: (0, 0, a_block), pipeline_mode=pl.Buffered(1)),
            pl.BlockSpec((2, D, 1536), lambda i: (0, 0, f_block), pipeline_mode=pl.Buffered(1)),
            full_spec(vec.shape),
        ],
        out_specs=[block_of(dz.shape, steps)] + [full_spec(s) for s in shapes],
        out_shape=[jax.ShapeDtypeStruct(dz.shape, f32)]
        + [jax.ShapeDtypeStruct(s, f32) for s in shapes],
        scratch_shapes=[
            pltpu.VMEM((D, 3 * D), bf16),
            pltpu.VMEM((D, D), bf16),
            pltpu.VMEM((3 * D, 512), f32),
            pltpu.VMEM((D, D), f32),
            pltpu.VMEM((ROWS, D), bf16),
            pltpu.VMEM((ROWS, D), f32),
            pltpu.VMEM((ROWS, D), f32),
            pltpu.VMEM((ROWS, HALF), bf16),
            pltpu.VMEM((GRP, 3 * D, TP), bf16),
        ],
        compiler_params=pltpu.CompilerParams(vmem_limit_bytes=60 * MIB),
        name="backward_layer",
    )(dz, *kept, weights, weights, vec)


def patch_grad_kernel(
    inv_ref, mix_ref, dz_ref, own_ref, far_ref, gv0_ref, gv1_ref, gve_ref, gp_ref, ge_ref, dzo, dzf, tok
):
    count = far_ref.shape[0] // PATCHES
    both = own_ref.shape[0] // PATCHES
    dzo[...] = jnp.zeros_like(dzo)
    total = jnp.zeros((TP, D), f32)
    for k in range(count):
        w = mix_ref[k]
        for j in range(3):
            part = dz_ref[k * TP : k * TP + PATCHES, 128 * j : 128 * (j + 1)]
            dzo[j, pl.ds(inv_ref[k], PATCHES, stride=both), :] = w * part
            dzf[j, pl.ds(k, PATCHES, stride=count), :] = (1.0 - w) * part
        total = total + dz_ref[k * TP : (k + 1) * TP]
    tok[...] = jnp.zeros_like(tok)
    tok[:TP] = total
    for i, ref in enumerate((gv0_ref, gv1_ref)):
        tok[TP + 6 * i : TP + 6 * i + 6] = ref[0:6]
    tok[TP + 6 * LAYERS : TP + 6 * LAYERS + 2] = gve_ref[0:2]
    turned = jnp.transpose(tok[...], (1, 0))
    for m in range(2):
        ge_ref[m] = turned[:, 128 * m : 128 * (m + 1)]
    for j in range(3):
        lo = jnp.transpose(dzo[j].astype(bf16), (1, 0))
        lf = jnp.transpose(dzf[j].astype(bf16), (1, 0))
        for m in range(2):
            cols = slice(D * m, D * (m + 1))
            gp_ref[m, 128 * j : 128 * (j + 1)] = mm(lo, own_ref[:, cols]) + mm(lf, far_ref[:, cols])


def patch_grad(inv, mix, dz, own, far, gv0, gv1, gve):
    shapes = [(2, D, D), (2, D, 128)]
    return pl.pallas_call(
        patch_grad_kernel,
        grid=(1,),
        in_specs=[pl.BlockSpec(memory_space=pltpu.SMEM)] * 2
        + [full_spec(a.shape) for a in (dz, own, far, gv0, gv1, gve)],
        out_specs=[full_spec(s) for s in shapes],
        out_shape=[jax.ShapeDtypeStruct(s, f32) for s in shapes],
        scratch_shapes=[
            pltpu.VMEM((3, own.shape[0], 128), f32),
            pltpu.VMEM((3, far.shape[0], 128), f32),
            pltpu.VMEM((256, D), f32),
        ],
        compiler_params=pltpu.CompilerParams(vmem_limit_bytes=56 * MIB),
        name="patch_gradient",
    )(inv, mix, dz, own, far, gv0, gv1, gve)


def link_orders(bits):
    far = [b for b in (range(1, bits, 2) if bits == 6 else [3]) if b < bits]
    near = [b for b in range(bits) if b not in far]
    return [near[i:] + near[:i] for i in range(len(near))], far


def chunk_plan(bits, gather):
    near, far = link_orders(bits)
    cuts = [0, 2048, 4096, COLS]
    plan = []
    for i in range(3):
        order = near[i % len(near)]
        order = far + order if gather else order + far
        plan.append((cuts[i], cuts[i + 1] - cuts[i], order))
    return plan


def mesh_place():
    return lax.axis_index("dp"), lax.axis_index("mp")


def bit_of(value, bit):
    return (value // 2**bit) % 2


def flipped(value, bit):
    return value + 2**bit * (1 - 2 * bit_of(value, bit))


def meet(bits):
    dp, mp = mesh_place()
    barrier = pltpu.get_barrier_semaphore()
    for peer in [(dp, 1 - mp)] + [(flipped(dp, b), mp) for b in range(bits)]:
        pl.semaphore_signal(barrier, inc=1, device_id=peer, device_id_type=MESH)
    pl.semaphore_wait(barrier, bits + 1)


def push(src, dst, send, recv, peer):
    copy = pltpu.make_async_remote_copy(
        src_ref=src, dst_ref=dst, send_sem=send, recv_sem=recv, device_id=peer, device_id_type=MESH
    )
    copy.start()
    return copy


def gather_kernel(
    bits, tab_ref, sh_ref, sb_ref, w_ref, sbo_ref, tabr, stage, s_loc, s_tab, s_send, s_recv, f_send, f_recv
):
    dp, mp = mesh_place()
    mate = (dp, 1 - mp)
    plan = chunk_plan(bits, True)
    small = tab_ref.shape[1]

    def part(col, width, done=(), flip=None):
        idx = [mp]
        for b in reversed(range(bits)):
            mine = bit_of(dp, b)
            idx.append(pl.ds(0, 2) if b in done else (1 - mine if b == flip else mine))
        return w_ref.at[tuple(idx) + (slice(None), pl.ds(col, width))]

    meet(bits)
    c_tab = push(tab_ref.at[1 - mp], tabr, s_tab.at[0], s_tab.at[1], mate)
    c_sb = push(sb_ref, sbo_ref.at[mp], s_tab.at[2], s_tab.at[3], mate)
    l_sb = pltpu.make_async_copy(sb_ref, sbo_ref.at[mp], s_loc.at[0])
    l_sh = pltpu.make_async_copy(sh_ref, part(T_COLS, COLS - T_COLS), s_loc.at[1])
    l_sb.start()
    l_sh.start()
    c_tab.wait()
    mine = tab_ref[mp].astype(f32)
    other = tabr[...].astype(f32)
    first = jnp.where(mp == 0, mine, other)
    second = jnp.where(mp == 0, other, mine)
    stage[...] = jnp.concatenate([first, second], 0).astype(bf16)
    l_tab = pltpu.make_async_copy(stage, part(0, T_COLS), s_loc.at[2])
    l_tab.start()
    l_sh.wait()
    l_tab.wait()
    copies = {}
    forwards = []
    for s in range(bits + 1):
        for c, (col, width, order) in enumerate(plan):
            if s:
                copies[c, s - 1].wait_recv()
            if s < bits:
                held = part(col, width, order[:s])
                copies[c, s] = push(
                    held, held, s_send.at[c, s], s_recv.at[c, s], (flipped(dp, order[s]), mp)
                )
            got = part(col, width, order[: s - 1], order[s - 1]) if s else part(col, width)
            forwards.append(push(got, got, f_send.at[c, s], f_recv.at[c, s], mate))
    for copy in forwards:
        copy.wait()
    for copy in copies.values():
        copy.wait_send()
    c_sb.wait()
    l_sb.wait()


def gather(tab, shard, sb, n_data):
    bits = n_data.bit_length() - 1
    rows = D // n_data
    chunks = 3
    sems = pltpu.SemaphoreType.DMA
    anywhere = pl.BlockSpec(memory_space=pl.ANY)
    inside = pl.BlockSpec(memory_space=pltpu.VMEM)
    w, sbo = pl.pallas_call(
        functools.partial(gather_kernel, bits),
        in_specs=[inside, anywhere, inside],
        out_specs=[anywhere, inside],
        out_shape=[
            jax.ShapeDtypeStruct((2,) * (bits + 1) + (rows, COLS), bf16),
            jax.ShapeDtypeStruct((2,) + sb.shape, f32),
        ],
        scratch_shapes=[
            pltpu.VMEM(tab.shape[1:], bf16),
            pltpu.VMEM((rows, T_COLS), bf16),
            sems((3,)),
            sems((4,)),
            sems((chunks, bits)),
            sems((chunks, bits)),
            sems((chunks, bits + 1)),
            sems((chunks, bits + 1)),
        ],
        compiler_params=pltpu.CompilerParams(
            collective_id=0, has_side_effects=True, vmem_limit_bytes=32 * MIB
        ),
        name="gather_weights",
    )(tab, shard, sb)
    return w.reshape(2, D, COLS), sbo


def reduce_kernel(bits, *refs):
    srcs = refs[:7]
    bun_ref = refs[7]
    ot_ref, oa_ref, obun_ref = refs[8:11]
    msend, mrecv, acc, tsend, bun, bunr, sq, sqr = refs[11:19]
    plan = chunk_plan(bits, False)
    nst = 3 * bits
    sbufs = refs[19 : 19 + nst]
    rbufs = refs[19 + nst : 19 + 2 * nst]
    m_sem, s_sem, r_sem, b_sem, q_sem, t_sem = refs[19 + 2 * nst :]
    dp, mp = mesh_place()
    mate = (dp, 1 - mp)
    blocks = 2**bits
    rows = D // blocks
    small = ot_ref.shape[1]

    meet(bits)

    segs = []
    at = 0
    for ref in srcs:
        segs.append((at, ref.shape[-1], ref))
        at += ref.shape[-1]

    group = max(rows, 24)
    per = group // rows

    def over_blocks(body):
        def step(b, carry):
            body(b)
            return carry

        lax.fori_loop(0, D // group, step, 0)

    def piece(ref, half, b, lo, hi):
        return ref[half, pl.ds(pl.multiple_of(b * group, group), group), lo:hi]

    mcopies = []
    bun[...] = bun_ref[...]
    cb = push(bun, bunr.at[0], b_sem.at[0, 0], b_sem.at[0, 1], mate)
    for c, (col, width, order) in enumerate(plan):

        def body(b):
            for at, size, ref in segs:
                lo, hi = max(at, col), min(at + size, col + width)
                if lo < hi:
                    got = piece(ref, 1 - mp, b, lo - at, hi - at)
                    for i in range(per):
                        msend[b * per + i, :, lo:hi] = got[rows * i : rows * (i + 1)].astype(bf16)

        over_blocks(body)
        cut = (slice(None), slice(None), pl.ds(col, width))
        mcopies.append(push(msend.at[cut], mrecv.at[cut], m_sem.at[c, 0], m_sem.at[c, 1], mate))

    def block_index(free, fixed):
        def index(t):
            total = fixed
            for j, b in enumerate(free):
                total = total + ((t // 2**j) % 2) * 2**b
            return total

        return index

    copies = {}

    def send_stage(c, s):
        col, width, order = plan[c]
        free = [b for b in range(bits) if b not in order[: s + 1]]
        fixed = sum(bit_of(dp, b) * 2**b for b in order[:s])
        fixed = fixed + (1 - bit_of(dp, order[s])) * 2 ** order[s]
        index = block_index(free, fixed)
        sbuf = sbufs[c * bits + s]

        def step(t, carry):
            sbuf[t] = acc[index(t), :, col : col + width].astype(bf16)
            return carry

        lax.fori_loop(0, 2 ** len(free), step, 0)
        copies[c, s] = push(
            sbuf,
            rbufs[c * bits + s],
            s_sem.at[c, s],
            r_sem.at[c, s],
            (flipped(dp, order[s]), mp),
        )

    def take_stage(c, s):
        col, width, order = plan[c]
        copies[c, s].wait_recv()
        free = [b for b in range(bits) if b not in order[: s + 1]]
        fixed = sum(bit_of(dp, b) * 2**b for b in order[: s + 1])
        index = block_index(free, fixed)
        rbuf = rbufs[c * bits + s]

        def step(t, carry):
            acc[index(t), :, col : col + width] += rbuf[t].astype(f32)
            return carry

        lax.fori_loop(0, 2 ** len(free), step, 0)

    for c, (col, width, order) in enumerate(plan):
        mcopies[c].wait_recv()

        def body(b):
            for at, size, ref in segs:
                lo, hi = max(at, col), min(at + size, col + width)
                if lo < hi:
                    got = piece(ref, mp, b, lo - at, hi - at)
                    for i in range(per):
                        acc[b * per + i, :, lo:hi] = got[rows * i : rows * (i + 1)] + mrecv[
                            b * per + i, :, lo:hi
                        ].astype(f32)

        over_blocks(body)
        send_stage(c, 0)
    bcopies = [cb]
    for s in range(1, bits + 1):
        for c in range(3):
            take_stage(c, s - 1)
            if s < bits:
                send_stage(c, s)
        bcopies[-1].wait()
        bun[...] = bun[...] + bunr[s - 1]
        bcopies.append(
            push(bun, bunr.at[s], b_sem.at[s, 0], b_sem.at[s, 1], (flipped(dp, s - 1), mp))
        )
    mine = acc[dp]
    oa_ref[...] = mine[:, T_COLS:]
    tab = mine[:, :T_COLS]
    tsend[0] = jnp.where(mp == 0, tab[small:], tab[:small])
    ct = push(tsend.at[0], tsend.at[1], t_sem.at[0], t_sem.at[1], mate)
    ot_ref[mp] = jnp.where(mp == 0, tab[:small], tab[small:])
    ct.wait()
    ot_ref[1 - mp] = tsend[1]
    bcopies[-1].wait()
    obun_ref[0 : bun.shape[0]] = bun[...] + bunr[bits]
    own = jnp.sum(ot_ref[0] * ot_ref[0], keepdims=True) + jnp.sum(
        ot_ref[1] * ot_ref[1], keepdims=True
    )
    own = own + jnp.sum(oa_ref[...] * oa_ref[...], keepdims=True)
    sq[0] = jnp.broadcast_to(own, (8, 128))
    for s in range(bits + 1):
        peer = mate if s == 0 else (flipped(dp, s - 1), mp)
        copy = push(sq.at[s], sqr.at[s], q_sem.at[s, 0], q_sem.at[s, 1], peer)
        copy.wait()
        sq[s + 1] = sq[s] + sqr[s]
    obun_ref[bun.shape[0] :] = sq[bits + 1]
    for copy in mcopies:
        copy.wait_send()
    for copy in copies.values():
        copy.wait_send()


def reduce_all(srcs, bundle, n_data):
    bits = n_data.bit_length() - 1
    rows = D // n_data
    small = rows // 2
    blocks = n_data
    plan = chunk_plan(bits, False)
    sems = pltpu.SemaphoreType.DMA
    inside = pl.BlockSpec(memory_space=pltpu.VMEM)
    bufs = [
        pltpu.VMEM((2 ** (bits - 1 - s), rows, width), bf16)
        for _, width, _ in plan
        for s in range(bits)
    ]
    return pl.pallas_call(
        functools.partial(reduce_kernel, bits),
        in_specs=[inside] * 8,
        out_specs=[inside] * 3,
        out_shape=[
            jax.ShapeDtypeStruct((2, small, T_COLS), f32),
            jax.ShapeDtypeStruct((rows, COLS - T_COLS), f32),
            jax.ShapeDtypeStruct((bundle.shape[0] + 8, 128), f32),
        ],
        scratch_shapes=[
            pltpu.VMEM((blocks, rows, COLS), bf16),
            pltpu.VMEM((blocks, rows, COLS), bf16),
            pltpu.VMEM((blocks, rows, COLS), f32),
            pltpu.VMEM((2, small, T_COLS), f32),
            pltpu.VMEM(bundle.shape, f32),
            pltpu.VMEM((bits + 1,) + bundle.shape, f32),
            pltpu.VMEM((bits + 2, 8, 128), f32),
            pltpu.VMEM((bits + 1, 8, 128), f32),
        ]
        + bufs
        + bufs
        + [
            sems((3, 2)),
            sems((3, bits)),
            sems((3, bits)),
            sems((bits + 1, 2)),
            sems((bits + 1, 2)),
            sems((2,)),
        ],
        compiler_params=pltpu.CompilerParams(
            collective_id=1, has_side_effects=True, vmem_limit_bytes=62 * MIB
        ),
        name="reduce_gradients",
    )(*srcs, bundle)


def adamw(master, first, second, gradient, rate, decay):
    first = beta_one * first + (1.0 - beta_one) * gradient
    second = beta_two * second + (1.0 - beta_two) * gradient * gradient
    first_hat = first / (1.0 - beta_one**STEP)
    second_hat = second / (1.0 - beta_two**STEP)
    master = master - rate * (first_hat / (jnp.sqrt(second_hat) + adam_eps) + decay * master)
    return (master, first, second)


def pack_tables(tab, vec):
    small = tab.shape[0]
    token = tab[:, PD : PD + TOK]
    seg = jnp.concatenate(
        [
            token[:, 2:],
            token[:, :2],
            jnp.zeros((small, TP - TOK), f32),
            vec,
            jnp.zeros((small, 256 - TP - vec.shape[1]), f32),
        ],
        1,
    )
    heads = jnp.pad(tab[:, PD + TOK :].reshape(small, 2, CLS), ((0, 0), (0, 0), (0, 1024 - CLS)))
    parts = [tab[:, :PD], seg, heads[:, 0], heads[:, 1]]
    return [
        jnp.concatenate([x[:, x.shape[1] // 2 * m : x.shape[1] // 2 * (m + 1)] for x in parts], 1)
        for m in range(2)
    ]


def unpack_tables(halves):
    cuts = (0, D, D + 128, 1024, T_COLS)
    segs = [
        jnp.concatenate([halves[m][:, cuts[i] : cuts[i + 1]] for m in range(2)], 1)
        for i in range(4)
    ]
    token = segs[1]
    tab = jnp.concatenate(
        [
            segs[0],
            token[:, PATCHES:TOK],
            token[:, :PATCHES],
            segs[2][:, :CLS],
            segs[3][:, :CLS],
        ],
        1,
    )
    return tab, token[:, TP : TP + 6 * LAYERS + 2]


def pack_attention(attn):
    layers, rows, _ = attn.shape
    a = attn.reshape(layers, rows, 3, 4, HD)
    two = a[:, :, :2].transpose(0, 1, 3, 2, 4).reshape(layers, rows, 512)
    one = a[:, :, 2].reshape(layers, rows, 256)
    return jnp.concatenate([two, one], -1)


def unpack_attention(packed):
    layers, rows, _ = packed.shape
    two = packed[..., :512].reshape(layers, rows, 4, 2, HD).transpose(0, 1, 3, 2, 4)
    one = packed[..., 512:].reshape(layers, rows, 1, 4, HD)
    return jnp.concatenate([two, one], 2).reshape(layers, rows, 768)


PAIRS = (0, 1, 3, 4, 2, 5)


def shards(
    pixels,
    labels,
    teacher,
    partner,
    mix_weight,
    class_weight,
    tables,
    tables_first,
    tables_second,
    vectors,
    vectors_first,
    vectors_second,
    attention,
    attention_first,
    attention_second,
    feedforward,
    feedforward_first,
    feedforward_second,
    split_bias,
    split_bias_first,
    split_bias_second,
    head_bias,
    head_bias_first,
    head_bias_second,
):
    n_data = lax.axis_size("dp")
    dp, mp = mesh_place()
    images_here = pixels.shape[0]
    count = images_here // 2
    rows = D // n_data
    far_rank = (dp + n_data // 2) % n_data
    far_pairs = [(i, (i + n_data // 2) % n_data) for i in range(n_data)]
    pix = pixels.transpose(1, 0, 2)
    far_ids = mp * count + jnp.arange(count, dtype=jnp.int32)
    match = (partner - far_rank * images_here)[None, :] == far_ids[:, None]
    inv = jnp.sum(
        jnp.where(match, jnp.arange(images_here, dtype=jnp.int32)[None, :], 0), 1
    ).astype(jnp.int32)
    mix = jnp.sum(jnp.where(match, mix_weight[None, :], 0.0), 1)
    own_lab = jnp.take(labels, dp * images_here + inv)
    far_lab = lax.dynamic_slice_in_dim(labels, far_rank * images_here + mp * count, count, 0)
    own_teach = jnp.sum(jnp.where(match, teacher[None, :], 0), 1).astype(jnp.int32)
    labs = jnp.stack([own_lab, far_lab, own_teach], 1)
    lws = jnp.take(class_weight, labs) * jnp.stack([mix, 1.0 - mix, jnp.ones_like(mix)], 1)
    labs = jnp.pad(labs, ((0, 0), (0, 125)))
    lws = jnp.pad(lws, ((0, 0), (0, 125)))

    tab_halves = pack_tables(tables.T, vectors.T)
    tab = jnp.stack(tab_halves).astype(bf16)
    shard = jnp.concatenate(
        [
            pack_attention(attention).transpose(1, 0, 2).reshape(rows, -1),
            feedforward.transpose(1, 0, 2, 3).reshape(rows, -1),
        ],
        1,
    ).astype(bf16)
    weights, sb = gather(tab, shard, split_bias, n_data)
    sb = sb.astype(bf16).astype(f32)
    qv = sb[:, :, :D].transpose(1, 0, 2).reshape(LAYERS, HEADS, 2, HD)[:, jnp.array(PAIRS)]
    bias = qv.transpose(0, 2, 1, 3).reshape(LAYERS, 2 * D)
    bias = jnp.pad(bias, ((0, 8 - LAYERS), (0, 0)))
    ub = jnp.pad(sb[:, :, D:].transpose(1, 0, 2).reshape(LAYERS, FF), ((0, 8 - LAYERS), (0, 0)))
    hb = jnp.pad(
        head_bias.astype(bf16).astype(f32).reshape(2, CLS),
        ((0, 0), (0, 1024 - CLS)),
        constant_values=-1e30,
    ).reshape(1, -1)
    hb = jnp.pad(hb, ((0, 7), (0, 0)))

    base = jnp.reshape(mp * count, (1,)).astype(jnp.int32)
    pix_flat = pix.reshape(PATCHES * images_here, PD)
    own, send = embed(inv, base, pix_flat, weights, count)
    far = lax.ppermute(send, "dp", far_pairs)
    pix_mine = lax.dynamic_slice_in_dim(pix, mp * count, count, 1)
    pix_mine, far = lax.optimization_barrier((pix_mine, far))
    pix_far = lax.ppermute(pix_mine, "dp", far_pairs)
    outs = forward(mix, own, far, weights, bias, ub)
    kept, tail, tok = outs[: 7 * LAYERS], outs[7 * LAYERS], outs[7 * LAYERS + 1]
    tail = tail.reshape(count, 16, D)
    ends = jnp.stack([tail[:, PATCHES - 192], tail[:, PATCHES - 191]])
    v_end = TP + 6 * LAYERS
    dh, dx, gve, dhb, stat = head(
        ends, weights[:, :, 512:T_COLS], hb, labs, lws, tok[v_end : v_end + 8]
    )
    dz = jnp.zeros((count, TP, D), f32)
    dz = dz.at[:, PATCHES].set(dx[0]).at[:, PATCHES + 1].set(dx[1]).reshape(count * TP, D)
    grads = [None] * LAYERS
    for layer in reversed(range(LAYERS)):
        v0 = TP + 6 * layer
        dz, *grads[layer] = backward(
            layer, dz, kept[7 * layer : 7 * layer + 7], weights, tok[v0 : v0 + 8]
        )
    gp, ge = patch_grad(
        inv,
        mix,
        dz,
        pix_flat,
        pix_far.reshape(PATCHES * count, PD),
        grads[0][2],
        grads[1][2],
        gve,
    )
    biases = []
    for layer in range(LAYERS):
        gb, gu = grads[layer][3][0], grads[layer][4][0]
        biases += [gb[:D], gb[2 * D :], gu]
    bundle = jnp.concatenate([stat[0]] + biases + [dhb[0]]).reshape(-1, 128)
    lines = bundle.shape[0]
    bundle = jnp.pad(bundle, ((0, -lines % 8), (0, 0)))
    srcs = [gp, ge, dh, grads[0][0], grads[1][0], grads[0][1], grads[1][1]]
    g_tab, g_main, info = reduce_all(srcs, bundle, n_data)
    flat = info.reshape(-1)
    loss_sum, weight_sum = flat[0], flat[1]
    squares = info[bundle.shape[0], 0]
    at = 128
    g_split = []
    for layer in range(LAYERS):
        q = flat[at : at + D].reshape(3, 2, HD)
        v = flat[at + D : at + 2 * D].reshape(3, 2, HD)
        up = lax.dynamic_slice_in_dim(flat[at + 2 * D : at + 2 * D + FF], mp * HALF, HALF, 0)
        at += 2 * D + FF
        qv = jnp.stack([q, v], 2)
        pick = lax.dynamic_index_in_dim(
            jnp.stack(
                [
                    jnp.stack([qv[0, 0], qv[0, 1], qv[2, 0]]),
                    jnp.stack([qv[1, 0], qv[1, 1], qv[2, 1]]),
                ]
            ),
            mp,
            0,
            False,
        )
        g_split.append(jnp.concatenate([pick.reshape(-1), up]))
    g_split = jnp.stack(g_split)
    g_head = flat[at : at + 2048].reshape(2, 1024)[:, :CLS].reshape(-1)
    every = flat[128 : at + 2048]
    squares = squares + jnp.sum(every * every)
    g_tables, g_vectors = unpack_tables(g_tab)
    g_attention = unpack_attention(
        g_main[:, : 768 * LAYERS].reshape(rows, LAYERS, 768).transpose(1, 0, 2)
    )
    g_feedforward = (
        g_main[:, 768 * LAYERS :].reshape(rows, LAYERS, 2, HALF).transpose(1, 0, 2, 3)
    )
    grad_norm = jnp.sqrt(squares) / weight_sum
    factor = jnp.minimum(1.0, clip_limit / grad_norm) / weight_sum
    t_new, t_one, t_two = (
        x.T
        for x in adamw(
            tables.T,
            tables_first.T,
            tables_second.T,
            g_tables * factor,
            matrix_rate,
            matrix_decay,
        )
    )
    v_new, v_one, v_two = (
        x.T
        for x in adamw(
            vectors.T, vectors_first.T, vectors_second.T, g_vectors * factor, vector_rate, 0.0
        )
    )
    a_new, a_one, a_two = adamw(
        attention,
        attention_first,
        attention_second,
        g_attention * factor,
        matrix_rate,
        matrix_decay,
    )
    f_new, f_one, f_two = adamw(
        feedforward,
        feedforward_first,
        feedforward_second,
        g_feedforward * factor,
        matrix_rate,
        matrix_decay,
    )
    s_new, s_one, s_two = adamw(
        split_bias, split_bias_first, split_bias_second, g_split * factor, vector_rate, 0.0
    )
    h_new, h_one, h_two = adamw(
        head_bias, head_bias_first, head_bias_second, g_head * factor, vector_rate, 0.0
    )
    return (
        loss_sum,
        weight_sum,
        grad_norm,
        t_new,
        t_one,
        t_two,
        t_new.astype(bf16),
        v_new,
        v_one,
        v_two,
        a_new,
        a_one,
        a_two,
        a_new.astype(bf16),
        f_new,
        f_one,
        f_two,
        f_new.astype(bf16),
        s_new,
        s_one,
        s_two,
        h_new,
        h_one,
        h_two,
    )


def solution(mesh):
    table = P(None, ("dp", "mp"))
    attn = P(None, "dp", "mp")
    ffw = P(None, "dp", None, "mp")
    split = P(None, "mp")
    return jax.shard_map(
        shards,
        mesh=mesh,
        in_specs=(P("dp", None, None), P(), P("dp"), P("dp"), P("dp"), P())
        + (table,) * 6
        + (attn,) * 3
        + (ffw,) * 3
        + (split,) * 3
        + (P(),) * 3,
        out_specs=(P(),) * 3
        + (table,) * 7
        + (attn,) * 4
        + (ffw,) * 4
        + (split,) * 3
        + (P(),) * 3,
        check_vma=False,
    )
```

```python
import functools

import jax
import jax.numpy as jnp
from jax import lax
from jax.experimental import pallas as pl
from jax.experimental.pallas import tpu as pltpu
from jax.sharding import PartitionSpec as P

D = 384
HEADS = 6
HD = 64
FF = 1536
CLS = 1000
PD = 768
PATCHES = 196
LAYERS = 2
STEP = 10
TOK = 198
TP = 208
GRP = 2
ROWS = GRP * TP
HALF = FF // 2
COLS = 6144
T_COLS = 1536
F_COLS = 512
REDUCE_CUTS = (0, 2048, 4096, COLS)
MAIN_WIDTHS = (768, 768, 768, 768, 768, 768, 1024)
MAIN_TURNS = (0, 0, 0, 1, 0, 1, 1)
FRONT_WIDTHS = (384, 128)
FRONT_TURNS = (0, 1)
M_COLS = 4608
MIB = 1 << 20
NORM_ROWS = ROWS
GELU_ROWS = 32

norm_eps = 1e-06
clip_limit = 0.02
beta_one = 0.9
beta_two = 0.999
adam_eps = 1e-08
matrix_rate = 0.08
vector_rate = 0.5
matrix_decay = 0.05

f32 = jnp.float32
bf16 = jnp.bfloat16
MESH = pl.DeviceIdType.MESH
AB = ((1,), (0,))
ABT = ((1,), (1,))
ATB = ((0,), (0,))


def mm(left, right, dims=AB):
    return lax.dot_general(left, right, (dims, ((), ())), preferred_element_type=f32)


def full_spec(shape):
    return pl.BlockSpec(shape, lambda *_: (0,) * len(shape), pipeline_mode=pl.Buffered(1))


def row_loop(total, chunk, body):
    def step(index, carry):
        body(pl.ds(pl.multiple_of(index * chunk, chunk), chunk))
        return carry

    if total == chunk:
        body(slice(0, total))
    else:
        lax.fori_loop(0, total // chunk, step, 0)


def center(x):
    mean = jnp.mean(x, -1, keepdims=True)
    xc = x - mean
    scale = lax.rsqrt(jnp.mean(xc * xc, -1, keepdims=True) + norm_eps)
    return xc * scale, scale


def gelu_pair(x):
    z = x * 0.7071067811865476
    e = jnp.exp(-(z * z))
    den = 1.0 + 0.3275911 * jnp.abs(z)
    r = pl.reciprocal(den, approx=True)
    r = r * (2.0 - den * r)
    poly = r * (
        0.127414796
        + r * (-0.142248368 + r * (0.7107068705 + r * (-0.7265760135 + r * 0.5307027145)))
    )
    tail = poly * e
    cdf = jnp.where(x > 0.0, 1.0 - tail, tail)
    return x * cdf, cdf + x * (e * 0.3989422804014327)


def embed_kernel(inv_ref, base_ref, pix_ref, w_ref, own_ref, send_ref, flat):
    rows = pix_ref.shape[0]
    count = rows // PATCHES
    chunk = rows // 7
    for c in range(7):
        pix = pix_ref[c * chunk : (c + 1) * chunk]
        out = mm(pix[:, :D], w_ref[0], ABT) + mm(pix[:, D:], w_ref[1], ABT)
        for j in range(3):
            flat[j, c * chunk : (c + 1) * chunk] = out[:, 128 * j : 128 * (j + 1)]
    for k in range(own_ref.shape[0]):
        for j in range(3):
            cols = slice(128 * j, 128 * (j + 1))
            own_ref[k, :, cols] = flat[j, pl.ds(inv_ref[k], PATCHES, stride=count), :]
            send_ref[k, :, cols] = flat[j, pl.ds(base_ref[0] + k, PATCHES, stride=count), :].astype(
                bf16
            )


def embed(inv, base, pix, weights, count):
    return pl.pallas_call(
        embed_kernel,
        grid=(1,),
        in_specs=[
            pl.BlockSpec(memory_space=pltpu.SMEM),
            pl.BlockSpec(memory_space=pltpu.SMEM),
            full_spec(pix.shape),
            full_spec(weights.shape),
        ],
        out_specs=[full_spec((count, PATCHES, D)), full_spec((count, PATCHES, D))],
        out_shape=[
            jax.ShapeDtypeStruct((count, PATCHES, D), f32),
            jax.ShapeDtypeStruct((count, PATCHES, D), bf16),
        ],
        scratch_shapes=[pltpu.VMEM((3, pix.shape[0], 128), f32)],
        compiler_params=pltpu.CompilerParams(vmem_limit_bytes=60 * MIB),
        name="embed_images",
    )(inv, base, pix, weights)


def split_tokens(w_ref, col):
    seg = jnp.concatenate([w_ref[0, :, col : col + 128], w_ref[1, :, col : col + 128]], 1)
    return jnp.transpose(seg.astype(f32), (1, 0))


def attend(g, qkv_ref, p_ref, ho_ref):
    rows = slice(g * TP, (g + 1) * TP)
    lane = lax.broadcasted_iota(jnp.int32, (TP, 128), 1)
    key_mask = jnp.where(lax.broadcasted_iota(jnp.int32, (1, TP), 1) < TOK, 0.0, -1e30).astype(f32)
    for j in range(3):
        q = qkv_ref[rows, 128 * j : 128 * (j + 1)]
        k = qkv_ref[rows, D + 128 * j : D + 128 * (j + 1)]
        v = qkv_ref[rows, 2 * D + 128 * j : 2 * D + 128 * (j + 1)]
        outs = []
        for s in range(2):
            mine = (lane < 64) if s == 0 else (lane >= 64)
            scores = mm(jnp.where(mine, q, jnp.zeros_like(q)), k, ABT) + key_mask
            exps = jnp.exp(scores - jnp.max(scores, -1, keepdims=True))
            probs = (exps * (1.0 / jnp.sum(exps, -1, keepdims=True))).astype(bf16)
            p_ref[6 * g + 2 * j + s] = probs
            outs.append(mm(probs, v))
        ho_ref[rows, 128 * j : 128 * (j + 1)] = jnp.where(lane < 64, outs[0], outs[1]).astype(bf16)


def forward_kernel(mix_ref, own_ref, far_ref, t_ref, w_ref, bias_ref, ub_ref, *refs):
    kept = refs[: 7 * LAYERS]
    tail_ref, tok_ref = refs[7 * LAYERS : 7 * LAYERS + 2]
    qkv_w, out_w, nbuf, up_s, last = refs[7 * LAYERS + 2 :]
    step = pl.program_id(0)

    @pl.when(step == 0)
    def _():
        tok_ref[...] = split_tokens(t_ref, 0)
        for layer in range(LAYERS):
            attn_tiles(w_ref.at[layer], qkv_w.at[layer], out_w.at[layer])

    for g in range(GRP):
        w = mix_ref[step * GRP + g]
        x_ref = kept[0]
        x_ref[g * TP : g * TP + PATCHES] = (
            w * own_ref[g] + (1.0 - w) * far_ref[g].astype(f32) + tok_ref[:PATCHES]
        )
        x_ref[g * TP + PATCHES : (g + 1) * TP] = tok_ref[PATCHES:TP]
    for layer in range(LAYERS):
        x_ref, mid_ref, qkv_ref, p_ref, ho_ref, hid_ref, gp_ref = kept[7 * layer : 7 * layer + 7]
        v0 = TP + 6 * layer
        row = [tok_ref[v0 + i : v0 + i + 1] for i in range(6)]

        def norm(src, gain, shift):
            def body(rs):
                nbuf[rs] = (center(src[rs])[0] * gain + shift).astype(bf16)

            row_loop(ROWS, NORM_ROWS, body)

        norm(x_ref, row[0], row[1])
        n = nbuf[...]
        q = mm(n, qkv_w[layer, :, :D]) + bias_ref[layer : layer + 1, :D]
        qkv_ref[:, :D] = (q.astype(bf16).astype(f32) * 0.125).astype(bf16)
        qkv_ref[:, D : 2 * D] = mm(n, qkv_w[layer, :, D : 2 * D]).astype(bf16)
        v = mm(n, qkv_w[layer, :, 2 * D :]) + bias_ref[layer : layer + 1, D : 2 * D]
        qkv_ref[:, 2 * D :] = v.astype(bf16)
        for g in range(GRP):
            attend(g, qkv_ref, p_ref, ho_ref)
        mid_ref[...] = x_ref[...] + mm(ho_ref[...], out_w[layer], ABT) + row[4]
        norm(mid_ref, row[2], row[3])
        up_w, down_w = w_ref.at[LAYERS + 2 * layer], w_ref.at[LAYERS + 2 * layer + 1]
        for m in range(2):
            cols = slice(HALF * m, HALF * (m + 1))
            up_s[...] = (
                mm(nbuf[...], up_w[m]) + ub_ref[layer : layer + 1, cols]
            )

            def body(rs):
                hid, gp = gelu_pair(up_s[rs])
                hid_ref[rs, cols] = hid.astype(bf16)
                gp_ref[rs, cols] = gp.astype(bf16)

            row_loop(ROWS, GELU_ROWS, body)
        out = mid_ref[...] + row[5]
        for m in range(2):
            cols = slice(HALF * m, HALF * (m + 1))
            out = out + mm(hid_ref[:, cols], down_w[m], ABT)
        if layer + 1 < LAYERS:
            kept[7 * (layer + 1)][...] = out
        else:
            last[...] = out
            for g in range(GRP):
                tail_ref[16 * g : 16 * (g + 1)] = last[g * TP + 192 : (g + 1) * TP]


def kept_shapes(count):
    n = count * TP
    return [
        ((n, D), f32),
        ((n, D), f32),
        ((n, 3 * D), bf16),
        ((count * HEADS, TP, TP), bf16),
        ((n, D), bf16),
        ((n, FF), bf16),
        ((n, FF), bf16),
    ]


def block_of(shape, steps):
    block = (shape[0] // steps,) + tuple(shape[1:])
    return pl.BlockSpec(block, lambda i: (i,) + (0,) * (len(block) - 1))


def forward(mix, own, far, front, weights, bias, ub):
    count = own.shape[0]
    steps = count // GRP
    outs = kept_shapes(count) * LAYERS + [((count * 16, D), f32)]
    shapes = [jax.ShapeDtypeStruct(s, t) for s, t in outs] + [jax.ShapeDtypeStruct((256, D), f32)]
    specs = [block_of(s, steps) for s, _ in outs] + [full_spec((256, D))]
    return pl.pallas_call(
        forward_kernel,
        grid=(steps,),
        in_specs=[
            pl.BlockSpec(memory_space=pltpu.SMEM),
            block_of(own.shape, steps),
            block_of(far.shape, steps),
            full_spec(front.shape),
            full_spec(weights.shape),
            full_spec(bias.shape),
            full_spec(ub.shape),
        ],
        out_specs=specs,
        out_shape=shapes,
        scratch_shapes=[
            pltpu.VMEM((LAYERS, D, 3 * D), bf16),
            pltpu.VMEM((LAYERS, D, D), bf16),
            pltpu.VMEM((ROWS, D), bf16),
            pltpu.VMEM((ROWS, HALF), f32),
            pltpu.VMEM((ROWS, D), f32),
        ],
        compiler_params=pltpu.CompilerParams(vmem_limit_bytes=60 * MIB),
        name="forward_layers",
    )(mix, own, far, front, weights, bias, ub)


def norm_back(dy, xhat, scale, gain):
    dyg = dy * gain
    c1 = jnp.mean(dyg, -1, keepdims=True)
    c2 = jnp.mean(dyg * xhat, -1, keepdims=True)
    return scale * (dyg - c1 - xhat * c2)


def head_kernel(
    rows_ref, w_ref, hb_ref, lab_ref, lw_ref, vec_ref, dh_ref, dx_ref, dv_ref, dhb_ref, stat_ref
):
    gain, shift = vec_ref[0:1], vec_ref[1:2]
    loss = jnp.zeros((1, 1), f32)
    weight = jnp.zeros((1, 1), f32)
    dgain = jnp.zeros((1, D), f32)
    dshift = jnp.zeros((1, D), f32)
    count = rows_ref.shape[1]
    for h in range(2):
        xhat, scale = center(rows_ref[h])
        final = (xhat * gain + shift).astype(bf16)
        halves = []
        for m in range(2):
            wh = w_ref[m, :, 512 * h : 512 * (h + 1)]
            at = 1024 * h + 512 * m
            logits = mm(final, wh) + hb_ref[0:1, at : at + 512]
            ids = lax.broadcasted_iota(jnp.int32, (count, 512), 1) + 512 * m
            coef = jnp.where(ids == lab_ref[:, 2 * h : 2 * h + 1], lw_ref[:, 2 * h : 2 * h + 1], 0.0)
            if h == 0:
                coef = coef + jnp.where(ids == lab_ref[:, 1:2], lw_ref[:, 1:2], 0.0)
            halves.append((wh, logits, coef))
        top = jnp.maximum(*[jnp.max(x[1], -1, keepdims=True) for x in halves])
        exps = [jnp.exp(x[1] - top) for x in halves]
        total = sum(jnp.sum(x, -1, keepdims=True) for x in exps)
        lse = top + jnp.log(total)
        csum = sum(jnp.sum(x[2], -1, keepdims=True) for x in halves)
        dfinal = jnp.zeros((count, D), f32)
        for m in range(2):
            wh, logits, coef = halves[m]
            loss = loss + jnp.sum(jnp.sum(coef * (lse - logits), -1, keepdims=True), 0, keepdims=True)
            dl = csum * (exps[m] / total) - coef
            at = 1024 * h + 512 * m
            dhb_ref[0:1, at : at + 512] = jnp.sum(dl, 0, keepdims=True)
            low = dl.astype(bf16)
            dh_ref[m, :, 512 * h : 512 * (h + 1)] = mm(final, low, ATB)
            dfinal = dfinal + mm(low, wh, ABT)
        weight = weight + jnp.sum(csum, 0, keepdims=True)
        dx_ref[h] = norm_back(dfinal, xhat, scale, gain)
        dgain = dgain + jnp.sum(dfinal * xhat, 0, keepdims=True)
        dshift = dshift + jnp.sum(dfinal, 0, keepdims=True)
    dv_ref[...] = jnp.zeros_like(dv_ref)
    dv_ref[0:1] = dgain
    dv_ref[1:2] = dshift
    which = lax.broadcasted_iota(jnp.int32, stat_ref.shape, 1)
    stat_ref[...] = jnp.where(which == 0, loss, jnp.where(which == 1, weight, 0.0))


def head(rows, weights, hb, labs, lws, vec):
    count = rows.shape[1]
    shapes = [(2, D, 1024), (2, count, D), (8, D), (8, 2048), (8, 128)]
    return pl.pallas_call(
        head_kernel,
        grid=(1,),
        in_specs=[
            full_spec(rows.shape),
            full_spec(weights.shape),
            full_spec(hb.shape),
            full_spec(labs.shape),
            full_spec(lws.shape),
            full_spec(vec.shape),
        ],
        out_specs=[full_spec(s) for s in shapes],
        out_shape=[jax.ShapeDtypeStruct(s, f32) for s in shapes],
        compiler_params=pltpu.CompilerParams(vmem_limit_bytes=48 * MIB),
        name="loss_heads",
    )(rows, weights, hb, labs, lws, vec)


def attend_back(g, dho, qkv_ref, p_ref, dproj):
    rows = slice(g * TP, (g + 1) * TP)
    lane = lax.broadcasted_iota(jnp.int32, (TP, 128), 1)
    for j in range(3):
        q = qkv_ref[rows, 128 * j : 128 * (j + 1)]
        k = qkv_ref[rows, D + 128 * j : D + 128 * (j + 1)]
        v = qkv_ref[rows, 2 * D + 128 * j : 2 * D + 128 * (j + 1)]
        do = dho[rows, 128 * j : 128 * (j + 1)]
        qt, kt, dot_ = (jnp.transpose(a, (1, 0)) for a in (q, k, do))
        for s in range(2):
            mine = (lane < 64) if s == 0 else (lane >= 64)
            sub = slice(64 * s, 64 * (s + 1))
            at = 128 * j + 64 * s
            probs = p_ref[6 * g + 2 * j + s]
            dproj[g, 2 * D + at : 2 * D + at + 64] = mm(dot_[sub], probs).astype(bf16)
            dprob = mm(jnp.where(mine, do, jnp.zeros_like(do)), v, ABT)
            p32 = probs.astype(f32)
            delta = jnp.sum(dprob * p32, -1, keepdims=True)
            ds = (p32 * (dprob - delta)).astype(bf16)
            dproj[g, at : at + 64] = (mm(kt[sub], ds, ABT) * 0.125).astype(bf16)
            dproj[g, D + at : D + at + 64] = mm(qt[sub], ds).astype(bf16)


def backward_kernel(
    dz_ref,
    x_ref,
    mid_ref,
    qkv_ref,
    p_ref,
    ho_ref,
    hid_ref,
    gp_ref,
    wa_ref,
    wf_ref,
    vec_ref,
    dzo_ref,
    ga_ref,
    gf_ref,
    gv_ref,
    gb_ref,
    gu_ref,
    qkv_w,
    out_w,
    dqkv,
    dout,
    nbuf,
    dz,
    dn,
    du,
    dproj,
):
    step = pl.program_id(0)
    gain1, shift1, gain2, shift2 = (vec_ref[i : i + 1] for i in range(4))

    @pl.when(step == 0)
    def _():
        gf_ref[...] = jnp.zeros_like(gf_ref)
        gv_ref[...] = jnp.zeros_like(gv_ref)
        gu_ref[...] = jnp.zeros_like(gu_ref)
        dqkv[...] = jnp.zeros_like(dqkv)
        dout[...] = jnp.zeros_like(dout)
        attn_tiles(wa_ref.at[0], qkv_w, out_w)

    def norm(src, gain, shift):
        def body(rs):
            nbuf[rs] = (center(src[rs])[0] * gain + shift).astype(bf16)

        row_loop(ROWS, NORM_ROWS, body)

    norm(mid_ref, gain2, shift2)
    gv_ref[5:6] += jnp.sum(dz_ref[...], 0, keepdims=True)
    rz = dz_ref[...].astype(bf16)
    rzt = jnp.transpose(rz, (1, 0))
    nt = jnp.transpose(nbuf[...], (1, 0))
    for m in range(2):
        cols = slice(HALF * m, HALF * (m + 1))
        dh = mm(rz, wf_ref[1, m])
        du_val = dh.astype(bf16).astype(f32) * gp_ref[:, cols].astype(f32)
        du[...] = du_val.astype(bf16)
        gu_ref[0:1, cols] += jnp.sum(du[...].astype(f32), 0, keepdims=True)
        gf_ref[m, :, HALF:] += mm(rzt, hid_ref[:, cols])
        gf_ref[m, :, :HALF] += mm(nt, du[...])
        part = mm(du[...], wf_ref[0, m], ABT)
        dn[...] = part if m == 0 else dn[...] + part

    def pull(src, gain, dz_in, dz_out, at):
        def body(rs, carry):
            dg, db, total = carry
            rs = pl.ds(pl.multiple_of(rs * NORM_ROWS, 8), NORM_ROWS)
            xhat, scale = center(src[rs])
            dy = dn[rs]
            new = dz_in[rs] + norm_back(dy, xhat, scale, gain)
            dz_out[rs] = new
            return (
                dg + jnp.sum(dy * xhat, 0, keepdims=True),
                db + jnp.sum(dy, 0, keepdims=True),
                total + jnp.sum(new, 0, keepdims=True),
            )

        zero = jnp.zeros((1, D), f32)
        dg, db, total = lax.fori_loop(0, ROWS // NORM_ROWS, body, (zero, zero, zero))
        gv_ref[at : at + 1] += jnp.sum(dg, 0, keepdims=True)
        gv_ref[at + 1 : at + 2] += jnp.sum(db, 0, keepdims=True)
        return total

    total = pull(mid_ref, gain2, dz_ref, dz, 2)
    gv_ref[4:5] += jnp.sum(total, 0, keepdims=True)
    rz2 = dz[...].astype(bf16)
    dout[...] += mm(jnp.transpose(rz2, (1, 0)), ho_ref[...])
    dho = mm(rz2, out_w[...]).astype(bf16)
    norm(x_ref, gain1, shift1)
    ones = jnp.ones((TP, 128), bf16)
    for g in range(GRP):
        rows = slice(g * TP, (g + 1) * TP)
        attend_back(g, dho, qkv_ref, p_ref, dproj)
        dqkv[:, :D] += mm(dproj[g], nbuf[rows])
        dqkv[:, D:] += mm(dproj[g], ones)
        dn[rows] = jnp.transpose(mm(qkv_w[...], dproj[g]), (1, 0))
    pull(x_ref, gain1, dz, dzo_ref, 0)

    @pl.when(step == pl.num_programs(0) - 1)
    def _():
        for t in range(4):
            for j in range(3):
                at = D * t + 128 * j
                tile = (
                    jnp.transpose(dqkv[at : at + 128, :D], (1, 0))
                    if t < 3
                    else dout[:, 128 * j : 128 * (j + 1)]
                )
                if j < 2:
                    ga_ref[j, :, 128 * t : 128 * (t + 1)] = tile
                else:
                    for m in range(2):
                        lo = 512 + 64 * t
                        ga_ref[m, :, lo : lo + 64] = tile[:, 64 * m : 64 * (m + 1)]
        gb_ref[...] = jnp.transpose(dqkv[:, D:], (1, 0))[0:8]


def attn_tiles(w_ref, qkv_w, out_w):
    for t in range(4):
        cols = 128 * t
        pieces = [w_ref[0, :, cols : cols + 128], w_ref[1, :, cols : cols + 128]]
        tile = 512 + 128 * (t // 2)
        lane = 64 * (t % 2)
        pieces.append(
            jnp.concatenate(
                [w_ref[m, :, tile : tile + 128][:, lane : lane + 64] for m in range(2)], 1
            )
        )
        for j in range(3):
            if t < 3:
                at = D * t + 128 * j
                qkv_w[:, at : at + 128] = pieces[j]
            else:
                out_w[:, 128 * j : 128 * (j + 1)] = pieces[j]


def backward(layer, dz, kept, weights, vec):
    steps = dz.shape[0] // ROWS
    shapes = [(2, D, 768), (2, D, 1536), (8, D), (8, 3 * D), (8, FF)]
    return pl.pallas_call(
        backward_kernel,
        grid=(steps,),
        in_specs=[block_of(a.shape, steps) for a in (dz,) + tuple(kept)]
        + [
            pl.BlockSpec(
                (1, 2, D, 768), lambda i: (layer, 0, 0, 0), pipeline_mode=pl.Buffered(1)
            ),
            pl.BlockSpec(
                (2, 2, D, 768), lambda i: (1 + layer, 0, 0, 0), pipeline_mode=pl.Buffered(1)
            ),
            full_spec(vec.shape),
        ],
        out_specs=[block_of(dz.shape, steps)] + [full_spec(s) for s in shapes],
        out_shape=[jax.ShapeDtypeStruct(dz.shape, f32)]
        + [jax.ShapeDtypeStruct(s, f32) for s in shapes],
        scratch_shapes=[
            pltpu.VMEM((D, 3 * D), bf16),
            pltpu.VMEM((D, D), bf16),
            pltpu.VMEM((3 * D, 512), f32),
            pltpu.VMEM((D, D), f32),
            pltpu.VMEM((ROWS, D), bf16),
            pltpu.VMEM((ROWS, D), f32),
            pltpu.VMEM((ROWS, D), f32),
            pltpu.VMEM((ROWS, HALF), bf16),
            pltpu.VMEM((GRP, 3 * D, TP), bf16),
        ],
        compiler_params=pltpu.CompilerParams(vmem_limit_bytes=60 * MIB),
        name="backward_layer",
    )(dz, *kept, weights, weights, vec)


def patch_grad_kernel(
    inv_ref, mix_ref, dz_ref, own_ref, far_ref, gv0_ref, gv1_ref, gve_ref, gp_ref, ge_ref, dzo, dzf, tok
):
    count = far_ref.shape[0] // PATCHES
    both = own_ref.shape[0] // PATCHES
    dzo[...] = jnp.zeros_like(dzo)
    total = jnp.zeros((TP, D), f32)
    for k in range(count):
        w = mix_ref[k]
        for j in range(3):
            part = dz_ref[k * TP : k * TP + PATCHES, 128 * j : 128 * (j + 1)]
            dzo[j, pl.ds(inv_ref[k], PATCHES, stride=both), :] = w * part
            dzf[j, pl.ds(k, PATCHES, stride=count), :] = (1.0 - w) * part
        total = total + dz_ref[k * TP : (k + 1) * TP]
    tok[...] = jnp.zeros_like(tok)
    tok[:TP] = total
    for i, ref in enumerate((gv0_ref, gv1_ref)):
        tok[TP + 6 * i : TP + 6 * i + 6] = ref[0:6]
    tok[TP + 6 * LAYERS : TP + 6 * LAYERS + 2] = gve_ref[0:2]
    turned = jnp.transpose(tok[...], (1, 0))
    for m in range(2):
        ge_ref[m] = turned[:, 128 * m : 128 * (m + 1)]
    for j in range(3):
        lo = jnp.transpose(dzo[j].astype(bf16), (1, 0))
        lf = jnp.transpose(dzf[j].astype(bf16), (1, 0))
        for m in range(2):
            cols = slice(D * m, D * (m + 1))
            gp_ref[m, 128 * j : 128 * (j + 1)] = mm(lo, own_ref[:, cols]) + mm(lf, far_ref[:, cols])


def patch_grad(inv, mix, dz, own, far, gv0, gv1, gve):
    shapes = [(2, D, D), (2, D, 128)]
    return pl.pallas_call(
        patch_grad_kernel,
        grid=(1,),
        in_specs=[pl.BlockSpec(memory_space=pltpu.SMEM)] * 2
        + [full_spec(a.shape) for a in (dz, own, far, gv0, gv1, gve)],
        out_specs=[full_spec(s) for s in shapes],
        out_shape=[jax.ShapeDtypeStruct(s, f32) for s in shapes],
        scratch_shapes=[
            pltpu.VMEM((3, own.shape[0], 128), f32),
            pltpu.VMEM((3, far.shape[0], 128), f32),
            pltpu.VMEM((256, D), f32),
        ],
        compiler_params=pltpu.CompilerParams(vmem_limit_bytes=56 * MIB),
        name="patch_gradient",
    )(inv, mix, dz, own, far, gv0, gv1, gve)


def link_orders(bits):
    far = [b for b in (range(1, bits, 2) if bits == 6 else [3]) if b < bits]
    near = [b for b in range(bits) if b not in far]
    return [near[i:] + near[:i] for i in range(len(near))], far


def gather_plan(bits, turns):
    near, far = link_orders(bits)
    deep = far + [near[0][-1]]
    flat = near[0][:-1]
    return [flat[t:] + flat[:t] for t in turns], deep


def chunk_plan(bits, cuts):
    near, far = link_orders(bits)
    return [
        (cuts[i], cuts[i + 1] - cuts[i], near[i % len(near)], far) for i in range(len(cuts) - 1)
    ]


def mesh_place():
    return lax.axis_index("dp"), lax.axis_index("mp")


def bit_of(value, bit):
    return (value // 2**bit) % 2


def flipped(value, bit):
    return value + 2**bit * (1 - 2 * bit_of(value, bit))


def meet(bits):
    dp, mp = mesh_place()
    barrier = pltpu.get_barrier_semaphore()
    for peer in [(dp, 1 - mp)] + [(flipped(dp, b), mp) for b in range(bits)]:
        pl.semaphore_signal(barrier, inc=1, device_id=peer, device_id_type=MESH)
    pl.semaphore_wait(barrier, bits + 1)


def push(src, dst, send, recv, peer):
    copy = pltpu.make_async_remote_copy(
        src_ref=src, dst_ref=dst, send_sem=send, recv_sem=recv, device_id=peer, device_id_type=MESH
    )
    copy.start()
    return copy


def held_part(ref, bits, lead, dp, done=(), flip=None):
    idx = list(lead)
    for b in reversed(bits):
        mine = bit_of(dp, b)
        idx.append(pl.ds(0, 2) if b in done else (1 - mine if b == flip else mine))
    return ref.at[tuple(idx)]


def gather_front_kernel(bits, tab_ref, att_ref, ffw_ref, sb_ref, *refs):
    w_refs = refs[:2]
    far_refs = refs[2:5]
    sbo_ref, tabr, stage_p, stage_e, stage_h, s_loc, s_tab = refs[5:12]
    s_send, s_recv, f_send, f_recv, m_send, m_recv = refs[12:]
    dp, mp = mesh_place()
    mate = (dp, 1 - mp)
    turns, deep = gather_plan(bits, FRONT_TURNS)
    far = deep[:-1]
    every = list(range(bits))

    def part(c, *args):
        return held_part(w_refs[c], every, (mp,), dp, *args)

    def main(c, *args):
        return held_part(far_refs[c], far, (), dp, *args)

    meet(bits)
    c_tab = push(tab_ref.at[1 - mp], tabr, s_tab.at[0], s_tab.at[1], mate)
    c_sb = push(sb_ref, sbo_ref.at[mp], s_tab.at[2], s_tab.at[3], mate)
    local = [
        pltpu.make_async_copy(sb_ref, sbo_ref.at[mp], s_loc.at[0]),
        pltpu.make_async_copy(att_ref, main(0), s_loc.at[1]),
        pltpu.make_async_copy(ffw_ref, main(1), s_loc.at[2]),
    ]
    for copy in local:
        copy.start()
    c_tab.wait()
    mine = tab_ref[mp].astype(f32)
    other = tabr[...].astype(f32)
    first = jnp.where(mp == 0, mine, other)
    second = jnp.where(mp == 0, other, mine)
    table = jnp.concatenate([first, second], 0).astype(bf16)
    stage_p[...] = table[:, :D]
    stage_e[...] = table[:, D:F_COLS]
    stage_h[...] = table[:, F_COLS:]
    tables = [
        pltpu.make_async_copy(stage_p, part(0), s_loc.at[3]),
        pltpu.make_async_copy(stage_e, part(1), s_loc.at[4]),
        pltpu.make_async_copy(stage_h, main(2), s_loc.at[5]),
    ]
    for copy in tables:
        copy.start()
    for copy in tables + local:
        copy.wait()
    copies = {}
    forwards = []
    wide = {}
    for s in range(bits + 1):
        for c in range(2):
            order = deep + turns[c]
            if s:
                copies[c, s - 1].wait_recv()
            if s < bits:
                held = part(c, order[:s])
                copies[c, s] = push(
                    held, held, s_send.at[c, s], s_recv.at[c, s], (flipped(dp, order[s]), mp)
                )
            got = part(c, order[: s - 1], order[s - 1]) if s else part(c)
            forwards.append(push(got, got, f_send.at[c, s], f_recv.at[c, s], mate))
        at = s - len(deep)
        if 0 <= at < len(far):
            for c in range(3):
                if at:
                    wide[c, at - 1].wait_recv()
                held = main(c, far[:at])
                wide[c, at] = push(
                    held, held, m_send.at[c, at], m_recv.at[c, at], (flipped(dp, far[at]), mp)
                )
    for copy in forwards:
        copy.wait()
    for copy in copies.values():
        copy.wait_send()
    for copy in wide.values():
        copy.wait_send()
    for c in range(3):
        wide[c, len(far) - 1].wait_recv()
    c_sb.wait()


def gather_front(tab, att, ffw, sb, n_data):
    bits = n_data.bit_length() - 1
    rows = D // n_data
    _, far = link_orders(bits)
    sems = pltpu.SemaphoreType.DMA
    anywhere = pl.BlockSpec(memory_space=pl.ANY)
    inside = pl.BlockSpec(memory_space=pltpu.VMEM)
    heads = T_COLS - F_COLS
    deep_shape = (2,) * len(far)
    return pl.pallas_call(
        functools.partial(gather_front_kernel, bits),
        in_specs=[inside] * 4,
        out_specs=[anywhere] * 5 + [inside],
        out_shape=[
            jax.ShapeDtypeStruct((2,) * (bits + 1) + (rows, w), bf16) for w in FRONT_WIDTHS
        ]
        + [
            jax.ShapeDtypeStruct(deep_shape + att.shape, bf16),
            jax.ShapeDtypeStruct(deep_shape + ffw.shape, bf16),
            jax.ShapeDtypeStruct(deep_shape + (rows, heads), bf16),
            jax.ShapeDtypeStruct((2,) + sb.shape, f32),
        ],
        scratch_shapes=[
            pltpu.VMEM(tab.shape[1:], bf16),
            pltpu.VMEM((rows, FRONT_WIDTHS[0]), bf16),
            pltpu.VMEM((rows, FRONT_WIDTHS[1]), bf16),
            pltpu.VMEM((rows, heads), bf16),
            sems((6,)),
            sems((4,)),
            sems((2, bits)),
            sems((2, bits)),
            sems((2, bits + 1)),
            sems((2, bits + 1)),
            sems((3, len(far))),
            sems((3, len(far))),
        ],
        compiler_params=pltpu.CompilerParams(
            collective_id=2, has_side_effects=True, vmem_limit_bytes=60 * MIB
        ),
        name="gather_front",
    )(tab, att, ffw, sb)


def gather_main_kernel(bits, *refs):
    far_refs, deep_refs = refs[:3], refs[3:6]
    w_ref, h_ref = refs[6:8]
    s_loc, s_send, s_recv, f_send, f_recv = refs[8:]
    dp, mp = mesh_place()
    mate = (dp, 1 - mp)
    turns, deep = gather_plan(bits, MAIN_TURNS)
    far, last = deep[:-1], deep[-1]
    every = list(range(bits))
    steps = bits - len(deep)
    chunks = len(MAIN_WIDTHS)

    def part(c, *args):
        if c < chunks - 1:
            return held_part(w_ref, every, (c, mp), dp, *args)
        return held_part(h_ref, every, (mp,), dp, *args)

    def piece(c, deep_side):
        refs_in = deep_refs if deep_side else far_refs
        lead = (slice(None),) * len(far)
        if c == chunks - 1:
            return refs_in[2]
        if c < LAYERS:
            return refs_in[0].at[lead + (c,)]
        return refs_in[1].at[lead + (c - LAYERS,)]

    meet(bits)
    copies = {}
    forwards = []
    local = []
    for c in range(chunks):
        for i in range(2):
            dst = part(c, far, last) if i else part(c, far)
            local.append(pltpu.make_async_copy(piece(c, i), dst, s_loc.at[c, i]))
            local[-1].start()
    for s in range(steps + 1):
        for c in range(chunks):
            order = turns[c]
            if s:
                copies[c, s - 1].wait_recv()
            else:
                local[2 * c].wait()
                local[2 * c + 1].wait()
            done = deep + order[:s]
            if s < steps:
                held = part(c, done)
                copies[c, s] = push(
                    held, held, s_send.at[c, s], s_recv.at[c, s], (flipped(dp, order[s]), mp)
                )
            got = part(c, done[:-1], done[-1]) if s else part(c, done)
            forwards.append(push(got, got, f_send.at[c, s], f_recv.at[c, s], mate))
    for copy in forwards:
        copy.wait()
    for copy in copies.values():
        copy.wait_send()


def gather_main(far_parts, deep_parts, n_data):
    bits = n_data.bit_length() - 1
    rows = D // n_data
    near, _ = link_orders(bits)
    steps = len(near[0]) - 1
    chunks = len(MAIN_WIDTHS)
    sems = pltpu.SemaphoreType.DMA
    anywhere = pl.BlockSpec(memory_space=pl.ANY)
    places = (2,) * (bits + 1) + (rows,)
    main, heads = pl.pallas_call(
        functools.partial(gather_main_kernel, bits),
        in_specs=[pl.BlockSpec(memory_space=pltpu.VMEM)] * 6,
        out_specs=[anywhere] * 2,
        out_shape=[
            jax.ShapeDtypeStruct((chunks - 1,) + places + (768,), bf16),
            jax.ShapeDtypeStruct(places + (1024,), bf16),
        ],
        scratch_shapes=[
            sems((chunks, 2)),
            sems((chunks, steps)),
            sems((chunks, steps)),
            sems((chunks, steps + 1)),
            sems((chunks, steps + 1)),
        ],
        compiler_params=pltpu.CompilerParams(
            collective_id=0, has_side_effects=True, vmem_limit_bytes=60 * MIB
        ),
        name="gather_main",
    )(*far_parts, *deep_parts)
    return main.reshape(chunks - 1, 2, D, 768), heads.reshape(2, D, 1024)


def reduce_kernel(bits, *refs):
    srcs = refs[:7]
    bun_ref = refs[7]
    ot_ref, oa_ref, obun_ref = refs[8:11]
    msend, mrecv, acc, tsend, bun, bunr, sq, sqr = refs[11:19]
    plan = [(c, w, near + far) for c, w, near, far in chunk_plan(bits, REDUCE_CUTS)]
    nst = 3 * bits
    sbufs = refs[19 : 19 + nst]
    rbufs = refs[19 + nst : 19 + 2 * nst]
    m_sem, s_sem, r_sem, b_sem, q_sem, t_sem = refs[19 + 2 * nst :]
    dp, mp = mesh_place()
    mate = (dp, 1 - mp)
    blocks = 2**bits
    rows = D // blocks
    small = ot_ref.shape[1]

    meet(bits)

    segs = []
    at = 0
    for ref in srcs:
        segs.append((at, ref.shape[-1], ref))
        at += ref.shape[-1]

    group = max(rows, 24)
    per = group // rows

    def over_blocks(body):
        def step(b, carry):
            body(b)
            return carry

        lax.fori_loop(0, D // group, step, 0)

    def piece(ref, half, b, lo, hi):
        return ref[half, pl.ds(pl.multiple_of(b * group, group), group), lo:hi]

    mcopies = []
    bun[...] = bun_ref[...]
    cb = push(bun, bunr.at[0], b_sem.at[0, 0], b_sem.at[0, 1], mate)
    for c, (col, width, order) in enumerate(plan):

        def body(b):
            for at, size, ref in segs:
                lo, hi = max(at, col), min(at + size, col + width)
                if lo < hi:
                    got = piece(ref, 1 - mp, b, lo - at, hi - at)
                    for i in range(per):
                        msend[b * per + i, :, lo:hi] = got[rows * i : rows * (i + 1)].astype(bf16)

        over_blocks(body)
        cut = (slice(None), slice(None), pl.ds(col, width))
        mcopies.append(push(msend.at[cut], mrecv.at[cut], m_sem.at[c, 0], m_sem.at[c, 1], mate))

    def block_index(free, fixed):
        def index(t):
            total = fixed
            for j, b in enumerate(free):
                total = total + ((t // 2**j) % 2) * 2**b
            return total

        return index

    copies = {}

    def send_stage(c, s):
        col, width, order = plan[c]
        free = [b for b in range(bits) if b not in order[: s + 1]]
        fixed = sum(bit_of(dp, b) * 2**b for b in order[:s])
        fixed = fixed + (1 - bit_of(dp, order[s])) * 2 ** order[s]
        index = block_index(free, fixed)
        sbuf = sbufs[c * bits + s]

        def step(t, carry):
            sbuf[t] = acc[index(t), :, col : col + width].astype(bf16)
            return carry

        lax.fori_loop(0, 2 ** len(free), step, 0)
        copies[c, s] = push(
            sbuf,
            rbufs[c * bits + s],
            s_sem.at[c, s],
            r_sem.at[c, s],
            (flipped(dp, order[s]), mp),
        )

    def take_stage(c, s):
        col, width, order = plan[c]
        copies[c, s].wait_recv()
        free = [b for b in range(bits) if b not in order[: s + 1]]
        fixed = sum(bit_of(dp, b) * 2**b for b in order[: s + 1])
        index = block_index(free, fixed)
        rbuf = rbufs[c * bits + s]

        def step(t, carry):
            acc[index(t), :, col : col + width] += rbuf[t].astype(f32)
            return carry

        lax.fori_loop(0, 2 ** len(free), step, 0)

    for c, (col, width, order) in enumerate(plan):
        mcopies[c].wait_recv()

        def body(b):
            for at, size, ref in segs:
                lo, hi = max(at, col), min(at + size, col + width)
                if lo < hi:
                    got = piece(ref, mp, b, lo - at, hi - at)
                    for i in range(per):
                        acc[b * per + i, :, lo:hi] = got[rows * i : rows * (i + 1)] + mrecv[
                            b * per + i, :, lo:hi
                        ].astype(f32)

        over_blocks(body)
        send_stage(c, 0)
    bcopies = [cb]
    for s in range(1, bits + 1):
        for c in range(3):
            take_stage(c, s - 1)
            if s < bits:
                send_stage(c, s)
        bcopies[-1].wait()
        bun[...] = bun[...] + bunr[s - 1]
        bcopies.append(
            push(bun, bunr.at[s], b_sem.at[s, 0], b_sem.at[s, 1], (flipped(dp, s - 1), mp))
        )
    mine = acc[dp]
    oa_ref[...] = mine[:, T_COLS:]
    tab = mine[:, :T_COLS]
    tsend[0] = jnp.where(mp == 0, tab[small:], tab[:small])
    ct = push(tsend.at[0], tsend.at[1], t_sem.at[0], t_sem.at[1], mate)
    ot_ref[mp] = jnp.where(mp == 0, tab[:small], tab[small:])
    ct.wait()
    ot_ref[1 - mp] = tsend[1]
    bcopies[-1].wait()
    obun_ref[0 : bun.shape[0]] = bun[...] + bunr[bits]
    own = jnp.sum(ot_ref[0] * ot_ref[0], keepdims=True) + jnp.sum(
        ot_ref[1] * ot_ref[1], keepdims=True
    )
    own = own + jnp.sum(oa_ref[...] * oa_ref[...], keepdims=True)
    sq[0] = jnp.broadcast_to(own, (8, 128))
    for s in range(bits + 1):
        peer = mate if s == 0 else (flipped(dp, s - 1), mp)
        copy = push(sq.at[s], sqr.at[s], q_sem.at[s, 0], q_sem.at[s, 1], peer)
        copy.wait()
        sq[s + 1] = sq[s] + sqr[s]
    obun_ref[bun.shape[0] :] = sq[bits + 1]
    for copy in mcopies:
        copy.wait_send()
    for copy in copies.values():
        copy.wait_send()


def reduce_all(srcs, bundle, n_data):
    bits = n_data.bit_length() - 1
    rows = D // n_data
    small = rows // 2
    blocks = n_data
    plan = [(c, w, near + far) for c, w, near, far in chunk_plan(bits, REDUCE_CUTS)]
    sems = pltpu.SemaphoreType.DMA
    inside = pl.BlockSpec(memory_space=pltpu.VMEM)
    bufs = [
        pltpu.VMEM((2 ** (bits - 1 - s), rows, width), bf16)
        for _, width, _ in plan
        for s in range(bits)
    ]
    return pl.pallas_call(
        functools.partial(reduce_kernel, bits),
        in_specs=[inside] * 8,
        out_specs=[inside] * 3,
        out_shape=[
            jax.ShapeDtypeStruct((2, small, T_COLS), f32),
            jax.ShapeDtypeStruct((rows, COLS - T_COLS), f32),
            jax.ShapeDtypeStruct((bundle.shape[0] + 8, 128), f32),
        ],
        scratch_shapes=[
            pltpu.VMEM((blocks, rows, COLS), bf16),
            pltpu.VMEM((blocks, rows, COLS), bf16),
            pltpu.VMEM((blocks, rows, COLS), f32),
            pltpu.VMEM((2, small, T_COLS), f32),
            pltpu.VMEM(bundle.shape, f32),
            pltpu.VMEM((bits + 1,) + bundle.shape, f32),
            pltpu.VMEM((bits + 2, 8, 128), f32),
            pltpu.VMEM((bits + 1, 8, 128), f32),
        ]
        + bufs
        + bufs
        + [
            sems((3, 2)),
            sems((3, bits)),
            sems((3, bits)),
            sems((bits + 1, 2)),
            sems((bits + 1, 2)),
            sems((2,)),
        ],
        compiler_params=pltpu.CompilerParams(
            collective_id=1, has_side_effects=True, vmem_limit_bytes=62 * MIB
        ),
        name="reduce_gradients",
    )(*srcs, bundle)


def adamw(master, first, second, gradient, rate, decay):
    first = beta_one * first + (1.0 - beta_one) * gradient
    second = beta_two * second + (1.0 - beta_two) * gradient * gradient
    first_hat = first / (1.0 - beta_one**STEP)
    second_hat = second / (1.0 - beta_two**STEP)
    master = master - rate * (first_hat / (jnp.sqrt(second_hat) + adam_eps) + decay * master)
    return (master, first, second)


def pack_tables(tab, vec):
    small = tab.shape[0]
    token = tab[:, PD : PD + TOK]
    seg = jnp.concatenate(
        [
            token[:, 2:],
            token[:, :2],
            jnp.zeros((small, TP - TOK), f32),
            vec,
            jnp.zeros((small, 256 - TP - vec.shape[1]), f32),
        ],
        1,
    )
    heads = jnp.pad(tab[:, PD + TOK :].reshape(small, 2, CLS), ((0, 0), (0, 0), (0, 1024 - CLS)))
    parts = [tab[:, :PD], seg, heads[:, 0], heads[:, 1]]
    return [
        jnp.concatenate([x[:, x.shape[1] // 2 * m : x.shape[1] // 2 * (m + 1)] for x in parts], 1)
        for m in range(2)
    ]


def unpack_tables(halves):
    cuts = (0, D, D + 128, 1024, T_COLS)
    segs = [
        jnp.concatenate([halves[m][:, cuts[i] : cuts[i + 1]] for m in range(2)], 1)
        for i in range(4)
    ]
    token = segs[1]
    tab = jnp.concatenate(
        [
            segs[0],
            token[:, PATCHES:TOK],
            token[:, :PATCHES],
            segs[2][:, :CLS],
            segs[3][:, :CLS],
        ],
        1,
    )
    return tab, token[:, TP : TP + 6 * LAYERS + 2]


def pack_attention(attn):
    layers, rows, _ = attn.shape
    a = attn.reshape(layers, rows, 3, 4, HD)
    two = a[:, :, :2].transpose(0, 1, 3, 2, 4).reshape(layers, rows, 512)
    one = a[:, :, 2].reshape(layers, rows, 256)
    return jnp.concatenate([two, one], -1)


def unpack_attention(packed):
    layers, rows, _ = packed.shape
    two = packed[..., :512].reshape(layers, rows, 4, 2, HD).transpose(0, 1, 3, 2, 4)
    one = packed[..., 512:].reshape(layers, rows, 1, 4, HD)
    return jnp.concatenate([two, one], 2).reshape(layers, rows, 768)


PAIRS = (0, 1, 3, 4, 2, 5)


def shards(
    pixels,
    labels,
    teacher,
    partner,
    mix_weight,
    class_weight,
    tables,
    tables_first,
    tables_second,
    vectors,
    vectors_first,
    vectors_second,
    attention,
    attention_first,
    attention_second,
    feedforward,
    feedforward_first,
    feedforward_second,
    split_bias,
    split_bias_first,
    split_bias_second,
    head_bias,
    head_bias_first,
    head_bias_second,
):
    n_data = lax.axis_size("dp")
    dp, mp = mesh_place()
    images_here = pixels.shape[0]
    count = images_here // 2
    rows = D // n_data
    far_rank = (dp + n_data // 2) % n_data
    far_pairs = [(i, (i + n_data // 2) % n_data) for i in range(n_data)]
    pix = pixels.transpose(1, 0, 2)
    far_ids = mp * count + jnp.arange(count, dtype=jnp.int32)
    match = (partner - far_rank * images_here)[None, :] == far_ids[:, None]
    inv = jnp.sum(
        jnp.where(match, jnp.arange(images_here, dtype=jnp.int32)[None, :], 0), 1
    ).astype(jnp.int32)
    mix = jnp.sum(jnp.where(match, mix_weight[None, :], 0.0), 1)
    own_lab = jnp.take(labels, dp * images_here + inv)
    far_lab = lax.dynamic_slice_in_dim(labels, far_rank * images_here + mp * count, count, 0)
    own_teach = jnp.sum(jnp.where(match, teacher[None, :], 0), 1).astype(jnp.int32)
    labs = jnp.stack([own_lab, far_lab, own_teach], 1)
    lws = jnp.take(class_weight, labs) * jnp.stack([mix, 1.0 - mix, jnp.ones_like(mix)], 1)
    labs = jnp.pad(labs, ((0, 0), (0, 125)))
    lws = jnp.pad(lws, ((0, 0), (0, 125)))

    tab_halves = pack_tables(tables.T, vectors.T)
    tab = jnp.stack(tab_halves).astype(bf16)
    att = pack_attention(attention).astype(bf16)
    ffw = feedforward.transpose(0, 2, 1, 3).reshape(2 * LAYERS, rows, HALF).astype(bf16)
    front, seg, *far_parts, sb = gather_front(tab, att, ffw, split_bias, n_data)
    front = front.reshape(2, D, FRONT_WIDTHS[0])
    seg = seg.reshape(2, D, FRONT_WIDTHS[1])
    base = jnp.reshape(mp * count, (1,)).astype(jnp.int32)
    pix_flat = pix.reshape(PATCHES * images_here, PD)
    deep = link_orders(n_data.bit_length() - 1)[0][0][-1]
    pairs = [(i, i ^ (1 << deep)) for i in range(n_data)]
    deep_parts = [lax.ppermute(x, "dp", pairs) for x in far_parts]
    own, send = embed(inv, base, pix_flat, front, count)
    deep_parts, send = lax.optimization_barrier((deep_parts, send))
    far = lax.ppermute(send, "dp", far_pairs)
    weights, w_heads = gather_main(far_parts, deep_parts, n_data)
    sb = sb.astype(bf16).astype(f32)
    qv = sb[:, :, :D].transpose(1, 0, 2).reshape(LAYERS, HEADS, 2, HD)[:, jnp.array(PAIRS)]
    bias = qv.transpose(0, 2, 1, 3).reshape(LAYERS, 2 * D)
    bias = jnp.pad(bias, ((0, 8 - LAYERS), (0, 0)))
    ub = jnp.pad(sb[:, :, D:].transpose(1, 0, 2).reshape(LAYERS, FF), ((0, 8 - LAYERS), (0, 0)))
    hb = jnp.pad(
        head_bias.astype(bf16).astype(f32).reshape(2, CLS),
        ((0, 0), (0, 1024 - CLS)),
        constant_values=-1e30,
    ).reshape(1, -1)
    hb = jnp.pad(hb, ((0, 7), (0, 0)))

    pix_mine = lax.dynamic_slice_in_dim(pix, mp * count, count, 1)
    pix_mine, far = lax.optimization_barrier((pix_mine, far))
    pix_far = lax.ppermute(pix_mine, "dp", far_pairs)
    outs = forward(mix, own, far, seg, weights, bias, ub)
    kept, tail, tok = outs[: 7 * LAYERS], outs[7 * LAYERS], outs[7 * LAYERS + 1]
    tail = tail.reshape(count, 16, D)
    ends = jnp.stack([tail[:, PATCHES - 192], tail[:, PATCHES - 191]])
    v_end = TP + 6 * LAYERS
    dh, dx, gve, dhb, stat = head(
        ends, w_heads, hb, labs, lws, tok[v_end : v_end + 8]
    )
    dz = jnp.zeros((count, TP, D), f32)
    dz = dz.at[:, PATCHES].set(dx[0]).at[:, PATCHES + 1].set(dx[1]).reshape(count * TP, D)
    grads = [None] * LAYERS
    for layer in reversed(range(LAYERS)):
        v0 = TP + 6 * layer
        dz, *grads[layer] = backward(
            layer, dz, kept[7 * layer : 7 * layer + 7], weights, tok[v0 : v0 + 8]
        )
    gp, ge = patch_grad(
        inv,
        mix,
        dz,
        pix_flat,
        pix_far.reshape(PATCHES * count, PD),
        grads[0][2],
        grads[1][2],
        gve,
    )
    biases = []
    for layer in range(LAYERS):
        gb, gu = grads[layer][3][0], grads[layer][4][0]
        biases += [gb[:D], gb[2 * D :], gu]
    bundle = jnp.concatenate([stat[0]] + biases + [dhb[0]]).reshape(-1, 128)
    lines = bundle.shape[0]
    bundle = jnp.pad(bundle, ((0, -lines % 8), (0, 0)))
    srcs = [gp, ge, dh, grads[0][0], grads[1][0], grads[0][1], grads[1][1]]
    g_tab, g_main, info = reduce_all(srcs, bundle, n_data)
    flat = info.reshape(-1)
    loss_sum, weight_sum = flat[0], flat[1]
    squares = info[bundle.shape[0], 0]
    at = 128
    g_split = []
    for layer in range(LAYERS):
        q = flat[at : at + D].reshape(3, 2, HD)
        v = flat[at + D : at + 2 * D].reshape(3, 2, HD)
        up = lax.dynamic_slice_in_dim(flat[at + 2 * D : at + 2 * D + FF], mp * HALF, HALF, 0)
        at += 2 * D + FF
        qv = jnp.stack([q, v], 2)
        pick = lax.dynamic_index_in_dim(
            jnp.stack(
                [
                    jnp.stack([qv[0, 0], qv[0, 1], qv[2, 0]]),
                    jnp.stack([qv[1, 0], qv[1, 1], qv[2, 1]]),
                ]
            ),
            mp,
            0,
            False,
        )
        g_split.append(jnp.concatenate([pick.reshape(-1), up]))
    g_split = jnp.stack(g_split)
    g_head = flat[at : at + 2048].reshape(2, 1024)[:, :CLS].reshape(-1)
    every = flat[128 : at + 2048]
    squares = squares + jnp.sum(every * every)
    g_tables, g_vectors = unpack_tables(g_tab)
    g_attention = unpack_attention(
        g_main[:, : 768 * LAYERS].reshape(rows, LAYERS, 768).transpose(1, 0, 2)
    )
    g_feedforward = (
        g_main[:, 768 * LAYERS :].reshape(rows, LAYERS, 2, HALF).transpose(1, 0, 2, 3)
    )
    grad_norm = jnp.sqrt(squares) / weight_sum
    factor = jnp.minimum(1.0, clip_limit / grad_norm) / weight_sum
    t_new, t_one, t_two = (
        x.T
        for x in adamw(
            tables.T,
            tables_first.T,
            tables_second.T,
            g_tables * factor,
            matrix_rate,
            matrix_decay,
        )
    )
    v_new, v_one, v_two = (
        x.T
        for x in adamw(
            vectors.T, vectors_first.T, vectors_second.T, g_vectors * factor, vector_rate, 0.0
        )
    )
    a_new, a_one, a_two = adamw(
        attention,
        attention_first,
        attention_second,
        g_attention * factor,
        matrix_rate,
        matrix_decay,
    )
    f_new, f_one, f_two = adamw(
        feedforward,
        feedforward_first,
        feedforward_second,
        g_feedforward * factor,
        matrix_rate,
        matrix_decay,
    )
    s_new, s_one, s_two = adamw(
        split_bias, split_bias_first, split_bias_second, g_split * factor, vector_rate, 0.0
    )
    h_new, h_one, h_two = adamw(
        head_bias, head_bias_first, head_bias_second, g_head * factor, vector_rate, 0.0
    )
    return (
        loss_sum,
        weight_sum,
        grad_norm,
        t_new,
        t_one,
        t_two,
        t_new.astype(bf16),
        v_new,
        v_one,
        v_two,
        a_new,
        a_one,
        a_two,
        a_new.astype(bf16),
        f_new,
        f_one,
        f_two,
        f_new.astype(bf16),
        s_new,
        s_one,
        s_two,
        h_new,
        h_one,
        h_two,
    )


def solution(mesh):
    table = P(None, ("dp", "mp"))
    attn = P(None, "dp", "mp")
    ffw = P(None, "dp", None, "mp")
    split = P(None, "mp")
    return jax.shard_map(
        shards,
        mesh=mesh,
        in_specs=(P("dp", None, None), P(), P("dp"), P("dp"), P("dp"), P())
        + (table,) * 6
        + (attn,) * 3
        + (ffw,) * 3
        + (split,) * 3
        + (P(),) * 3,
        out_specs=(P(),) * 3
        + (table,) * 7
        + (attn,) * 4
        + (ffw,) * 4
        + (split,) * 3
        + (P(),) * 3,
        check_vma=False,
    )
```

```python
import functools

import jax
import jax.numpy as jnp
from jax import lax
from jax.experimental import pallas as pl
from jax.experimental.pallas import tpu as pltpu
from jax.sharding import PartitionSpec as P

D = 384
HEADS = 6
HD = 64
FF = 1536
CLS = 1000
PD = 768
PATCHES = 196
LAYERS = 2
STEP = 10
TOK = 198
TP = 208
GRP = 2
ENDS = 16
END_AT = 4
ROWS = GRP * TP
HALF = FF // 2
COLS = 6144
T_COLS = 1536
F_COLS = 512
TABLE_CHUNKS = (6, 7, 8)
REDUCE_TURNS = (0, 0, 1, 1, 2, 1, 2, 0, 0)
MAIN_WIDTHS = (768, 768, 768, 768, 768, 768, 1024)
MAIN_TURNS = (0, 0, 0, 1, 0, 1, 1)
FRONT_WIDTHS = (384, 128)
FRONT_TURNS = (0, 1)
M_COLS = 4608
MIB = 1 << 20
NORM_ROWS = ROWS
GELU_ROWS = 32

norm_eps = 1e-06
clip_limit = 0.02
beta_one = 0.9
beta_two = 0.999
adam_eps = 1e-08
matrix_rate = 0.08
vector_rate = 0.5
matrix_decay = 0.05

f32 = jnp.float32
bf16 = jnp.bfloat16
MESH = pl.DeviceIdType.MESH
AB = ((1,), (0,))
ABT = ((1,), (1,))
ATB = ((0,), (0,))


def mm(left, right, dims=AB):
    return lax.dot_general(left, right, (dims, ((), ())), preferred_element_type=f32)


def full_spec(shape):
    return pl.BlockSpec(shape, lambda *_: (0,) * len(shape), pipeline_mode=pl.Buffered(1))


def row_loop(total, chunk, body):
    def step(index, carry):
        body(pl.ds(pl.multiple_of(index * chunk, chunk), chunk))
        return carry

    if total == chunk:
        body(slice(0, total))
    else:
        lax.fori_loop(0, total // chunk, step, 0)


def center(x):
    mean = jnp.mean(x, -1, keepdims=True)
    xc = x - mean
    scale = lax.rsqrt(jnp.mean(xc * xc, -1, keepdims=True) + norm_eps)
    return xc * scale, scale


def gelu_pair(x):
    z = x * 0.7071067811865476
    e = jnp.exp(-(z * z))
    den = 1.0 + 0.3275911 * jnp.abs(z)
    r = pl.reciprocal(den, approx=True)
    r = r * (2.0 - den * r)
    poly = r * (
        0.127414796
        + r * (-0.142248368 + r * (0.7107068705 + r * (-0.7265760135 + r * 0.5307027145)))
    )
    tail = poly * e
    cdf = jnp.where(x > 0.0, 1.0 - tail, tail)
    return x * cdf, cdf + x * (e * 0.3989422804014327)


def embed_kernel(inv_ref, base_ref, pix_ref, w_ref, own_ref, send_ref, flat):
    rows = pix_ref.shape[0]
    count = rows // PATCHES
    chunk = rows // 7
    for c in range(7):
        pix = pix_ref[c * chunk : (c + 1) * chunk]
        out = mm(pix[:, :D], w_ref[0], ABT) + mm(pix[:, D:], w_ref[1], ABT)
        for j in range(3):
            flat[j, c * chunk : (c + 1) * chunk] = out[:, 128 * j : 128 * (j + 1)]
    for k in range(own_ref.shape[0]):
        for j in range(3):
            cols = slice(128 * j, 128 * (j + 1))
            own_ref[k, :, cols] = flat[j, pl.ds(inv_ref[k], PATCHES, stride=count), :]
            send_ref[k, :, cols] = flat[j, pl.ds(base_ref[0] + k, PATCHES, stride=count), :].astype(
                bf16
            )


def embed(inv, base, pix, weights, count):
    return pl.pallas_call(
        embed_kernel,
        grid=(1,),
        in_specs=[
            pl.BlockSpec(memory_space=pltpu.SMEM),
            pl.BlockSpec(memory_space=pltpu.SMEM),
            full_spec(pix.shape),
            full_spec(weights.shape),
        ],
        out_specs=[full_spec((count, PATCHES, D)), full_spec((count, PATCHES, D))],
        out_shape=[
            jax.ShapeDtypeStruct((count, PATCHES, D), f32),
            jax.ShapeDtypeStruct((count, PATCHES, D), bf16),
        ],
        scratch_shapes=[pltpu.VMEM((3, pix.shape[0], 128), f32)],
        compiler_params=pltpu.CompilerParams(vmem_limit_bytes=60 * MIB),
        name="embed_images",
    )(inv, base, pix, weights)


def split_tokens(w_ref, col):
    seg = jnp.concatenate([w_ref[0, :, col : col + 128], w_ref[1, :, col : col + 128]], 1)
    return jnp.transpose(seg.astype(f32), (1, 0))


def attend(g, qkv_ref, p_ref, ho_ref):
    rows = slice(g * TP, (g + 1) * TP)
    lane = lax.broadcasted_iota(jnp.int32, (TP, 128), 1)
    key_mask = jnp.where(lax.broadcasted_iota(jnp.int32, (1, TP), 1) < TOK, 0.0, -1e30).astype(f32)
    for j in range(3):
        q = qkv_ref[rows, 128 * j : 128 * (j + 1)]
        k = qkv_ref[rows, D + 128 * j : D + 128 * (j + 1)]
        v = qkv_ref[rows, 2 * D + 128 * j : 2 * D + 128 * (j + 1)]
        outs = []
        for s in range(2):
            mine = (lane < 64) if s == 0 else (lane >= 64)
            scores = mm(jnp.where(mine, q, jnp.zeros_like(q)), k, ABT) + key_mask
            exps = jnp.exp(scores - jnp.max(scores, -1, keepdims=True))
            probs = (exps * (1.0 / jnp.sum(exps, -1, keepdims=True))).astype(bf16)
            p_ref[6 * g + 2 * j + s] = probs
            outs.append(mm(probs, v))
        ho_ref[rows, 128 * j : 128 * (j + 1)] = jnp.where(lane < 64, outs[0], outs[1]).astype(bf16)


def norm_rows(src, gain, shift, dst):
    dst[...] = (center(src[...])[0] * gain + shift).astype(bf16)


def token_row(tok_ref, layer, i):
    at = TP + 6 * layer + i
    return tok_ref[at : at + 1]


def attend_ends(g, kv_ref, q_ref, p_ref, ho_ref):
    rows = slice(g * TP, (g + 1) * TP)
    ends = slice(g * ENDS, (g + 1) * ENDS)
    lane = lax.broadcasted_iota(jnp.int32, (ENDS, 128), 1)
    key_mask = jnp.where(lax.broadcasted_iota(jnp.int32, (1, TP), 1) < TOK, 0.0, -1e30).astype(f32)
    for j in range(3):
        q = q_ref[ends, 128 * j : 128 * (j + 1)]
        k = kv_ref[rows, 128 * j : 128 * (j + 1)]
        v = kv_ref[rows, D + 128 * j : D + 128 * (j + 1)]
        outs = []
        for s in range(2):
            mine = (lane < 64) if s == 0 else (lane >= 64)
            scores = mm(jnp.where(mine, q, jnp.zeros_like(q)), k, ABT) + key_mask
            exps = jnp.exp(scores - jnp.max(scores, -1, keepdims=True))
            probs = (exps * (1.0 / jnp.sum(exps, -1, keepdims=True))).astype(bf16)
            p_ref[6 * g + 2 * j + s] = probs
            outs.append(mm(probs, v))
        ho_ref[ends, 128 * j : 128 * (j + 1)] = jnp.where(lane < 64, outs[0], outs[1]).astype(bf16)


def forward_kernel(mix_ref, own_ref, far_ref, t_ref, w_ref, bias_ref, ub_ref, *refs):
    x_ref, mid_ref, qkv_ref, p_ref, ho_ref, hid_ref, gp_ref = refs[:7]
    x1_ref, kv_ref, q1_ref, p1_ref, ho1_ref, mid1_ref, tok_ref = refs[7:14]
    qkv_w, out_w, nbuf, up_s = refs[14:]
    step = pl.program_id(0)

    @pl.when(step == 0)
    def _():
        tok_ref[...] = split_tokens(t_ref, 0)
        for layer in range(LAYERS):
            attn_tiles(w_ref.at[layer], qkv_w.at[layer], out_w.at[layer])

    def row(layer, i):
        return token_row(tok_ref, layer, i)

    for g in range(GRP):
        w = mix_ref[step * GRP + g]
        x_ref[g * TP : g * TP + PATCHES] = (
            w * own_ref[g] + (1.0 - w) * far_ref[g].astype(f32) + tok_ref[:PATCHES]
        )
        x_ref[g * TP + PATCHES : (g + 1) * TP] = tok_ref[PATCHES:TP]
    norm_rows(x_ref, row(0, 0), row(0, 1), nbuf)
    n = nbuf[...]
    q = mm(n, qkv_w[0, :, :D]) + bias_ref[0:1, :D]
    qkv_ref[:, :D] = (q.astype(bf16).astype(f32) * 0.125).astype(bf16)
    qkv_ref[:, D : 2 * D] = mm(n, qkv_w[0, :, D : 2 * D]).astype(bf16)
    v = mm(n, qkv_w[0, :, 2 * D :]) + bias_ref[0:1, D : 2 * D]
    qkv_ref[:, 2 * D :] = v.astype(bf16)
    for g in range(GRP):
        attend(g, qkv_ref, p_ref, ho_ref)
    mid_ref[...] = x_ref[...] + mm(ho_ref[...], out_w[0], ABT) + row(0, 4)
    norm_rows(mid_ref, row(0, 2), row(0, 3), nbuf)
    up_w, down_w = w_ref.at[LAYERS], w_ref.at[LAYERS + 1]
    for m in range(2):
        cols = slice(HALF * m, HALF * (m + 1))
        up_s[...] = mm(nbuf[...], up_w[m]) + ub_ref[0:1, cols]

        def body(rs):
            hid, gp = gelu_pair(up_s[rs])
            hid_ref[rs, cols] = hid.astype(bf16)
            gp_ref[rs, cols] = gp.astype(bf16)

        row_loop(ROWS, GELU_ROWS, body)
    out = mid_ref[...] + row(0, 5)
    for m in range(2):
        cols = slice(HALF * m, HALF * (m + 1))
        out = out + mm(hid_ref[:, cols], down_w[m], ABT)
    x1_ref[...] = out
    norm_rows(x1_ref, row(1, 0), row(1, 1), nbuf)
    n = nbuf[...]
    kv_ref[:, :D] = mm(n, qkv_w[1, :, D : 2 * D]).astype(bf16)
    kv_ref[:, D:] = (mm(n, qkv_w[1, :, 2 * D :]) + bias_ref[1:2, D : 2 * D]).astype(bf16)
    ends = jnp.concatenate([nbuf[(g + 1) * TP - ENDS : (g + 1) * TP] for g in range(GRP)], 0)
    q = mm(ends, qkv_w[1, :, :D]) + bias_ref[1:2, :D]
    q1_ref[...] = (q.astype(bf16).astype(f32) * 0.125).astype(bf16)
    for g in range(GRP):
        attend_ends(g, kv_ref, q1_ref, p1_ref, ho1_ref)
    x_ends = jnp.concatenate([x1_ref[(g + 1) * TP - ENDS : (g + 1) * TP] for g in range(GRP)], 0)
    mid1_ref[...] = x_ends + mm(ho1_ref[...], out_w[1], ABT) + row(1, 4)


def kept_shapes(count):
    n = count * TP
    return [
        ((n, D), f32),
        ((n, D), f32),
        ((n, 3 * D), bf16),
        ((count * HEADS, TP, TP), bf16),
        ((n, D), bf16),
        ((n, FF), bf16),
        ((n, FF), bf16),
        ((n, D), f32),
        ((n, 2 * D), bf16),
        ((count * ENDS, D), bf16),
        ((count * HEADS, ENDS, TP), bf16),
        ((count * ENDS, D), bf16),
        ((count * ENDS, D), f32),
    ]


def block_of(shape, steps):
    block = (shape[0] // steps,) + tuple(shape[1:])
    return pl.BlockSpec(block, lambda i: (i,) + (0,) * (len(block) - 1))


def forward(mix, own, far, seg, weights, bias, ub):
    count = own.shape[0]
    steps = count // GRP
    outs = kept_shapes(count)
    shapes = [jax.ShapeDtypeStruct(s, t) for s, t in outs] + [jax.ShapeDtypeStruct((256, D), f32)]
    specs = [block_of(s, steps) for s, _ in outs] + [full_spec((256, D))]
    return pl.pallas_call(
        forward_kernel,
        grid=(steps,),
        in_specs=[
            pl.BlockSpec(memory_space=pltpu.SMEM),
            block_of(own.shape, steps),
            block_of(far.shape, steps),
            full_spec(seg.shape),
            pl.BlockSpec((4, 2, D, 768), lambda i: (0, 0, 0, 0), pipeline_mode=pl.Buffered(1)),
            full_spec(bias.shape),
            full_spec(ub.shape),
        ],
        out_specs=specs,
        out_shape=shapes,
        scratch_shapes=[
            pltpu.VMEM((LAYERS, D, 3 * D), bf16),
            pltpu.VMEM((LAYERS, D, D), bf16),
            pltpu.VMEM((ROWS, D), bf16),
            pltpu.VMEM((ROWS, HALF), f32),
        ],
        compiler_params=pltpu.CompilerParams(vmem_limit_bytes=60 * MIB),
        name="forward_layers",
    )(mix, own, far, seg, weights, bias, ub)


def norm_back(dy, xhat, scale, gain):
    dyg = dy * gain
    c1 = jnp.mean(dyg, -1, keepdims=True)
    c2 = jnp.mean(dyg * xhat, -1, keepdims=True)
    return scale * (dyg - c1 - xhat * c2)


def share(part, own_ref, mate_ref, mp):
    own_ref[...] = part[mp]
    mate_ref[...] = part[1 - mp].astype(bf16)


def head_kernel(
    mid_ref,
    wf_ref,
    w_ref,
    ub_ref,
    hb_ref,
    lab_ref,
    lw_ref,
    tok_ref,
    uo_ref,
    um_ref,
    do_ref,
    dm_ref,
    ho_ref,
    hm_ref,
    dz_ref,
    gv_ref,
    gu_ref,
    dhb_ref,
    stat_ref,
    lanes,
    g_ffw,
    g_head,
):
    mp = lax.axis_index("mp")
    gain2, shift2, bias_f = (token_row(tok_ref, 1, i) for i in (2, 3, 5))
    gain, shift = (token_row(tok_ref, 2, i) for i in range(2))
    count = mid_ref.shape[0] // ENDS
    for j in range(3):
        lanes[j] = mid_ref[:, 128 * j : 128 * (j + 1)]
    mid = jnp.concatenate(
        [
            jnp.concatenate(
                [lanes[j, pl.ds(END_AT + h, count, stride=ENDS), :] for j in range(3)], 1
            )
            for h in range(2)
        ],
        0,
    )
    xhat2, scale2 = center(mid)
    normed = (xhat2 * gain2 + shift2).astype(bf16)
    out = mid + bias_f
    hids, gps = [], []
    for m in range(2):
        up = mm(normed, wf_ref[0, m]) + ub_ref[1:2, HALF * m : HALF * (m + 1)]
        hid, gp = gelu_pair(up)
        hids.append(hid.astype(bf16))
        gps.append(gp)
        out = out + mm(hids[m], wf_ref[1, m], ABT)
    xhat, scale = center(out)
    final = (xhat * gain + shift).astype(bf16)
    loss = jnp.zeros((1, 1), f32)
    weight = jnp.zeros((1, 1), f32)
    dfinals = []
    for h in range(2):
        mine = final[count * h : count * (h + 1)]
        halves = []
        for m in range(2):
            wh = w_ref[m, :, 512 * h : 512 * (h + 1)]
            at = 1024 * h + 512 * m
            logits = mm(mine, wh) + hb_ref[0:1, at : at + 512]
            ids = lax.broadcasted_iota(jnp.int32, (count, 512), 1) + 512 * m
            coef = jnp.where(ids == lab_ref[:, 2 * h : 2 * h + 1], lw_ref[:, 2 * h : 2 * h + 1], 0.0)
            if h == 0:
                coef = coef + jnp.where(ids == lab_ref[:, 1:2], lw_ref[:, 1:2], 0.0)
            halves.append((wh, logits, coef))
        top = jnp.maximum(*[jnp.max(x[1], -1, keepdims=True) for x in halves])
        exps = [jnp.exp(x[1] - top) for x in halves]
        total = sum(jnp.sum(x, -1, keepdims=True) for x in exps)
        lse = top + jnp.log(total)
        csum = sum(jnp.sum(x[2], -1, keepdims=True) for x in halves)
        dfinal = jnp.zeros((count, D), f32)
        for m in range(2):
            wh, logits, coef = halves[m]
            loss = loss + jnp.sum(jnp.sum(coef * (lse - logits), -1, keepdims=True), 0, keepdims=True)
            dl = csum * (exps[m] / total) - coef
            at = 1024 * h + 512 * m
            dhb_ref[0:1, at : at + 512] = jnp.sum(dl, 0, keepdims=True)
            low = dl.astype(bf16)
            g_head[m, :, 512 * h : 512 * (h + 1)] = mm(mine, low, ATB)
            dfinal = dfinal + mm(low, wh, ABT)
        weight = weight + jnp.sum(csum, 0, keepdims=True)
        dfinals.append(dfinal)
    dfinal = jnp.concatenate(dfinals, 0)
    dz = norm_back(dfinal, xhat, scale, gain)
    low = dz.astype(bf16)
    dn = jnp.zeros_like(dz)
    for m in range(2):
        dh = mm(low, wf_ref[1, m])
        du = (dh.astype(bf16).astype(f32) * gps[m]).astype(bf16)
        gu_ref[0:1, HALF * m : HALF * (m + 1)] = jnp.sum(du.astype(f32), 0, keepdims=True)
        g_ffw[0, m] = mm(normed, du, ATB)
        g_ffw[1, m] = mm(low, hids[m], ATB)
        dn = dn + mm(du, wf_ref[0, m], ABT)
    dmid = dz + norm_back(dn, xhat2, scale2, gain2)
    gv_ref[...] = jnp.zeros_like(gv_ref)
    sums = [dn * xhat2, dn, dmid, dz, dfinal * xhat, dfinal]
    for i, item in enumerate(sums):
        gv_ref[i + 2 : i + 3] = jnp.sum(item, 0, keepdims=True)
    lanes[...] = jnp.zeros_like(lanes)
    for j in range(3):
        for h in range(2):
            lanes[j, pl.ds(END_AT + h, count, stride=ENDS), :] = dmid[
                count * h : count * (h + 1), 128 * j : 128 * (j + 1)
            ]
        dz_ref[:, 128 * j : 128 * (j + 1)] = lanes[j]
    which = lax.broadcasted_iota(jnp.int32, stat_ref.shape, 1)
    stat_ref[...] = jnp.where(which == 0, loss, jnp.where(which == 1, weight, 0.0))
    share(g_ffw.at[0], uo_ref, um_ref, mp)
    share(g_ffw.at[1], do_ref, dm_ref, mp)
    share(g_head, ho_ref, hm_ref, mp)


def pair_shapes(shapes):
    return [jax.ShapeDtypeStruct(s, t) for s in shapes for t in (f32, bf16)]


def head(mid, weights, w_heads, ub, hb, labs, lws, tok):
    outs = pair_shapes([(D, 768), (D, 768), (D, 1024)]) + [
        jax.ShapeDtypeStruct(s, f32)
        for s in (mid.shape, (8, D), (1, FF), (1, 2048), (1, 128))
    ]
    return pl.pallas_call(
        head_kernel,
        grid=(1,),
        in_specs=[
            full_spec(mid.shape),
            pl.BlockSpec((2, 2, D, 768), lambda i: (2, 0, 0, 0), pipeline_mode=pl.Buffered(1)),
        ]
        + [full_spec(x.shape) for x in (w_heads, ub, hb, labs, lws, tok)],
        out_specs=[full_spec(x.shape) for x in outs],
        out_shape=outs,
        scratch_shapes=[
            pltpu.VMEM((3, mid.shape[0], 128), f32),
            pltpu.VMEM((2, 2, D, 768), f32),
            pltpu.VMEM((2, D, 1024), f32),
        ],
        compiler_params=pltpu.CompilerParams(vmem_limit_bytes=60 * MIB),
        name="loss_heads",
    )(mid, weights, w_heads, ub, hb, labs, lws, tok)


def attend_back(g, dho, qkv_ref, p_ref, dproj):
    rows = slice(g * TP, (g + 1) * TP)
    lane = lax.broadcasted_iota(jnp.int32, (TP, 128), 1)
    for j in range(3):
        q = qkv_ref[rows, 128 * j : 128 * (j + 1)]
        k = qkv_ref[rows, D + 128 * j : D + 128 * (j + 1)]
        v = qkv_ref[rows, 2 * D + 128 * j : 2 * D + 128 * (j + 1)]
        do = dho[rows, 128 * j : 128 * (j + 1)]
        qt, kt, dot_ = (jnp.transpose(a, (1, 0)) for a in (q, k, do))
        for s in range(2):
            mine = (lane < 64) if s == 0 else (lane >= 64)
            sub = slice(64 * s, 64 * (s + 1))
            at = 128 * j + 64 * s
            probs = p_ref[6 * g + 2 * j + s]
            dproj[g, 2 * D + at : 2 * D + at + 64] = mm(dot_[sub], probs).astype(bf16)
            dprob = mm(jnp.where(mine, do, jnp.zeros_like(do)), v, ABT)
            p32 = probs.astype(f32)
            delta = jnp.sum(dprob * p32, -1, keepdims=True)
            ds = (p32 * (dprob - delta)).astype(bf16)
            dproj[g, at : at + 64] = (mm(kt[sub], ds, ABT) * 0.125).astype(bf16)
            dproj[g, D + at : D + at + 64] = mm(qt[sub], ds).astype(bf16)


def ends_back(g, dho, kv_ref, q_ref, p_ref, dq, dproj):
    rows = slice(g * TP, (g + 1) * TP)
    ends = slice(g * ENDS, (g + 1) * ENDS)
    lane = lax.broadcasted_iota(jnp.int32, (ENDS, 128), 1)
    for j in range(3):
        tile = slice(128 * j, 128 * (j + 1))
        q = q_ref[ends, tile]
        k = kv_ref[rows, tile]
        v = kv_ref[rows, D + 128 * j : D + 128 * (j + 1)]
        do = dho[ends, tile]
        qt, dot_ = (jnp.transpose(a.astype(f32), (1, 0)).astype(bf16) for a in (q, do))
        outs = []
        for s in range(2):
            mine = (lane < 64) if s == 0 else (lane >= 64)
            sub = slice(64 * s, 64 * (s + 1))
            at = 128 * j + 64 * s
            probs = p_ref[6 * g + 2 * j + s]
            dproj[g, D + at : D + at + 64] = mm(dot_[sub], probs).astype(bf16)
            dprob = mm(jnp.where(mine, do, jnp.zeros_like(do)), v, ABT)
            p32 = probs.astype(f32)
            delta = jnp.sum(dprob * p32, -1, keepdims=True)
            ds = (p32 * (dprob - delta)).astype(bf16)
            outs.append(mm(ds, k))
            dproj[g, at : at + 64] = mm(qt[sub], ds).astype(bf16)
        dq[ends, tile] = (jnp.where(lane < 64, outs[0], outs[1]) * 0.125).astype(bf16)


def backward_kernel(
    dz_ref,
    x_ref,
    mid_ref,
    qkv_ref,
    p_ref,
    ho_ref,
    hid_ref,
    gp_ref,
    x1_ref,
    kv_ref,
    q1_ref,
    p1_ref,
    ho1_ref,
    wa_ref,
    wf_ref,
    tok_ref,
    dzo_ref,
    a0o_ref,
    a0m_ref,
    a1o_ref,
    a1m_ref,
    uo_ref,
    um_ref,
    do_ref,
    dm_ref,
    gv_ref,
    gb_ref,
    gu_ref,
    qkv_w,
    out_w,
    dqkv,
    dkv,
    dq1,
    dout,
    g_ffw,
    g_att,
    nbuf,
    dz,
    dn,
    du,
    dq,
    dproj,
):
    step = pl.program_id(0)
    mp = lax.axis_index("mp")

    def row(layer, i):
        return token_row(tok_ref, layer, i)

    @pl.when(step == 0)
    def _():
        for ref in (gv_ref, gb_ref, gu_ref, g_ffw, dqkv, dkv, dq1, dout):
            ref[...] = jnp.zeros_like(ref)
        for layer in range(LAYERS):
            attn_tiles(wa_ref.at[layer], qkv_w.at[layer], out_w.at[layer])

    def pull(src, gain, dz_out, at):
        xhat, scale = center(src[...])
        dy = dn[...]
        new = dz[...] + norm_back(dy, xhat, scale, gain)
        dz_out[...] = new
        gv_ref[at : at + 1] += jnp.sum(dy * xhat, 0, keepdims=True)
        gv_ref[at + 1 : at + 2] += jnp.sum(dy, 0, keepdims=True)

    ones = jnp.ones((TP, 128), bf16)
    low = dz_ref[...].astype(bf16)
    dout[1] += mm(low, ho1_ref[...], ATB)
    dho = mm(low, out_w[1]).astype(bf16)
    norm_rows(x1_ref, row(1, 0), row(1, 1), nbuf)
    dz[...] = jnp.zeros_like(dz)
    for g in range(GRP):
        rows = slice(g * TP, (g + 1) * TP)
        ends_back(g, dho, kv_ref, q1_ref, p1_ref, dq, dproj)
        dkv[:, :D] += mm(dproj[g, : 2 * D], nbuf[rows])
        dkv[:, D:] += mm(dproj[g, : 2 * D], ones)
        dn[rows] = jnp.transpose(mm(qkv_w[1, :, D:], dproj[g, : 2 * D]), (1, 0))
    dq_all = dq[...]
    ends = jnp.concatenate([nbuf[(g + 1) * TP - ENDS : (g + 1) * TP] for g in range(GRP)], 0)
    dq1[...] += mm(ends, dq_all, ATB)
    gb_ref[1:2, :D] += jnp.sum(dq_all.astype(f32), 0, keepdims=True)
    more = mm(dq_all, qkv_w[1, :, :D], ABT)
    for g in range(GRP):
        last = slice((g + 1) * TP - ENDS, (g + 1) * TP)
        part = slice(g * ENDS, (g + 1) * ENDS)
        dn[last] += more[part]
        dz[last] = dz_ref[part]
    pull(x1_ref, row(1, 0), dz, 6)

    norm_rows(mid_ref, row(0, 2), row(0, 3), nbuf)
    gv_ref[5:6] += jnp.sum(dz[...], 0, keepdims=True)
    rz = dz[...].astype(bf16)
    rzt = jnp.transpose(rz, (1, 0))
    nt = jnp.transpose(nbuf[...], (1, 0))
    for m in range(2):
        cols = slice(HALF * m, HALF * (m + 1))
        dh = mm(rz, wf_ref[1, m])
        du[...] = (dh.astype(bf16).astype(f32) * gp_ref[:, cols].astype(f32)).astype(bf16)
        gu_ref[0:1, cols] += jnp.sum(du[...].astype(f32), 0, keepdims=True)
        g_ffw[1, m] += mm(rzt, hid_ref[:, cols])
        g_ffw[0, m] += mm(nt, du[...])
        part = mm(du[...], wf_ref[0, m], ABT)
        dn[...] = part if m == 0 else dn[...] + part
    pull(mid_ref, row(0, 2), dz, 2)
    gv_ref[4:5] += jnp.sum(dz[...], 0, keepdims=True)
    rz2 = dz[...].astype(bf16)
    dout[0] += mm(jnp.transpose(rz2, (1, 0)), ho_ref[...])
    dho = mm(rz2, out_w[0]).astype(bf16)
    norm_rows(x_ref, row(0, 0), row(0, 1), nbuf)
    for g in range(GRP):
        rows = slice(g * TP, (g + 1) * TP)
        attend_back(g, dho, qkv_ref, p_ref, dproj)
        dqkv[:, :D] += mm(dproj[g], nbuf[rows])
        dqkv[:, D:] += mm(dproj[g], ones)
        dn[rows] = jnp.transpose(mm(qkv_w[0], dproj[g]), (1, 0))
    pull(x_ref, row(0, 0), dzo_ref, 0)

    @pl.when(step == pl.num_programs(0) - 1)
    def _():
        for layer in range(LAYERS):
            for t in range(4):
                for j in range(3):
                    at = D * t + 128 * j
                    if t == 3:
                        tile = dout[layer, :, 128 * j : 128 * (j + 1)]
                    elif layer == 0:
                        tile = jnp.transpose(dqkv[at : at + 128, :D], (1, 0))
                    elif t == 0:
                        tile = dq1[:, 128 * j : 128 * (j + 1)]
                    else:
                        tile = jnp.transpose(dkv[at - D : at - D + 128, :D], (1, 0))
                    if j < 2:
                        g_att[layer, j, :, 128 * t : 128 * (t + 1)] = tile
                    else:
                        for m in range(2):
                            lo = 512 + 64 * t
                            g_att[layer, m, :, lo : lo + 64] = tile[:, 64 * m : 64 * (m + 1)]
        share(g_att.at[0], a0o_ref, a0m_ref, mp)
        share(g_att.at[1], a1o_ref, a1m_ref, mp)
        share(g_ffw.at[0], uo_ref, um_ref, mp)
        share(g_ffw.at[1], do_ref, dm_ref, mp)
        sums = jnp.transpose(dqkv[:, D:], (1, 0))[0:1]
        gb_ref[0:1, :D] = sums[:, :D]
        gb_ref[0:1, D:] = sums[:, 2 * D :]
        gb_ref[1:2, D:] = jnp.transpose(dkv[:, D:], (1, 0))[0:1, D:]


def attn_tiles(w_ref, qkv_w, out_w):
    for t in range(4):
        cols = 128 * t
        pieces = [w_ref[0, :, cols : cols + 128], w_ref[1, :, cols : cols + 128]]
        tile = 512 + 128 * (t // 2)
        lane = 64 * (t % 2)
        pieces.append(
            jnp.concatenate(
                [w_ref[m, :, tile : tile + 128][:, lane : lane + 64] for m in range(2)], 1
            )
        )
        for j in range(3):
            if t < 3:
                at = D * t + 128 * j
                qkv_w[:, at : at + 128] = pieces[j]
            else:
                out_w[:, 128 * j : 128 * (j + 1)] = pieces[j]


def backward(dz, kept, weights, tok):
    steps = dz.shape[0] // (GRP * ENDS)
    x_shape = kept[0].shape
    shares = pair_shapes([(D, 768)] * 4)
    extra = [jax.ShapeDtypeStruct(s, f32) for s in ((8, D), (2, 2 * D), (1, FF))]
    return pl.pallas_call(
        backward_kernel,
        grid=(steps,),
        in_specs=[block_of(a.shape, steps) for a in (dz,) + tuple(kept)]
        + [
            pl.BlockSpec((2, 2, D, 768), lambda i: (0, 0, 0, 0), pipeline_mode=pl.Buffered(1)),
            pl.BlockSpec((2, 2, D, 768), lambda i: (1, 0, 0, 0), pipeline_mode=pl.Buffered(1)),
            full_spec(tok.shape),
        ],
        out_specs=[block_of(x_shape, steps)] + [full_spec(x.shape) for x in shares + extra],
        out_shape=[jax.ShapeDtypeStruct(x_shape, f32)] + shares + extra,
        scratch_shapes=[
            pltpu.VMEM((LAYERS, D, 3 * D), bf16),
            pltpu.VMEM((LAYERS, D, D), bf16),
            pltpu.VMEM((3 * D, 512), f32),
            pltpu.VMEM((2 * D, 512), f32),
            pltpu.VMEM((D, D), f32),
            pltpu.VMEM((LAYERS, D, D), f32),
            pltpu.VMEM((2, 2, D, 768), f32),
            pltpu.VMEM((LAYERS, 2, D, 768), f32),
            pltpu.VMEM((ROWS, D), bf16),
            pltpu.VMEM((ROWS, D), f32),
            pltpu.VMEM((ROWS, D), f32),
            pltpu.VMEM((ROWS, HALF), bf16),
            pltpu.VMEM((GRP * ENDS, D), bf16),
            pltpu.VMEM((GRP, 3 * D, TP), bf16),
        ],
        compiler_params=pltpu.CompilerParams(vmem_limit_bytes=62 * MIB),
        name="backward_layers",
    )(dz, *kept, weights, weights, tok)


def patch_grad_kernel(
    inv_ref,
    mix_ref,
    dz_ref,
    own_ref,
    far_ref,
    gvb_ref,
    gvh_ref,
    po_ref,
    pm_ref,
    eo_ref,
    em_ref,
    dzo,
    dzf,
    tok,
    g_patch,
    g_seg,
):
    mp = lax.axis_index("mp")
    count = far_ref.shape[0] // PATCHES
    both = own_ref.shape[0] // PATCHES
    dzo[...] = jnp.zeros_like(dzo)
    total = jnp.zeros((TP, D), f32)
    for k in range(count):
        w = mix_ref[k]
        for j in range(3):
            part = dz_ref[k * TP : k * TP + PATCHES, 128 * j : 128 * (j + 1)]
            dzo[j, pl.ds(inv_ref[k], PATCHES, stride=both), :] = w * part
            dzf[j, pl.ds(k, PATCHES, stride=count), :] = (1.0 - w) * part
        total = total + dz_ref[k * TP : (k + 1) * TP]
    tok[...] = jnp.zeros_like(tok)
    tok[:TP] = total
    tok[TP : TP + 8] = gvb_ref[...]
    tok[TP + 8 : TP + 14] = gvh_ref[2:8]
    turned = jnp.transpose(tok[...], (1, 0))
    for m in range(2):
        g_seg[m] = turned[:, 128 * m : 128 * (m + 1)]
    for j in range(3):
        lo = jnp.transpose(dzo[j].astype(bf16), (1, 0))
        lf = jnp.transpose(dzf[j].astype(bf16), (1, 0))
        for m in range(2):
            cols = slice(D * m, D * (m + 1))
            g_patch[m, 128 * j : 128 * (j + 1)] = mm(lo, own_ref[:, cols]) + mm(lf, far_ref[:, cols])
    share(g_patch, po_ref, pm_ref, mp)
    share(g_seg, eo_ref, em_ref, mp)


def patch_grad(inv, mix, dz, own, far, gvb, gvh):
    outs = pair_shapes([(D, D), (D, 128)])
    return pl.pallas_call(
        patch_grad_kernel,
        grid=(1,),
        in_specs=[pl.BlockSpec(memory_space=pltpu.SMEM)] * 2
        + [full_spec(a.shape) for a in (dz, own, far, gvb, gvh)],
        out_specs=[full_spec(x.shape) for x in outs],
        out_shape=outs,
        scratch_shapes=[
            pltpu.VMEM((3, own.shape[0], 128), f32),
            pltpu.VMEM((3, far.shape[0], 128), f32),
            pltpu.VMEM((256, D), f32),
            pltpu.VMEM((2, D, D), f32),
            pltpu.VMEM((2, D, 128), f32),
        ],
        compiler_params=pltpu.CompilerParams(vmem_limit_bytes=56 * MIB),
        name="patch_gradient",
    )(inv, mix, dz, own, far, gvb, gvh)


def link_orders(bits):
    far = [b for b in (range(1, bits, 2) if bits == 6 else [3]) if b < bits]
    near = [b for b in range(bits) if b not in far]
    return [near[i:] + near[:i] for i in range(len(near))], far


def gather_plan(bits, turns):
    near, far = link_orders(bits)
    deep = far + [near[0][-1]]
    flat = near[0][:-1]
    return [flat[t:] + flat[:t] for t in turns], deep


def chunk_plan(bits, cuts):
    near, far = link_orders(bits)
    return [
        (cuts[i], cuts[i + 1] - cuts[i], near[i % len(near)], far) for i in range(len(cuts) - 1)
    ]


def mesh_place():
    return lax.axis_index("dp"), lax.axis_index("mp")


def bit_of(value, bit):
    return (value // 2**bit) % 2


def flipped(value, bit):
    return value + 2**bit * (1 - 2 * bit_of(value, bit))


def meet(bits):
    dp, mp = mesh_place()
    barrier = pltpu.get_barrier_semaphore()
    for peer in [(dp, 1 - mp)] + [(flipped(dp, b), mp) for b in range(bits)]:
        pl.semaphore_signal(barrier, inc=1, device_id=peer, device_id_type=MESH)
    pl.semaphore_wait(barrier, bits + 1)


def push(src, dst, send, recv, peer):
    copy = pltpu.make_async_remote_copy(
        src_ref=src, dst_ref=dst, send_sem=send, recv_sem=recv, device_id=peer, device_id_type=MESH
    )
    copy.start()
    return copy


def held_part(ref, bits, lead, dp, done=(), flip=None):
    idx = list(lead)
    for b in reversed(bits):
        mine = bit_of(dp, b)
        idx.append(pl.ds(0, 2) if b in done else (1 - mine if b == flip else mine))
    return ref.at[tuple(idx)]


def gather_front_kernel(bits, tab_ref, att_ref, ffw_ref, sb_ref, *refs):
    w_refs = refs[:2]
    far_refs = refs[2:5]
    sbo_ref, tabr, stage_p, stage_e, stage_h, s_loc, s_tab = refs[5:12]
    s_send, s_recv, f_send, f_recv, m_send, m_recv = refs[12:]
    dp, mp = mesh_place()
    mate = (dp, 1 - mp)
    turns, deep = gather_plan(bits, FRONT_TURNS)
    far = deep[:-1]
    every = list(range(bits))

    def part(c, *args):
        return held_part(w_refs[c], every, (mp,), dp, *args)

    def main(c, *args):
        return held_part(far_refs[c], far, (), dp, *args)

    meet(bits)
    c_tab = push(tab_ref.at[1 - mp], tabr, s_tab.at[0], s_tab.at[1], mate)
    c_sb = push(sb_ref, sbo_ref.at[mp], s_tab.at[2], s_tab.at[3], mate)
    local = [
        pltpu.make_async_copy(sb_ref, sbo_ref.at[mp], s_loc.at[0]),
        pltpu.make_async_copy(att_ref, main(0), s_loc.at[1]),
        pltpu.make_async_copy(ffw_ref, main(1), s_loc.at[2]),
    ]
    for copy in local:
        copy.start()
    c_tab.wait()
    mine = tab_ref[mp].astype(f32)
    other = tabr[...].astype(f32)
    first = jnp.where(mp == 0, mine, other)
    second = jnp.where(mp == 0, other, mine)
    table = jnp.concatenate([first, second], 0).astype(bf16)
    stage_p[...] = table[:, :D]
    stage_e[...] = table[:, D:F_COLS]
    stage_h[...] = table[:, F_COLS:]
    tables = [
        pltpu.make_async_copy(stage_p, part(0), s_loc.at[3]),
        pltpu.make_async_copy(stage_e, part(1), s_loc.at[4]),
        pltpu.make_async_copy(stage_h, main(2), s_loc.at[5]),
    ]
    for copy in tables:
        copy.start()
    for copy in tables + local:
        copy.wait()
    copies = {}
    forwards = []
    wide = {}
    for s in range(bits + 1):
        for c in range(2):
            order = deep + turns[c]
            if s:
                copies[c, s - 1].wait_recv()
            if s < bits:
                held = part(c, order[:s])
                copies[c, s] = push(
                    held, held, s_send.at[c, s], s_recv.at[c, s], (flipped(dp, order[s]), mp)
                )
            got = part(c, order[: s - 1], order[s - 1]) if s else part(c)
            forwards.append(push(got, got, f_send.at[c, s], f_recv.at[c, s], mate))
        at = s - len(deep)
        if 0 <= at < len(far):
            for c in range(3):
                if at:
                    wide[c, at - 1].wait_recv()
                held = main(c, far[:at])
                wide[c, at] = push(
                    held, held, m_send.at[c, at], m_recv.at[c, at], (flipped(dp, far[at]), mp)
                )
    for copy in forwards:
        copy.wait()
    for copy in copies.values():
        copy.wait_send()
    for copy in wide.values():
        copy.wait_send()
    for c in range(3):
        wide[c, len(far) - 1].wait_recv()
    c_sb.wait()


def gather_front(tab, att, ffw, sb, n_data):
    bits = n_data.bit_length() - 1
    rows = D // n_data
    _, far = link_orders(bits)
    sems = pltpu.SemaphoreType.DMA
    anywhere = pl.BlockSpec(memory_space=pl.ANY)
    inside = pl.BlockSpec(memory_space=pltpu.VMEM)
    heads = T_COLS - F_COLS
    deep_shape = (2,) * len(far)
    return pl.pallas_call(
        functools.partial(gather_front_kernel, bits),
        in_specs=[inside] * 4,
        out_specs=[anywhere] * 5 + [inside],
        out_shape=[
            jax.ShapeDtypeStruct((2,) * (bits + 1) + (rows, w), bf16) for w in FRONT_WIDTHS
        ]
        + [
            jax.ShapeDtypeStruct(deep_shape + att.shape, bf16),
            jax.ShapeDtypeStruct(deep_shape + ffw.shape, bf16),
            jax.ShapeDtypeStruct(deep_shape + (rows, heads), bf16),
            jax.ShapeDtypeStruct((2,) + sb.shape, f32),
        ],
        scratch_shapes=[
            pltpu.VMEM(tab.shape[1:], bf16),
            pltpu.VMEM((rows, FRONT_WIDTHS[0]), bf16),
            pltpu.VMEM((rows, FRONT_WIDTHS[1]), bf16),
            pltpu.VMEM((rows, heads), bf16),
            sems((6,)),
            sems((4,)),
            sems((2, bits)),
            sems((2, bits)),
            sems((2, bits + 1)),
            sems((2, bits + 1)),
            sems((3, len(far))),
            sems((3, len(far))),
        ],
        compiler_params=pltpu.CompilerParams(
            collective_id=2, has_side_effects=True, vmem_limit_bytes=60 * MIB
        ),
        name="gather_front",
    )(tab, att, ffw, sb)


def gather_main_kernel(bits, *refs):
    far_refs, deep_refs = refs[:3], refs[3:6]
    w_ref, h_ref = refs[6:8]
    s_loc, s_send, s_recv, f_send, f_recv = refs[8:]
    dp, mp = mesh_place()
    mate = (dp, 1 - mp)
    turns, deep = gather_plan(bits, MAIN_TURNS)
    far, last = deep[:-1], deep[-1]
    every = list(range(bits))
    steps = bits - len(deep)
    chunks = len(MAIN_WIDTHS)

    def part(c, *args):
        if c < chunks - 1:
            return held_part(w_ref, every, (c, mp), dp, *args)
        return held_part(h_ref, every, (mp,), dp, *args)

    def piece(c, deep_side):
        refs_in = deep_refs if deep_side else far_refs
        lead = (slice(None),) * len(far)
        if c == chunks - 1:
            return refs_in[2]
        if c < LAYERS:
            return refs_in[0].at[lead + (c,)]
        return refs_in[1].at[lead + (c - LAYERS,)]

    meet(bits)
    copies = {}
    forwards = []
    local = []
    for c in range(chunks):
        for i in range(2):
            dst = part(c, far, last) if i else part(c, far)
            local.append(pltpu.make_async_copy(piece(c, i), dst, s_loc.at[c, i]))
            local[-1].start()
    for s in range(steps + 1):
        for c in range(chunks):
            order = turns[c]
            if s:
                copies[c, s - 1].wait_recv()
            else:
                local[2 * c].wait()
                local[2 * c + 1].wait()
            done = deep + order[:s]
            if s < steps:
                held = part(c, done)
                copies[c, s] = push(
                    held, held, s_send.at[c, s], s_recv.at[c, s], (flipped(dp, order[s]), mp)
                )
            got = part(c, done[:-1], done[-1]) if s else part(c, done)
            forwards.append(push(got, got, f_send.at[c, s], f_recv.at[c, s], mate))
    for copy in forwards:
        copy.wait()
    for copy in copies.values():
        copy.wait_send()


def gather_main(far_parts, deep_parts, n_data):
    bits = n_data.bit_length() - 1
    rows = D // n_data
    near, _ = link_orders(bits)
    steps = len(near[0]) - 1
    chunks = len(MAIN_WIDTHS)
    sems = pltpu.SemaphoreType.DMA
    anywhere = pl.BlockSpec(memory_space=pl.ANY)
    places = (2,) * (bits + 1) + (rows,)
    main, heads = pl.pallas_call(
        functools.partial(gather_main_kernel, bits),
        in_specs=[pl.BlockSpec(memory_space=pltpu.VMEM)] * 6,
        out_specs=[anywhere] * 2,
        out_shape=[
            jax.ShapeDtypeStruct((chunks - 1,) + places + (768,), bf16),
            jax.ShapeDtypeStruct(places + (1024,), bf16),
        ],
        scratch_shapes=[
            sems((chunks, 2)),
            sems((chunks, steps)),
            sems((chunks, steps)),
            sems((chunks, steps + 1)),
            sems((chunks, steps + 1)),
        ],
        compiler_params=pltpu.CompilerParams(
            collective_id=0, has_side_effects=True, vmem_limit_bytes=60 * MIB
        ),
        cost_estimate=pl.CostEstimate(flops=0, bytes_accessed=150 * MIB, transcendentals=0),
        name="gather_main",
    )(*far_parts, *deep_parts)
    return main.reshape(chunks - 1, 2, D, 768), heads.reshape(2, D, 1024)


def reduce_plan(bits, turns):
    near, far = link_orders(bits)
    return [near[t % len(near)] + far for t in turns]


def block_index(free, fixed):
    def index(t):
        total = fixed
        for j, b in enumerate(free):
            total = total + ((t // 2**j) % 2) * 2**b
        return total

    return index


def reduce_kernel(bits, widths, turns, *refs):
    n = len(widths)
    own, mate_src = refs[:n], refs[n : 2 * n]
    smalls = refs[2 * n : 2 * n + 5]
    outs = refs[2 * n + 5 : 3 * n + 5]
    obun_ref, info_ref = refs[3 * n + 5 : 3 * n + 7]
    refs = refs[3 * n + 7 :]
    mrecv, acc = refs[:n], refs[n : 2 * n]
    refs = refs[2 * n :]
    sbufs, rbufs = refs[: n * bits], refs[n * bits : 2 * n * bits]
    bun, bunr, tsend, sq, sqr, m_sem, s_sem, r_sem, b_sem, q_sem, t_sem = refs[2 * n * bits :]
    dp, mp = mesh_place()
    mate = (dp, 1 - mp)
    orders = reduce_plan(bits, turns)
    rows = D // 2**bits
    group = max(rows, 48)
    per = group // rows
    small = rows // 2

    at = 0
    for ref in smalls:
        for i in range(ref.shape[0]):
            bun[:, at : at + ref.shape[1]] = ref[i : i + 1]
            at += ref.shape[1]
    meet(bits)
    mcopies = [
        push(mate_src[c], mrecv[c], m_sem.at[c, 0], m_sem.at[c, 1], mate) for c in range(n)
    ]
    bcopies = [push(bun, bunr.at[0], b_sem.at[0, 0], b_sem.at[0, 1], mate)]

    def loop(total, body):
        def step(t, carry):
            body(t)
            return carry

        lax.fori_loop(0, total, step, 0)

    copies = {}

    def split(order, s, sent):
        free = [b for b in range(bits) if b not in order[: s + 1]]
        fixed = sum((bit_of(dp, b) * 2**b for b in order[:s]), 0)
        last = bit_of(dp, order[s])
        fixed = fixed + (1 - last if sent else last) * 2 ** order[s]
        return 2 ** len(free), block_index(free, fixed)

    def send_stage(c, s):
        total, index = split(orders[c], s, True)
        sbuf = sbufs[c * bits + s]

        def body(t):
            sbuf[t] = acc[c][index(t)].astype(bf16)

        loop(total, body)
        copies[c, s] = push(
            sbuf,
            rbufs[c * bits + s],
            s_sem.at[c, s],
            r_sem.at[c, s],
            (flipped(dp, orders[c][s]), mp),
        )

    def take_stage(c, s):
        copies[c, s].wait_recv()
        total, index = split(orders[c], s, False)
        rbuf = rbufs[c * bits + s]

        def body(t):
            acc[c][index(t)] += rbuf[t].astype(f32)

        loop(total, body)

    for c in range(n):
        mcopies[c].wait_recv()

        def body(b):
            rs = pl.ds(pl.multiple_of(b * group, group), group)
            got = own[c][rs] + mrecv[c][rs].astype(f32)
            for i in range(per):
                acc[c][b * per + i] = got[rows * i : rows * (i + 1)]

        loop(D // group, body)
        send_stage(c, 0)
    for s in range(1, bits + 1):
        for c in range(n):
            take_stage(c, s - 1)
            if s < bits:
                send_stage(c, s)
        bcopies[-1].wait()
        bun[...] = bun[...] + bunr[s - 1]
        bcopies.append(
            push(bun, bunr.at[s], b_sem.at[s, 0], b_sem.at[s, 1], (flipped(dp, s - 1), mp))
        )
    tails = []
    for c in range(n):
        mine = acc[c][dp]
        if c in TABLE_CHUNKS:
            k = TABLE_CHUNKS.index(c)
            send, recv = tsend[2 * k], tsend[2 * k + 1]
            send[...] = jnp.where(mp == 0, mine[small:], mine[:small])
            outs[c][mp] = jnp.where(mp == 0, mine[:small], mine[small:])
            tails.append((c, recv, push(send, recv, t_sem.at[k, 0], t_sem.at[k, 1], mate)))
        else:
            outs[c][...] = mine
    total = jnp.zeros((1, 1), f32)
    for c in range(n):
        if c not in TABLE_CHUNKS:
            total = total + jnp.sum(outs[c][...] * outs[c][...], keepdims=True)
    for c, recv, copy in tails:
        copy.wait()
        outs[c][1 - mp] = recv[...]
        for m in range(2):
            total = total + jnp.sum(outs[c][m] * outs[c][m], keepdims=True)
    sq[0] = jnp.broadcast_to(total, (8, 128))
    bcopies[-1].wait()
    final = bun[...] + bunr[bits]
    obun_ref[...] = final
    shared = jnp.sum(final[:, 128:] * final[:, 128:], keepdims=True)
    for s in range(bits + 1):
        peer = mate if s == 0 else (flipped(dp, s - 1), mp)
        copy = push(sq.at[s], sqr.at[s], q_sem.at[s, 0], q_sem.at[s, 1], peer)
        copy.wait()
        sq[s + 1] = sq[s] + sqr[s]
    squares = sq[bits + 1] + shared
    loss, weight = final[:, 0:1], final[:, 1:2]
    norm = jnp.sqrt(squares) / weight
    factor = jnp.minimum(1.0, clip_limit / norm) / weight
    which = lax.broadcasted_iota(jnp.int32, (8, 128), 1)
    info = jnp.where(which == 0, loss, jnp.where(which == 1, weight, norm))
    info_ref[...] = jnp.where(which == 3, factor, info)
    for copy in mcopies:
        copy.wait_send()
    for copy in copies.values():
        copy.wait_send()


def reduce_all(own, mates, smalls, turns, n_data):
    bits = n_data.bit_length() - 1
    rows = D // n_data
    widths = [x.shape[1] for x in own]
    n = len(widths)
    sems = pltpu.SemaphoreType.DMA
    inside = pl.BlockSpec(memory_space=pltpu.VMEM)
    anywhere = pl.BlockSpec(memory_space=pl.ANY)
    bufs = [
        pltpu.VMEM((2 ** (bits - 1 - s), rows, w), bf16) for w in widths for s in range(bits)
    ]
    length = sum(x.shape[0] * x.shape[1] for x in smalls)
    outs = [
        jax.ShapeDtypeStruct((2, rows // 2, w) if c in TABLE_CHUNKS else (rows, w), f32)
        for c, w in enumerate(widths)
    ]
    tails = [
        pltpu.VMEM((rows // 2, widths[c]), f32) for c in TABLE_CHUNKS for _ in range(2)
    ]

    def kernel(*refs):
        cut = len(refs) - 10 - len(tails)
        head, rest = refs[:cut], refs[cut:]
        tsend, rest = rest[: len(tails)], rest[len(tails) :]
        reduce_kernel(bits, widths, turns, *head, rest[0], rest[1], tsend, *rest[2:])

    return pl.pallas_call(
        kernel,
        in_specs=[inside] * n + [anywhere] * n + [inside] * len(smalls),
        out_specs=[inside] * (n + 2),
        out_shape=outs
        + [
            jax.ShapeDtypeStruct((1, length), f32),
            jax.ShapeDtypeStruct((8, 128), f32),
        ],
        scratch_shapes=[pltpu.VMEM((D, w), bf16) for w in widths]
        + [pltpu.VMEM((n_data, rows, w), f32) for w in widths]
        + bufs
        + bufs
        + tails
        + [
            pltpu.VMEM((1, length), f32),
            pltpu.VMEM((bits + 1, 1, length), f32),
            pltpu.VMEM((bits + 2, 8, 128), f32),
            pltpu.VMEM((bits + 1, 8, 128), f32),
            sems((n, 2)),
            sems((n, bits)),
            sems((n, bits)),
            sems((bits + 1, 2)),
            sems((bits + 1, 2)),
            sems((len(TABLE_CHUNKS), 2)),
        ],
        compiler_params=pltpu.CompilerParams(
            collective_id=1, has_side_effects=True, vmem_limit_bytes=62 * MIB
        ),
        name="reduce_gradients",
    )(*own, *mates, *smalls)


def adamw(master, first, second, gradient, rate, decay):
    first = beta_one * first + (1.0 - beta_one) * gradient
    second = beta_two * second + (1.0 - beta_two) * gradient * gradient
    first_hat = first / (1.0 - beta_one**STEP)
    second_hat = second / (1.0 - beta_two**STEP)
    master = master - rate * (first_hat / (jnp.sqrt(second_hat) + adam_eps) + decay * master)
    return (master, first, second)


def pack_tables(tab, vec):
    small = tab.shape[0]
    token = tab[:, PD : PD + TOK]
    seg = jnp.concatenate(
        [
            token[:, 2:],
            token[:, :2],
            jnp.zeros((small, TP - TOK), f32),
            vec,
            jnp.zeros((small, 256 - TP - vec.shape[1]), f32),
        ],
        1,
    )
    heads = jnp.pad(tab[:, PD + TOK :].reshape(small, 2, CLS), ((0, 0), (0, 0), (0, 1024 - CLS)))
    parts = [tab[:, :PD], seg, heads[:, 0], heads[:, 1]]
    return [
        jnp.concatenate([x[:, x.shape[1] // 2 * m : x.shape[1] // 2 * (m + 1)] for x in parts], 1)
        for m in range(2)
    ]


def unpack_tables(halves):
    cuts = (0, D, D + 128, 1024, T_COLS)
    segs = [
        jnp.concatenate([halves[m][:, cuts[i] : cuts[i + 1]] for m in range(2)], 1)
        for i in range(4)
    ]
    token = segs[1]
    tab = jnp.concatenate(
        [
            segs[0],
            token[:, PATCHES:TOK],
            token[:, :PATCHES],
            segs[2][:, :CLS],
            segs[3][:, :CLS],
        ],
        1,
    )
    return tab, token[:, TP : TP + 6 * LAYERS + 2]


def pack_attention(attn):
    layers, rows, _ = attn.shape
    a = attn.reshape(layers, rows, 3, 4, HD)
    two = a[:, :, :2].transpose(0, 1, 3, 2, 4).reshape(layers, rows, 512)
    one = a[:, :, 2].reshape(layers, rows, 256)
    return jnp.concatenate([two, one], -1)


def unpack_attention(packed):
    layers, rows, _ = packed.shape
    two = packed[..., :512].reshape(layers, rows, 4, 2, HD).transpose(0, 1, 3, 2, 4)
    one = packed[..., 512:].reshape(layers, rows, 1, 4, HD)
    return jnp.concatenate([two, one], 2).reshape(layers, rows, 768)


PAIRS = (0, 1, 3, 4, 2, 5)


def shards(
    pixels,
    labels,
    teacher,
    partner,
    mix_weight,
    class_weight,
    tables,
    tables_first,
    tables_second,
    vectors,
    vectors_first,
    vectors_second,
    attention,
    attention_first,
    attention_second,
    feedforward,
    feedforward_first,
    feedforward_second,
    split_bias,
    split_bias_first,
    split_bias_second,
    head_bias,
    head_bias_first,
    head_bias_second,
):
    n_data = lax.axis_size("dp")
    dp, mp = mesh_place()
    images_here = pixels.shape[0]
    count = images_here // 2
    rows = D // n_data
    far_rank = (dp + n_data // 2) % n_data
    far_pairs = [(i, (i + n_data // 2) % n_data) for i in range(n_data)]
    pix = pixels.transpose(1, 0, 2)
    far_ids = mp * count + jnp.arange(count, dtype=jnp.int32)
    match = (partner - far_rank * images_here)[None, :] == far_ids[:, None]
    inv = jnp.sum(
        jnp.where(match, jnp.arange(images_here, dtype=jnp.int32)[None, :], 0), 1
    ).astype(jnp.int32)
    mix = jnp.sum(jnp.where(match, mix_weight[None, :], 0.0), 1)
    own_lab = jnp.take(labels, dp * images_here + inv)
    far_lab = lax.dynamic_slice_in_dim(labels, far_rank * images_here + mp * count, count, 0)
    own_teach = jnp.sum(jnp.where(match, teacher[None, :], 0), 1).astype(jnp.int32)
    labs = jnp.stack([own_lab, far_lab, own_teach], 1)
    lws = jnp.take(class_weight, labs) * jnp.stack([mix, 1.0 - mix, jnp.ones_like(mix)], 1)
    labs = jnp.pad(labs, ((0, 0), (0, 125)))
    lws = jnp.pad(lws, ((0, 0), (0, 125)))

    tab_halves = pack_tables(tables.T, vectors.T)
    tab = jnp.stack(tab_halves).astype(bf16)
    att = pack_attention(attention).astype(bf16)
    ffw = feedforward.transpose(0, 2, 1, 3).reshape(2 * LAYERS, rows, HALF).astype(bf16)
    front, seg, *far_parts, sb = gather_front(tab, att, ffw, split_bias, n_data)
    front = front.reshape(2, D, FRONT_WIDTHS[0])
    seg = seg.reshape(2, D, FRONT_WIDTHS[1])
    base = jnp.reshape(mp * count, (1,)).astype(jnp.int32)
    pix_flat = pix.reshape(PATCHES * images_here, PD)
    deep = link_orders(n_data.bit_length() - 1)[0][0][-1]
    pairs = [(i, i ^ (1 << deep)) for i in range(n_data)]
    deep_parts = [lax.ppermute(x, "dp", pairs) for x in far_parts]
    own, send = embed(inv, base, pix_flat, front, count)
    deep_parts, send = lax.optimization_barrier((deep_parts, send))
    far = lax.ppermute(send, "dp", far_pairs)
    weights, w_heads = gather_main(far_parts, deep_parts, n_data)
    sb = sb.astype(bf16).astype(f32)
    qv = sb[:, :, :D].transpose(1, 0, 2).reshape(LAYERS, HEADS, 2, HD)[:, jnp.array(PAIRS)]
    bias = qv.transpose(0, 2, 1, 3).reshape(LAYERS, 2 * D)
    bias = jnp.pad(bias, ((0, 8 - LAYERS), (0, 0)))
    ub = jnp.pad(sb[:, :, D:].transpose(1, 0, 2).reshape(LAYERS, FF), ((0, 8 - LAYERS), (0, 0)))
    hb = jnp.pad(
        head_bias.astype(bf16).astype(f32).reshape(2, CLS),
        ((0, 0), (0, 1024 - CLS)),
        constant_values=-1e30,
    ).reshape(1, -1)
    hb = jnp.pad(hb, ((0, 7), (0, 0)))

    pix_mine = lax.dynamic_slice_in_dim(pix, mp * count, count, 1)
    pix_mine, far, weights = lax.optimization_barrier((pix_mine, far, weights))
    pix_far = lax.ppermute(pix_mine, "dp", far_pairs)
    *kept, mid, tok = forward(mix, own, far, seg, weights, bias, ub)
    u1o, u1m, d1o, d1m, ho, hm, dz, gvh, gu1, dhb, stat = head(
        mid, weights, w_heads, ub, hb, labs, lws, tok
    )
    dz0, a0o, a0m, a1o, a1m, u0o, u0m, d0o, d0m, gvb, gb, gu0 = backward(dz, kept, weights, tok)
    po, pm, eo, em = patch_grad(
        inv, mix, dz0, pix_flat, pix_far.reshape(PATCHES * count, PD), gvb, gvh
    )
    own_parts = [a0o, a1o, u0o, d0o, u1o, d1o, ho, po, eo]
    mate_parts = [a0m, a1m, u0m, d0m, u1m, d1m, hm, pm, em]
    *g, flat, info = reduce_all(
        own_parts, mate_parts, [stat, gb, gu0, gu1, dhb], REDUCE_TURNS, n_data
    )
    flat = flat.reshape(-1)
    loss_sum, weight_sum, grad_norm, factor = (info[0, i] for i in range(4))
    at = 128
    g_split = []
    for layer in range(LAYERS):
        q = flat[at : at + D].reshape(3, 2, HD)
        v = flat[at + D : at + 2 * D].reshape(3, 2, HD)
        ups = 128 + 4 * D + FF * layer
        up = lax.dynamic_slice_in_dim(flat[ups : ups + FF], mp * HALF, HALF, 0)
        at += 2 * D
        qv = jnp.stack([q, v], 2)
        pick = lax.dynamic_index_in_dim(
            jnp.stack(
                [
                    jnp.stack([qv[0, 0], qv[0, 1], qv[2, 0]]),
                    jnp.stack([qv[1, 0], qv[1, 1], qv[2, 1]]),
                ]
            ),
            mp,
            0,
            False,
        )
        g_split.append(jnp.concatenate([pick.reshape(-1), up]))
    g_split = jnp.stack(g_split)
    at = 128 + 4 * D + 2 * FF
    g_head = flat[at : at + 2048].reshape(2, 1024)[:, :CLS].reshape(-1)
    g_tables, g_vectors = unpack_tables(
        [jnp.concatenate([g[7][m], g[8][m], g[6][m]], 1) for m in range(2)]
    )
    g_attention = unpack_attention(jnp.stack(g[:2]))
    g_feedforward = jnp.stack([jnp.stack(g[2:4], 1), jnp.stack(g[4:6], 1)])
    t_new, t_one, t_two = (
        x.T
        for x in adamw(
            tables.T,
            tables_first.T,
            tables_second.T,
            g_tables * factor,
            matrix_rate,
            matrix_decay,
        )
    )
    v_new, v_one, v_two = (
        x.T
        for x in adamw(
            vectors.T, vectors_first.T, vectors_second.T, g_vectors * factor, vector_rate, 0.0
        )
    )
    a_new, a_one, a_two = adamw(
        attention,
        attention_first,
        attention_second,
        g_attention * factor,
        matrix_rate,
        matrix_decay,
    )
    f_new, f_one, f_two = adamw(
        feedforward,
        feedforward_first,
        feedforward_second,
        g_feedforward * factor,
        matrix_rate,
        matrix_decay,
    )
    s_new, s_one, s_two = adamw(
        split_bias, split_bias_first, split_bias_second, g_split * factor, vector_rate, 0.0
    )
    h_new, h_one, h_two = adamw(
        head_bias, head_bias_first, head_bias_second, g_head * factor, vector_rate, 0.0
    )
    return (
        loss_sum,
        weight_sum,
        grad_norm,
        t_new,
        t_one,
        t_two,
        t_new.astype(bf16),
        v_new,
        v_one,
        v_two,
        a_new,
        a_one,
        a_two,
        a_new.astype(bf16),
        f_new,
        f_one,
        f_two,
        f_new.astype(bf16),
        s_new,
        s_one,
        s_two,
        h_new,
        h_one,
        h_two,
    )


def solution(mesh):
    table = P(None, ("dp", "mp"))
    attn = P(None, "dp", "mp")
    ffw = P(None, "dp", None, "mp")
    split = P(None, "mp")
    return jax.shard_map(
        shards,
        mesh=mesh,
        in_specs=(P("dp", None, None), P(), P("dp"), P("dp"), P("dp"), P())
        + (table,) * 6
        + (attn,) * 3
        + (ffw,) * 3
        + (split,) * 3
        + (P(),) * 3,
        out_specs=(P(),) * 3
        + (table,) * 7
        + (attn,) * 4
        + (ffw,) * 4
        + (split,) * 3
        + (P(),) * 3,
        check_vma=False,
    )
```

```python
import functools

import jax
import jax.numpy as jnp
from jax import lax
from jax.experimental import pallas as pl
from jax.experimental.pallas import tpu as pltpu
from jax.sharding import PartitionSpec as P

D = 384
HEADS = 6
HD = 64
FF = 1536
CLS = 1000
PD = 768
PATCHES = 196
LAYERS = 2
STEP = 10
TOK = 198
TP = 208
GRP = 2
ENDS = 16
END_AT = 4
SENT = 200
ROWS = GRP * TP
HALF = FF // 2
COLS = 6144
T_COLS = 1536
F_COLS = 512
TABLE_CHUNKS = (6, 7, 8)
REDUCE_TURNS = (0, 0, 1, 1, 2, 1, 2, 0, 0)
MAIN_WIDTHS = (768, 768, 768, 768, 768, 768, 1024)
MAIN_TURNS = (0, 0, 0, 1, 0, 1, 1)
FRONT_WIDTHS = (384, 128)
FRONT_TURNS = (0, 1)
M_COLS = 4608
MIB = 1 << 20
NORM_ROWS = ROWS
GELU_ROWS = 32

norm_eps = 1e-06
clip_limit = 0.02
beta_one = 0.9
beta_two = 0.999
adam_eps = 1e-08
matrix_rate = 0.08
vector_rate = 0.5
matrix_decay = 0.05

f32 = jnp.float32
bf16 = jnp.bfloat16
MESH = pl.DeviceIdType.MESH
AB = ((1,), (0,))
ABT = ((1,), (1,))
ATB = ((0,), (0,))


def mm(left, right, dims=AB):
    return lax.dot_general(left, right, (dims, ((), ())), preferred_element_type=f32)


def full_spec(shape):
    return pl.BlockSpec(shape, lambda *_: (0,) * len(shape), pipeline_mode=pl.Buffered(1))


def row_loop(total, chunk, body):
    def step(index, carry):
        body(pl.ds(pl.multiple_of(index * chunk, chunk), chunk))
        return carry

    if total == chunk:
        body(slice(0, total))
    else:
        lax.fori_loop(0, total // chunk, step, 0)


def center(x):
    mean = jnp.mean(x, -1, keepdims=True)
    xc = x - mean
    scale = lax.rsqrt(jnp.mean(xc * xc, -1, keepdims=True) + norm_eps)
    return xc * scale, scale


def gelu_pair(x):
    z = x * 0.7071067811865476
    e = jnp.exp(-(z * z))
    den = 1.0 + 0.3275911 * jnp.abs(z)
    r = pl.reciprocal(den, approx=True)
    r = r * (2.0 - den * r)
    poly = r * (
        0.127414796
        + r * (-0.142248368 + r * (0.7107068705 + r * (-0.7265760135 + r * 0.5307027145)))
    )
    tail = poly * e
    cdf = jnp.where(x > 0.0, 1.0 - tail, tail)
    return x * cdf, cdf + x * (e * 0.3989422804014327)


def partner_place(partner_ref, k):
    images = partner_ref.shape[0]
    n_data = lax.axis_size("dp")
    far = lax.rem(lax.axis_index("dp") + n_data // 2, n_data)
    wanted = far * images + lax.axis_index("mp") * (images // 2) + k
    place = jnp.int32(0)
    for i in range(images):
        place = place + jnp.where(partner_ref[i] == wanted, i, 0)
    return place


def embed_kernel(partner_ref, pix_ref, w_ref, own_ref, send_ref, flat):
    step = pl.program_id(0)
    mp = lax.axis_index("mp")
    count = partner_ref.shape[0]
    images = count // 2
    patches = pix_ref.shape[0]
    part = patches // 7
    for c in range(7):
        pix = pix_ref[c * part : (c + 1) * part].reshape(part * count, PD)
        out = mm(pix[:, :D], w_ref[0], ABT) + mm(pix[:, D:], w_ref[1], ABT)
        for j in range(3):
            flat[j, c * part * count : (c + 1) * part * count] = out[:, 128 * j : 128 * (j + 1)]
    @pl.when(step == pl.num_programs(0) - 1)
    def _():
        for k in range(images):
            place = partner_place(partner_ref, k)
            for j in range(3):
                cols = slice(128 * j, 128 * (j + 1))
                own_ref[k, :, cols] = flat[j, pl.ds(place, PATCHES, stride=count), :]
                send_ref[k, :PATCHES, cols] = flat[
                    j, pl.ds(mp * images + k, PATCHES, stride=count), :
                ].astype(bf16)
                send_ref[k, PATCHES:, cols] = jnp.zeros((SENT - PATCHES, 128), bf16)


def embed(partner, pix, weights):
    count = pix.shape[1] // 2
    steps = 1
    return pl.pallas_call(
        embed_kernel,
        grid=(steps,),
        in_specs=[
            pl.BlockSpec(memory_space=pltpu.SMEM),
            block_of(pix.shape, steps),
            full_spec(weights.shape),
        ],
        out_specs=[
            full_spec((count, PATCHES, D)),
            full_spec((count, SENT, D)),
        ],
        out_shape=[
            jax.ShapeDtypeStruct((count, PATCHES, D), f32),
            jax.ShapeDtypeStruct((count, SENT, D), bf16),
        ],
        scratch_shapes=[pltpu.VMEM((3, PATCHES * 2 * count, 128), f32)],
        compiler_params=pltpu.CompilerParams(vmem_limit_bytes=60 * MIB),
        name="embed_images",
    )(partner, pix, weights)


def split_tokens(w_ref, col):
    seg = jnp.concatenate([w_ref[0, :, col : col + 128], w_ref[1, :, col : col + 128]], 1)
    return jnp.transpose(seg.astype(f32), (1, 0))


def attend(g, qkv_ref, p_ref, ho_ref):
    rows = slice(g * TP, (g + 1) * TP)
    lane = lax.broadcasted_iota(jnp.int32, (TP, 128), 1)
    key_mask = jnp.where(lax.broadcasted_iota(jnp.int32, (1, TP), 1) < TOK, 0.0, -1e30).astype(f32)
    for j in range(3):
        q = qkv_ref[rows, 128 * j : 128 * (j + 1)]
        k = qkv_ref[rows, D + 128 * j : D + 128 * (j + 1)]
        v = qkv_ref[rows, 2 * D + 128 * j : 2 * D + 128 * (j + 1)]
        outs = []
        for s in range(2):
            mine = (lane < 64) if s == 0 else (lane >= 64)
            scores = mm(jnp.where(mine, q, jnp.zeros_like(q)), k, ABT) + key_mask
            exps = jnp.exp(scores - jnp.max(scores, -1, keepdims=True))
            probs = (exps * (1.0 / jnp.sum(exps, -1, keepdims=True))).astype(bf16)
            p_ref[6 * g + 2 * j + s] = probs
            outs.append(mm(probs, v))
        ho_ref[rows, 128 * j : 128 * (j + 1)] = jnp.where(lane < 64, outs[0], outs[1]).astype(bf16)


PAIRS = (0, 1, 3, 4, 2, 5)


def rounded(x):
    return x.astype(bf16).astype(f32)


def norm_rows(src, gain, shift, dst):
    dst[...] = (center(src[...])[0] * gain + shift).astype(bf16)


def token_row(tok_ref, layer, i):
    at = TP + 6 * layer + i
    return tok_ref[at : at + 1]


def spread_heads(x):
    lane = lax.broadcasted_iota(jnp.int32, x.shape, 1)
    zero = jnp.zeros_like(x)
    return jnp.concatenate(
        [jnp.where((lane >= HD * h) & (lane < HD * (h + 1)), x, zero) for h in range(HEADS)], 0
    )


def gather_heads(x):
    lane = lax.broadcasted_iota(jnp.int32, (ENDS, D), 1)
    total = jnp.zeros((ENDS, D), f32)
    for h in range(HEADS):
        part = x[ENDS * h : ENDS * (h + 1)]
        total = total + jnp.where((lane >= HD * h) & (lane < HD * (h + 1)), part, 0.0)
    return total


def attend_ends(g, kv_ref, q_ref, p_ref, ho_ref):
    rows = slice(g * TP, (g + 1) * TP)
    ends = slice(g * ENDS, (g + 1) * ENDS)
    key_mask = jnp.where(lax.broadcasted_iota(jnp.int32, (1, TP), 1) < TOK, 0.0, -1e30).astype(f32)
    scores = mm(spread_heads(q_ref[ends]), kv_ref[rows, :D], ABT) + key_mask
    exps = jnp.exp(scores - jnp.max(scores, -1, keepdims=True))
    probs = (exps * (1.0 / jnp.sum(exps, -1, keepdims=True))).astype(bf16)
    p_ref[g] = probs
    ho_ref[ends] = gather_heads(mm(probs, kv_ref[rows, D:])).astype(bf16)


def forward_kernel(partner_ref, mix_ref, own_ref, far_ref, t_ref, w_ref, sb_ref, *refs):
    x_ref, mid_ref, qkv_ref, p_ref, ho_ref, hid_ref, gp_ref = refs[:7]
    x1_ref, kv_ref, q1_ref, p1_ref, ho1_ref, mid1_ref, tok_ref = refs[7:14]
    qkv_w, out_w, nbuf, up_s, bias_ref = refs[14:]
    step = pl.program_id(0)

    @pl.when(step == 0)
    def _():
        tok_ref[...] = split_tokens(t_ref, 0)
        for layer in range(LAYERS):
            attn_tiles(w_ref.at[layer], qkv_w.at[layer], out_w.at[layer])
            pieces = [
                sb_ref[h // 3, layer : layer + 1, 128 * (h % 3) + HD * t : 128 * (h % 3) + HD * (t + 1)]
                for t in range(2)
                for h in PAIRS
            ]
            bias_ref[layer : layer + 1] = rounded(jnp.concatenate(pieces, 1))

    def row(layer, i):
        return token_row(tok_ref, layer, i)

    for g in range(GRP):
        w = mix_ref[partner_place(partner_ref, step * GRP + g)]
        x_ref[g * TP : g * TP + PATCHES] = (
            w * own_ref[g] + (1.0 - w) * far_ref[g, :PATCHES].astype(f32) + tok_ref[:PATCHES]
        )
        x_ref[g * TP + PATCHES : (g + 1) * TP] = tok_ref[PATCHES:TP]
    norm_rows(x_ref, row(0, 0), row(0, 1), nbuf)
    n = nbuf[...]
    q = mm(n, qkv_w[0, :, :D]) + bias_ref[0:1, :D]
    qkv_ref[:, :D] = (q.astype(bf16).astype(f32) * 0.125).astype(bf16)
    qkv_ref[:, D : 2 * D] = mm(n, qkv_w[0, :, D : 2 * D]).astype(bf16)
    v = mm(n, qkv_w[0, :, 2 * D :]) + bias_ref[0:1, D : 2 * D]
    qkv_ref[:, 2 * D :] = v.astype(bf16)
    for g in range(GRP):
        attend(g, qkv_ref, p_ref, ho_ref)
    mid_ref[...] = x_ref[...] + mm(ho_ref[...], out_w[0], ABT) + row(0, 4)
    norm_rows(mid_ref, row(0, 2), row(0, 3), nbuf)
    up_w, down_w = w_ref.at[LAYERS], w_ref.at[LAYERS + 1]
    for m in range(2):
        cols = slice(HALF * m, HALF * (m + 1))
        up_s[...] = mm(nbuf[...], up_w[m]) + rounded(sb_ref[m, 0:1, D:])

        def body(rs):
            hid, gp = gelu_pair(up_s[rs])
            hid_ref[rs, cols] = hid.astype(bf16)
            gp_ref[rs, cols] = gp.astype(bf16)

        row_loop(ROWS, GELU_ROWS, body)
    out = mid_ref[...] + row(0, 5)
    for m in range(2):
        cols = slice(HALF * m, HALF * (m + 1))
        out = out + mm(hid_ref[:, cols], down_w[m], ABT)
    x1_ref[...] = out
    norm_rows(x1_ref, row(1, 0), row(1, 1), nbuf)
    n = nbuf[...]
    kv_ref[:, :D] = mm(n, qkv_w[1, :, D : 2 * D]).astype(bf16)
    kv_ref[:, D:] = (mm(n, qkv_w[1, :, 2 * D :]) + bias_ref[1:2, D : 2 * D]).astype(bf16)
    ends = jnp.concatenate([nbuf[(g + 1) * TP - ENDS : (g + 1) * TP] for g in range(GRP)], 0)
    q = mm(ends, qkv_w[1, :, :D]) + bias_ref[1:2, :D]
    q1_ref[...] = (q.astype(bf16).astype(f32) * 0.125).astype(bf16)
    for g in range(GRP):
        attend_ends(g, kv_ref, q1_ref, p1_ref, ho1_ref)
    x_ends = jnp.concatenate([x1_ref[(g + 1) * TP - ENDS : (g + 1) * TP] for g in range(GRP)], 0)
    mid1_ref[...] = x_ends + mm(ho1_ref[...], out_w[1], ABT) + row(1, 4)


def kept_shapes(count):
    n = count * TP
    return [
        ((n, D), f32),
        ((n, D), f32),
        ((n, 3 * D), bf16),
        ((count * HEADS, TP, TP), bf16),
        ((n, D), bf16),
        ((n, FF), bf16),
        ((n, FF), bf16),
        ((n, D), f32),
        ((n, 2 * D), bf16),
        ((count * ENDS, D), bf16),
        ((count, HEADS * ENDS, TP), bf16),
        ((count * ENDS, D), bf16),
        ((count * ENDS, D), f32),
    ]


def block_of(shape, steps):
    block = (shape[0] // steps,) + tuple(shape[1:])
    return pl.BlockSpec(block, lambda i: (i,) + (0,) * (len(block) - 1))


def forward(partner, mix, own, far, seg, weights, sb):
    count = own.shape[0]
    steps = count // GRP
    outs = kept_shapes(count)
    shapes = [jax.ShapeDtypeStruct(s, t) for s, t in outs] + [jax.ShapeDtypeStruct((256, D), f32)]
    specs = [block_of(s, steps) for s, _ in outs] + [full_spec((256, D))]
    return pl.pallas_call(
        forward_kernel,
        grid=(steps,),
        in_specs=[
            pl.BlockSpec(memory_space=pltpu.SMEM),
            pl.BlockSpec(memory_space=pltpu.SMEM),
            block_of(own.shape, steps),
            block_of(far.shape, steps),
            full_spec(seg.shape),
            pl.BlockSpec((4, 2, D, 768), lambda i: (0, 0, 0, 0), pipeline_mode=pl.Buffered(1)),
            full_spec(sb.shape),
        ],
        out_specs=specs,
        out_shape=shapes,
        scratch_shapes=[
            pltpu.VMEM((LAYERS, D, 3 * D), bf16),
            pltpu.VMEM((LAYERS, D, D), bf16),
            pltpu.VMEM((ROWS, D), bf16),
            pltpu.VMEM((ROWS, HALF), f32),
            pltpu.VMEM((LAYERS, 2 * D), f32),
        ],
        compiler_params=pltpu.CompilerParams(vmem_limit_bytes=60 * MIB),
        name="forward_layers",
    )(partner, mix, own, far, seg, weights, sb)


def norm_back(dy, xhat, scale, gain):
    dyg = dy * gain
    c1 = jnp.mean(dyg, -1, keepdims=True)
    c2 = jnp.mean(dyg * xhat, -1, keepdims=True)
    return scale * (dyg - c1 - xhat * c2)


def share(part, own_ref, mate_ref, mp):
    own_ref[...] = part[mp]
    mate_ref[...] = part[1 - mp].astype(bf16)


def head_kernel(
    partner_ref,
    mix_ref,
    label_ref,
    teacher_ref,
    mid_ref,
    wf_ref,
    w_ref,
    sb_ref,
    hb_ref,
    cw_ref,
    tok_ref,
    uo_ref,
    um_ref,
    do_ref,
    dm_ref,
    ho_ref,
    hm_ref,
    dz_ref,
    gv_ref,
    gu_ref,
    dhb_ref,
    stat_ref,
    lanes,
    g_ffw,
    g_head,
):
    mp = lax.axis_index("mp")
    gain2, shift2, bias_f = (token_row(tok_ref, 1, i) for i in (2, 3, 5))
    gain, shift = (token_row(tok_ref, 2, i) for i in range(2))
    count = mid_ref.shape[0] // ENDS
    images = partner_ref.shape[0]
    n_data = lax.axis_size("dp")
    dp = lax.axis_index("dp")
    far_base = lax.rem(dp + n_data // 2, n_data) * images + mp * count
    marks = []
    for k in range(count):
        place = partner_place(partner_ref, k)
        marks.append(
            (
                label_ref[dp * images + place],
                label_ref[far_base + k],
                teacher_ref[place],
                mix_ref[place],
            )
        )
    for j in range(3):
        lanes[j] = mid_ref[:, 128 * j : 128 * (j + 1)]
    mid = jnp.concatenate(
        [
            jnp.concatenate(
                [lanes[j, pl.ds(END_AT + h, count, stride=ENDS), :] for j in range(3)], 1
            )
            for h in range(2)
        ],
        0,
    )
    xhat2, scale2 = center(mid)
    normed = (xhat2 * gain2 + shift2).astype(bf16)
    out = mid + bias_f
    hids, gps = [], []
    for m in range(2):
        up = mm(normed, wf_ref[0, m]) + rounded(sb_ref[m, 1:2, D:])
        hid, gp = gelu_pair(up)
        hids.append(hid.astype(bf16))
        gps.append(gp)
        out = out + mm(hids[m], wf_ref[1, m], ABT)
    xhat, scale = center(out)
    final = (xhat * gain + shift).astype(bf16)
    loss = jnp.zeros((1, 1), f32)
    weight = jnp.zeros((1, 1), f32)
    dfinals = []
    for h in range(2):
        mine = final[count * h : count * (h + 1)]
        halves = []
        for m in range(2):
            wh = w_ref[m, :, 512 * h : 512 * (h + 1)]
            at = 1024 * h + 512 * m
            logits = mm(mine, wh) + hb_ref[0:1, at : at + 512]
            ids = lax.broadcasted_iota(jnp.int32, (1, 512), 1) + 512 * m
            shares = []
            for k in range(count):
                first, second, teach, mix = marks[k]
                if h == 0:
                    both = jnp.where(ids == first, mix, 0.0) + jnp.where(ids == second, 1.0 - mix, 0.0)
                    shares.append(both)
                else:
                    shares.append(jnp.where(ids == teach, 1.0, 0.0))
            coef = jnp.concatenate(shares, 0) * cw_ref[0:1, 512 * m : 512 * (m + 1)]
            halves.append((wh, logits, coef))
        top = jnp.maximum(*[jnp.max(x[1], -1, keepdims=True) for x in halves])
        exps = [jnp.exp(x[1] - top) for x in halves]
        total = sum(jnp.sum(x, -1, keepdims=True) for x in exps)
        lse = top + jnp.log(total)
        csum = sum(jnp.sum(x[2], -1, keepdims=True) for x in halves)
        dfinal = jnp.zeros((count, D), f32)
        for m in range(2):
            wh, logits, coef = halves[m]
            loss = loss + jnp.sum(jnp.sum(coef * (lse - logits), -1, keepdims=True), 0, keepdims=True)
            dl = csum * (exps[m] / total) - coef
            at = 1024 * h + 512 * m
            dhb_ref[0:1, at : at + 512] = jnp.sum(dl, 0, keepdims=True)
            low = dl.astype(bf16)
            g_head[m, :, 512 * h : 512 * (h + 1)] = mm(mine, low, ATB)
            dfinal = dfinal + mm(low, wh, ABT)
        weight = weight + jnp.sum(csum, 0, keepdims=True)
        dfinals.append(dfinal)
    dfinal = jnp.concatenate(dfinals, 0)
    dz = norm_back(dfinal, xhat, scale, gain)
    low = dz.astype(bf16)
    dn = jnp.zeros_like(dz)
    for m in range(2):
        dh = mm(low, wf_ref[1, m])
        du = (dh.astype(bf16).astype(f32) * gps[m]).astype(bf16)
        gu_ref[0:1, HALF * m : HALF * (m + 1)] = jnp.sum(du.astype(f32), 0, keepdims=True)
        g_ffw[0, m] = mm(normed, du, ATB)
        g_ffw[1, m] = mm(low, hids[m], ATB)
        dn = dn + mm(du, wf_ref[0, m], ABT)
    dmid = dz + norm_back(dn, xhat2, scale2, gain2)
    gv_ref[...] = jnp.zeros_like(gv_ref)
    sums = [dn * xhat2, dn, dmid, dz, dfinal * xhat, dfinal]
    for i, item in enumerate(sums):
        gv_ref[i + 2 : i + 3] = jnp.sum(item, 0, keepdims=True)
    lanes[...] = jnp.zeros_like(lanes)
    for j in range(3):
        for h in range(2):
            lanes[j, pl.ds(END_AT + h, count, stride=ENDS), :] = dmid[
                count * h : count * (h + 1), 128 * j : 128 * (j + 1)
            ]
        dz_ref[:, 128 * j : 128 * (j + 1)] = lanes[j]
    which = lax.broadcasted_iota(jnp.int32, stat_ref.shape, 1)
    stat_ref[...] = jnp.where(which == 0, loss, jnp.where(which == 1, weight, 0.0))
    share(g_ffw.at[0], uo_ref, um_ref, mp)
    share(g_ffw.at[1], do_ref, dm_ref, mp)
    share(g_head, ho_ref, hm_ref, mp)


def pair_shapes(shapes):
    return [jax.ShapeDtypeStruct(s, t) for s in shapes for t in (f32, bf16)]


def head(partner, mix, labels, teacher, mid, weights, w_heads, sb, hb, cw, tok):
    outs = pair_shapes([(D, 768), (D, 768), (D, 1024)]) + [
        jax.ShapeDtypeStruct(s, f32)
        for s in (mid.shape, (8, D), (1, FF), (1, 2048), (1, 128))
    ]
    return pl.pallas_call(
        head_kernel,
        grid=(1,),
        in_specs=[pl.BlockSpec(memory_space=pltpu.SMEM)] * 4
        + [
            full_spec(mid.shape),
            pl.BlockSpec((2, 2, D, 768), lambda i: (2, 0, 0, 0), pipeline_mode=pl.Buffered(1)),
        ]
        + [full_spec(x.shape) for x in (w_heads, sb, hb, cw, tok)],
        out_specs=[full_spec(x.shape) for x in outs],
        out_shape=outs,
        scratch_shapes=[
            pltpu.VMEM((3, mid.shape[0], 128), f32),
            pltpu.VMEM((2, 2, D, 768), f32),
            pltpu.VMEM((2, D, 1024), f32),
        ],
        compiler_params=pltpu.CompilerParams(vmem_limit_bytes=60 * MIB),
        name="loss_heads",
    )(partner, mix, labels, teacher, mid, weights, w_heads, sb, hb, cw, tok)


def attend_back(g, dho, qkv_ref, p_ref, dproj):
    rows = slice(g * TP, (g + 1) * TP)
    lane = lax.broadcasted_iota(jnp.int32, (TP, 128), 1)
    for j in range(3):
        q = qkv_ref[rows, 128 * j : 128 * (j + 1)]
        k = qkv_ref[rows, D + 128 * j : D + 128 * (j + 1)]
        v = qkv_ref[rows, 2 * D + 128 * j : 2 * D + 128 * (j + 1)]
        do = dho[rows, 128 * j : 128 * (j + 1)]
        qt, kt, dot_ = (jnp.transpose(a, (1, 0)) for a in (q, k, do))
        for s in range(2):
            mine = (lane < 64) if s == 0 else (lane >= 64)
            sub = slice(64 * s, 64 * (s + 1))
            at = 128 * j + 64 * s
            probs = p_ref[6 * g + 2 * j + s]
            dproj[g, 2 * D + at : 2 * D + at + 64] = mm(dot_[sub], probs).astype(bf16)
            dprob = mm(jnp.where(mine, do, jnp.zeros_like(do)), v, ABT)
            p32 = probs.astype(f32)
            delta = jnp.sum(dprob * p32, -1, keepdims=True)
            ds = (p32 * (dprob - delta)).astype(bf16)
            dproj[g, at : at + 64] = (mm(kt[sub], ds, ABT) * 0.125).astype(bf16)
            dproj[g, D + at : D + at + 64] = mm(qt[sub], ds).astype(bf16)


def ends_back(g, dho, kv_ref, q_ref, p_ref, dq, dproj):
    rows = slice(g * TP, (g + 1) * TP)
    ends = slice(g * ENDS, (g + 1) * ENDS)
    q = spread_heads(q_ref[ends])
    do = spread_heads(dho[ends])
    probs = p_ref[g]
    dprob = mm(do, kv_ref[rows, D:], ABT)
    p32 = probs.astype(f32)
    delta = jnp.sum(dprob * p32, -1, keepdims=True)
    ds = (p32 * (dprob - delta)).astype(bf16)
    dq[ends] = (gather_heads(mm(ds, kv_ref[rows, :D])) * 0.125).astype(bf16)
    dproj[g, :D] = mm(q, ds, ATB).astype(bf16)
    dproj[g, D : 2 * D] = mm(do, probs, ATB).astype(bf16)


def backward_kernel(
    dz_ref,
    x_ref,
    mid_ref,
    qkv_ref,
    p_ref,
    ho_ref,
    hid_ref,
    gp_ref,
    x1_ref,
    kv_ref,
    q1_ref,
    p1_ref,
    ho1_ref,
    wa_ref,
    wf_ref,
    tok_ref,
    dzo_ref,
    a0o_ref,
    a0m_ref,
    a1o_ref,
    a1m_ref,
    uo_ref,
    um_ref,
    do_ref,
    dm_ref,
    gv_ref,
    gb_ref,
    gu_ref,
    qkv_w,
    out_w,
    dqkv,
    dkv,
    dq1,
    dout,
    g_ffw,
    g_att,
    nbuf,
    dz,
    dn,
    du,
    dq,
    dproj,
):
    step = pl.program_id(0)
    mp = lax.axis_index("mp")

    def row(layer, i):
        return token_row(tok_ref, layer, i)

    @pl.when(step == 0)
    def _():
        for ref in (gv_ref, gb_ref, gu_ref, g_ffw, dqkv, dkv, dq1, dout):
            ref[...] = jnp.zeros_like(ref)
        for layer in range(LAYERS):
            attn_tiles(wa_ref.at[layer], qkv_w.at[layer], out_w.at[layer])

    def pull(src, gain, dz_out, at):
        xhat, scale = center(src[...])
        dy = dn[...]
        new = dz[...] + norm_back(dy, xhat, scale, gain)
        dz_out[...] = new
        gv_ref[at : at + 1] += jnp.sum(dy * xhat, 0, keepdims=True)
        gv_ref[at + 1 : at + 2] += jnp.sum(dy, 0, keepdims=True)

    ones = jnp.ones((TP, 128), bf16)
    low = dz_ref[...].astype(bf16)
    dout[1] += mm(low, ho1_ref[...], ATB)
    dho = mm(low, out_w[1]).astype(bf16)
    norm_rows(x1_ref, row(1, 0), row(1, 1), nbuf)
    dz[...] = jnp.zeros_like(dz)
    for g in range(GRP):
        rows = slice(g * TP, (g + 1) * TP)
        ends_back(g, dho, kv_ref, q1_ref, p1_ref, dq, dproj)
        dkv[:, :D] += mm(dproj[g, : 2 * D], nbuf[rows])
        dkv[:, D:] += mm(dproj[g, : 2 * D], ones)
        dn[rows] = jnp.transpose(mm(qkv_w[1, :, D:], dproj[g, : 2 * D]), (1, 0))
    dq_all = dq[...]
    ends = jnp.concatenate([nbuf[(g + 1) * TP - ENDS : (g + 1) * TP] for g in range(GRP)], 0)
    dq1[...] += mm(ends, dq_all, ATB)
    gb_ref[1:2, :D] += jnp.sum(dq_all.astype(f32), 0, keepdims=True)
    more = mm(dq_all, qkv_w[1, :, :D], ABT)
    for g in range(GRP):
        last = slice((g + 1) * TP - ENDS, (g + 1) * TP)
        part = slice(g * ENDS, (g + 1) * ENDS)
        dn[last] += more[part]
        dz[last] = dz_ref[part]
    pull(x1_ref, row(1, 0), dz, 6)

    norm_rows(mid_ref, row(0, 2), row(0, 3), nbuf)
    gv_ref[5:6] += jnp.sum(dz[...], 0, keepdims=True)
    rz = dz[...].astype(bf16)
    rzt = jnp.transpose(rz, (1, 0))
    nt = jnp.transpose(nbuf[...], (1, 0))
    for m in range(2):
        cols = slice(HALF * m, HALF * (m + 1))
        dh = mm(rz, wf_ref[1, m])
        du[...] = (dh.astype(bf16).astype(f32) * gp_ref[:, cols].astype(f32)).astype(bf16)
        gu_ref[0:1, cols] += jnp.sum(du[...].astype(f32), 0, keepdims=True)
        g_ffw[1, m] += mm(rzt, hid_ref[:, cols])
        g_ffw[0, m] += mm(nt, du[...])
        part = mm(du[...], wf_ref[0, m], ABT)
        dn[...] = part if m == 0 else dn[...] + part
    pull(mid_ref, row(0, 2), dz, 2)
    gv_ref[4:5] += jnp.sum(dz[...], 0, keepdims=True)
    rz2 = dz[...].astype(bf16)
    dout[0] += mm(jnp.transpose(rz2, (1, 0)), ho_ref[...])
    dho = mm(rz2, out_w[0]).astype(bf16)
    norm_rows(x_ref, row(0, 0), row(0, 1), nbuf)
    for g in range(GRP):
        rows = slice(g * TP, (g + 1) * TP)
        attend_back(g, dho, qkv_ref, p_ref, dproj)
        dqkv[:, :D] += mm(dproj[g], nbuf[rows])
        dqkv[:, D:] += mm(dproj[g], ones)
        dn[rows] = jnp.transpose(mm(qkv_w[0], dproj[g]), (1, 0))
    pull(x_ref, row(0, 0), dzo_ref, 0)

    @pl.when(step == pl.num_programs(0) - 1)
    def _():
        for layer in range(LAYERS):
            for t in range(4):
                for j in range(3):
                    at = D * t + 128 * j
                    if t == 3:
                        tile = dout[layer, :, 128 * j : 128 * (j + 1)]
                    elif layer == 0:
                        tile = jnp.transpose(dqkv[at : at + 128, :D], (1, 0))
                    elif t == 0:
                        tile = dq1[:, 128 * j : 128 * (j + 1)]
                    else:
                        tile = jnp.transpose(dkv[at - D : at - D + 128, :D], (1, 0))
                    if j < 2:
                        g_att[layer, j, :, 128 * t : 128 * (t + 1)] = tile
                    else:
                        for m in range(2):
                            lo = 512 + 64 * t
                            g_att[layer, m, :, lo : lo + 64] = tile[:, 64 * m : 64 * (m + 1)]
        share(g_att.at[0], a0o_ref, a0m_ref, mp)
        share(g_att.at[1], a1o_ref, a1m_ref, mp)
        share(g_ffw.at[0], uo_ref, um_ref, mp)
        share(g_ffw.at[1], do_ref, dm_ref, mp)
        sums = jnp.transpose(dqkv[:, D:], (1, 0))[0:1]
        gb_ref[0:1, :D] = sums[:, :D]
        gb_ref[0:1, D:] = sums[:, 2 * D :]
        gb_ref[1:2, D:] = jnp.transpose(dkv[:, D:], (1, 0))[0:1, D:]


def attn_tiles(w_ref, qkv_w, out_w):
    for t in range(4):
        cols = 128 * t
        pieces = [w_ref[0, :, cols : cols + 128], w_ref[1, :, cols : cols + 128]]
        tile = 512 + 128 * (t // 2)
        lane = 64 * (t % 2)
        pieces.append(
            jnp.concatenate(
                [w_ref[m, :, tile : tile + 128][:, lane : lane + 64] for m in range(2)], 1
            )
        )
        for j in range(3):
            if t < 3:
                at = D * t + 128 * j
                qkv_w[:, at : at + 128] = pieces[j]
            else:
                out_w[:, 128 * j : 128 * (j + 1)] = pieces[j]


def backward(dz, kept, weights, tok):
    steps = dz.shape[0] // (GRP * ENDS)
    x_shape = kept[0].shape
    shares = pair_shapes([(D, 768)] * 4)
    extra = [jax.ShapeDtypeStruct(s, f32) for s in ((8, D), (2, 2 * D), (1, FF))]
    return pl.pallas_call(
        backward_kernel,
        grid=(steps,),
        in_specs=[block_of(a.shape, steps) for a in (dz,) + tuple(kept)]
        + [
            pl.BlockSpec((2, 2, D, 768), lambda i: (0, 0, 0, 0), pipeline_mode=pl.Buffered(1)),
            pl.BlockSpec((2, 2, D, 768), lambda i: (1, 0, 0, 0), pipeline_mode=pl.Buffered(1)),
            full_spec(tok.shape),
        ],
        out_specs=[block_of(x_shape, steps)] + [full_spec(x.shape) for x in shares + extra],
        out_shape=[jax.ShapeDtypeStruct(x_shape, f32)] + shares + extra,
        scratch_shapes=[
            pltpu.VMEM((LAYERS, D, 3 * D), bf16),
            pltpu.VMEM((LAYERS, D, D), bf16),
            pltpu.VMEM((3 * D, 512), f32),
            pltpu.VMEM((2 * D, 512), f32),
            pltpu.VMEM((D, D), f32),
            pltpu.VMEM((LAYERS, D, D), f32),
            pltpu.VMEM((2, 2, D, 768), f32),
            pltpu.VMEM((LAYERS, 2, D, 768), f32),
            pltpu.VMEM((ROWS, D), bf16),
            pltpu.VMEM((ROWS, D), f32),
            pltpu.VMEM((ROWS, D), f32),
            pltpu.VMEM((ROWS, HALF), bf16),
            pltpu.VMEM((GRP * ENDS, D), bf16),
            pltpu.VMEM((GRP, 3 * D, TP), bf16),
        ],
        compiler_params=pltpu.CompilerParams(vmem_limit_bytes=62 * MIB),
        name="backward_layers",
    )(dz, *kept, weights, weights, tok)


def patch_grad_kernel(
    partner_ref,
    mix_ref,
    dz_ref,
    own_ref,
    far_ref,
    gvb_ref,
    gvh_ref,
    po_ref,
    pm_ref,
    eo_ref,
    em_ref,
    dzo,
    dzf,
    tok,
    g_patch,
    g_seg,
):
    mp = lax.axis_index("mp")
    count = far_ref.shape[0] // PATCHES
    both = own_ref.shape[0] // PATCHES
    dzo[...] = jnp.zeros_like(dzo)
    total = jnp.zeros((TP, D), f32)
    for k in range(count):
        place = partner_place(partner_ref, k)
        w = mix_ref[place]
        for j in range(3):
            part = dz_ref[k * TP : k * TP + PATCHES, 128 * j : 128 * (j + 1)]
            dzo[j, pl.ds(place, PATCHES, stride=both), :] = w * part
            dzf[j, pl.ds(k, PATCHES, stride=count), :] = (1.0 - w) * part
        total = total + dz_ref[k * TP : (k + 1) * TP]
    tok[...] = jnp.zeros_like(tok)
    tok[:TP] = total
    tok[TP : TP + 8] = gvb_ref[...]
    tok[TP + 8 : TP + 14] = gvh_ref[2:8]
    turned = jnp.transpose(tok[...], (1, 0))
    for m in range(2):
        g_seg[m] = turned[:, 128 * m : 128 * (m + 1)]
    for j in range(3):
        lo = jnp.transpose(dzo[j].astype(bf16), (1, 0))
        lf = jnp.transpose(dzf[j].astype(bf16), (1, 0))
        for m in range(2):
            cols = slice(D * m, D * (m + 1))
            g_patch[m, 128 * j : 128 * (j + 1)] = mm(lo, own_ref[:, cols]) + mm(lf, far_ref[:, cols])
    share(g_patch, po_ref, pm_ref, mp)
    share(g_seg, eo_ref, em_ref, mp)


def patch_grad(partner, mix, dz, own, far, gvb, gvh):
    outs = pair_shapes([(D, D), (D, 128)])
    return pl.pallas_call(
        patch_grad_kernel,
        grid=(1,),
        in_specs=[pl.BlockSpec(memory_space=pltpu.SMEM)] * 2
        + [full_spec(a.shape) for a in (dz, own, far, gvb, gvh)],
        out_specs=[full_spec(x.shape) for x in outs],
        out_shape=outs,
        scratch_shapes=[
            pltpu.VMEM((3, own.shape[0], 128), f32),
            pltpu.VMEM((3, far.shape[0], 128), f32),
            pltpu.VMEM((256, D), f32),
            pltpu.VMEM((2, D, D), f32),
            pltpu.VMEM((2, D, 128), f32),
        ],
        compiler_params=pltpu.CompilerParams(vmem_limit_bytes=56 * MIB),
        name="patch_gradient",
    )(partner, mix, dz, own, far, gvb, gvh)


def link_orders(bits):
    far = [b for b in (range(1, bits, 2) if bits == 6 else [3]) if b < bits]
    near = [b for b in range(bits) if b not in far]
    return [near[i:] + near[:i] for i in range(len(near))], far


def gather_plan(bits, turns):
    near, far = link_orders(bits)
    deep = far + [near[0][-1]]
    flat = near[0][:-1]
    return [flat[t:] + flat[:t] for t in turns], deep


def chunk_plan(bits, cuts):
    near, far = link_orders(bits)
    return [
        (cuts[i], cuts[i + 1] - cuts[i], near[i % len(near)], far) for i in range(len(cuts) - 1)
    ]


def mesh_place():
    return lax.axis_index("dp"), lax.axis_index("mp")


def bit_of(value, bit):
    return (value // 2**bit) % 2


def flipped(value, bit):
    return value + 2**bit * (1 - 2 * bit_of(value, bit))


def meet(bits):
    dp, mp = mesh_place()
    barrier = pltpu.get_barrier_semaphore()
    for peer in [(dp, 1 - mp)] + [(flipped(dp, b), mp) for b in range(bits)]:
        pl.semaphore_signal(barrier, inc=1, device_id=peer, device_id_type=MESH)
    pl.semaphore_wait(barrier, bits + 1)


def push(src, dst, send, recv, peer):
    copy = pltpu.make_async_remote_copy(
        src_ref=src, dst_ref=dst, send_sem=send, recv_sem=recv, device_id=peer, device_id_type=MESH
    )
    copy.start()
    return copy


def held_part(ref, bits, lead, dp, done=(), flip=None):
    idx = list(lead)
    for b in reversed(bits):
        mine = bit_of(dp, b)
        idx.append(pl.ds(0, 2) if b in done else (1 - mine if b == flip else mine))
    return ref.at[tuple(idx)]


def gather_front_kernel(bits, tab_ref, main_ref, sb_ref, *refs):
    w_refs = refs[:2]
    far_refs = refs[2:4]
    sbo_ref, tabr, stage_p, stage_e, stage_h, s_loc, s_tab = refs[4:11]
    s_send, s_recv, f_send, f_recv, m_send, m_recv = refs[11:]
    dp, mp = mesh_place()
    mate = (dp, 1 - mp)
    turns, deep = gather_plan(bits, FRONT_TURNS)
    every = list(range(bits))

    far = deep[:-1]
    wide = {}

    def part(c, *args):
        return held_part(w_refs[c], every, (mp,), dp, *args)

    def main(c, *args):
        return held_part(far_refs[c], far, (), dp, *args)

    meet(bits)
    c_tab = push(tab_ref.at[1 - mp], tabr, s_tab.at[0], s_tab.at[1], mate)
    c_sb = push(sb_ref, sbo_ref.at[mp], s_tab.at[2], s_tab.at[3], mate)
    local = [pltpu.make_async_copy(sb_ref, sbo_ref.at[mp], s_loc.at[0])]
    local[0].start()
    c_tab.wait()
    mine = tab_ref[mp].astype(f32)
    other = tabr[...].astype(f32)
    first = jnp.where(mp == 0, mine, other)
    second = jnp.where(mp == 0, other, mine)
    table = jnp.concatenate([first, second], 0).astype(bf16)
    stage_p[...] = table[:, :D]
    stage_e[...] = table[:, D:F_COLS]
    stage_h[...] = table[:, F_COLS:]
    stages = (stage_p, stage_e)
    wides = (main_ref, stage_h)
    copies = {}
    forwards = []
    for s in range(bits + 1):
        for c in range(2):
            order = deep + turns[c]
            if s:
                copies[c, s - 1].wait_recv()
            if s < bits:
                held = part(c, order[:s])
                copies[c, s] = push(
                    held if s else stages[c],
                    held,
                    s_send.at[c, s],
                    s_recv.at[c, s],
                    (flipped(dp, order[s]), mp),
                )
            got = part(c, order[: s - 1], order[s - 1]) if s else part(c)
            forwards.append(
                push(got if s else stages[c], got, f_send.at[c, s], f_recv.at[c, s], mate)
            )
        if s == 0:
            for c in range(2):
                local.append(pltpu.make_async_copy(stages[c], part(c), s_loc.at[c + 1]))
                local[-1].start()
                local.append(pltpu.make_async_copy(wides[c], main(c), s_loc.at[c + 3]))
                local[-1].start()
            for copy in local:
                copy.wait()
        at = s - len(deep) + 1
        if 0 <= at < len(far):
            for c in range(2):
                if at:
                    wide[c, at - 1].wait_recv()
                dst = main(c, far[:at])
                wide[c, at] = push(
                    dst if at else wides[c],
                    dst,
                    m_send.at[c, at],
                    m_recv.at[c, at],
                    (flipped(dp, far[at]), mp),
                )
    for copy in forwards:
        copy.wait()
    for copy in copies.values():
        copy.wait_send()
    for copy in wide.values():
        copy.wait_send()
    for c in range(2):
        wide[c, len(far) - 1].wait_recv()
    c_sb.wait()


def gather_front(tab, shard, sb, n_data):
    bits = n_data.bit_length() - 1
    rows = D // n_data
    _, far = link_orders(bits)
    deep_shape = (2,) * len(far)
    sems = pltpu.SemaphoreType.DMA
    anywhere = pl.BlockSpec(memory_space=pl.ANY)
    inside = pl.BlockSpec(memory_space=pltpu.VMEM)
    return pl.pallas_call(
        functools.partial(gather_front_kernel, bits),
        in_specs=[inside] * 3,
        out_specs=[anywhere] * 4 + [inside],
        out_shape=[
            jax.ShapeDtypeStruct((2,) * (bits + 1) + (rows, w), bf16) for w in FRONT_WIDTHS
        ]
        + [
            jax.ShapeDtypeStruct(deep_shape + shard.shape, bf16),
            jax.ShapeDtypeStruct(deep_shape + (rows, T_COLS - F_COLS), bf16),
            jax.ShapeDtypeStruct((2,) + sb.shape, f32),
        ],
        scratch_shapes=[
            pltpu.VMEM(tab.shape[1:], bf16),
            pltpu.VMEM((rows, FRONT_WIDTHS[0]), bf16),
            pltpu.VMEM((rows, FRONT_WIDTHS[1]), bf16),
            pltpu.VMEM((rows, T_COLS - F_COLS), bf16),
            sems((5,)),
            sems((4,)),
            sems((2, bits)),
            sems((2, bits)),
            sems((2, bits + 1)),
            sems((2, bits + 1)),
            sems((2, len(far))),
            sems((2, len(far))),
        ],
        compiler_params=pltpu.CompilerParams(
            collective_id=2, has_side_effects=True, vmem_limit_bytes=60 * MIB
        ),
        name="gather_front",
    )(tab, shard, sb)


def gather_main_kernel(bits, *refs):
    turns, deep = gather_plan(bits, MAIN_TURNS)
    far, last = deep[:-1], deep[-1]
    mains, heads, pix_ref = refs[:2], refs[2:4], refs[4]
    w_ref, h_ref, mine_ref = refs[5:8]
    pix, s_pix, s_loc, s_send, s_recv, f_send, f_recv = refs[8:]
    dp, mp = mesh_place()
    mate = (dp, 1 - mp)
    every = list(range(bits))
    steps = bits - len(deep)
    chunks = len(MAIN_WIDTHS)

    def lead(c):
        return (w_ref, (c, mp)) if c < chunks - 1 else (h_ref, (mp,))

    def part(c, *args):
        return held_part(lead(c)[0], every, lead(c)[1], dp, *args)

    meet(bits)
    pix_in = pltpu.make_async_copy(pix_ref.at[:, mp], pix, s_pix.at[0])
    pix_in.start()
    copies = {}
    forwards = []
    local = []
    for c in range(chunks):
        for i, dst in enumerate((part(c, far), part(c, far, last))):
            lead_cut = (slice(None),) * len(far) + (c,)
            src = mains[i].at[lead_cut] if c < chunks - 1 else heads[i]
            local.append(pltpu.make_async_copy(src, dst, s_loc.at[c, i]))
            local[-1].start()
    pix_in.wait()
    pix_out = pltpu.make_async_copy(pix, mine_ref, s_pix.at[1])
    pix_out.start()
    for s in range(steps + 1):
        for c in range(chunks):
            order = turns[c]
            if s:
                copies[c, s - 1].wait_recv()
            else:
                for copy in local[2 * c : 2 * c + 2]:
                    copy.wait()
            done = deep + order[:s]
            if s < steps:
                held = part(c, done)
                copies[c, s] = push(
                    held, held, s_send.at[c, s], s_recv.at[c, s], (flipped(dp, order[s]), mp)
                )
            got = part(c, done[:-1], done[-1]) if s else part(c, done)
            forwards.append(push(got, got, f_send.at[c, s], f_recv.at[c, s], mate))
    for copy in forwards:
        copy.wait()
    for copy in copies.values():
        copy.wait_send()
    pix_out.wait()


def gather_main(mains, heads, pix, n_data):
    bits = n_data.bit_length() - 1
    rows = D // n_data
    near, _ = link_orders(bits)
    steps = len(near[0]) - 1
    chunks = len(MAIN_WIDTHS)
    sems = pltpu.SemaphoreType.DMA
    anywhere = pl.BlockSpec(memory_space=pl.ANY)
    inside = pl.BlockSpec(memory_space=pltpu.VMEM)
    places = (2,) * (bits + 1) + (rows,)
    mine = pix.shape[:1] + pix.shape[2:]
    main, head_w, pix_mine = pl.pallas_call(
        functools.partial(gather_main_kernel, bits),
        in_specs=[inside] * (2 * len(mains)) + [anywhere],
        out_specs=[anywhere] * 3,
        out_shape=[
            jax.ShapeDtypeStruct((chunks - 1,) + places + (768,), bf16),
            jax.ShapeDtypeStruct(places + (1024,), bf16),
            jax.ShapeDtypeStruct(mine, bf16),
        ],
        scratch_shapes=[
            pltpu.VMEM(mine, bf16),
            sems((2,)),
            sems((chunks, len(mains))),
            sems((chunks, steps)),
            sems((chunks, steps)),
            sems((chunks, steps + 1)),
            sems((chunks, steps + 1)),
        ],
        compiler_params=pltpu.CompilerParams(
            collective_id=0, has_side_effects=True, vmem_limit_bytes=60 * MIB
        ),
        cost_estimate=pl.CostEstimate(flops=0, bytes_accessed=150 * MIB, transcendentals=0),
        name="gather_main",
    )(*mains, *heads, pix)
    return main.reshape(chunks - 1, 2, D, 768), head_w.reshape(2, D, 1024), pix_mine


def reduce_plan(bits, turns):
    near, far = link_orders(bits)
    return [near[t % len(near)] + far for t in turns]


def block_index(free, fixed):
    def index(t):
        total = fixed
        for j, b in enumerate(free):
            total = total + ((t // 2**j) % 2) * 2**b
        return total

    return index


def reduce_kernel(bits, widths, turns, *refs):
    n = len(widths)
    own, mate_src = refs[:n], refs[n : 2 * n]
    smalls = refs[2 * n : 2 * n + 5]
    outs = refs[2 * n + 5 : 3 * n + 5]
    obun_ref, info_ref = refs[3 * n + 5 : 3 * n + 7]
    refs = refs[3 * n + 7 :]
    mrecv, acc = refs[:n], refs[n : 2 * n]
    refs = refs[2 * n :]
    sbufs, rbufs = refs[: n * bits], refs[n * bits : 2 * n * bits]
    bun, bunr, tsend, sq, sqr, m_sem, s_sem, r_sem, b_sem, q_sem, t_sem = refs[2 * n * bits :]
    dp, mp = mesh_place()
    mate = (dp, 1 - mp)
    orders = reduce_plan(bits, turns)
    rows = D // 2**bits
    group = max(rows, 48)
    per = group // rows
    small = rows // 2

    at = 0
    for ref in smalls:
        for i in range(ref.shape[0]):
            bun[:, at : at + ref.shape[1]] = ref[i : i + 1]
            at += ref.shape[1]
    meet(bits)
    mcopies = [
        push(mate_src[c], mrecv[c], m_sem.at[c, 0], m_sem.at[c, 1], mate) for c in range(n)
    ]
    bcopies = [push(bun, bunr.at[0], b_sem.at[0, 0], b_sem.at[0, 1], mate)]

    def loop(total, body):
        def step(t, carry):
            body(t)
            return carry

        lax.fori_loop(0, total, step, 0)

    copies = {}

    def split(order, s, sent):
        free = [b for b in range(bits) if b not in order[: s + 1]]
        fixed = sum((bit_of(dp, b) * 2**b for b in order[:s]), 0)
        last = bit_of(dp, order[s])
        fixed = fixed + (1 - last if sent else last) * 2 ** order[s]
        return 2 ** len(free), block_index(free, fixed)

    def send_stage(c, s):
        total, index = split(orders[c], s, True)
        sbuf = sbufs[c * bits + s]

        def body(t):
            sbuf[t] = acc[c][index(t)].astype(bf16)

        loop(total, body)
        copies[c, s] = push(
            sbuf,
            rbufs[c * bits + s],
            s_sem.at[c, s],
            r_sem.at[c, s],
            (flipped(dp, orders[c][s]), mp),
        )

    def take_stage(c, s):
        copies[c, s].wait_recv()
        total, index = split(orders[c], s, False)
        rbuf = rbufs[c * bits + s]

        def body(t):
            acc[c][index(t)] += rbuf[t].astype(f32)

        loop(total, body)

    for c in range(n):
        mcopies[c].wait_recv()

        def body(b):
            rs = pl.ds(pl.multiple_of(b * group, group), group)
            got = own[c][rs] + mrecv[c][rs].astype(f32)
            for i in range(per):
                acc[c][b * per + i] = got[rows * i : rows * (i + 1)]

        loop(D // group, body)
        send_stage(c, 0)
    for s in range(1, bits + 1):
        for c in range(n):
            take_stage(c, s - 1)
            if s < bits:
                send_stage(c, s)
        bcopies[-1].wait()
        bun[...] = bun[...] + bunr[s - 1]
        bcopies.append(
            push(bun, bunr.at[s], b_sem.at[s, 0], b_sem.at[s, 1], (flipped(dp, s - 1), mp))
        )
    tails = []
    for c in range(n):
        mine = acc[c][dp]
        if c in TABLE_CHUNKS:
            k = TABLE_CHUNKS.index(c)
            send, recv = tsend[2 * k], tsend[2 * k + 1]
            send[...] = jnp.where(mp == 0, mine[small:], mine[:small])
            outs[c][mp] = jnp.where(mp == 0, mine[:small], mine[small:])
            tails.append((c, recv, push(send, recv, t_sem.at[k, 0], t_sem.at[k, 1], mate)))
        else:
            outs[c][...] = mine
    total = jnp.zeros((1, 1), f32)
    for c in range(n):
        if c not in TABLE_CHUNKS:
            total = total + jnp.sum(outs[c][...] * outs[c][...], keepdims=True)
    for c, recv, copy in tails:
        copy.wait()
        outs[c][1 - mp] = recv[...]
        for m in range(2):
            total = total + jnp.sum(outs[c][m] * outs[c][m], keepdims=True)
    sq[0] = jnp.broadcast_to(total, (8, 128))
    bcopies[-1].wait()
    final = bun[...] + bunr[bits]
    obun_ref[...] = final
    shared = jnp.sum(final[:, 128:] * final[:, 128:], keepdims=True)
    for s in range(bits + 1):
        peer = mate if s == 0 else (flipped(dp, s - 1), mp)
        copy = push(sq.at[s], sqr.at[s], q_sem.at[s, 0], q_sem.at[s, 1], peer)
        copy.wait()
        sq[s + 1] = sq[s] + sqr[s]
    squares = sq[bits + 1] + shared
    loss, weight = final[:, 0:1], final[:, 1:2]
    norm = jnp.sqrt(squares) / weight
    factor = jnp.minimum(1.0, clip_limit / norm) / weight
    which = lax.broadcasted_iota(jnp.int32, (8, 128), 1)
    info = jnp.where(which == 0, loss, jnp.where(which == 1, weight, norm))
    info_ref[...] = jnp.where(which == 3, factor, info)
    for copy in mcopies:
        copy.wait_send()
    for copy in copies.values():
        copy.wait_send()


def reduce_all(own, mates, smalls, turns, n_data):
    bits = n_data.bit_length() - 1
    rows = D // n_data
    widths = [x.shape[1] for x in own]
    n = len(widths)
    sems = pltpu.SemaphoreType.DMA
    inside = pl.BlockSpec(memory_space=pltpu.VMEM)
    anywhere = pl.BlockSpec(memory_space=pl.ANY)
    bufs = [
        pltpu.VMEM((2 ** (bits - 1 - s), rows, w), bf16) for w in widths for s in range(bits)
    ]
    length = sum(x.shape[0] * x.shape[1] for x in smalls)
    outs = [
        jax.ShapeDtypeStruct((2, rows // 2, w) if c in TABLE_CHUNKS else (rows, w), f32)
        for c, w in enumerate(widths)
    ]
    tails = [
        pltpu.VMEM((rows // 2, widths[c]), f32) for c in TABLE_CHUNKS for _ in range(2)
    ]

    def kernel(*refs):
        cut = len(refs) - 10 - len(tails)
        head, rest = refs[:cut], refs[cut:]
        tsend, rest = rest[: len(tails)], rest[len(tails) :]
        reduce_kernel(bits, widths, turns, *head, rest[0], rest[1], tsend, *rest[2:])

    return pl.pallas_call(
        kernel,
        in_specs=[inside] * n + [anywhere] * n + [inside] * len(smalls),
        out_specs=[inside] * (n + 2),
        out_shape=outs
        + [
            jax.ShapeDtypeStruct((1, length), f32),
            jax.ShapeDtypeStruct((8, 128), f32),
        ],
        scratch_shapes=[pltpu.VMEM((D, w), bf16) for w in widths]
        + [pltpu.VMEM((n_data, rows, w), f32) for w in widths]
        + bufs
        + bufs
        + tails
        + [
            pltpu.VMEM((1, length), f32),
            pltpu.VMEM((bits + 1, 1, length), f32),
            pltpu.VMEM((bits + 2, 8, 128), f32),
            pltpu.VMEM((bits + 1, 8, 128), f32),
            sems((n, 2)),
            sems((n, bits)),
            sems((n, bits)),
            sems((bits + 1, 2)),
            sems((bits + 1, 2)),
            sems((len(TABLE_CHUNKS), 2)),
        ],
        compiler_params=pltpu.CompilerParams(
            collective_id=1, has_side_effects=True, vmem_limit_bytes=62 * MIB
        ),
        name="reduce_gradients",
    )(*own, *mates, *smalls)


def adamw(master, first, second, gradient, rate, decay):
    first = beta_one * first + (1.0 - beta_one) * gradient
    second = beta_two * second + (1.0 - beta_two) * gradient * gradient
    first_hat = first / (1.0 - beta_one**STEP)
    second_hat = second / (1.0 - beta_two**STEP)
    master = master - rate * (first_hat / (jnp.sqrt(second_hat) + adam_eps) + decay * master)
    return (master, first, second)


def local_split(flat, layer):
    mp = lax.axis_index("mp")
    rows = []
    for m in range(2):
        pieces = []
        for h in range(3):
            at = 128 + 2 * D * layer + (128 * m + HD * h if h < 2 else 256 + HD * m)
            pieces += [flat[:, at : at + HD], flat[:, at + D : at + D + HD]]
        at = 128 + 2 * D * LAYERS + FF * layer + HALF * m
        rows.append(jnp.concatenate(pieces + [flat[:, at : at + HALF]], 1))
    return jnp.where(mp == 0, rows[0], rows[1])


def update_kernel(info_ref, *refs):
    g = refs[:9]
    flat_ref = refs[9]
    params = refs[10:25]
    outs = refs[25:]
    factor = info_ref[0, 3]

    def write(grad, item, rate, decay, at, outs, low):
        new, one, two = adamw(
            item[0][at], item[1][at], item[2][at], grad * factor, rate, decay
        )
        outs[0][at], outs[1][at], outs[2][at] = new, one, two
        if low:
            outs[3][at] = new.astype(bf16)

    everything = (slice(None), slice(None))
    heads = [
        jnp.concatenate([g[6][m, :, 512 * h : 512 * (h + 1)] for m in range(2)], 1)[:, :CLS]
        for h in range(2)
    ]
    token = jnp.concatenate([g[8][0], g[8][1]], 1)
    table = jnp.concatenate(
        [g[7][0], g[7][1], token[:, PATCHES:TOK], token[:, :PATCHES]] + heads, 1
    )
    write(table, params[0:3], matrix_rate, matrix_decay, everything, outs[0:4], True)
    vec = jnp.transpose(token, (1, 0))[TP : TP + 6 * LAYERS + 2]
    write(vec, params[3:6], vector_rate, 0.0, everything, outs[4:7], False)
    for layer in range(LAYERS):
        packed = g[layer][...]
        pieces = []
        for h in range(3):
            for t in range(4):
                lo = 128 * t + HD * h if h < 2 else 512 + HD * t
                pieces.append(packed[:, lo : lo + HD])
        grad = jnp.concatenate(pieces, 1)
        write(grad, params[6:9], matrix_rate, matrix_decay, layer, outs[7:11], True)
        for half in range(2):
            write(
                g[LAYERS + 2 * layer + half][...],
                params[9:12],
                matrix_rate,
                matrix_decay,
                (layer, slice(None), half),
                outs[11:15],
                True,
            )
    flat = flat_ref[...]
    for layer in range(LAYERS):
        grad = local_split(flat, layer)
        write(grad, params[12:15], vector_rate, 0.0, slice(layer, layer + 1), outs[15:18], False)


def update(info, grads, split, params):
    outs = []
    for i in range(5):
        low = i in (0, 2, 3)
        shape = params[3 * i].shape
        outs += [jax.ShapeDtypeStruct(shape, f32)] * 3
        outs += [jax.ShapeDtypeStruct(shape, bf16)] if low else []
    ins = list(grads) + [split] + list(params)
    return pl.pallas_call(
        update_kernel,
        grid=(1,),
        in_specs=[pl.BlockSpec(memory_space=pltpu.SMEM)] + [full_spec(x.shape) for x in ins],
        out_specs=[full_spec(x.shape) for x in outs],
        out_shape=outs,
        compiler_params=pltpu.CompilerParams(vmem_limit_bytes=60 * MIB),
        name="update_weights",
    )(info, *ins)


def pack_kernel(t_ref, v_ref, a_ref, f_ref, tab_ref, main_ref):
    small = t_ref.shape[0]
    table = t_ref[...]

    def zeros(n):
        return jnp.zeros((small, n), f32)

    turned = jnp.transpose(v_ref[...], (1, 0))
    low = PD + 2
    seg = jnp.concatenate(
        [
            table[:, low : low + PATCHES],
            table[:, PD:low],
            zeros(TP - TOK),
            turned,
            zeros(256 - TP - turned.shape[1]),
        ],
        1,
    )
    heads = [
        jnp.concatenate(
            [table[:, PD + TOK + CLS * h : PD + TOK + CLS * (h + 1)], zeros(1024 - CLS)], 1
        )
        for h in range(2)
    ]
    parts = [table[:, :PD], seg] + heads
    for m in range(2):
        at = 0
        for x in parts:
            half = x.shape[1] // 2
            tab_ref[m, :, at : at + half] = x[:, half * m : half * (m + 1)].astype(bf16)
            at += half
    for layer in range(LAYERS):
        a = a_ref[layer]
        for t in range(4):
            pair = jnp.concatenate(
                [a[:, 256 * h + HD * t : 256 * h + HD * (t + 1)] for h in range(2)], 1
            )
            main_ref[layer, :, 128 * t : 128 * (t + 1)] = pair.astype(bf16)
        main_ref[layer, :, 512:] = a[:, 512:].astype(bf16)
        for half in range(2):
            main_ref[LAYERS + 2 * layer + half] = f_ref[layer, :, half].astype(bf16)


def pack(tab, vec, attn, ffw):
    layers, rows, _ = attn.shape
    ins = [tab, vec, attn, ffw]
    shapes = [(2, tab.shape[0], T_COLS), (3 * layers, rows, HALF)]
    return pl.pallas_call(
        pack_kernel,
        grid=(1,),
        in_specs=[full_spec(x.shape) for x in ins],
        out_specs=[full_spec(x) for x in shapes],
        out_shape=[jax.ShapeDtypeStruct(x, bf16) for x in shapes],
        compiler_params=pltpu.CompilerParams(vmem_limit_bytes=60 * MIB),
        name="pack_shards",
    )(*ins)


def shards(
    pixels,
    labels,
    teacher,
    partner,
    mix_weight,
    class_weight,
    tables,
    tables_first,
    tables_second,
    vectors,
    vectors_first,
    vectors_second,
    attention,
    attention_first,
    attention_second,
    feedforward,
    feedforward_first,
    feedforward_second,
    split_bias,
    split_bias_first,
    split_bias_second,
    head_bias,
    head_bias_first,
    head_bias_second,
):
    n_data = lax.axis_size("dp")
    dp, mp = mesh_place()
    images_here = pixels.shape[0]
    count = images_here // 2
    rows = D // n_data
    far_pairs = [(i, (i + n_data // 2) % n_data) for i in range(n_data)]
    pix = pixels.transpose(1, 0, 2)
    tab, shard = pack(tables.T, vectors, attention, feedforward)
    deep = gather_plan(n_data.bit_length() - 1, MAIN_TURNS)[1]
    front, seg, *heights, sb = gather_front(tab, shard, split_bias, n_data)
    front = front.reshape(2, D, FRONT_WIDTHS[0])
    seg = seg.reshape(2, D, FRONT_WIDTHS[1])
    near_pairs = [(i, i ^ (1 << deep[-1])) for i in range(n_data)]
    mains, heads = ([x, lax.ppermute(x, "dp", near_pairs)] for x in heights)
    own, send = embed(partner, pix, front)
    mains, heads, send = lax.optimization_barrier((mains, heads, send))
    far = lax.ppermute(send, "dp", far_pairs)
    weights, w_heads, pix_mine = gather_main(
        mains, heads, pix.reshape(PATCHES, 2, count, PD), n_data
    )
    pix_mine, far, weights = lax.optimization_barrier((pix_mine, far, weights))
    pix_far = lax.ppermute(pix_mine, "dp", far_pairs)
    hb = jnp.pad(
        head_bias.astype(bf16).astype(f32).reshape(2, CLS),
        ((0, 0), (0, 1024 - CLS)),
        constant_values=-1e30,
    ).reshape(1, -1)
    cw = jnp.pad(class_weight, (0, 1024 - CLS)).reshape(1, -1)
    *kept, mid, tok = forward(
        partner, mix_weight, own, far, seg, weights, sb
    )
    u1o, u1m, d1o, d1m, ho, hm, dz, gvh, gu1, dhb, stat = head(
        partner, mix_weight, labels, teacher, mid, weights, w_heads, sb, hb, cw, tok
    )
    dz0, a0o, a0m, a1o, a1m, u0o, u0m, d0o, d0m, gvb, gb, gu0 = backward(dz, kept, weights, tok)
    po, pm, eo, em = patch_grad(
        partner,
        mix_weight,
        dz0,
        pix.reshape(PATCHES * images_here, PD),
        pix_far.reshape(PATCHES * count, PD),
        gvb,
        gvh,
    )
    own_parts = [a0o, a1o, u0o, d0o, u1o, d1o, ho, po, eo]
    mate_parts = [a0m, a1m, u0m, d0m, u1m, d1m, hm, pm, em]
    *g, flat, info = reduce_all(
        own_parts, mate_parts, [stat, gb, gu0, gu1, dhb], REDUCE_TURNS, n_data
    )
    loss_sum, weight_sum, grad_norm, factor = (info[0, i] for i in range(4))
    at = 128 + 2 * D * LAYERS + FF * LAYERS
    g_head = flat[0, at : at + 2048].reshape(2, 1024)[:, :CLS].reshape(-1)
    fresh = update(
        info,
        g,
        flat,
        [
            tables.T,
            tables_first.T,
            tables_second.T,
            vectors,
            vectors_first,
            vectors_second,
            attention,
            attention_first,
            attention_second,
            feedforward,
            feedforward_first,
            feedforward_second,
            split_bias,
            split_bias_first,
            split_bias_second,
        ],
    )
    fresh = [x.T for x in fresh[:4]] + list(fresh[4:])
    h_new, h_one, h_two = adamw(
        head_bias, head_bias_first, head_bias_second, g_head * factor, vector_rate, 0.0
    )
    return (loss_sum, weight_sum, grad_norm, *fresh, h_new, h_one, h_two)


def solution(mesh):
    table = P(None, ("dp", "mp"))
    attn = P(None, "dp", "mp")
    ffw = P(None, "dp", None, "mp")
    split = P(None, "mp")
    return jax.shard_map(
        shards,
        mesh=mesh,
        in_specs=(P("dp", None, None), P(), P("dp"), P("dp"), P("dp"), P())
        + (table,) * 6
        + (attn,) * 3
        + (ffw,) * 3
        + (split,) * 3
        + (P(),) * 3,
        out_specs=(P(),) * 3
        + (table,) * 7
        + (attn,) * 4
        + (ffw,) * 4
        + (split,) * 3
        + (P(),) * 3,
        check_vma=False,
    )
```

```python
import functools

import jax
import jax.numpy as jnp
from jax import lax
from jax.experimental import pallas as pl
from jax.experimental.pallas import tpu as pltpu
from jax.sharding import PartitionSpec as P

D = 384
HEADS = 6
HD = 64
FF = 1536
CLS = 1000
PD = 768
PATCHES = 196
LAYERS = 2
STEP = 10
TOK = 198
TP = 208
GRP = 2
F_GRP = 4
ENDS = 16
END_AT = 4
SENT = 200
ROWS = GRP * TP
HALF = FF // 2
COLS = 6144
T_COLS = 1536
F_COLS = 512
TABLE_CHUNKS = (6, 7, 8)
REDUCE_ORDER = (0, 2, 4, 1, 3, 6, 5, 7, 8)
REDUCE_TURNS = (0, 0, 1, 1, 2, 1, 2, 0, 0)
MAIN_WIDTHS = (768, 768, 768, 768, 768, 768, 1024)
MAIN_TURNS = (0, 0, 0, 1, 0, 1, 1)
FRONT_WIDTHS = (384, 128)
FRONT_TURNS = (0, 1)
M_COLS = 4608
MIB = 1 << 20
NORM_ROWS = ROWS
GELU_ROWS = 32

norm_eps = 1e-06
clip_limit = 0.02
beta_one = 0.9
beta_two = 0.999
adam_eps = 1e-08
matrix_rate = 0.08
vector_rate = 0.5
matrix_decay = 0.05

f32 = jnp.float32
bf16 = jnp.bfloat16
MESH = pl.DeviceIdType.MESH
AB = ((1,), (0,))
ABT = ((1,), (1,))
ATB = ((0,), (0,))


def mm(left, right, dims=AB):
    return lax.dot_general(left, right, (dims, ((), ())), preferred_element_type=f32)


def full_spec(shape):
    return pl.BlockSpec(shape, lambda *_: (0,) * len(shape), pipeline_mode=pl.Buffered(1))


def row_loop(total, chunk, body):
    def step(index, carry):
        body(pl.ds(pl.multiple_of(index * chunk, chunk), chunk))
        return carry

    if total == chunk:
        body(slice(0, total))
    else:
        lax.fori_loop(0, total // chunk, step, 0)


def center(x):
    mean = jnp.mean(x, -1, keepdims=True)
    xc = x - mean
    scale = lax.rsqrt(jnp.mean(xc * xc, -1, keepdims=True) + norm_eps)
    return xc * scale, scale


def gelu_pair(x):
    e = jnp.exp2((x * x) * -0.7213475204444817)
    den = 1.0 + 0.23164189 * jnp.abs(x)
    r = pl.reciprocal(den, approx=True)
    r = r * (2.0 - den * r)
    poly = r * (
        0.127414796
        + r * (-0.142248368 + r * (0.7107068705 + r * (-0.7265760135 + r * 0.5307027145)))
    )
    tail = poly * e
    cdf = jnp.where(x > 0.0, 1.0 - tail, tail)
    return x * cdf, cdf + x * (e * 0.3989422804014327)


def partner_place(partner_ref, k):
    images = partner_ref.shape[0]
    n_data = lax.axis_size("dp")
    far = lax.rem(lax.axis_index("dp") + n_data // 2, n_data)
    wanted = far * images + lax.axis_index("mp") * (images // 2) + k
    place = jnp.int32(0)
    for i in range(images):
        place = place + jnp.where(partner_ref[i] == wanted, i, 0)
    return place


def project(pix, w_ref):
    return mm(pix[:, :D], w_ref[0], ABT) + mm(pix[:, D:], w_ref[1], ABT)


def embed_send_kernel(pix_ref, w_ref, send_ref, flat):
    mp = lax.axis_index("mp")
    patches, _, images, _ = pix_ref.shape
    part = patches // 7
    for c in range(7):
        out = project(pix_ref[c * part : (c + 1) * part, mp].reshape(part * images, PD), w_ref)
        for j in range(3):
            flat[j, c * part * images : (c + 1) * part * images] = out[:, 128 * j : 128 * (j + 1)]
    for k in range(images):
        for j in range(3):
            cols = slice(128 * j, 128 * (j + 1))
            send_ref[k, :patches, cols] = flat[j, pl.ds(k, patches, stride=images), :].astype(bf16)
        send_ref[k, patches:] = jnp.zeros((SENT - patches, D), bf16)


def embed_own_kernel(partner_ref, pix_ref, w_ref, own_ref, flat):
    count = partner_ref.shape[0]
    patches = pix_ref.shape[0]
    part = patches // 7
    for c in range(7):
        out = project(pix_ref[c * part : (c + 1) * part].reshape(part * count, PD), w_ref)
        for j in range(3):
            flat[j, c * part * count : (c + 1) * part * count] = out[:, 128 * j : 128 * (j + 1)]
    for k in range(count // 2):
        place = partner_place(partner_ref, k)
        for j in range(3):
            cols = slice(128 * j, 128 * (j + 1))
            own_ref[k, :, cols] = flat[j, pl.ds(place, patches, stride=count), :]


def embed_call(kernel, prefix, pix, weights, shape, dtype, rows, name):
    return pl.pallas_call(
        kernel,
        grid=(1,),
        in_specs=[pl.BlockSpec(memory_space=pltpu.SMEM)] * len(prefix)
        + [full_spec(pix.shape), full_spec(weights.shape)],
        out_specs=full_spec(shape),
        out_shape=jax.ShapeDtypeStruct(shape, dtype),
        scratch_shapes=[pltpu.VMEM((3, rows, 128), f32)],
        compiler_params=pltpu.CompilerParams(vmem_limit_bytes=60 * MIB),
        name=name,
    )(*prefix, pix, weights)


def embed_send(pix, weights):
    images = pix.shape[2]
    shape = (images, SENT, D)
    rows = PATCHES * images
    return embed_call(embed_send_kernel, [], pix, weights, shape, bf16, rows, "embed_sent_images")


def embed_own(partner, pix, weights):
    images = pix.shape[1]
    shape = (images // 2, PATCHES, D)
    rows = PATCHES * images
    return embed_call(
        embed_own_kernel, [partner], pix, weights, shape, f32, rows, "embed_own_images"
    )


def split_tokens(w_ref, col):
    seg = jnp.concatenate([w_ref[0, :, col : col + 128], w_ref[1, :, col : col + 128]], 1)
    return jnp.transpose(seg.astype(f32), (1, 0))


def attend(g, qkv_ref, p_ref, ho_ref):
    rows = slice(g * TP, (g + 1) * TP)
    lane = lax.broadcasted_iota(jnp.int32, (TP, 128), 1)
    key_mask = jnp.where(lax.broadcasted_iota(jnp.int32, (1, TP), 1) < TOK, 0.0, -1e30).astype(f32)
    for j in range(3):
        q = qkv_ref[rows, 128 * j : 128 * (j + 1)]
        k = qkv_ref[rows, D + 128 * j : D + 128 * (j + 1)]
        v = qkv_ref[rows, 2 * D + 128 * j : 2 * D + 128 * (j + 1)]
        outs = []
        for s in range(2):
            mine = (lane < 64) if s == 0 else (lane >= 64)
            scores = mm(jnp.where(mine, q, jnp.zeros_like(q)), k, ABT) + key_mask
            exps = jnp.exp(scores - jnp.max(scores, -1, keepdims=True))
            probs = (exps * (1.0 / jnp.sum(exps, -1, keepdims=True))).astype(bf16)
            p_ref[6 * g + 2 * j + s] = probs
            outs.append(mm(probs, v))
        ho_ref[rows, 128 * j : 128 * (j + 1)] = jnp.where(lane < 64, outs[0], outs[1]).astype(bf16)


PAIRS = (0, 1, 3, 4, 2, 5)


def rounded(x):
    return x.astype(bf16).astype(f32)


def norm_rows(src, gain, shift, dst):
    dst[...] = (center(src[...])[0] * gain + shift).astype(bf16)


def token_row(tok_ref, layer, i):
    at = TP + 6 * layer + i
    return tok_ref[at : at + 1]


def spread_heads(x):
    lane = lax.broadcasted_iota(jnp.int32, x.shape, 1)
    zero = jnp.zeros_like(x)
    return jnp.concatenate(
        [jnp.where((lane >= HD * h) & (lane < HD * (h + 1)), x, zero) for h in range(HEADS)], 0
    )


def gather_heads(x):
    lane = lax.broadcasted_iota(jnp.int32, (ENDS, D), 1)
    total = jnp.zeros((ENDS, D), f32)
    for h in range(HEADS):
        part = x[ENDS * h : ENDS * (h + 1)]
        total = total + jnp.where((lane >= HD * h) & (lane < HD * (h + 1)), part, 0.0)
    return total


def attend_ends(g, kv_ref, q_ref, p_ref, ho_ref):
    rows = slice(g * TP, (g + 1) * TP)
    ends = slice(g * ENDS, (g + 1) * ENDS)
    key_mask = jnp.where(lax.broadcasted_iota(jnp.int32, (1, TP), 1) < TOK, 0.0, -1e30).astype(f32)
    scores = mm(spread_heads(q_ref[ends]), kv_ref[rows, :D], ABT) + key_mask
    exps = jnp.exp(scores - jnp.max(scores, -1, keepdims=True))
    probs = (exps * (1.0 / jnp.sum(exps, -1, keepdims=True))).astype(bf16)
    p_ref[g] = probs
    ho_ref[ends] = gather_heads(mm(probs, kv_ref[rows, D:])).astype(bf16)


def forward_kernel(partner_ref, mix_ref, own_ref, far_ref, t_ref, w_ref, sb_ref, *refs):
    x_ref, mid_ref, qkv_ref, p_ref, ho_ref, hid_ref, gp_ref = refs[:7]
    x1_ref, kv_ref, q1_ref, p1_ref, ho1_ref, mid1_ref, tok_ref = refs[7:14]
    qkv_w, out_w, nbuf, up_s, bias_ref = refs[14:]
    step = pl.program_id(0)

    @pl.when(step == 0)
    def _():
        tok_ref[...] = split_tokens(t_ref, 0)
        for layer in range(LAYERS):
            attn_tiles(w_ref.at[layer], qkv_w.at[layer], out_w.at[layer])
            pieces = [
                sb_ref[h // 3, layer : layer + 1, 128 * (h % 3) + HD * t : 128 * (h % 3) + HD * (t + 1)]
                for t in range(2)
                for h in PAIRS
            ]
            bias_ref[layer : layer + 1] = rounded(jnp.concatenate(pieces, 1))

    def row(layer, i):
        return token_row(tok_ref, layer, i)

    for g in range(F_GRP):
        w = mix_ref[partner_place(partner_ref, step * F_GRP + g)]
        x_ref[g * TP : g * TP + PATCHES] = (
            w * own_ref[g] + (1.0 - w) * far_ref[g, :PATCHES].astype(f32) + tok_ref[:PATCHES]
        )
        x_ref[g * TP + PATCHES : (g + 1) * TP] = tok_ref[PATCHES:TP]
    norm_rows(x_ref, row(0, 0), row(0, 1), nbuf)
    n = nbuf[...]
    q = mm(n, qkv_w[0, :, :D]) + bias_ref[0:1, :D]
    qkv_ref[:, :D] = (q.astype(bf16).astype(f32) * 0.125).astype(bf16)
    qkv_ref[:, D : 2 * D] = mm(n, qkv_w[0, :, D : 2 * D]).astype(bf16)
    v = mm(n, qkv_w[0, :, 2 * D :]) + bias_ref[0:1, D : 2 * D]
    qkv_ref[:, 2 * D :] = v.astype(bf16)
    for g in range(F_GRP):
        attend(g, qkv_ref, p_ref, ho_ref)
    mid_ref[...] = x_ref[...] + mm(ho_ref[...], out_w[0], ABT) + row(0, 4)
    norm_rows(mid_ref, row(0, 2), row(0, 3), nbuf)
    up_w, down_w = w_ref.at[LAYERS], w_ref.at[LAYERS + 1]
    for m in range(2):
        cols = slice(HALF * m, HALF * (m + 1))
        up_s[...] = mm(nbuf[...], up_w[m]) + rounded(sb_ref[m, 0:1, D:])

        def body(rs):
            hid, gp = gelu_pair(up_s[rs])
            hid_ref[rs, cols] = hid.astype(bf16)
            gp_ref[rs, cols] = gp.astype(bf16)

        row_loop(F_GRP * TP, GELU_ROWS, body)
    out = mid_ref[...] + row(0, 5)
    for m in range(2):
        cols = slice(HALF * m, HALF * (m + 1))
        out = out + mm(hid_ref[:, cols], down_w[m], ABT)
    x1_ref[...] = out
    norm_rows(x1_ref, row(1, 0), row(1, 1), nbuf)
    n = nbuf[...]
    kv_ref[:, :D] = mm(n, qkv_w[1, :, D : 2 * D]).astype(bf16)
    kv_ref[:, D:] = (mm(n, qkv_w[1, :, 2 * D :]) + bias_ref[1:2, D : 2 * D]).astype(bf16)
    ends = jnp.concatenate([nbuf[(g + 1) * TP - ENDS : (g + 1) * TP] for g in range(F_GRP)], 0)
    q = mm(ends, qkv_w[1, :, :D]) + bias_ref[1:2, :D]
    q1_ref[...] = (q.astype(bf16).astype(f32) * 0.125).astype(bf16)
    for g in range(F_GRP):
        attend_ends(g, kv_ref, q1_ref, p1_ref, ho1_ref)
    x_ends = jnp.concatenate([x1_ref[(g + 1) * TP - ENDS : (g + 1) * TP] for g in range(F_GRP)], 0)
    mid1_ref[...] = x_ends + mm(ho1_ref[...], out_w[1], ABT) + row(1, 4)


def kept_shapes(count):
    n = count * TP
    return [
        ((n, D), f32),
        ((n, D), f32),
        ((n, 3 * D), bf16),
        ((count * HEADS, TP, TP), bf16),
        ((n, D), bf16),
        ((n, FF), bf16),
        ((n, FF), bf16),
        ((n, D), f32),
        ((n, 2 * D), bf16),
        ((count * ENDS, D), bf16),
        ((count, HEADS * ENDS, TP), bf16),
        ((count * ENDS, D), bf16),
        ((count * ENDS, D), f32),
    ]


def block_of(shape, steps):
    block = (shape[0] // steps,) + tuple(shape[1:])
    return pl.BlockSpec(block, lambda i: (i,) + (0,) * (len(block) - 1))


def forward(partner, mix, own, far, seg, weights, sb):
    count = own.shape[0]
    steps = count // F_GRP
    outs = kept_shapes(count)
    shapes = [jax.ShapeDtypeStruct(s, t) for s, t in outs] + [jax.ShapeDtypeStruct((256, D), f32)]
    specs = [block_of(s, steps) for s, _ in outs] + [full_spec((256, D))]
    return pl.pallas_call(
        forward_kernel,
        grid=(steps,),
        in_specs=[
            pl.BlockSpec(memory_space=pltpu.SMEM),
            pl.BlockSpec(memory_space=pltpu.SMEM),
            block_of(own.shape, steps),
            block_of(far.shape, steps),
            full_spec(seg.shape),
            pl.BlockSpec((4, 2, D, 768), lambda i: (0, 0, 0, 0), pipeline_mode=pl.Buffered(1)),
            full_spec(sb.shape),
        ],
        out_specs=specs,
        out_shape=shapes,
        scratch_shapes=[
            pltpu.VMEM((LAYERS, D, 3 * D), bf16),
            pltpu.VMEM((LAYERS, D, D), bf16),
            pltpu.VMEM((F_GRP * TP, D), bf16),
            pltpu.VMEM((F_GRP * TP, HALF), f32),
            pltpu.VMEM((LAYERS, 2 * D), f32),
        ],
        compiler_params=pltpu.CompilerParams(vmem_limit_bytes=60 * MIB),
        name="forward_layers",
    )(partner, mix, own, far, seg, weights, sb)


def norm_back(dy, xhat, scale, gain):
    dyg = dy * gain
    c1 = jnp.mean(dyg, -1, keepdims=True)
    c2 = jnp.mean(dyg * xhat, -1, keepdims=True)
    return scale * (dyg - c1 - xhat * c2)


def share(part, own_ref, mate_ref, mp):
    own_ref[...] = part[mp]
    mate_ref[...] = part[1 - mp].astype(bf16)


def head_kernel(
    partner_ref,
    mix_ref,
    label_ref,
    teacher_ref,
    mid_ref,
    wf_ref,
    w_ref,
    sb_ref,
    hb_ref,
    cw_ref,
    tok_ref,
    uo_ref,
    um_ref,
    do_ref,
    dm_ref,
    ho_ref,
    hm_ref,
    dz_ref,
    gv_ref,
    gu_ref,
    dhb_ref,
    stat_ref,
    lanes,
    g_ffw,
    g_head,
):
    mp = lax.axis_index("mp")
    gain2, shift2, bias_f = (token_row(tok_ref, 1, i) for i in (2, 3, 5))
    gain, shift = (token_row(tok_ref, 2, i) for i in range(2))
    count = mid_ref.shape[0] // ENDS
    images = partner_ref.shape[0]
    n_data = lax.axis_size("dp")
    dp = lax.axis_index("dp")
    far_base = lax.rem(dp + n_data // 2, n_data) * images + mp * count
    marks = []
    for k in range(count):
        place = partner_place(partner_ref, k)
        marks.append(
            (
                label_ref[dp * images + place],
                label_ref[far_base + k],
                teacher_ref[place],
                mix_ref[place],
            )
        )
    for j in range(3):
        lanes[j] = mid_ref[:, 128 * j : 128 * (j + 1)]
    mid = jnp.concatenate(
        [
            jnp.concatenate(
                [lanes[j, pl.ds(END_AT + h, count, stride=ENDS), :] for j in range(3)], 1
            )
            for h in range(2)
        ],
        0,
    )
    xhat2, scale2 = center(mid)
    normed = (xhat2 * gain2 + shift2).astype(bf16)
    out = mid + bias_f
    hids, gps = [], []
    for m in range(2):
        up = mm(normed, wf_ref[0, m]) + rounded(sb_ref[m, 1:2, D:])
        hid, gp = gelu_pair(up)
        hids.append(hid.astype(bf16))
        gps.append(gp)
        out = out + mm(hids[m], wf_ref[1, m], ABT)
    xhat, scale = center(out)
    final = (xhat * gain + shift).astype(bf16)
    loss = jnp.zeros((1, 1), f32)
    weight = jnp.zeros((1, 1), f32)
    dfinals = []
    for h in range(2):
        mine = final[count * h : count * (h + 1)]
        halves = []
        for m in range(2):
            wh = w_ref[m, :, 512 * h : 512 * (h + 1)]
            at = 1024 * h + 512 * m
            logits = mm(mine, wh) + hb_ref[0:1, at : at + 512]
            ids = lax.broadcasted_iota(jnp.int32, (1, 512), 1) + 512 * m
            shares = []
            for k in range(count):
                first, second, teach, mix = marks[k]
                if h == 0:
                    both = jnp.where(ids == first, mix, 0.0) + jnp.where(ids == second, 1.0 - mix, 0.0)
                    shares.append(both)
                else:
                    shares.append(jnp.where(ids == teach, 1.0, 0.0))
            coef = jnp.concatenate(shares, 0) * cw_ref[0:1, 512 * m : 512 * (m + 1)]
            halves.append((wh, logits, coef))
        top = jnp.maximum(*[jnp.max(x[1], -1, keepdims=True) for x in halves])
        exps = [jnp.exp(x[1] - top) for x in halves]
        total = sum(jnp.sum(x, -1, keepdims=True) for x in exps)
        lse = top + jnp.log(total)
        csum = sum(jnp.sum(x[2], -1, keepdims=True) for x in halves)
        dfinal = jnp.zeros((count, D), f32)
        for m in range(2):
            wh, logits, coef = halves[m]
            loss = loss + jnp.sum(jnp.sum(coef * (lse - logits), -1, keepdims=True), 0, keepdims=True)
            dl = csum * (exps[m] / total) - coef
            at = 1024 * h + 512 * m
            dhb_ref[0:1, at : at + 512] = jnp.sum(dl, 0, keepdims=True)
            low = dl.astype(bf16)
            g_head[m, :, 512 * h : 512 * (h + 1)] = mm(mine, low, ATB)
            dfinal = dfinal + mm(low, wh, ABT)
        weight = weight + jnp.sum(csum, 0, keepdims=True)
        dfinals.append(dfinal)
    dfinal = jnp.concatenate(dfinals, 0)
    dz = norm_back(dfinal, xhat, scale, gain)
    low = dz.astype(bf16)
    dn = jnp.zeros_like(dz)
    for m in range(2):
        dh = mm(low, wf_ref[1, m])
        du = (dh.astype(bf16).astype(f32) * gps[m]).astype(bf16)
        gu_ref[0:1, HALF * m : HALF * (m + 1)] = jnp.sum(du.astype(f32), 0, keepdims=True)
        g_ffw[0, m] = mm(normed, du, ATB)
        g_ffw[1, m] = mm(low, hids[m], ATB)
        dn = dn + mm(du, wf_ref[0, m], ABT)
    dmid = dz + norm_back(dn, xhat2, scale2, gain2)
    gv_ref[...] = jnp.zeros_like(gv_ref)
    sums = [dn * xhat2, dn, dmid, dz, dfinal * xhat, dfinal]
    for i, item in enumerate(sums):
        gv_ref[i + 2 : i + 3] = jnp.sum(item, 0, keepdims=True)
    lanes[...] = jnp.zeros_like(lanes)
    for j in range(3):
        for h in range(2):
            lanes[j, pl.ds(END_AT + h, count, stride=ENDS), :] = dmid[
                count * h : count * (h + 1), 128 * j : 128 * (j + 1)
            ]
        dz_ref[:, 128 * j : 128 * (j + 1)] = lanes[j]
    which = lax.broadcasted_iota(jnp.int32, stat_ref.shape, 1)
    stat_ref[...] = jnp.where(which == 0, loss, jnp.where(which == 1, weight, 0.0))
    share(g_ffw.at[0], uo_ref, um_ref, mp)
    share(g_ffw.at[1], do_ref, dm_ref, mp)
    share(g_head, ho_ref, hm_ref, mp)


def pair_shapes(shapes):
    return [jax.ShapeDtypeStruct(s, t) for s in shapes for t in (f32, bf16)]


def head(partner, mix, labels, teacher, mid, weights, w_heads, sb, hb, cw, tok):
    outs = pair_shapes([(D, 768), (D, 768), (D, 1024)]) + [
        jax.ShapeDtypeStruct(s, f32)
        for s in (mid.shape, (8, D), (1, FF), (1, 2048), (1, 128))
    ]
    return pl.pallas_call(
        head_kernel,
        grid=(1,),
        in_specs=[pl.BlockSpec(memory_space=pltpu.SMEM)] * 4
        + [
            full_spec(mid.shape),
            pl.BlockSpec((2, 2, D, 768), lambda i: (2, 0, 0, 0), pipeline_mode=pl.Buffered(1)),
        ]
        + [full_spec(x.shape) for x in (w_heads, sb, hb, cw, tok)],
        out_specs=[full_spec(x.shape) for x in outs],
        out_shape=outs,
        scratch_shapes=[
            pltpu.VMEM((3, mid.shape[0], 128), f32),
            pltpu.VMEM((2, 2, D, 768), f32),
            pltpu.VMEM((2, D, 1024), f32),
        ],
        compiler_params=pltpu.CompilerParams(vmem_limit_bytes=60 * MIB),
        name="loss_heads",
    )(partner, mix, labels, teacher, mid, weights, w_heads, sb, hb, cw, tok)


def attend_back(g, dho, qkv_ref, p_ref, dproj):
    rows = slice(g * TP, (g + 1) * TP)
    lane = lax.broadcasted_iota(jnp.int32, (TP, 128), 1)
    for j in range(3):
        q = qkv_ref[rows, 128 * j : 128 * (j + 1)]
        k = qkv_ref[rows, D + 128 * j : D + 128 * (j + 1)]
        v = qkv_ref[rows, 2 * D + 128 * j : 2 * D + 128 * (j + 1)]
        do = dho[rows, 128 * j : 128 * (j + 1)]
        qt, kt, dot_ = (jnp.transpose(a, (1, 0)) for a in (q, k, do))
        for s in range(2):
            mine = (lane < 64) if s == 0 else (lane >= 64)
            sub = slice(64 * s, 64 * (s + 1))
            at = 128 * j + 64 * s
            probs = p_ref[6 * g + 2 * j + s]
            dproj[g, 2 * D + at : 2 * D + at + 64] = mm(dot_[sub], probs).astype(bf16)
            dprob = mm(jnp.where(mine, do, jnp.zeros_like(do)), v, ABT)
            p32 = probs.astype(f32)
            delta = jnp.sum(dprob * p32, -1, keepdims=True)
            ds = (p32 * (dprob - delta)).astype(bf16)
            dproj[g, at : at + 64] = (mm(kt[sub], ds, ABT) * 0.125).astype(bf16)
            dproj[g, D + at : D + at + 64] = mm(qt[sub], ds).astype(bf16)


def ends_back(g, dho, kv_ref, q_ref, p_ref, dq, dproj):
    rows = slice(g * TP, (g + 1) * TP)
    ends = slice(g * ENDS, (g + 1) * ENDS)
    q = spread_heads(q_ref[ends])
    do = spread_heads(dho[ends])
    probs = p_ref[g]
    dprob = mm(do, kv_ref[rows, D:], ABT)
    p32 = probs.astype(f32)
    delta = jnp.sum(dprob * p32, -1, keepdims=True)
    ds = (p32 * (dprob - delta)).astype(bf16)
    dq[ends] = (gather_heads(mm(ds, kv_ref[rows, :D])) * 0.125).astype(bf16)
    dproj[g, :D] = mm(q, ds, ATB).astype(bf16)
    dproj[g, D : 2 * D] = mm(do, probs, ATB).astype(bf16)


def backward_kernel(
    dz_ref,
    x_ref,
    mid_ref,
    qkv_ref,
    p_ref,
    ho_ref,
    hid_ref,
    gp_ref,
    x1_ref,
    kv_ref,
    q1_ref,
    p1_ref,
    ho1_ref,
    wa_ref,
    wf_ref,
    tok_ref,
    dzo_ref,
    a0o_ref,
    a0m_ref,
    a1o_ref,
    a1m_ref,
    uo_ref,
    um_ref,
    do_ref,
    dm_ref,
    gv_ref,
    gb_ref,
    gu_ref,
    qkv_w,
    out_w,
    dqkv,
    dkv,
    dq1,
    dout,
    g_ffw,
    g_att,
    nbuf,
    dz,
    dn,
    du,
    dq,
    dproj,
):
    step = pl.program_id(0)
    mp = lax.axis_index("mp")

    def row(layer, i):
        return token_row(tok_ref, layer, i)

    @pl.when(step == 0)
    def _():
        for ref in (gv_ref, gb_ref, gu_ref, g_ffw, dqkv, dkv, dq1, dout):
            ref[...] = jnp.zeros_like(ref)
        for layer in range(LAYERS):
            attn_tiles(wa_ref.at[layer], qkv_w.at[layer], out_w.at[layer])

    def pull(src, gain, dz_out, at):
        xhat, scale = center(src[...])
        dy = dn[...]
        new = dz[...] + norm_back(dy, xhat, scale, gain)
        dz_out[...] = new
        gv_ref[at : at + 1] += jnp.sum(dy * xhat, 0, keepdims=True)
        gv_ref[at + 1 : at + 2] += jnp.sum(dy, 0, keepdims=True)

    ones = jnp.ones((TP, 128), bf16)
    low = dz_ref[...].astype(bf16)
    dout[1] += mm(low, ho1_ref[...], ATB)
    dho = mm(low, out_w[1]).astype(bf16)
    norm_rows(x1_ref, row(1, 0), row(1, 1), nbuf)
    dz[...] = jnp.zeros_like(dz)
    for g in range(GRP):
        rows = slice(g * TP, (g + 1) * TP)
        ends_back(g, dho, kv_ref, q1_ref, p1_ref, dq, dproj)
        dkv[:, :D] += mm(dproj[g, : 2 * D], nbuf[rows])
        dkv[:, D:] += mm(dproj[g, : 2 * D], ones)
        dn[rows] = jnp.transpose(mm(qkv_w[1, :, D:], dproj[g, : 2 * D]), (1, 0))
    dq_all = dq[...]
    ends = jnp.concatenate([nbuf[(g + 1) * TP - ENDS : (g + 1) * TP] for g in range(GRP)], 0)
    dq1[...] += mm(ends, dq_all, ATB)
    gb_ref[1:2, :D] += jnp.sum(dq_all.astype(f32), 0, keepdims=True)
    more = mm(dq_all, qkv_w[1, :, :D], ABT)
    for g in range(GRP):
        last = slice((g + 1) * TP - ENDS, (g + 1) * TP)
        part = slice(g * ENDS, (g + 1) * ENDS)
        dn[last] += more[part]
        dz[last] = dz_ref[part]
    pull(x1_ref, row(1, 0), dz, 6)

    norm_rows(mid_ref, row(0, 2), row(0, 3), nbuf)
    gv_ref[5:6] += jnp.sum(dz[...], 0, keepdims=True)
    rz = dz[...].astype(bf16)
    rzt = jnp.transpose(rz, (1, 0))
    nt = jnp.transpose(nbuf[...], (1, 0))
    for m in range(2):
        cols = slice(HALF * m, HALF * (m + 1))
        dh = mm(rz, wf_ref[1, m])
        du[...] = (dh.astype(bf16).astype(f32) * gp_ref[:, cols].astype(f32)).astype(bf16)
        gu_ref[0:1, cols] += jnp.sum(du[...].astype(f32), 0, keepdims=True)
        g_ffw[1, m] += mm(rzt, hid_ref[:, cols])
        g_ffw[0, m] += mm(nt, du[...])
        part = mm(du[...], wf_ref[0, m], ABT)
        dn[...] = part if m == 0 else dn[...] + part
    pull(mid_ref, row(0, 2), dz, 2)
    gv_ref[4:5] += jnp.sum(dz[...], 0, keepdims=True)
    rz2 = dz[...].astype(bf16)
    dout[0] += mm(jnp.transpose(rz2, (1, 0)), ho_ref[...])
    dho = mm(rz2, out_w[0]).astype(bf16)
    norm_rows(x_ref, row(0, 0), row(0, 1), nbuf)
    for g in range(GRP):
        rows = slice(g * TP, (g + 1) * TP)
        attend_back(g, dho, qkv_ref, p_ref, dproj)
        dqkv[:, :D] += mm(dproj[g], nbuf[rows])
        dqkv[:, D:] += mm(dproj[g], ones)
        dn[rows] = jnp.transpose(mm(qkv_w[0], dproj[g]), (1, 0))
    pull(x_ref, row(0, 0), dzo_ref, 0)

    @pl.when(step == pl.num_programs(0) - 1)
    def _():
        for layer in range(LAYERS):
            for t in range(4):
                for j in range(3):
                    at = D * t + 128 * j
                    if t == 3:
                        tile = dout[layer, :, 128 * j : 128 * (j + 1)]
                    elif layer == 0:
                        tile = jnp.transpose(dqkv[at : at + 128, :D], (1, 0))
                    elif t == 0:
                        tile = dq1[:, 128 * j : 128 * (j + 1)]
                    else:
                        tile = jnp.transpose(dkv[at - D : at - D + 128, :D], (1, 0))
                    if j < 2:
                        g_att[layer, j, :, 128 * t : 128 * (t + 1)] = tile
                    else:
                        for m in range(2):
                            lo = 512 + 64 * t
                            g_att[layer, m, :, lo : lo + 64] = tile[:, 64 * m : 64 * (m + 1)]
        share(g_att.at[0], a0o_ref, a0m_ref, mp)
        share(g_att.at[1], a1o_ref, a1m_ref, mp)
        share(g_ffw.at[0], uo_ref, um_ref, mp)
        share(g_ffw.at[1], do_ref, dm_ref, mp)
        sums = jnp.transpose(dqkv[:, D:], (1, 0))[0:1]
        gb_ref[0:1, :D] = sums[:, :D]
        gb_ref[0:1, D:] = sums[:, 2 * D :]
        gb_ref[1:2, D:] = jnp.transpose(dkv[:, D:], (1, 0))[0:1, D:]


def attn_tiles(w_ref, qkv_w, out_w):
    for t in range(4):
        cols = 128 * t
        pieces = [w_ref[0, :, cols : cols + 128], w_ref[1, :, cols : cols + 128]]
        tile = 512 + 128 * (t // 2)
        lane = 64 * (t % 2)
        pieces.append(
            jnp.concatenate(
                [w_ref[m, :, tile : tile + 128][:, lane : lane + 64] for m in range(2)], 1
            )
        )
        for j in range(3):
            if t < 3:
                at = D * t + 128 * j
                qkv_w[:, at : at + 128] = pieces[j]
            else:
                out_w[:, 128 * j : 128 * (j + 1)] = pieces[j]


def backward(dz, kept, weights, tok):
    steps = dz.shape[0] // (GRP * ENDS)
    x_shape = kept[0].shape
    shares = pair_shapes([(D, 768)] * 4)
    extra = [jax.ShapeDtypeStruct(s, f32) for s in ((8, D), (2, 2 * D), (1, FF))]
    return pl.pallas_call(
        backward_kernel,
        grid=(steps,),
        in_specs=[block_of(a.shape, steps) for a in (dz,) + tuple(kept)]
        + [
            pl.BlockSpec((2, 2, D, 768), lambda i: (0, 0, 0, 0), pipeline_mode=pl.Buffered(1)),
            pl.BlockSpec((2, 2, D, 768), lambda i: (1, 0, 0, 0), pipeline_mode=pl.Buffered(1)),
            full_spec(tok.shape),
        ],
        out_specs=[block_of(x_shape, steps)] + [full_spec(x.shape) for x in shares + extra],
        out_shape=[jax.ShapeDtypeStruct(x_shape, f32)] + shares + extra,
        scratch_shapes=[
            pltpu.VMEM((LAYERS, D, 3 * D), bf16),
            pltpu.VMEM((LAYERS, D, D), bf16),
            pltpu.VMEM((3 * D, 512), f32),
            pltpu.VMEM((2 * D, 512), f32),
            pltpu.VMEM((D, D), f32),
            pltpu.VMEM((LAYERS, D, D), f32),
            pltpu.VMEM((2, 2, D, 768), f32),
            pltpu.VMEM((LAYERS, 2, D, 768), f32),
            pltpu.VMEM((ROWS, D), bf16),
            pltpu.VMEM((ROWS, D), f32),
            pltpu.VMEM((ROWS, D), f32),
            pltpu.VMEM((ROWS, HALF), bf16),
            pltpu.VMEM((GRP * ENDS, D), bf16),
            pltpu.VMEM((GRP, 3 * D, TP), bf16),
        ],
        compiler_params=pltpu.CompilerParams(vmem_limit_bytes=62 * MIB),
        name="backward_layers",
    )(dz, *kept, weights, weights, tok)


def patch_grad_kernel(
    partner_ref,
    mix_ref,
    dz_ref,
    own_ref,
    far_ref,
    gvb_ref,
    gvh_ref,
    po_ref,
    pm_ref,
    eo_ref,
    em_ref,
    dzo,
    dzf,
    tok,
    g_patch,
    g_seg,
):
    mp = lax.axis_index("mp")
    count = far_ref.shape[0] // PATCHES
    both = own_ref.shape[0] // PATCHES
    dzo[...] = jnp.zeros_like(dzo)
    total = jnp.zeros((TP, D), f32)
    for k in range(count):
        place = partner_place(partner_ref, k)
        w = mix_ref[place]
        for j in range(3):
            part = dz_ref[k * TP : k * TP + PATCHES, 128 * j : 128 * (j + 1)]
            dzo[j, pl.ds(place, PATCHES, stride=both), :] = w * part
            dzf[j, pl.ds(k, PATCHES, stride=count), :] = (1.0 - w) * part
        total = total + dz_ref[k * TP : (k + 1) * TP]
    tok[...] = jnp.zeros_like(tok)
    tok[:TP] = total
    tok[TP : TP + 8] = gvb_ref[...]
    tok[TP + 8 : TP + 14] = gvh_ref[2:8]
    turned = jnp.transpose(tok[...], (1, 0))
    for m in range(2):
        g_seg[m] = turned[:, 128 * m : 128 * (m + 1)]
    for j in range(3):
        lo = jnp.transpose(dzo[j].astype(bf16), (1, 0))
        lf = jnp.transpose(dzf[j].astype(bf16), (1, 0))
        for m in range(2):
            cols = slice(D * m, D * (m + 1))
            g_patch[m, 128 * j : 128 * (j + 1)] = mm(lo, own_ref[:, cols]) + mm(lf, far_ref[:, cols])
    share(g_patch, po_ref, pm_ref, mp)
    share(g_seg, eo_ref, em_ref, mp)


def patch_grad(partner, mix, dz, own, far, gvb, gvh):
    outs = pair_shapes([(D, D), (D, 128)])
    return pl.pallas_call(
        patch_grad_kernel,
        grid=(1,),
        in_specs=[pl.BlockSpec(memory_space=pltpu.SMEM)] * 2
        + [full_spec(a.shape) for a in (dz, own, far, gvb, gvh)],
        out_specs=[full_spec(x.shape) for x in outs],
        out_shape=outs,
        scratch_shapes=[
            pltpu.VMEM((3, own.shape[0], 128), f32),
            pltpu.VMEM((3, far.shape[0], 128), f32),
            pltpu.VMEM((256, D), f32),
            pltpu.VMEM((2, D, D), f32),
            pltpu.VMEM((2, D, 128), f32),
        ],
        compiler_params=pltpu.CompilerParams(vmem_limit_bytes=56 * MIB),
        name="patch_gradient",
    )(partner, mix, dz, own, far, gvb, gvh)


def link_orders(bits):
    far = [b for b in (range(1, bits, 2) if bits == 6 else [3]) if b < bits]
    near = [b for b in range(bits) if b not in far]
    return [near[i:] + near[:i] for i in range(len(near))], far


def gather_plan(bits, turns):
    near, far = link_orders(bits)
    deep = far + [near[0][-1]]
    flat = near[0][:-1]
    return [flat[t:] + flat[:t] for t in turns], deep


def chunk_plan(bits, cuts):
    near, far = link_orders(bits)
    return [
        (cuts[i], cuts[i + 1] - cuts[i], near[i % len(near)], far) for i in range(len(cuts) - 1)
    ]


def mesh_place():
    return lax.axis_index("dp"), lax.axis_index("mp")


def bit_of(value, bit):
    return (value // 2**bit) % 2


def flipped(value, bit):
    return value + 2**bit * (1 - 2 * bit_of(value, bit))


def meet(bits):
    dp, mp = mesh_place()
    barrier = pltpu.get_barrier_semaphore()
    for peer in [(dp, 1 - mp)] + [(flipped(dp, b), mp) for b in range(bits)]:
        pl.semaphore_signal(barrier, inc=1, device_id=peer, device_id_type=MESH)
    pl.semaphore_wait(barrier, bits + 1)


def push(src, dst, send, recv, peer):
    copy = pltpu.make_async_remote_copy(
        src_ref=src, dst_ref=dst, send_sem=send, recv_sem=recv, device_id=peer, device_id_type=MESH
    )
    copy.start()
    return copy


def held_part(ref, bits, lead, dp, done=(), flip=None):
    idx = list(lead)
    for b in reversed(bits):
        mine = bit_of(dp, b)
        idx.append(pl.ds(0, 2) if b in done else (1 - mine if b == flip else mine))
    return ref.at[tuple(idx)]


def gather_front_kernel(bits, tab_ref, main_ref, sb_ref, *refs):
    w_refs = refs[:2]
    far_refs = refs[2:4]
    sbo_ref, tabr, stage_p, stage_e, stage_h, s_loc, s_tab = refs[4:11]
    s_send, s_recv, f_send, f_recv, m_send, m_recv = refs[11:]
    dp, mp = mesh_place()
    mate = (dp, 1 - mp)
    turns, deep = gather_plan(bits, FRONT_TURNS)
    every = list(range(bits))

    far = deep[:-1]
    wide = {}

    def part(c, *args):
        return held_part(w_refs[c], every, (mp,), dp, *args)

    def main(c, *args):
        return held_part(far_refs[c], far, (), dp, *args)

    meet(bits)
    c_tab = push(tab_ref.at[1 - mp], tabr, s_tab.at[0], s_tab.at[1], mate)
    c_sb = push(sb_ref, sbo_ref.at[mp], s_tab.at[2], s_tab.at[3], mate)
    local = [pltpu.make_async_copy(sb_ref, sbo_ref.at[mp], s_loc.at[0])]
    local[0].start()
    c_tab.wait()
    mine = tab_ref[mp].astype(f32)
    other = tabr[...].astype(f32)
    first = jnp.where(mp == 0, mine, other)
    second = jnp.where(mp == 0, other, mine)
    table = jnp.concatenate([first, second], 0).astype(bf16)
    stage_p[...] = table[:, :D]
    stage_e[...] = table[:, D:F_COLS]
    stage_h[...] = table[:, F_COLS:]
    stages = (stage_p, stage_e)
    wides = (main_ref, stage_h)
    copies = {}
    forwards = []
    for s in range(bits + 1):
        for c in range(2):
            order = deep + turns[c]
            if s:
                copies[c, s - 1].wait_recv()
            if s < bits:
                held = part(c, order[:s])
                copies[c, s] = push(
                    held if s else stages[c],
                    held,
                    s_send.at[c, s],
                    s_recv.at[c, s],
                    (flipped(dp, order[s]), mp),
                )
            got = part(c, order[: s - 1], order[s - 1]) if s else part(c)
            forwards.append(
                push(got if s else stages[c], got, f_send.at[c, s], f_recv.at[c, s], mate)
            )
        if s == 0:
            for c in range(2):
                local.append(pltpu.make_async_copy(stages[c], part(c), s_loc.at[c + 1]))
                local[-1].start()
                local.append(pltpu.make_async_copy(wides[c], main(c), s_loc.at[c + 3]))
                local[-1].start()
            for copy in local:
                copy.wait()
        at = s - len(deep) + 1
        if 0 <= at < len(far):
            for c in range(2):
                if at:
                    wide[c, at - 1].wait_recv()
                dst = main(c, far[:at])
                wide[c, at] = push(
                    dst if at else wides[c],
                    dst,
                    m_send.at[c, at],
                    m_recv.at[c, at],
                    (flipped(dp, far[at]), mp),
                )
    for copy in forwards:
        copy.wait()
    for copy in copies.values():
        copy.wait_send()
    for copy in wide.values():
        copy.wait_send()
    for c in range(2):
        wide[c, len(far) - 1].wait_recv()
    c_sb.wait()


def gather_front(tab, shard, sb, n_data):
    bits = n_data.bit_length() - 1
    rows = D // n_data
    _, far = link_orders(bits)
    deep_shape = (2,) * len(far)
    sems = pltpu.SemaphoreType.DMA
    anywhere = pl.BlockSpec(memory_space=pl.ANY)
    inside = pl.BlockSpec(memory_space=pltpu.VMEM)
    return pl.pallas_call(
        functools.partial(gather_front_kernel, bits),
        in_specs=[inside] * 3,
        out_specs=[anywhere] * 4 + [inside],
        out_shape=[
            jax.ShapeDtypeStruct((2,) * (bits + 1) + (rows, w), bf16) for w in FRONT_WIDTHS
        ]
        + [
            jax.ShapeDtypeStruct(deep_shape + shard.shape, bf16),
            jax.ShapeDtypeStruct(deep_shape + (rows, T_COLS - F_COLS), bf16),
            jax.ShapeDtypeStruct((2,) + sb.shape, f32),
        ],
        scratch_shapes=[
            pltpu.VMEM(tab.shape[1:], bf16),
            pltpu.VMEM((rows, FRONT_WIDTHS[0]), bf16),
            pltpu.VMEM((rows, FRONT_WIDTHS[1]), bf16),
            pltpu.VMEM((rows, T_COLS - F_COLS), bf16),
            sems((5,)),
            sems((4,)),
            sems((2, bits)),
            sems((2, bits)),
            sems((2, bits + 1)),
            sems((2, bits + 1)),
            sems((2, len(far))),
            sems((2, len(far))),
        ],
        compiler_params=pltpu.CompilerParams(
            collective_id=2, has_side_effects=True, vmem_limit_bytes=60 * MIB
        ),
        name="gather_front",
    )(tab, shard, sb)


def gather_main_kernel(bits, *refs):
    turns, deep = gather_plan(bits, MAIN_TURNS)
    far, last = deep[:-1], deep[-1]
    mains, heads, pix_ref = refs[:2], refs[2:4], refs[4]
    w_ref, h_ref, mine_ref = refs[5:8]
    pix, s_pix, s_loc, s_send, s_recv, f_send, f_recv = refs[8:]
    dp, mp = mesh_place()
    mate = (dp, 1 - mp)
    every = list(range(bits))
    steps = bits - len(deep)
    chunks = len(MAIN_WIDTHS)

    def lead(c):
        return (w_ref, (c, mp)) if c < chunks - 1 else (h_ref, (mp,))

    def part(c, *args):
        return held_part(lead(c)[0], every, lead(c)[1], dp, *args)

    meet(bits)
    pix_in = pltpu.make_async_copy(pix_ref.at[:, mp], pix, s_pix.at[0])
    pix_in.start()
    copies = {}
    forwards = []
    local = []
    for c in range(chunks):
        for i, dst in enumerate((part(c, far), part(c, far, last))):
            lead_cut = (slice(None),) * len(far) + (c,)
            src = mains[i].at[lead_cut] if c < chunks - 1 else heads[i]
            local.append(pltpu.make_async_copy(src, dst, s_loc.at[c, i]))
            local[-1].start()
    pix_in.wait()
    pix_out = pltpu.make_async_copy(pix, mine_ref, s_pix.at[1])
    pix_out.start()
    for s in range(steps + 1):
        for c in range(chunks):
            order = turns[c]
            if s:
                copies[c, s - 1].wait_recv()
            else:
                for copy in local[2 * c : 2 * c + 2]:
                    copy.wait()
            done = deep + order[:s]
            if s < steps:
                held = part(c, done)
                copies[c, s] = push(
                    held, held, s_send.at[c, s], s_recv.at[c, s], (flipped(dp, order[s]), mp)
                )
            got = part(c, done[:-1], done[-1]) if s else part(c, done)
            forwards.append(push(got, got, f_send.at[c, s], f_recv.at[c, s], mate))
    for copy in forwards:
        copy.wait()
    for copy in copies.values():
        copy.wait_send()
    pix_out.wait()


def gather_main(mains, heads, pix, n_data):
    bits = n_data.bit_length() - 1
    rows = D // n_data
    near, _ = link_orders(bits)
    steps = len(near[0]) - 1
    chunks = len(MAIN_WIDTHS)
    sems = pltpu.SemaphoreType.DMA
    anywhere = pl.BlockSpec(memory_space=pl.ANY)
    inside = pl.BlockSpec(memory_space=pltpu.VMEM)
    places = (2,) * (bits + 1) + (rows,)
    mine = pix.shape[:1] + pix.shape[2:]
    main, head_w, pix_mine = pl.pallas_call(
        functools.partial(gather_main_kernel, bits),
        in_specs=[inside] * (2 * len(mains)) + [anywhere],
        out_specs=[anywhere] * 3,
        out_shape=[
            jax.ShapeDtypeStruct((chunks - 1,) + places + (768,), bf16),
            jax.ShapeDtypeStruct(places + (1024,), bf16),
            jax.ShapeDtypeStruct(mine, bf16),
        ],
        scratch_shapes=[
            pltpu.VMEM(mine, bf16),
            sems((2,)),
            sems((chunks, len(mains))),
            sems((chunks, steps)),
            sems((chunks, steps)),
            sems((chunks, steps + 1)),
            sems((chunks, steps + 1)),
        ],
        compiler_params=pltpu.CompilerParams(
            collective_id=0, has_side_effects=True, vmem_limit_bytes=60 * MIB
        ),
        cost_estimate=pl.CostEstimate(flops=0, bytes_accessed=150 * MIB, transcendentals=0),
        name="gather_main",
    )(*mains, *heads, pix)
    return main.reshape(chunks - 1, 2, D, 768), head_w.reshape(2, D, 1024), pix_mine


def reduce_plan(bits, turns):
    near, far = link_orders(bits)
    return [near[t % len(near)] + far for t in turns]


def block_index(free, fixed):
    def index(t):
        total = fixed
        for j, b in enumerate(free):
            total = total + ((t // 2**j) % 2) * 2**b
        return total

    return index


def reduce_kernel(bits, widths, turns, *refs):
    n = len(widths)
    own, mate_src = refs[:n], refs[n : 2 * n]
    smalls = refs[2 * n : 2 * n + 5]
    outs = refs[2 * n + 5 : 3 * n + 5]
    obun_ref, info_ref = refs[3 * n + 5 : 3 * n + 7]
    refs = refs[3 * n + 7 :]
    mrecv, acc, held = refs[:n], refs[n : 2 * n], refs[2 * n : 3 * n]
    refs = refs[3 * n :]
    sbufs, rbufs = refs[: n * bits], refs[n * bits : 2 * n * bits]
    bun, bunr, tsend, sq, sqr, o_sem, m_sem, s_sem, r_sem, b_sem, q_sem, t_sem = refs[2 * n * bits :]
    dp, mp = mesh_place()
    mate = (dp, 1 - mp)
    orders = reduce_plan(bits, turns)
    rows = D // 2**bits
    group = max(rows, 48)
    per = group // rows
    small = rows // 2

    loads = {}
    for c in REDUCE_ORDER:
        loads[c] = pltpu.make_async_copy(own[c], held[c], o_sem.at[c])
        loads[c].start()
    at = 0
    for ref in smalls:
        for i in range(ref.shape[0]):
            bun[:, at : at + ref.shape[1]] = ref[i : i + 1]
            at += ref.shape[1]
    meet(bits)
    mcopies = {
        c: push(mate_src[c], mrecv[c], m_sem.at[c, 0], m_sem.at[c, 1], mate) for c in REDUCE_ORDER
    }
    bcopies = [push(bun, bunr.at[0], b_sem.at[0, 0], b_sem.at[0, 1], mate)]

    def loop(total, body):
        def step(t, carry):
            body(t)
            return carry

        lax.fori_loop(0, total, step, 0)

    copies = {}

    def split(order, s, sent):
        free = [b for b in range(bits) if b not in order[: s + 1]]
        fixed = sum((bit_of(dp, b) * 2**b for b in order[:s]), 0)
        last = bit_of(dp, order[s])
        fixed = fixed + (1 - last if sent else last) * 2 ** order[s]
        return 2 ** len(free), block_index(free, fixed)

    def send_stage(c, s):
        total, index = split(orders[c], s, True)
        sbuf = sbufs[c * bits + s]

        def body(t):
            sbuf[t] = acc[c][index(t)].astype(bf16)

        loop(total, body)
        copies[c, s] = push(
            sbuf,
            rbufs[c * bits + s],
            s_sem.at[c, s],
            r_sem.at[c, s],
            (flipped(dp, orders[c][s]), mp),
        )

    def take_stage(c, s):
        copies[c, s].wait_recv()
        total, index = split(orders[c], s, False)
        rbuf = rbufs[c * bits + s]

        def body(t):
            acc[c][index(t)] += rbuf[t].astype(f32)

        loop(total, body)

    for c in REDUCE_ORDER:
        loads[c].wait()
        mcopies[c].wait_recv()

        def body(b):
            rs = pl.ds(pl.multiple_of(b * group, group), group)
            got = held[c][rs] + mrecv[c][rs].astype(f32)
            for i in range(per):
                acc[c][b * per + i] = got[rows * i : rows * (i + 1)]

        loop(D // group, body)
        send_stage(c, 0)
    for s in range(1, bits + 1):
        for c in REDUCE_ORDER:
            take_stage(c, s - 1)
            if s < bits:
                send_stage(c, s)
        bcopies[-1].wait()
        bun[...] = bun[...] + bunr[s - 1]
        bcopies.append(
            push(bun, bunr.at[s], b_sem.at[s, 0], b_sem.at[s, 1], (flipped(dp, s - 1), mp))
        )
    tails = []
    for c in range(n):
        mine = acc[c][dp]
        if c in TABLE_CHUNKS:
            k = TABLE_CHUNKS.index(c)
            send, recv = tsend[2 * k], tsend[2 * k + 1]
            send[...] = jnp.where(mp == 0, mine[small:], mine[:small])
            outs[c][mp] = jnp.where(mp == 0, mine[:small], mine[small:])
            tails.append((c, recv, push(send, recv, t_sem.at[k, 0], t_sem.at[k, 1], mate)))
        else:
            outs[c][...] = mine
    total = jnp.zeros((1, 1), f32)
    for c in range(n):
        if c not in TABLE_CHUNKS:
            total = total + jnp.sum(outs[c][...] * outs[c][...], keepdims=True)
    for c, recv, copy in tails:
        copy.wait()
        outs[c][1 - mp] = recv[...]
        for m in range(2):
            total = total + jnp.sum(outs[c][m] * outs[c][m], keepdims=True)
    sq[0] = jnp.broadcast_to(total, (8, 128))
    bcopies[-1].wait()
    final = bun[...] + bunr[bits]
    obun_ref[...] = final
    shared = jnp.sum(final[:, 128:] * final[:, 128:], keepdims=True)
    for s in range(bits + 1):
        peer = mate if s == 0 else (flipped(dp, s - 1), mp)
        copy = push(sq.at[s], sqr.at[s], q_sem.at[s, 0], q_sem.at[s, 1], peer)
        copy.wait()
        sq[s + 1] = sq[s] + sqr[s]
    squares = sq[bits + 1] + shared
    loss, weight = final[:, 0:1], final[:, 1:2]
    norm = jnp.sqrt(squares) / weight
    factor = jnp.minimum(1.0, clip_limit / norm) / weight
    which = lax.broadcasted_iota(jnp.int32, (8, 128), 1)
    info = jnp.where(which == 0, loss, jnp.where(which == 1, weight, norm))
    info_ref[...] = jnp.where(which == 3, factor, info)
    for copy in mcopies.values():
        copy.wait_send()
    for copy in copies.values():
        copy.wait_send()


def reduce_all(own, mates, smalls, turns, n_data):
    bits = n_data.bit_length() - 1
    rows = D // n_data
    widths = [x.shape[1] for x in own]
    n = len(widths)
    sems = pltpu.SemaphoreType.DMA
    inside = pl.BlockSpec(memory_space=pltpu.VMEM)
    anywhere = pl.BlockSpec(memory_space=pl.ANY)
    bufs = [
        pltpu.VMEM((2 ** (bits - 1 - s), rows, w), bf16) for w in widths for s in range(bits)
    ]
    length = sum(x.shape[0] * x.shape[1] for x in smalls)
    outs = [
        jax.ShapeDtypeStruct((2, rows // 2, w) if c in TABLE_CHUNKS else (rows, w), f32)
        for c, w in enumerate(widths)
    ]
    tails = [
        pltpu.VMEM((rows // 2, widths[c]), f32) for c in TABLE_CHUNKS for _ in range(2)
    ]

    def kernel(*refs):
        cut = len(refs) - 11 - len(tails)
        head, rest = refs[:cut], refs[cut:]
        tsend, rest = rest[: len(tails)], rest[len(tails) :]
        reduce_kernel(bits, widths, turns, *head, rest[0], rest[1], tsend, *rest[2:])

    return pl.pallas_call(
        kernel,
        in_specs=[anywhere] * (2 * n) + [inside] * len(smalls),
        out_specs=[inside] * (n + 2),
        out_shape=outs
        + [
            jax.ShapeDtypeStruct((1, length), f32),
            jax.ShapeDtypeStruct((8, 128), f32),
        ],
        scratch_shapes=[pltpu.VMEM((D, w), bf16) for w in widths]
        + [pltpu.VMEM((n_data, rows, w), f32) for w in widths]
        + [pltpu.VMEM((D, w), f32) for w in widths]
        + bufs
        + bufs
        + tails
        + [
            pltpu.VMEM((1, length), f32),
            pltpu.VMEM((bits + 1, 1, length), f32),
            pltpu.VMEM((bits + 2, 8, 128), f32),
            pltpu.VMEM((bits + 1, 8, 128), f32),
            sems((n,)),
            sems((n, 2)),
            sems((n, bits)),
            sems((n, bits)),
            sems((bits + 1, 2)),
            sems((bits + 1, 2)),
            sems((len(TABLE_CHUNKS), 2)),
        ],
        compiler_params=pltpu.CompilerParams(
            collective_id=1, has_side_effects=True, vmem_limit_bytes=62 * MIB
        ),
        name="reduce_gradients",
    )(*own, *mates, *smalls)


def adamw(master, first, second, gradient, rate, decay):
    first = beta_one * first + (1.0 - beta_one) * gradient
    second = beta_two * second + (1.0 - beta_two) * gradient * gradient
    first_hat = first / (1.0 - beta_one**STEP)
    second_hat = second / (1.0 - beta_two**STEP)
    master = master - rate * (first_hat / (jnp.sqrt(second_hat) + adam_eps) + decay * master)
    return (master, first, second)


def local_split(flat, layer):
    mp = lax.axis_index("mp")
    rows = []
    for m in range(2):
        pieces = []
        for h in range(3):
            at = 128 + 2 * D * layer + (128 * m + HD * h if h < 2 else 256 + HD * m)
            pieces += [flat[:, at : at + HD], flat[:, at + D : at + D + HD]]
        at = 128 + 2 * D * LAYERS + FF * layer + HALF * m
        rows.append(jnp.concatenate(pieces + [flat[:, at : at + HALF]], 1))
    return jnp.where(mp == 0, rows[0], rows[1])


def update_kernel(info_ref, *refs):
    g = refs[:9]
    flat_ref = refs[9]
    params = refs[10:25]
    outs = refs[25:]
    factor = info_ref[0, 3]

    def write(grad, item, rate, decay, at, outs, low):
        new, one, two = adamw(
            item[0][at], item[1][at], item[2][at], grad * factor, rate, decay
        )
        outs[0][at], outs[1][at], outs[2][at] = new, one, two
        if low:
            outs[3][at] = new.astype(bf16)

    everything = (slice(None), slice(None))
    heads = [
        jnp.concatenate([g[6][m, :, 512 * h : 512 * (h + 1)] for m in range(2)], 1)[:, :CLS]
        for h in range(2)
    ]
    token = jnp.concatenate([g[8][0], g[8][1]], 1)
    table = jnp.concatenate(
        [g[7][0], g[7][1], token[:, PATCHES:TOK], token[:, :PATCHES]] + heads, 1
    )
    write(table, params[0:3], matrix_rate, matrix_decay, everything, outs[0:4], True)
    vec = jnp.transpose(token, (1, 0))[TP : TP + 6 * LAYERS + 2]
    write(vec, params[3:6], vector_rate, 0.0, everything, outs[4:7], False)
    for layer in range(LAYERS):
        packed = g[layer][...]
        pieces = []
        for h in range(3):
            for t in range(4):
                lo = 128 * t + HD * h if h < 2 else 512 + HD * t
                pieces.append(packed[:, lo : lo + HD])
        grad = jnp.concatenate(pieces, 1)
        write(grad, params[6:9], matrix_rate, matrix_decay, layer, outs[7:11], True)
        for half in range(2):
            write(
                g[LAYERS + 2 * layer + half][...],
                params[9:12],
                matrix_rate,
                matrix_decay,
                (layer, slice(None), half),
                outs[11:15],
                True,
            )
    flat = flat_ref[...]
    for layer in range(LAYERS):
        grad = local_split(flat, layer)
        write(grad, params[12:15], vector_rate, 0.0, slice(layer, layer + 1), outs[15:18], False)


def update(info, grads, split, params):
    outs = []
    for i in range(5):
        low = i in (0, 2, 3)
        shape = params[3 * i].shape
        outs += [jax.ShapeDtypeStruct(shape, f32)] * 3
        outs += [jax.ShapeDtypeStruct(shape, bf16)] if low else []
    ins = list(grads) + [split] + list(params)
    return pl.pallas_call(
        update_kernel,
        grid=(1,),
        in_specs=[pl.BlockSpec(memory_space=pltpu.SMEM)] + [full_spec(x.shape) for x in ins],
        out_specs=[full_spec(x.shape) for x in outs],
        out_shape=outs,
        compiler_params=pltpu.CompilerParams(vmem_limit_bytes=60 * MIB),
        name="update_weights",
    )(info, *ins)


def pack_kernel(t_ref, v_ref, a_ref, f_ref, tab_ref, main_ref):
    small = t_ref.shape[0]
    table = t_ref[...]

    def zeros(n):
        return jnp.zeros((small, n), f32)

    turned = jnp.transpose(v_ref[...], (1, 0))
    low = PD + 2
    seg = jnp.concatenate(
        [
            table[:, low : low + PATCHES],
            table[:, PD:low],
            zeros(TP - TOK),
            turned,
            zeros(256 - TP - turned.shape[1]),
        ],
        1,
    )
    heads = [
        jnp.concatenate(
            [table[:, PD + TOK + CLS * h : PD + TOK + CLS * (h + 1)], zeros(1024 - CLS)], 1
        )
        for h in range(2)
    ]
    parts = [table[:, :PD], seg] + heads
    for m in range(2):
        at = 0
        for x in parts:
            half = x.shape[1] // 2
            tab_ref[m, :, at : at + half] = x[:, half * m : half * (m + 1)].astype(bf16)
            at += half
    for layer in range(LAYERS):
        a = a_ref[layer]
        for t in range(4):
            pair = jnp.concatenate(
                [a[:, 256 * h + HD * t : 256 * h + HD * (t + 1)] for h in range(2)], 1
            )
            main_ref[layer, :, 128 * t : 128 * (t + 1)] = pair.astype(bf16)
        main_ref[layer, :, 512:] = a[:, 512:].astype(bf16)
        for half in range(2):
            main_ref[LAYERS + 2 * layer + half] = f_ref[layer, :, half].astype(bf16)


def pack(tab, vec, attn, ffw):
    layers, rows, _ = attn.shape
    ins = [tab, vec, attn, ffw]
    shapes = [(2, tab.shape[0], T_COLS), (3 * layers, rows, HALF)]
    return pl.pallas_call(
        pack_kernel,
        grid=(1,),
        in_specs=[full_spec(x.shape) for x in ins],
        out_specs=[full_spec(x) for x in shapes],
        out_shape=[jax.ShapeDtypeStruct(x, bf16) for x in shapes],
        compiler_params=pltpu.CompilerParams(vmem_limit_bytes=60 * MIB),
        name="pack_shards",
    )(*ins)


def shards(
    pixels,
    labels,
    teacher,
    partner,
    mix_weight,
    class_weight,
    tables,
    tables_first,
    tables_second,
    vectors,
    vectors_first,
    vectors_second,
    attention,
    attention_first,
    attention_second,
    feedforward,
    feedforward_first,
    feedforward_second,
    split_bias,
    split_bias_first,
    split_bias_second,
    head_bias,
    head_bias_first,
    head_bias_second,
):
    n_data = lax.axis_size("dp")
    dp, mp = mesh_place()
    images_here = pixels.shape[0]
    count = images_here // 2
    rows = D // n_data
    far_pairs = [(i, (i + n_data // 2) % n_data) for i in range(n_data)]
    pix = pixels.transpose(1, 0, 2)
    tab, shard = pack(tables.T, vectors, attention, feedforward)
    deep = gather_plan(n_data.bit_length() - 1, MAIN_TURNS)[1]
    front, seg, *heights, sb = gather_front(tab, shard, split_bias, n_data)
    front = front.reshape(2, D, FRONT_WIDTHS[0])
    seg = seg.reshape(2, D, FRONT_WIDTHS[1])
    near_pairs = [(i, i ^ (1 << deep[-1])) for i in range(n_data)]
    mains, heads = ([x, lax.ppermute(x, "dp", near_pairs)] for x in heights)
    pix_halves = pix.reshape(PATCHES, 2, count, PD)
    send = embed_send(pix_halves, front)
    mains, heads, send = lax.optimization_barrier((mains, heads, send))
    far = lax.ppermute(send, "dp", far_pairs)
    weights, w_heads, pix_mine = gather_main(mains, heads, pix_halves, n_data)
    hb = jnp.pad(
        head_bias.astype(bf16).astype(f32).reshape(2, CLS),
        ((0, 0), (0, 1024 - CLS)),
        constant_values=-1e30,
    ).reshape(1, -1)
    cw = jnp.pad(class_weight, (0, 1024 - CLS)).reshape(1, -1)
    front, hb, cw, weights = lax.optimization_barrier((front, hb, cw, weights))
    own = embed_own(partner, pix, front)
    pix_mine, far, own = lax.optimization_barrier((pix_mine, far, own))
    pix_far = lax.ppermute(pix_mine, "dp", far_pairs)
    *kept, mid, tok = forward(
        partner, mix_weight, own, far, seg, weights, sb
    )
    u1o, u1m, d1o, d1m, ho, hm, dz, gvh, gu1, dhb, stat = head(
        partner, mix_weight, labels, teacher, mid, weights, w_heads, sb, hb, cw, tok
    )
    dz0, a0o, a0m, a1o, a1m, u0o, u0m, d0o, d0m, gvb, gb, gu0 = backward(dz, kept, weights, tok)
    po, pm, eo, em = patch_grad(
        partner,
        mix_weight,
        dz0,
        pix.reshape(PATCHES * images_here, PD),
        pix_far.reshape(PATCHES * count, PD),
        gvb,
        gvh,
    )
    own_parts = [a0o, a1o, u0o, d0o, u1o, d1o, ho, po, eo]
    mate_parts = [a0m, a1m, u0m, d0m, u1m, d1m, hm, pm, em]
    *g, flat, info = reduce_all(
        own_parts, mate_parts, [stat, gb, gu0, gu1, dhb], REDUCE_TURNS, n_data
    )
    loss_sum, weight_sum, grad_norm, factor = (info[0, i] for i in range(4))
    at = 128 + 2 * D * LAYERS + FF * LAYERS
    g_head = flat[0, at : at + 2048].reshape(2, 1024)[:, :CLS].reshape(-1)
    fresh = update(
        info,
        g,
        flat,
        [
            tables.T,
            tables_first.T,
            tables_second.T,
            vectors,
            vectors_first,
            vectors_second,
            attention,
            attention_first,
            attention_second,
            feedforward,
            feedforward_first,
            feedforward_second,
            split_bias,
            split_bias_first,
            split_bias_second,
        ],
    )
    fresh = [x.T for x in fresh[:4]] + list(fresh[4:])
    h_new, h_one, h_two = adamw(
        head_bias, head_bias_first, head_bias_second, g_head * factor, vector_rate, 0.0
    )
    return (loss_sum, weight_sum, grad_norm, *fresh, h_new, h_one, h_two)


def solution(mesh):
    table = P(None, ("dp", "mp"))
    attn = P(None, "dp", "mp")
    ffw = P(None, "dp", None, "mp")
    split = P(None, "mp")
    return jax.shard_map(
        shards,
        mesh=mesh,
        in_specs=(P("dp", None, None), P(), P("dp"), P("dp"), P("dp"), P())
        + (table,) * 6
        + (attn,) * 3
        + (ffw,) * 3
        + (split,) * 3
        + (P(),) * 3,
        out_specs=(P(),) * 3
        + (table,) * 7
        + (attn,) * 4
        + (ffw,) * 4
        + (split,) * 3
        + (P(),) * 3,
        check_vma=False,
    )
```

```python
import functools

import jax
import jax.numpy as jnp
from jax import lax
from jax.experimental import pallas as pl
from jax.experimental.pallas import tpu as pltpu
from jax.sharding import PartitionSpec as P

D = 384
HEADS = 6
HD = 64
FF = 1536
CLS = 1000
PD = 768
PATCHES = 196
LAYERS = 2
STEP = 10
TOK = 198
TP = 208
GRP = 2
F_GRP = 4
ENDS = 16
END_AT = 4
SENT = 200
ROWS = GRP * TP
HALF = FF // 2
COLS = 6144
T_COLS = 1536
F_COLS = 512
TABLE_CHUNKS = (6, 7, 8)
REDUCE_ORDER = (0, 2, 4, 1, 3, 6, 5, 7, 8)
REDUCE_TURNS = (0, 0, 1, 1, 2, 1, 2, 0, 0)
MAIN_WIDTHS = (768, 768, 768, 768, 768, 768, 1024)
MAIN_TURNS = (0, 0, 0, 1, 0, 1, 1)
FRONT_WIDTHS = (384, 128)
FRONT_TURNS = (0, 1)
M_COLS = 4608
MIB = 1 << 20
NORM_ROWS = ROWS
GELU_ROWS = 32

norm_eps = 1e-06
clip_limit = 0.02
beta_one = 0.9
beta_two = 0.999
adam_eps = 1e-08
matrix_rate = 0.08
vector_rate = 0.5
matrix_decay = 0.05

f32 = jnp.float32
bf16 = jnp.bfloat16
MESH = pl.DeviceIdType.MESH
AB = ((1,), (0,))
ABT = ((1,), (1,))
ATB = ((0,), (0,))


def mm(left, right, dims=AB):
    return lax.dot_general(left, right, (dims, ((), ())), preferred_element_type=f32)


def full_spec(shape):
    return pl.BlockSpec(shape, lambda *_: (0,) * len(shape), pipeline_mode=pl.Buffered(1))


def row_loop(total, chunk, body):
    def step(index, carry):
        body(pl.ds(pl.multiple_of(index * chunk, chunk), chunk))
        return carry

    if total == chunk:
        body(slice(0, total))
    else:
        lax.fori_loop(0, total // chunk, step, 0)


def center(x):
    mean = jnp.mean(x, -1, keepdims=True)
    xc = x - mean
    scale = lax.rsqrt(jnp.mean(xc * xc, -1, keepdims=True) + norm_eps)
    return xc * scale, scale


def gelu_pair(x):
    e = jnp.exp2((x * x) * -0.7213475204444817)
    den = 1.0 + 0.23164189 * jnp.abs(x)
    r = pl.reciprocal(den, approx=True)
    r = r * (2.0 - den * r)
    poly = r * (
        0.127414796
        + r * (-0.142248368 + r * (0.7107068705 + r * (-0.7265760135 + r * 0.5307027145)))
    )
    tail = poly * e
    cdf = jnp.where(x > 0.0, 1.0 - tail, tail)
    return x * cdf, cdf + x * (e * 0.3989422804014327)


def partner_place(partner_ref, k):
    images = partner_ref.shape[0]
    n_data = lax.axis_size("dp")
    far = lax.rem(lax.axis_index("dp") + n_data // 2, n_data)
    wanted = far * images + lax.axis_index("mp") * (images // 2) + k
    place = jnp.int32(0)
    for i in range(images):
        place = place + jnp.where(partner_ref[i] == wanted, i, 0)
    return place


def project(pix, w_ref):
    return mm(pix[:, :D], w_ref[0], ABT) + mm(pix[:, D:], w_ref[1], ABT)


def embed_send_kernel(pix_ref, w_ref, send_ref, flat):
    mp = lax.axis_index("mp")
    patches, _, images, _ = pix_ref.shape
    part = patches // 7
    for c in range(7):
        out = project(pix_ref[c * part : (c + 1) * part, mp].reshape(part * images, PD), w_ref)
        for j in range(3):
            flat[j, c * part * images : (c + 1) * part * images] = out[:, 128 * j : 128 * (j + 1)]
    for k in range(images):
        for j in range(3):
            cols = slice(128 * j, 128 * (j + 1))
            send_ref[k, :patches, cols] = flat[j, pl.ds(k, patches, stride=images), :].astype(bf16)
        send_ref[k, patches:] = jnp.zeros((SENT - patches, D), bf16)


def embed_own_kernel(partner_ref, pix_ref, w_ref, own_ref, flat):
    count = partner_ref.shape[0]
    patches = pix_ref.shape[0]
    part = patches // 7
    for c in range(7):
        out = project(pix_ref[c * part : (c + 1) * part].reshape(part * count, PD), w_ref)
        for j in range(3):
            flat[j, c * part * count : (c + 1) * part * count] = out[:, 128 * j : 128 * (j + 1)]
    for k in range(count // 2):
        place = partner_place(partner_ref, k)
        for j in range(3):
            cols = slice(128 * j, 128 * (j + 1))
            own_ref[k, :, cols] = flat[j, pl.ds(place, patches, stride=count), :]


def embed_call(kernel, prefix, pix, weights, shape, dtype, rows, name):
    return pl.pallas_call(
        kernel,
        grid=(1,),
        in_specs=[pl.BlockSpec(memory_space=pltpu.SMEM)] * len(prefix)
        + [full_spec(pix.shape), full_spec(weights.shape)],
        out_specs=full_spec(shape),
        out_shape=jax.ShapeDtypeStruct(shape, dtype),
        scratch_shapes=[pltpu.VMEM((3, rows, 128), f32)],
        compiler_params=pltpu.CompilerParams(vmem_limit_bytes=60 * MIB),
        name=name,
    )(*prefix, pix, weights)


def embed_send(pix, weights):
    images = pix.shape[2]
    shape = (images, SENT, D)
    rows = PATCHES * images
    return embed_call(embed_send_kernel, [], pix, weights, shape, bf16, rows, "embed_sent_images")


def embed_own(partner, pix, weights):
    images = pix.shape[1]
    shape = (images // 2, PATCHES, D)
    rows = PATCHES * images
    return embed_call(
        embed_own_kernel, [partner], pix, weights, shape, f32, rows, "embed_own_images"
    )


def split_tokens(w_ref, col):
    seg = jnp.concatenate([w_ref[0, :, col : col + 128], w_ref[1, :, col : col + 128]], 1)
    return jnp.transpose(seg.astype(f32), (1, 0))


def attend(g, qkv_ref, p_ref, ho_ref):
    rows = slice(g * TP, (g + 1) * TP)
    lane = lax.broadcasted_iota(jnp.int32, (TP, 128), 1)
    key_mask = jnp.where(lax.broadcasted_iota(jnp.int32, (1, TP), 1) < TOK, 0.0, -1e30).astype(f32)
    for j in range(3):
        q = qkv_ref[rows, 128 * j : 128 * (j + 1)]
        k = qkv_ref[rows, D + 128 * j : D + 128 * (j + 1)]
        v = qkv_ref[rows, 2 * D + 128 * j : 2 * D + 128 * (j + 1)]
        outs = []
        for s in range(2):
            mine = (lane < 64) if s == 0 else (lane >= 64)
            scores = mm(jnp.where(mine, q, jnp.zeros_like(q)), k, ABT) + key_mask
            exps = jnp.exp(scores - jnp.max(scores, -1, keepdims=True))
            probs = (exps * (1.0 / jnp.sum(exps, -1, keepdims=True))).astype(bf16)
            p_ref[6 * g + 2 * j + s] = probs
            outs.append(mm(probs, v))
        ho_ref[rows, 128 * j : 128 * (j + 1)] = jnp.where(lane < 64, outs[0], outs[1]).astype(bf16)


PAIRS = (0, 1, 3, 4, 2, 5)


def rounded(x):
    return x.astype(bf16).astype(f32)


def norm_rows(src, gain, shift, dst):
    dst[...] = (center(src[...])[0] * gain + shift).astype(bf16)


def token_row(tok_ref, layer, i):
    at = TP + 6 * layer + i
    return tok_ref[at : at + 1]


def spread_heads(x):
    lane = lax.broadcasted_iota(jnp.int32, x.shape, 1)
    zero = jnp.zeros_like(x)
    return jnp.concatenate(
        [jnp.where((lane >= HD * h) & (lane < HD * (h + 1)), x, zero) for h in range(HEADS)], 0
    )


def gather_heads(x):
    lane = lax.broadcasted_iota(jnp.int32, (ENDS, D), 1)
    total = jnp.zeros((ENDS, D), f32)
    for h in range(HEADS):
        part = x[ENDS * h : ENDS * (h + 1)]
        total = total + jnp.where((lane >= HD * h) & (lane < HD * (h + 1)), part, 0.0)
    return total


def attend_ends(g, kv_ref, q_ref, p_ref, ho_ref):
    rows = slice(g * TP, (g + 1) * TP)
    ends = slice(g * ENDS, (g + 1) * ENDS)
    key_mask = jnp.where(lax.broadcasted_iota(jnp.int32, (1, TP), 1) < TOK, 0.0, -1e30).astype(f32)
    scores = mm(spread_heads(q_ref[ends]), kv_ref[rows, :D], ABT) + key_mask
    exps = jnp.exp(scores - jnp.max(scores, -1, keepdims=True))
    probs = (exps * (1.0 / jnp.sum(exps, -1, keepdims=True))).astype(bf16)
    p_ref[g] = probs
    ho_ref[ends] = gather_heads(mm(probs, kv_ref[rows, D:])).astype(bf16)


def forward_kernel(partner_ref, mix_ref, own_ref, far_ref, t_ref, w_ref, sb_ref, *refs):
    x_ref, mid_ref, qkv_ref, p_ref, ho_ref, hid_ref, gp_ref = refs[:7]
    x1_ref, kv_ref, q1_ref, p1_ref, ho1_ref, mid1_ref, tok_ref = refs[7:14]
    qkv_w, out_w, nbuf, up_s, bias_ref = refs[14:]
    step = pl.program_id(0)

    @pl.when(step == 0)
    def _():
        tok_ref[...] = split_tokens(t_ref, 0)
        for layer in range(LAYERS):
            attn_tiles(w_ref.at[layer], qkv_w.at[layer], out_w.at[layer])
            pieces = [
                sb_ref[h // 3, layer : layer + 1, 128 * (h % 3) + HD * t : 128 * (h % 3) + HD * (t + 1)]
                for t in range(2)
                for h in PAIRS
            ]
            bias_ref[layer : layer + 1] = rounded(jnp.concatenate(pieces, 1))

    def row(layer, i):
        return token_row(tok_ref, layer, i)

    for g in range(F_GRP):
        w = mix_ref[partner_place(partner_ref, step * F_GRP + g)]
        x_ref[g * TP : g * TP + PATCHES] = (
            w * own_ref[g] + (1.0 - w) * far_ref[g, :PATCHES].astype(f32) + tok_ref[:PATCHES]
        )
        x_ref[g * TP + PATCHES : (g + 1) * TP] = tok_ref[PATCHES:TP]
    norm_rows(x_ref, row(0, 0), row(0, 1), nbuf)
    qkv = mm(nbuf[...], qkv_w[0])
    q = qkv[:, :D] + bias_ref[0:1, :D]
    qkv_ref[:, :D] = (q.astype(bf16).astype(f32) * 0.125).astype(bf16)
    qkv_ref[:, D : 2 * D] = qkv[:, D : 2 * D].astype(bf16)
    qkv_ref[:, 2 * D :] = (qkv[:, 2 * D :] + bias_ref[0:1, D : 2 * D]).astype(bf16)
    for g in range(F_GRP):
        attend(g, qkv_ref, p_ref, ho_ref)
    mid_ref[...] = x_ref[...] + mm(ho_ref[...], out_w[0], ABT) + row(0, 4)
    norm_rows(mid_ref, row(0, 2), row(0, 3), nbuf)
    up_w, down_w = w_ref.at[LAYERS], w_ref.at[LAYERS + 1]
    for m in range(2):
        cols = slice(HALF * m, HALF * (m + 1))
        up_s[...] = mm(nbuf[...], up_w[m]) + rounded(sb_ref[m, 0:1, D:])

        def body(rs):
            hid, gp = gelu_pair(up_s[rs])
            hid_ref[rs, cols] = hid.astype(bf16)
            gp_ref[rs, cols] = gp.astype(bf16)

        row_loop(F_GRP * TP, GELU_ROWS, body)
    out = mid_ref[...] + row(0, 5)
    for m in range(2):
        cols = slice(HALF * m, HALF * (m + 1))
        out = out + mm(hid_ref[:, cols], down_w[m], ABT)
    x1_ref[...] = out
    norm_rows(x1_ref, row(1, 0), row(1, 1), nbuf)
    kv = mm(nbuf[...], qkv_w[1, :, D:])
    kv_ref[:, :D] = kv[:, :D].astype(bf16)
    kv_ref[:, D:] = (kv[:, D:] + bias_ref[1:2, D : 2 * D]).astype(bf16)
    ends = jnp.concatenate([nbuf[(g + 1) * TP - ENDS : (g + 1) * TP] for g in range(F_GRP)], 0)
    q = mm(ends, qkv_w[1, :, :D]) + bias_ref[1:2, :D]
    q1_ref[...] = (q.astype(bf16).astype(f32) * 0.125).astype(bf16)
    for g in range(F_GRP):
        attend_ends(g, kv_ref, q1_ref, p1_ref, ho1_ref)
    x_ends = jnp.concatenate([x1_ref[(g + 1) * TP - ENDS : (g + 1) * TP] for g in range(F_GRP)], 0)
    mid1_ref[...] = x_ends + mm(ho1_ref[...], out_w[1], ABT) + row(1, 4)


def kept_shapes(count):
    n = count * TP
    return [
        ((n, D), f32),
        ((n, D), f32),
        ((n, 3 * D), bf16),
        ((count * HEADS, TP, TP), bf16),
        ((n, D), bf16),
        ((n, FF), bf16),
        ((n, FF), bf16),
        ((n, D), f32),
        ((n, 2 * D), bf16),
        ((count * ENDS, D), bf16),
        ((count, HEADS * ENDS, TP), bf16),
        ((count * ENDS, D), bf16),
        ((count * ENDS, D), f32),
    ]


def block_of(shape, steps):
    block = (shape[0] // steps,) + tuple(shape[1:])
    return pl.BlockSpec(block, lambda i: (i,) + (0,) * (len(block) - 1))


def forward(partner, mix, own, far, seg, weights, sb):
    count = own.shape[0]
    steps = count // F_GRP
    outs = kept_shapes(count)
    shapes = [jax.ShapeDtypeStruct(s, t) for s, t in outs] + [jax.ShapeDtypeStruct((256, D), f32)]
    specs = [block_of(s, steps) for s, _ in outs] + [full_spec((256, D))]
    return pl.pallas_call(
        forward_kernel,
        grid=(steps,),
        in_specs=[
            pl.BlockSpec(memory_space=pltpu.SMEM),
            pl.BlockSpec(memory_space=pltpu.SMEM),
            block_of(own.shape, steps),
            block_of(far.shape, steps),
            full_spec(seg.shape),
            pl.BlockSpec((4, 2, D, 768), lambda i: (0, 0, 0, 0), pipeline_mode=pl.Buffered(1)),
            full_spec(sb.shape),
        ],
        out_specs=specs,
        out_shape=shapes,
        scratch_shapes=[
            pltpu.VMEM((LAYERS, D, 3 * D), bf16),
            pltpu.VMEM((LAYERS, D, D), bf16),
            pltpu.VMEM((F_GRP * TP, D), bf16),
            pltpu.VMEM((F_GRP * TP, HALF), f32),
            pltpu.VMEM((LAYERS, 2 * D), f32),
        ],
        compiler_params=pltpu.CompilerParams(vmem_limit_bytes=60 * MIB),
        name="forward_layers",
    )(partner, mix, own, far, seg, weights, sb)


def norm_back(dy, xhat, scale, gain):
    dyg = dy * gain
    c1 = jnp.mean(dyg, -1, keepdims=True)
    c2 = jnp.mean(dyg * xhat, -1, keepdims=True)
    return scale * (dyg - c1 - xhat * c2)


def share(part, own_ref, mate_ref, mp):
    own_ref[...] = part[mp]
    mate_ref[...] = part[1 - mp].astype(bf16)


def head_kernel(
    partner_ref,
    mix_ref,
    label_ref,
    teacher_ref,
    mid_ref,
    wf_ref,
    w_ref,
    sb_ref,
    hb_ref,
    cw_ref,
    tok_ref,
    uo_ref,
    um_ref,
    do_ref,
    dm_ref,
    ho_ref,
    hm_ref,
    dz_ref,
    gv_ref,
    gu_ref,
    dhb_ref,
    stat_ref,
    lanes,
    g_ffw,
    g_head,
):
    mp = lax.axis_index("mp")
    gain2, shift2, bias_f = (token_row(tok_ref, 1, i) for i in (2, 3, 5))
    gain, shift = (token_row(tok_ref, 2, i) for i in range(2))
    count = mid_ref.shape[0] // ENDS
    images = partner_ref.shape[0]
    n_data = lax.axis_size("dp")
    dp = lax.axis_index("dp")
    far_base = lax.rem(dp + n_data // 2, n_data) * images + mp * count
    marks = []
    for k in range(count):
        place = partner_place(partner_ref, k)
        marks.append(
            (
                label_ref[dp * images + place],
                label_ref[far_base + k],
                teacher_ref[place],
                mix_ref[place],
            )
        )
    for j in range(3):
        lanes[j] = mid_ref[:, 128 * j : 128 * (j + 1)]
    mid = jnp.concatenate(
        [
            jnp.concatenate(
                [lanes[j, pl.ds(END_AT + h, count, stride=ENDS), :] for j in range(3)], 1
            )
            for h in range(2)
        ],
        0,
    )
    xhat2, scale2 = center(mid)
    normed = (xhat2 * gain2 + shift2).astype(bf16)
    out = mid + bias_f
    hids, gps = [], []
    for m in range(2):
        up = mm(normed, wf_ref[0, m]) + rounded(sb_ref[m, 1:2, D:])
        hid, gp = gelu_pair(up)
        hids.append(hid.astype(bf16))
        gps.append(gp)
        out = out + mm(hids[m], wf_ref[1, m], ABT)
    xhat, scale = center(out)
    final = (xhat * gain + shift).astype(bf16)
    loss = jnp.zeros((1, 1), f32)
    weight = jnp.zeros((1, 1), f32)
    dfinals = []
    for h in range(2):
        mine = final[count * h : count * (h + 1)]
        halves = []
        for m in range(2):
            wh = w_ref[m, :, 512 * h : 512 * (h + 1)]
            at = 1024 * h + 512 * m
            logits = mm(mine, wh) + hb_ref[0:1, at : at + 512]
            ids = lax.broadcasted_iota(jnp.int32, (1, 512), 1) + 512 * m
            shares = []
            for k in range(count):
                first, second, teach, mix = marks[k]
                if h == 0:
                    both = jnp.where(ids == first, mix, 0.0) + jnp.where(ids == second, 1.0 - mix, 0.0)
                    shares.append(both)
                else:
                    shares.append(jnp.where(ids == teach, 1.0, 0.0))
            coef = jnp.concatenate(shares, 0) * cw_ref[0:1, 512 * m : 512 * (m + 1)]
            halves.append((wh, logits, coef))
        top = jnp.maximum(*[jnp.max(x[1], -1, keepdims=True) for x in halves])
        exps = [jnp.exp(x[1] - top) for x in halves]
        total = sum(jnp.sum(x, -1, keepdims=True) for x in exps)
        lse = top + jnp.log(total)
        csum = sum(jnp.sum(x[2], -1, keepdims=True) for x in halves)
        dfinal = jnp.zeros((count, D), f32)
        for m in range(2):
            wh, logits, coef = halves[m]
            loss = loss + jnp.sum(jnp.sum(coef * (lse - logits), -1, keepdims=True), 0, keepdims=True)
            dl = csum * (exps[m] / total) - coef
            at = 1024 * h + 512 * m
            dhb_ref[0:1, at : at + 512] = jnp.sum(dl, 0, keepdims=True)
            low = dl.astype(bf16)
            g_head[m, :, 512 * h : 512 * (h + 1)] = mm(mine, low, ATB)
            dfinal = dfinal + mm(low, wh, ABT)
        weight = weight + jnp.sum(csum, 0, keepdims=True)
        dfinals.append(dfinal)
    dfinal = jnp.concatenate(dfinals, 0)
    dz = norm_back(dfinal, xhat, scale, gain)
    low = dz.astype(bf16)
    dn = jnp.zeros_like(dz)
    for m in range(2):
        dh = mm(low, wf_ref[1, m])
        du = (dh.astype(bf16).astype(f32) * gps[m]).astype(bf16)
        gu_ref[0:1, HALF * m : HALF * (m + 1)] = jnp.sum(du.astype(f32), 0, keepdims=True)
        g_ffw[0, m] = mm(normed, du, ATB)
        g_ffw[1, m] = mm(low, hids[m], ATB)
        dn = dn + mm(du, wf_ref[0, m], ABT)
    dmid = dz + norm_back(dn, xhat2, scale2, gain2)
    gv_ref[...] = jnp.zeros_like(gv_ref)
    sums = [dn * xhat2, dn, dmid, dz, dfinal * xhat, dfinal]
    for i, item in enumerate(sums):
        gv_ref[i + 2 : i + 3] = jnp.sum(item, 0, keepdims=True)
    lanes[...] = jnp.zeros_like(lanes)
    for j in range(3):
        for h in range(2):
            lanes[j, pl.ds(END_AT + h, count, stride=ENDS), :] = dmid[
                count * h : count * (h + 1), 128 * j : 128 * (j + 1)
            ]
        dz_ref[:, 128 * j : 128 * (j + 1)] = lanes[j]
    which = lax.broadcasted_iota(jnp.int32, stat_ref.shape, 1)
    stat_ref[...] = jnp.where(which == 0, loss, jnp.where(which == 1, weight, 0.0))
    share(g_ffw.at[0], uo_ref, um_ref, mp)
    share(g_ffw.at[1], do_ref, dm_ref, mp)
    share(g_head, ho_ref, hm_ref, mp)


def pair_shapes(shapes):
    return [jax.ShapeDtypeStruct(s, t) for s in shapes for t in (f32, bf16)]


def head(partner, mix, labels, teacher, mid, weights, w_heads, sb, hb, cw, tok):
    outs = pair_shapes([(D, 768), (D, 768), (D, 1024)]) + [
        jax.ShapeDtypeStruct(s, f32)
        for s in (mid.shape, (8, D), (1, FF), (1, 2048), (1, 128))
    ]
    return pl.pallas_call(
        head_kernel,
        grid=(1,),
        in_specs=[pl.BlockSpec(memory_space=pltpu.SMEM)] * 4
        + [
            full_spec(mid.shape),
            pl.BlockSpec((2, 2, D, 768), lambda i: (2, 0, 0, 0), pipeline_mode=pl.Buffered(1)),
        ]
        + [full_spec(x.shape) for x in (w_heads, sb, hb, cw, tok)],
        out_specs=[full_spec(x.shape) for x in outs],
        out_shape=outs,
        scratch_shapes=[
            pltpu.VMEM((3, mid.shape[0], 128), f32),
            pltpu.VMEM((2, 2, D, 768), f32),
            pltpu.VMEM((2, D, 1024), f32),
        ],
        compiler_params=pltpu.CompilerParams(vmem_limit_bytes=60 * MIB),
        name="loss_heads",
    )(partner, mix, labels, teacher, mid, weights, w_heads, sb, hb, cw, tok)


def attend_back(g, dho, qkv_ref, p_ref, dproj):
    rows = slice(g * TP, (g + 1) * TP)
    lane = lax.broadcasted_iota(jnp.int32, (TP, 128), 1)
    for j in range(3):
        q = qkv_ref[rows, 128 * j : 128 * (j + 1)]
        k = qkv_ref[rows, D + 128 * j : D + 128 * (j + 1)]
        v = qkv_ref[rows, 2 * D + 128 * j : 2 * D + 128 * (j + 1)]
        do = dho[rows, 128 * j : 128 * (j + 1)]
        qt, kt, dot_ = (jnp.transpose(a, (1, 0)) for a in (q, k, do))
        for s in range(2):
            mine = (lane < 64) if s == 0 else (lane >= 64)
            sub = slice(64 * s, 64 * (s + 1))
            at = 128 * j + 64 * s
            probs = p_ref[6 * g + 2 * j + s]
            dproj[g, 2 * D + at : 2 * D + at + 64] = mm(dot_[sub], probs).astype(bf16)
            dprob = mm(jnp.where(mine, do, jnp.zeros_like(do)), v, ABT)
            p32 = probs.astype(f32)
            delta = jnp.sum(dprob * p32, -1, keepdims=True)
            ds = (p32 * (dprob - delta)).astype(bf16)
            dproj[g, at : at + 64] = (mm(kt[sub], ds, ABT) * 0.125).astype(bf16)
            dproj[g, D + at : D + at + 64] = mm(qt[sub], ds).astype(bf16)


def ends_back(g, dho, kv_ref, q_ref, p_ref, dq, dproj):
    rows = slice(g * TP, (g + 1) * TP)
    ends = slice(g * ENDS, (g + 1) * ENDS)
    q = spread_heads(q_ref[ends])
    do = spread_heads(dho[ends])
    probs = p_ref[g]
    dprob = mm(do, kv_ref[rows, D:], ABT)
    p32 = probs.astype(f32)
    delta = jnp.sum(dprob * p32, -1, keepdims=True)
    ds = (p32 * (dprob - delta)).astype(bf16)
    dq[ends] = (gather_heads(mm(ds, kv_ref[rows, :D])) * 0.125).astype(bf16)
    dproj[g, :D] = mm(q, ds, ATB).astype(bf16)
    dproj[g, D : 2 * D] = mm(do, probs, ATB).astype(bf16)


def backward_kernel(
    dz_ref,
    x_ref,
    mid_ref,
    qkv_ref,
    p_ref,
    ho_ref,
    hid_ref,
    gp_ref,
    x1_ref,
    kv_ref,
    q1_ref,
    p1_ref,
    ho1_ref,
    wa_ref,
    wf_ref,
    tok_ref,
    dzo_ref,
    a0o_ref,
    a0m_ref,
    a1o_ref,
    a1m_ref,
    uo_ref,
    um_ref,
    do_ref,
    dm_ref,
    gv_ref,
    gb_ref,
    gu_ref,
    qkv_w,
    out_w,
    dqkv,
    dkv,
    dq1,
    dout,
    g_ffw,
    g_att,
    nbuf,
    dz,
    dn,
    du,
    dq,
    dproj,
):
    step = pl.program_id(0)
    mp = lax.axis_index("mp")

    def row(layer, i):
        return token_row(tok_ref, layer, i)

    @pl.when(step == 0)
    def _():
        for ref in (gv_ref, gb_ref, gu_ref, g_ffw, dqkv, dkv, dq1, dout):
            ref[...] = jnp.zeros_like(ref)
        nbuf[:, D:] = jnp.ones((ROWS, 128), bf16)
        for layer in range(LAYERS):
            attn_tiles(wa_ref.at[layer], qkv_w.at[layer], out_w.at[layer])

    def pull(src, gain, dz_out, at):
        xhat, scale = center(src[...])
        dy = dn[...]
        new = dz[...] + norm_back(dy, xhat, scale, gain)
        dz_out[...] = new
        gv_ref[at : at + 1] += jnp.sum(dy * xhat, 0, keepdims=True)
        gv_ref[at + 1 : at + 2] += jnp.sum(dy, 0, keepdims=True)

    normed = nbuf.at[:, :D]
    low = dz_ref[...].astype(bf16)
    dout[1] += mm(low, ho1_ref[...], ATB)
    dho = mm(low, out_w[1]).astype(bf16)
    norm_rows(x1_ref, row(1, 0), row(1, 1), normed)
    dz[...] = jnp.zeros_like(dz)
    for g in range(GRP):
        rows = slice(g * TP, (g + 1) * TP)
        ends_back(g, dho, kv_ref, q1_ref, p1_ref, dq, dproj)
        dkv[...] += mm(dproj[g, : 2 * D], nbuf[rows])
        dn[rows] = jnp.transpose(mm(qkv_w[1, :, D:], dproj[g, : 2 * D]), (1, 0))
    dq_all = dq[...]
    ends = jnp.concatenate([nbuf[(g + 1) * TP - ENDS : (g + 1) * TP, :D] for g in range(GRP)], 0)
    dq1[...] += mm(ends, dq_all, ATB)
    gb_ref[1:2, :D] += jnp.sum(dq_all.astype(f32), 0, keepdims=True)
    more = mm(dq_all, qkv_w[1, :, :D], ABT)
    for g in range(GRP):
        last = slice((g + 1) * TP - ENDS, (g + 1) * TP)
        part = slice(g * ENDS, (g + 1) * ENDS)
        dn[last] += more[part]
        dz[last] = dz_ref[part]
    pull(x1_ref, row(1, 0), dz, 6)

    norm_rows(mid_ref, row(0, 2), row(0, 3), normed)
    gv_ref[5:6] += jnp.sum(dz[...], 0, keepdims=True)
    rz = dz[...].astype(bf16)
    rzt = jnp.transpose(rz, (1, 0))
    nt = jnp.transpose(nbuf[:, :D], (1, 0))
    for m in range(2):
        cols = slice(HALF * m, HALF * (m + 1))
        dh = mm(rz, wf_ref[1, m])
        du[...] = (dh.astype(bf16).astype(f32) * gp_ref[:, cols].astype(f32)).astype(bf16)
        gu_ref[0:1, cols] += jnp.sum(du[...].astype(f32), 0, keepdims=True)
        g_ffw[1, m] += mm(rzt, hid_ref[:, cols])
        g_ffw[0, m] += mm(nt, du[...])
        part = mm(du[...], wf_ref[0, m], ABT)
        dn[...] = part if m == 0 else dn[...] + part
    pull(mid_ref, row(0, 2), dz, 2)
    gv_ref[4:5] += jnp.sum(dz[...], 0, keepdims=True)
    rz2 = dz[...].astype(bf16)
    dout[0] += mm(jnp.transpose(rz2, (1, 0)), ho_ref[...])
    dho = mm(rz2, out_w[0]).astype(bf16)
    norm_rows(x_ref, row(0, 0), row(0, 1), normed)
    for g in range(GRP):
        rows = slice(g * TP, (g + 1) * TP)
        attend_back(g, dho, qkv_ref, p_ref, dproj)
        dqkv[...] += mm(dproj[g], nbuf[rows])
        dn[rows] = jnp.transpose(mm(qkv_w[0], dproj[g]), (1, 0))
    pull(x_ref, row(0, 0), dzo_ref, 0)

    @pl.when(step == pl.num_programs(0) - 1)
    def _():
        for layer in range(LAYERS):
            for t in range(4):
                for j in range(3):
                    at = D * t + 128 * j
                    if t == 3:
                        tile = dout[layer, :, 128 * j : 128 * (j + 1)]
                    elif layer == 0:
                        tile = jnp.transpose(dqkv[at : at + 128, :D], (1, 0))
                    elif t == 0:
                        tile = dq1[:, 128 * j : 128 * (j + 1)]
                    else:
                        tile = jnp.transpose(dkv[at - D : at - D + 128, :D], (1, 0))
                    if j < 2:
                        g_att[layer, j, :, 128 * t : 128 * (t + 1)] = tile
                    else:
                        for m in range(2):
                            lo = 512 + 64 * t
                            g_att[layer, m, :, lo : lo + 64] = tile[:, 64 * m : 64 * (m + 1)]
        share(g_att.at[0], a0o_ref, a0m_ref, mp)
        share(g_att.at[1], a1o_ref, a1m_ref, mp)
        share(g_ffw.at[0], uo_ref, um_ref, mp)
        share(g_ffw.at[1], do_ref, dm_ref, mp)
        sums = jnp.transpose(dqkv[:, D:], (1, 0))[0:1]
        gb_ref[0:1, :D] = sums[:, :D]
        gb_ref[0:1, D:] = sums[:, 2 * D :]
        gb_ref[1:2, D:] = jnp.transpose(dkv[:, D:], (1, 0))[0:1, D:]


def attn_tiles(w_ref, qkv_w, out_w):
    for t in range(4):
        cols = 128 * t
        pieces = [w_ref[0, :, cols : cols + 128], w_ref[1, :, cols : cols + 128]]
        tile = 512 + 128 * (t // 2)
        lane = 64 * (t % 2)
        pieces.append(
            jnp.concatenate(
                [w_ref[m, :, tile : tile + 128][:, lane : lane + 64] for m in range(2)], 1
            )
        )
        for j in range(3):
            if t < 3:
                at = D * t + 128 * j
                qkv_w[:, at : at + 128] = pieces[j]
            else:
                out_w[:, 128 * j : 128 * (j + 1)] = pieces[j]


def backward(dz, kept, weights, tok):
    steps = dz.shape[0] // (GRP * ENDS)
    x_shape = kept[0].shape
    shares = pair_shapes([(D, 768)] * 4)
    extra = [jax.ShapeDtypeStruct(s, f32) for s in ((8, D), (2, 2 * D), (1, FF))]
    return pl.pallas_call(
        backward_kernel,
        grid=(steps,),
        in_specs=[block_of(a.shape, steps) for a in (dz,) + tuple(kept)]
        + [
            pl.BlockSpec((2, 2, D, 768), lambda i: (0, 0, 0, 0), pipeline_mode=pl.Buffered(1)),
            pl.BlockSpec((2, 2, D, 768), lambda i: (1, 0, 0, 0), pipeline_mode=pl.Buffered(1)),
            full_spec(tok.shape),
        ],
        out_specs=[block_of(x_shape, steps)] + [full_spec(x.shape) for x in shares + extra],
        out_shape=[jax.ShapeDtypeStruct(x_shape, f32)] + shares + extra,
        scratch_shapes=[
            pltpu.VMEM((LAYERS, D, 3 * D), bf16),
            pltpu.VMEM((LAYERS, D, D), bf16),
            pltpu.VMEM((3 * D, 512), f32),
            pltpu.VMEM((2 * D, 512), f32),
            pltpu.VMEM((D, D), f32),
            pltpu.VMEM((LAYERS, D, D), f32),
            pltpu.VMEM((2, 2, D, 768), f32),
            pltpu.VMEM((LAYERS, 2, D, 768), f32),
            pltpu.VMEM((ROWS, D + 128), bf16),
            pltpu.VMEM((ROWS, D), f32),
            pltpu.VMEM((ROWS, D), f32),
            pltpu.VMEM((ROWS, HALF), bf16),
            pltpu.VMEM((GRP * ENDS, D), bf16),
            pltpu.VMEM((GRP, 3 * D, TP), bf16),
        ],
        compiler_params=pltpu.CompilerParams(vmem_limit_bytes=62 * MIB),
        name="backward_layers",
    )(dz, *kept, weights, weights, tok)


def patch_grad_kernel(
    partner_ref,
    mix_ref,
    dz_ref,
    own_ref,
    far_ref,
    gvb_ref,
    gvh_ref,
    po_ref,
    pm_ref,
    eo_ref,
    em_ref,
    dzo,
    dzf,
    tok,
    g_patch,
    g_seg,
):
    mp = lax.axis_index("mp")
    count = far_ref.shape[0] // PATCHES
    both = own_ref.shape[0] // PATCHES
    dzo[...] = jnp.zeros_like(dzo)
    total = jnp.zeros((TP, D), f32)
    for k in range(count):
        place = partner_place(partner_ref, k)
        w = mix_ref[place]
        for j in range(3):
            part = dz_ref[k * TP : k * TP + PATCHES, 128 * j : 128 * (j + 1)]
            dzo[j, pl.ds(place, PATCHES, stride=both), :] = w * part
            dzf[j, pl.ds(k, PATCHES, stride=count), :] = (1.0 - w) * part
        total = total + dz_ref[k * TP : (k + 1) * TP]
    tok[...] = jnp.zeros_like(tok)
    tok[:TP] = total
    tok[TP : TP + 8] = gvb_ref[...]
    tok[TP + 8 : TP + 14] = gvh_ref[2:8]
    turned = jnp.transpose(tok[...], (1, 0))
    for m in range(2):
        g_seg[m] = turned[:, 128 * m : 128 * (m + 1)]
    lo, lf = (
        jnp.concatenate([jnp.transpose(ref[j].astype(bf16), (1, 0)) for j in range(3)], 0)
        for ref in (dzo, dzf)
    )
    for m in range(2):
        cols = slice(D * m, D * (m + 1))
        g_patch[m] = mm(lo, own_ref[:, cols]) + mm(lf, far_ref[:, cols])
    share(g_patch, po_ref, pm_ref, mp)
    share(g_seg, eo_ref, em_ref, mp)


def patch_grad(partner, mix, dz, own, far, gvb, gvh):
    outs = pair_shapes([(D, D), (D, 128)])
    return pl.pallas_call(
        patch_grad_kernel,
        grid=(1,),
        in_specs=[pl.BlockSpec(memory_space=pltpu.SMEM)] * 2
        + [full_spec(a.shape) for a in (dz, own, far, gvb, gvh)],
        out_specs=[full_spec(x.shape) for x in outs],
        out_shape=outs,
        scratch_shapes=[
            pltpu.VMEM((3, own.shape[0], 128), f32),
            pltpu.VMEM((3, far.shape[0], 128), f32),
            pltpu.VMEM((256, D), f32),
            pltpu.VMEM((2, D, D), f32),
            pltpu.VMEM((2, D, 128), f32),
        ],
        compiler_params=pltpu.CompilerParams(vmem_limit_bytes=56 * MIB),
        name="patch_gradient",
    )(partner, mix, dz, own, far, gvb, gvh)


def link_orders(bits):
    far = [b for b in (range(1, bits, 2) if bits == 6 else [3]) if b < bits]
    near = [b for b in range(bits) if b not in far]
    return [near[i:] + near[:i] for i in range(len(near))], far


def gather_plan(bits, turns):
    near, far = link_orders(bits)
    deep = far + [near[0][-1]]
    flat = near[0][:-1]
    return [flat[t:] + flat[:t] for t in turns], deep


def chunk_plan(bits, cuts):
    near, far = link_orders(bits)
    return [
        (cuts[i], cuts[i + 1] - cuts[i], near[i % len(near)], far) for i in range(len(cuts) - 1)
    ]


def mesh_place():
    return lax.axis_index("dp"), lax.axis_index("mp")


def bit_of(value, bit):
    return (value // 2**bit) % 2


def flipped(value, bit):
    return value + 2**bit * (1 - 2 * bit_of(value, bit))


def meet(bits):
    dp, mp = mesh_place()
    barrier = pltpu.get_barrier_semaphore()
    for peer in [(dp, 1 - mp)] + [(flipped(dp, b), mp) for b in range(bits)]:
        pl.semaphore_signal(barrier, inc=1, device_id=peer, device_id_type=MESH)
    pl.semaphore_wait(barrier, bits + 1)


def push(src, dst, send, recv, peer):
    copy = pltpu.make_async_remote_copy(
        src_ref=src, dst_ref=dst, send_sem=send, recv_sem=recv, device_id=peer, device_id_type=MESH
    )
    copy.start()
    return copy


def held_part(ref, bits, lead, dp, done=(), flip=None):
    idx = list(lead)
    for b in reversed(bits):
        mine = bit_of(dp, b)
        idx.append(pl.ds(0, 2) if b in done else (1 - mine if b == flip else mine))
    return ref.at[tuple(idx)]


def gather_front_kernel(bits, tab_ref, main_ref, sb_ref, *refs):
    w_refs = refs[:2]
    far_refs = refs[2:4]
    sbo_ref, tabr, stage_p, stage_e, stage_h, s_loc, s_tab = refs[4:11]
    s_send, s_recv, f_send, f_recv, m_send, m_recv = refs[11:]
    dp, mp = mesh_place()
    mate = (dp, 1 - mp)
    turns, deep = gather_plan(bits, FRONT_TURNS)
    every = list(range(bits))

    far = deep[:-1]
    wide = {}

    def part(c, *args):
        return held_part(w_refs[c], every, (mp,), dp, *args)

    def main(c, *args):
        return held_part(far_refs[c], far, (), dp, *args)

    meet(bits)
    c_tab = push(tab_ref.at[1 - mp], tabr, s_tab.at[0], s_tab.at[1], mate)
    c_sb = push(sb_ref, sbo_ref.at[mp], s_tab.at[2], s_tab.at[3], mate)
    local = [pltpu.make_async_copy(sb_ref, sbo_ref.at[mp], s_loc.at[0])]
    local[0].start()
    c_tab.wait()
    mine = tab_ref[mp].astype(f32)
    other = tabr[...].astype(f32)
    first = jnp.where(mp == 0, mine, other)
    second = jnp.where(mp == 0, other, mine)
    table = jnp.concatenate([first, second], 0).astype(bf16)
    stage_p[...] = table[:, :D]
    stage_e[...] = table[:, D:F_COLS]
    stage_h[...] = table[:, F_COLS:]
    stages = (stage_p, stage_e)
    wides = (main_ref, stage_h)
    copies = {}
    forwards = []
    for s in range(bits + 1):
        for c in range(2):
            order = deep + turns[c]
            if s:
                copies[c, s - 1].wait_recv()
            if s < bits:
                held = part(c, order[:s])
                copies[c, s] = push(
                    held if s else stages[c],
                    held,
                    s_send.at[c, s],
                    s_recv.at[c, s],
                    (flipped(dp, order[s]), mp),
                )
            got = part(c, order[: s - 1], order[s - 1]) if s else part(c)
            forwards.append(
                push(got if s else stages[c], got, f_send.at[c, s], f_recv.at[c, s], mate)
            )
        if s == 0:
            for c in range(2):
                local.append(pltpu.make_async_copy(stages[c], part(c), s_loc.at[c + 1]))
                local[-1].start()
                local.append(pltpu.make_async_copy(wides[c], main(c), s_loc.at[c + 3]))
                local[-1].start()
            for copy in local:
                copy.wait()
        at = s - len(deep) + 1
        if 0 <= at < len(far):
            for c in range(2):
                if at:
                    wide[c, at - 1].wait_recv()
                dst = main(c, far[:at])
                wide[c, at] = push(
                    dst if at else wides[c],
                    dst,
                    m_send.at[c, at],
                    m_recv.at[c, at],
                    (flipped(dp, far[at]), mp),
                )
    for copy in forwards:
        copy.wait()
    for copy in copies.values():
        copy.wait_send()
    for copy in wide.values():
        copy.wait_send()
    for c in range(2):
        wide[c, len(far) - 1].wait_recv()
    c_sb.wait()


def gather_front(tab, shard, sb, n_data):
    bits = n_data.bit_length() - 1
    rows = D // n_data
    _, far = link_orders(bits)
    deep_shape = (2,) * len(far)
    sems = pltpu.SemaphoreType.DMA
    anywhere = pl.BlockSpec(memory_space=pl.ANY)
    inside = pl.BlockSpec(memory_space=pltpu.VMEM)
    return pl.pallas_call(
        functools.partial(gather_front_kernel, bits),
        in_specs=[inside] * 3,
        out_specs=[anywhere] * 4 + [inside],
        out_shape=[
            jax.ShapeDtypeStruct((2,) * (bits + 1) + (rows, w), bf16) for w in FRONT_WIDTHS
        ]
        + [
            jax.ShapeDtypeStruct(deep_shape + shard.shape, bf16),
            jax.ShapeDtypeStruct(deep_shape + (rows, T_COLS - F_COLS), bf16),
            jax.ShapeDtypeStruct((2,) + sb.shape, f32),
        ],
        scratch_shapes=[
            pltpu.VMEM(tab.shape[1:], bf16),
            pltpu.VMEM((rows, FRONT_WIDTHS[0]), bf16),
            pltpu.VMEM((rows, FRONT_WIDTHS[1]), bf16),
            pltpu.VMEM((rows, T_COLS - F_COLS), bf16),
            sems((5,)),
            sems((4,)),
            sems((2, bits)),
            sems((2, bits)),
            sems((2, bits + 1)),
            sems((2, bits + 1)),
            sems((2, len(far))),
            sems((2, len(far))),
        ],
        compiler_params=pltpu.CompilerParams(
            collective_id=2, has_side_effects=True, vmem_limit_bytes=60 * MIB
        ),
        name="gather_front",
    )(tab, shard, sb)


def gather_main_kernel(bits, *refs):
    turns, deep = gather_plan(bits, MAIN_TURNS)
    far, last = deep[:-1], deep[-1]
    mains, heads, pix_ref = refs[:2], refs[2:4], refs[4]
    w_ref, h_ref, mine_ref = refs[5:8]
    pix, s_pix, s_loc, s_send, s_recv, f_send, f_recv = refs[8:]
    dp, mp = mesh_place()
    mate = (dp, 1 - mp)
    every = list(range(bits))
    steps = bits - len(deep)
    chunks = len(MAIN_WIDTHS)

    def lead(c):
        return (w_ref, (c, mp)) if c < chunks - 1 else (h_ref, (mp,))

    def part(c, *args):
        return held_part(lead(c)[0], every, lead(c)[1], dp, *args)

    meet(bits)
    pix_in = pltpu.make_async_copy(pix_ref.at[:, mp], pix, s_pix.at[0])
    pix_in.start()
    copies = {}
    forwards = []
    local = []
    for c in range(chunks):
        for i, dst in enumerate((part(c, far), part(c, far, last))):
            lead_cut = (slice(None),) * len(far) + (c,)
            src = mains[i].at[lead_cut] if c < chunks - 1 else heads[i]
            local.append(pltpu.make_async_copy(src, dst, s_loc.at[c, i]))
            local[-1].start()
    pix_in.wait()
    pix_out = pltpu.make_async_copy(pix, mine_ref, s_pix.at[1])
    pix_out.start()
    for s in range(steps + 1):
        for c in range(chunks):
            order = turns[c]
            if s:
                copies[c, s - 1].wait_recv()
            else:
                for copy in local[2 * c : 2 * c + 2]:
                    copy.wait()
            done = deep + order[:s]
            if s < steps:
                held = part(c, done)
                copies[c, s] = push(
                    held, held, s_send.at[c, s], s_recv.at[c, s], (flipped(dp, order[s]), mp)
                )
            got = part(c, done[:-1], done[-1]) if s else part(c, done)
            forwards.append(push(got, got, f_send.at[c, s], f_recv.at[c, s], mate))
    for copy in forwards:
        copy.wait()
    for copy in copies.values():
        copy.wait_send()
    pix_out.wait()


def gather_main(mains, heads, pix, n_data):
    bits = n_data.bit_length() - 1
    rows = D // n_data
    near, _ = link_orders(bits)
    steps = len(near[0]) - 1
    chunks = len(MAIN_WIDTHS)
    sems = pltpu.SemaphoreType.DMA
    anywhere = pl.BlockSpec(memory_space=pl.ANY)
    inside = pl.BlockSpec(memory_space=pltpu.VMEM)
    places = (2,) * (bits + 1) + (rows,)
    mine = pix.shape[:1] + pix.shape[2:]
    main, head_w, pix_mine = pl.pallas_call(
        functools.partial(gather_main_kernel, bits),
        in_specs=[inside] * (2 * len(mains)) + [anywhere],
        out_specs=[anywhere] * 3,
        out_shape=[
            jax.ShapeDtypeStruct((chunks - 1,) + places + (768,), bf16),
            jax.ShapeDtypeStruct(places + (1024,), bf16),
            jax.ShapeDtypeStruct(mine, bf16),
        ],
        scratch_shapes=[
            pltpu.VMEM(mine, bf16),
            sems((2,)),
            sems((chunks, len(mains))),
            sems((chunks, steps)),
            sems((chunks, steps)),
            sems((chunks, steps + 1)),
            sems((chunks, steps + 1)),
        ],
        compiler_params=pltpu.CompilerParams(
            collective_id=0, has_side_effects=True, vmem_limit_bytes=60 * MIB
        ),
        cost_estimate=pl.CostEstimate(flops=0, bytes_accessed=150 * MIB, transcendentals=0),
        name="gather_main",
    )(*mains, *heads, pix)
    return main.reshape(chunks - 1, 2, D, 768), head_w.reshape(2, D, 1024), pix_mine


def reduce_plan(bits, turns):
    near, far = link_orders(bits)
    return [near[t % len(near)] + far for t in turns]


def block_index(free, fixed):
    def index(t):
        total = fixed
        for j, b in enumerate(free):
            total = total + ((t // 2**j) % 2) * 2**b
        return total

    return index


def reduce_kernel(bits, widths, turns, *refs):
    n = len(widths)
    own, mate_src = refs[:n], refs[n : 2 * n]
    smalls = refs[2 * n : 2 * n + 5]
    outs = refs[2 * n + 5 : 3 * n + 5]
    obun_ref, info_ref = refs[3 * n + 5 : 3 * n + 7]
    refs = refs[3 * n + 7 :]
    mrecv, acc, held = refs[:n], refs[n : 2 * n], refs[2 * n : 3 * n]
    refs = refs[3 * n :]
    sbufs, rbufs = refs[: n * bits], refs[n * bits : 2 * n * bits]
    bun, bunr, tsend, sq, sqr, o_sem, m_sem, s_sem, r_sem, b_sem, q_sem, t_sem = refs[2 * n * bits :]
    dp, mp = mesh_place()
    mate = (dp, 1 - mp)
    orders = reduce_plan(bits, turns)
    rows = D // 2**bits
    group = max(rows, 48)
    per = group // rows
    small = rows // 2

    loads = {}
    for c in REDUCE_ORDER:
        loads[c] = pltpu.make_async_copy(own[c], held[c], o_sem.at[c])
        loads[c].start()
    at = 0
    for ref in smalls:
        for i in range(ref.shape[0]):
            bun[:, at : at + ref.shape[1]] = ref[i : i + 1]
            at += ref.shape[1]
    meet(bits)
    mcopies = {
        c: push(mate_src[c], mrecv[c], m_sem.at[c, 0], m_sem.at[c, 1], mate) for c in REDUCE_ORDER
    }
    bcopies = [push(bun, bunr.at[0], b_sem.at[0, 0], b_sem.at[0, 1], mate)]

    def loop(total, body):
        def step(t, carry):
            body(t)
            return carry

        lax.fori_loop(0, total, step, 0)

    copies = {}

    def split(order, s, sent):
        free = [b for b in range(bits) if b not in order[: s + 1]]
        fixed = sum((bit_of(dp, b) * 2**b for b in order[:s]), 0)
        last = bit_of(dp, order[s])
        fixed = fixed + (1 - last if sent else last) * 2 ** order[s]
        return 2 ** len(free), block_index(free, fixed)

    def send_stage(c, s):
        total, index = split(orders[c], s, True)
        sbuf = sbufs[c * bits + s]

        def body(t):
            sbuf[t] = acc[c][index(t)].astype(bf16)

        loop(total, body)
        copies[c, s] = push(
            sbuf,
            rbufs[c * bits + s],
            s_sem.at[c, s],
            r_sem.at[c, s],
            (flipped(dp, orders[c][s]), mp),
        )

    def take_stage(c, s):
        copies[c, s].wait_recv()
        total, index = split(orders[c], s, False)
        rbuf = rbufs[c * bits + s]

        def body(t):
            acc[c][index(t)] += rbuf[t].astype(f32)

        loop(total, body)

    for c in REDUCE_ORDER:
        loads[c].wait()
        mcopies[c].wait_recv()

        def body(b):
            rs = pl.ds(pl.multiple_of(b * group, group), group)
            got = held[c][rs] + mrecv[c][rs].astype(f32)
            for i in range(per):
                acc[c][b * per + i] = got[rows * i : rows * (i + 1)]

        loop(D // group, body)
        send_stage(c, 0)
    for s in range(1, bits + 1):
        for c in REDUCE_ORDER:
            take_stage(c, s - 1)
            if s < bits:
                send_stage(c, s)
        bcopies[-1].wait()
        bun[...] = bun[...] + bunr[s - 1]
        bcopies.append(
            push(bun, bunr.at[s], b_sem.at[s, 0], b_sem.at[s, 1], (flipped(dp, s - 1), mp))
        )
    tails = []
    total = jnp.zeros((1, 1), f32)
    for c in range(n):
        mine = acc[c][dp]
        total = total + jnp.sum(mine * mine, keepdims=True)
        if c in TABLE_CHUNKS:
            k = TABLE_CHUNKS.index(c)
            send, recv = tsend[2 * k], tsend[2 * k + 1]
            send[...] = jnp.where(mp == 0, mine[small:], mine[:small])
            outs[c][mp] = jnp.where(mp == 0, mine[:small], mine[small:])
            tails.append((c, recv, push(send, recv, t_sem.at[k, 0], t_sem.at[k, 1], mate)))
        else:
            outs[c][...] = mine
    sq[0] = jnp.broadcast_to(total, (8, 128))
    bcopies[-1].wait()
    final = bun[...] + bunr[bits]
    obun_ref[...] = final
    shared = jnp.sum(final[:, 128:] * final[:, 128:], keepdims=True)
    for s in range(bits + 1):
        peer = mate if s == 0 else (flipped(dp, s - 1), mp)
        copy = push(sq.at[s], sqr.at[s], q_sem.at[s, 0], q_sem.at[s, 1], peer)
        copy.wait()
        sq[s + 1] = sq[s] + sqr[s]
    for c, recv, copy in tails:
        copy.wait()
        outs[c][1 - mp] = recv[...]
    squares = sq[bits + 1] + shared
    loss, weight = final[:, 0:1], final[:, 1:2]
    norm = jnp.sqrt(squares) / weight
    factor = jnp.minimum(1.0, clip_limit / norm) / weight
    which = lax.broadcasted_iota(jnp.int32, (8, 128), 1)
    info = jnp.where(which == 0, loss, jnp.where(which == 1, weight, norm))
    info_ref[...] = jnp.where(which == 3, factor, info)
    for copy in mcopies.values():
        copy.wait_send()
    for copy in copies.values():
        copy.wait_send()


def reduce_all(own, mates, smalls, turns, n_data):
    bits = n_data.bit_length() - 1
    rows = D // n_data
    widths = [x.shape[1] for x in own]
    n = len(widths)
    sems = pltpu.SemaphoreType.DMA
    inside = pl.BlockSpec(memory_space=pltpu.VMEM)
    anywhere = pl.BlockSpec(memory_space=pl.ANY)
    bufs = [
        pltpu.VMEM((2 ** (bits - 1 - s), rows, w), bf16) for w in widths for s in range(bits)
    ]
    length = sum(x.shape[0] * x.shape[1] for x in smalls)
    outs = [
        jax.ShapeDtypeStruct((2, rows // 2, w) if c in TABLE_CHUNKS else (rows, w), f32)
        for c, w in enumerate(widths)
    ]
    tails = [
        pltpu.VMEM((rows // 2, widths[c]), f32) for c in TABLE_CHUNKS for _ in range(2)
    ]

    def kernel(*refs):
        cut = len(refs) - 11 - len(tails)
        head, rest = refs[:cut], refs[cut:]
        tsend, rest = rest[: len(tails)], rest[len(tails) :]
        reduce_kernel(bits, widths, turns, *head, rest[0], rest[1], tsend, *rest[2:])

    return pl.pallas_call(
        kernel,
        in_specs=[anywhere] * (2 * n) + [inside] * len(smalls),
        out_specs=[inside] * (n + 2),
        out_shape=outs
        + [
            jax.ShapeDtypeStruct((1, length), f32),
            jax.ShapeDtypeStruct((8, 128), f32),
        ],
        scratch_shapes=[pltpu.VMEM((D, w), bf16) for w in widths]
        + [pltpu.VMEM((n_data, rows, w), f32) for w in widths]
        + [pltpu.VMEM((D, w), f32) for w in widths]
        + bufs
        + bufs
        + tails
        + [
            pltpu.VMEM((1, length), f32),
            pltpu.VMEM((bits + 1, 1, length), f32),
            pltpu.VMEM((bits + 2, 8, 128), f32),
            pltpu.VMEM((bits + 1, 8, 128), f32),
            sems((n,)),
            sems((n, 2)),
            sems((n, bits)),
            sems((n, bits)),
            sems((bits + 1, 2)),
            sems((bits + 1, 2)),
            sems((len(TABLE_CHUNKS), 2)),
        ],
        compiler_params=pltpu.CompilerParams(
            collective_id=1, has_side_effects=True, vmem_limit_bytes=62 * MIB
        ),
        name="reduce_gradients",
    )(*own, *mates, *smalls)


def adamw(master, first, second, gradient, rate, decay):
    first = beta_one * first + (1.0 - beta_one) * gradient
    second = beta_two * second + (1.0 - beta_two) * gradient * gradient
    first_hat = first / (1.0 - beta_one**STEP)
    second_hat = second / (1.0 - beta_two**STEP)
    master = master - rate * (first_hat / (jnp.sqrt(second_hat) + adam_eps) + decay * master)
    return (master, first, second)


def local_split(flat, layer):
    mp = lax.axis_index("mp")
    rows = []
    for m in range(2):
        pieces = []
        for h in range(3):
            at = 128 + 2 * D * layer + (128 * m + HD * h if h < 2 else 256 + HD * m)
            pieces += [flat[:, at : at + HD], flat[:, at + D : at + D + HD]]
        at = 128 + 2 * D * LAYERS + FF * layer + HALF * m
        rows.append(jnp.concatenate(pieces + [flat[:, at : at + HALF]], 1))
    return jnp.where(mp == 0, rows[0], rows[1])


def update_kernel(info_ref, *refs):
    g = refs[:9]
    flat_ref = refs[9]
    params = refs[10:25]
    outs = refs[25:]
    factor = info_ref[0, 3]

    def write(grad, item, rate, decay, at, outs, low):
        new, one, two = adamw(
            item[0][at], item[1][at], item[2][at], grad * factor, rate, decay
        )
        outs[0][at], outs[1][at], outs[2][at] = new, one, two
        if low:
            outs[3][at] = new.astype(bf16)

    everything = (slice(None), slice(None))
    heads = [
        jnp.concatenate([g[6][m, :, 512 * h : 512 * (h + 1)] for m in range(2)], 1)[:, :CLS]
        for h in range(2)
    ]
    token = jnp.concatenate([g[8][0], g[8][1]], 1)
    table = jnp.concatenate(
        [g[7][0], g[7][1], token[:, PATCHES:TOK], token[:, :PATCHES]] + heads, 1
    )
    write(table, params[0:3], matrix_rate, matrix_decay, everything, outs[0:4], True)
    vec = jnp.transpose(token, (1, 0))[TP : TP + 6 * LAYERS + 2]
    write(vec, params[3:6], vector_rate, 0.0, everything, outs[4:7], False)
    for layer in range(LAYERS):
        packed = g[layer][...]
        pieces = []
        for h in range(3):
            for t in range(4):
                lo = 128 * t + HD * h if h < 2 else 512 + HD * t
                pieces.append(packed[:, lo : lo + HD])
        grad = jnp.concatenate(pieces, 1)
        write(grad, params[6:9], matrix_rate, matrix_decay, layer, outs[7:11], True)
        for half in range(2):
            write(
                g[LAYERS + 2 * layer + half][...],
                params[9:12],
                matrix_rate,
                matrix_decay,
                (layer, slice(None), half),
                outs[11:15],
                True,
            )
    flat = flat_ref[...]
    for layer in range(LAYERS):
        grad = local_split(flat, layer)
        write(grad, params[12:15], vector_rate, 0.0, slice(layer, layer + 1), outs[15:18], False)


def update(info, grads, split, params):
    outs = []
    for i in range(5):
        low = i in (0, 2, 3)
        shape = params[3 * i].shape
        outs += [jax.ShapeDtypeStruct(shape, f32)] * 3
        outs += [jax.ShapeDtypeStruct(shape, bf16)] if low else []
    ins = list(grads) + [split] + list(params)
    return pl.pallas_call(
        update_kernel,
        grid=(1,),
        in_specs=[pl.BlockSpec(memory_space=pltpu.SMEM)] + [full_spec(x.shape) for x in ins],
        out_specs=[full_spec(x.shape) for x in outs],
        out_shape=outs,
        compiler_params=pltpu.CompilerParams(vmem_limit_bytes=60 * MIB),
        name="update_weights",
    )(info, *ins)


def pack_kernel(t_ref, v_ref, a_ref, f_ref, tab_ref, main_ref):
    small = t_ref.shape[0]
    table = t_ref[...]

    def zeros(n):
        return jnp.zeros((small, n), f32)

    turned = jnp.transpose(v_ref[...], (1, 0))
    low = PD + 2
    seg = jnp.concatenate(
        [
            table[:, low : low + PATCHES],
            table[:, PD:low],
            zeros(TP - TOK),
            turned,
            zeros(256 - TP - turned.shape[1]),
        ],
        1,
    )
    heads = [
        jnp.concatenate(
            [table[:, PD + TOK + CLS * h : PD + TOK + CLS * (h + 1)], zeros(1024 - CLS)], 1
        )
        for h in range(2)
    ]
    parts = [table[:, :PD], seg] + heads
    for m in range(2):
        at = 0
        for x in parts:
            half = x.shape[1] // 2
            tab_ref[m, :, at : at + half] = x[:, half * m : half * (m + 1)].astype(bf16)
            at += half
    for layer in range(LAYERS):
        a = a_ref[layer]
        for t in range(4):
            pair = jnp.concatenate(
                [a[:, 256 * h + HD * t : 256 * h + HD * (t + 1)] for h in range(2)], 1
            )
            main_ref[layer, :, 128 * t : 128 * (t + 1)] = pair.astype(bf16)
        main_ref[layer, :, 512:] = a[:, 512:].astype(bf16)
        for half in range(2):
            main_ref[LAYERS + 2 * layer + half] = f_ref[layer, :, half].astype(bf16)


def pack(tab, vec, attn, ffw):
    layers, rows, _ = attn.shape
    ins = [tab, vec, attn, ffw]
    shapes = [(2, tab.shape[0], T_COLS), (3 * layers, rows, HALF)]
    return pl.pallas_call(
        pack_kernel,
        grid=(1,),
        in_specs=[full_spec(x.shape) for x in ins],
        out_specs=[full_spec(x) for x in shapes],
        out_shape=[jax.ShapeDtypeStruct(x, bf16) for x in shapes],
        compiler_params=pltpu.CompilerParams(vmem_limit_bytes=60 * MIB),
        name="pack_shards",
    )(*ins)


def shards(
    pixels,
    labels,
    teacher,
    partner,
    mix_weight,
    class_weight,
    tables,
    tables_first,
    tables_second,
    vectors,
    vectors_first,
    vectors_second,
    attention,
    attention_first,
    attention_second,
    feedforward,
    feedforward_first,
    feedforward_second,
    split_bias,
    split_bias_first,
    split_bias_second,
    head_bias,
    head_bias_first,
    head_bias_second,
):
    n_data = lax.axis_size("dp")
    dp, mp = mesh_place()
    images_here = pixels.shape[0]
    count = images_here // 2
    rows = D // n_data
    far_pairs = [(i, (i + n_data // 2) % n_data) for i in range(n_data)]
    pix = pixels.transpose(1, 0, 2)
    tab, shard = pack(tables.T, vectors, attention, feedforward)
    deep = gather_plan(n_data.bit_length() - 1, MAIN_TURNS)[1]
    front, seg, *heights, sb = gather_front(tab, shard, split_bias, n_data)
    front = front.reshape(2, D, FRONT_WIDTHS[0])
    seg = seg.reshape(2, D, FRONT_WIDTHS[1])
    near_pairs = [(i, i ^ (1 << deep[-1])) for i in range(n_data)]
    mains, heads = ([x, lax.ppermute(x, "dp", near_pairs)] for x in heights)
    pix_halves = pix.reshape(PATCHES, 2, count, PD)
    send = embed_send(pix_halves, front)
    mains, heads, send = lax.optimization_barrier((mains, heads, send))
    far = lax.ppermute(send, "dp", far_pairs)
    weights, w_heads, pix_mine = gather_main(mains, heads, pix_halves, n_data)
    hb = jnp.pad(
        head_bias.astype(bf16).astype(f32).reshape(2, CLS),
        ((0, 0), (0, 1024 - CLS)),
        constant_values=-1e30,
    ).reshape(1, -1)
    cw = jnp.pad(class_weight, (0, 1024 - CLS)).reshape(1, -1)
    front, hb, cw, weights = lax.optimization_barrier((front, hb, cw, weights))
    own = embed_own(partner, pix, front)
    pix_mine, far, own = lax.optimization_barrier((pix_mine, far, own))
    pix_far = lax.ppermute(pix_mine, "dp", far_pairs)
    *kept, mid, tok = forward(
        partner, mix_weight, own, far, seg, weights, sb
    )
    u1o, u1m, d1o, d1m, ho, hm, dz, gvh, gu1, dhb, stat = head(
        partner, mix_weight, labels, teacher, mid, weights, w_heads, sb, hb, cw, tok
    )
    dz0, a0o, a0m, a1o, a1m, u0o, u0m, d0o, d0m, gvb, gb, gu0 = backward(dz, kept, weights, tok)
    po, pm, eo, em = patch_grad(
        partner,
        mix_weight,
        dz0,
        pix.reshape(PATCHES * images_here, PD),
        pix_far.reshape(PATCHES * count, PD),
        gvb,
        gvh,
    )
    own_parts = [a0o, a1o, u0o, d0o, u1o, d1o, ho, po, eo]
    mate_parts = [a0m, a1m, u0m, d0m, u1m, d1m, hm, pm, em]
    *g, flat, info = reduce_all(
        own_parts, mate_parts, [stat, gb, gu0, gu1, dhb], REDUCE_TURNS, n_data
    )
    loss_sum, weight_sum, grad_norm, factor = (info[0, i] for i in range(4))
    at = 128 + 2 * D * LAYERS + FF * LAYERS
    g_head = flat[0, at : at + 2048].reshape(2, 1024)[:, :CLS].reshape(-1)
    fresh = update(
        info,
        g,
        flat,
        [
            tables.T,
            tables_first.T,
            tables_second.T,
            vectors,
            vectors_first,
            vectors_second,
            attention,
            attention_first,
            attention_second,
            feedforward,
            feedforward_first,
            feedforward_second,
            split_bias,
            split_bias_first,
            split_bias_second,
        ],
    )
    fresh = [x.T for x in fresh[:4]] + list(fresh[4:])
    h_new, h_one, h_two = adamw(
        head_bias, head_bias_first, head_bias_second, g_head * factor, vector_rate, 0.0
    )
    return (loss_sum, weight_sum, grad_norm, *fresh, h_new, h_one, h_two)


def solution(mesh):
    table = P(None, ("dp", "mp"))
    attn = P(None, "dp", "mp")
    ffw = P(None, "dp", None, "mp")
    split = P(None, "mp")
    return jax.shard_map(
        shards,
        mesh=mesh,
        in_specs=(P("dp", None, None), P(), P("dp"), P("dp"), P("dp"), P())
        + (table,) * 6
        + (attn,) * 3
        + (ffw,) * 3
        + (split,) * 3
        + (P(),) * 3,
        out_specs=(P(),) * 3
        + (table,) * 7
        + (attn,) * 4
        + (ffw,) * 4
        + (split,) * 3
        + (P(),) * 3,
        check_vma=False,
    )
```

```python
import functools

import jax
import jax.numpy as jnp
from jax import lax
from jax.experimental import pallas as pl
from jax.experimental.pallas import tpu as pltpu
from jax.sharding import PartitionSpec as P

D = 384
HEADS = 6
HD = 64
FF = 1536
CLS = 1000
PD = 768
PATCHES = 196
LAYERS = 2
STEP = 10
TOK = 198
TP = 208
GRP = 2
F_GRP = 4
ENDS = 16
END_AT = 4
SENT = 200
ROWS = GRP * TP
HALF = FF // 2
COLS = 6144
T_COLS = 1536
F_COLS = 512
TABLE_CHUNKS = (6, 7, 8)
REDUCE_ORDER = (0, 2, 4, 1, 3, 6, 5, 7, 8)
REDUCE_TURNS = (0, 0, 1, 1, 2, 1, 2, 0, 0)
MAIN_WIDTHS = (768, 768, 768, 768, 768, 768, 1024)
MAIN_TURNS = (0, 0, 0, 1, 0, 1, 1)
FRONT_WIDTHS = (384, 128)
FRONT_TURNS = (0, 1)
M_COLS = 4608
MIB = 1 << 20
NORM_ROWS = ROWS
GELU_ROWS = 32

norm_eps = 1e-06
clip_limit = 0.02
beta_one = 0.9
beta_two = 0.999
adam_eps = 1e-08
matrix_rate = 0.08
vector_rate = 0.5
matrix_decay = 0.05

f32 = jnp.float32
bf16 = jnp.bfloat16
MESH = pl.DeviceIdType.MESH
AB = ((1,), (0,))
ABT = ((1,), (1,))
ATB = ((0,), (0,))


def mm(left, right, dims=AB):
    return lax.dot_general(left, right, (dims, ((), ())), preferred_element_type=f32)


def full_spec(shape):
    return pl.BlockSpec(shape, lambda *_: (0,) * len(shape), pipeline_mode=pl.Buffered(1))


def row_loop(total, chunk, body):
    def step(index, carry):
        body(pl.ds(pl.multiple_of(index * chunk, chunk), chunk))
        return carry

    if total == chunk:
        body(slice(0, total))
    else:
        lax.fori_loop(0, total // chunk, step, 0)


def center(x):
    mean = jnp.mean(x, -1, keepdims=True)
    xc = x - mean
    scale = lax.rsqrt(jnp.mean(xc * xc, -1, keepdims=True) + norm_eps)
    return xc * scale, scale


def gelu_pair(x):
    e = jnp.exp2((x * x) * -0.7213475204444817)
    den = 1.0 + 0.23164189 * jnp.abs(x)
    r = pl.reciprocal(den, approx=True)
    r = r * (2.0 - den * r)
    poly = r * (
        0.127414796
        + r * (-0.142248368 + r * (0.7107068705 + r * (-0.7265760135 + r * 0.5307027145)))
    )
    tail = poly * e
    cdf = jnp.where(x > 0.0, 1.0 - tail, tail)
    return x * cdf, cdf + x * (e * 0.3989422804014327)


def partner_place(partner_ref, k):
    images = partner_ref.shape[0]
    n_data = lax.axis_size("dp")
    far = lax.rem(lax.axis_index("dp") + n_data // 2, n_data)
    wanted = far * images + lax.axis_index("mp") * (images // 2) + k
    place = jnp.int32(0)
    for i in range(images):
        place = place + jnp.where(partner_ref[i] == wanted, i, 0)
    return place


def project(pix, w_ref):
    return mm(pix[:, :D], w_ref[0], ABT) + mm(pix[:, D:], w_ref[1], ABT)


def embed_send_kernel(pix_ref, w_ref, send_ref, flat):
    mp = lax.axis_index("mp")
    patches, _, images, _ = pix_ref.shape
    part = patches // 7
    for c in range(7):
        out = project(pix_ref[c * part : (c + 1) * part, mp].reshape(part * images, PD), w_ref)
        for j in range(3):
            flat[j, c * part * images : (c + 1) * part * images] = out[:, 128 * j : 128 * (j + 1)]
    for k in range(images):
        for j in range(3):
            cols = slice(128 * j, 128 * (j + 1))
            send_ref[k, :patches, cols] = flat[j, pl.ds(k, patches, stride=images), :].astype(bf16)
        send_ref[k, patches:] = jnp.zeros((SENT - patches, D), bf16)


def embed_own_kernel(partner_ref, pix_ref, w_ref, own_ref, flat):
    count = partner_ref.shape[0]
    patches = pix_ref.shape[0]
    part = patches // 7
    for c in range(7):
        out = project(pix_ref[c * part : (c + 1) * part].reshape(part * count, PD), w_ref)
        for j in range(3):
            flat[j, c * part * count : (c + 1) * part * count] = out[:, 128 * j : 128 * (j + 1)]
    for k in range(count // 2):
        place = partner_place(partner_ref, k)
        for j in range(3):
            cols = slice(128 * j, 128 * (j + 1))
            own_ref[k, :, cols] = flat[j, pl.ds(place, patches, stride=count), :]


def embed_call(kernel, prefix, pix, weights, shape, dtype, rows, name):
    return pl.pallas_call(
        kernel,
        grid=(1,),
        in_specs=[pl.BlockSpec(memory_space=pltpu.SMEM)] * len(prefix)
        + [full_spec(pix.shape), full_spec(weights.shape)],
        out_specs=full_spec(shape),
        out_shape=jax.ShapeDtypeStruct(shape, dtype),
        scratch_shapes=[pltpu.VMEM((3, rows, 128), f32)],
        compiler_params=pltpu.CompilerParams(vmem_limit_bytes=60 * MIB),
        name=name,
    )(*prefix, pix, weights)


def embed_send(pix, weights):
    images = pix.shape[2]
    shape = (images, SENT, D)
    rows = TP * images
    return embed_call(embed_send_kernel, [], pix, weights, shape, bf16, rows, "embed_sent_images")


def embed_own(partner, pix, weights):
    images = pix.shape[1]
    shape = (images // 2, PATCHES, D)
    rows = TP * images
    return embed_call(
        embed_own_kernel, [partner], pix, weights, shape, f32, rows, "embed_own_images"
    )


def split_tokens(w_ref, col):
    seg = jnp.concatenate([w_ref[0, :, col : col + 128], w_ref[1, :, col : col + 128]], 1)
    return jnp.transpose(seg.astype(f32), (1, 0))


def attend(g, qkv_ref, p_ref, ho_ref):
    rows = slice(g * TP, (g + 1) * TP)
    lane = lax.broadcasted_iota(jnp.int32, (TP, 128), 1)
    key_mask = jnp.where(lax.broadcasted_iota(jnp.int32, (1, TP), 1) < TOK, 0.0, -1e30).astype(f32)
    for j in range(3):
        q = qkv_ref[rows, 128 * j : 128 * (j + 1)]
        k = qkv_ref[rows, D + 128 * j : D + 128 * (j + 1)]
        v = qkv_ref[rows, 2 * D + 128 * j : 2 * D + 128 * (j + 1)]
        outs = []
        for s in range(2):
            mine = (lane < 64) if s == 0 else (lane >= 64)
            scores = mm(jnp.where(mine, q, jnp.zeros_like(q)), k, ABT) + key_mask
            exps = jnp.exp(scores - jnp.max(scores, -1, keepdims=True))
            probs = (exps * (1.0 / jnp.sum(exps, -1, keepdims=True))).astype(bf16)
            p_ref[6 * g + 2 * j + s] = probs
            outs.append(mm(probs, v))
        ho_ref[rows, 128 * j : 128 * (j + 1)] = jnp.where(lane < 64, outs[0], outs[1]).astype(bf16)


PAIRS = (0, 1, 3, 4, 2, 5)


def rounded(x):
    return x.astype(bf16).astype(f32)


def norm_rows(src, gain, shift, dst):
    dst[...] = (center(src[...])[0] * gain + shift).astype(bf16)


def token_row(tok_ref, layer, i):
    at = TP + 6 * layer + i
    return tok_ref[at : at + 1]


def spread_heads(x):
    lane = lax.broadcasted_iota(jnp.int32, x.shape, 1)
    zero = jnp.zeros_like(x)
    return jnp.concatenate(
        [jnp.where((lane >= HD * h) & (lane < HD * (h + 1)), x, zero) for h in range(HEADS)], 0
    )


def gather_heads(x):
    lane = lax.broadcasted_iota(jnp.int32, (ENDS, D), 1)
    total = jnp.zeros((ENDS, D), f32)
    for h in range(HEADS):
        part = x[ENDS * h : ENDS * (h + 1)]
        total = total + jnp.where((lane >= HD * h) & (lane < HD * (h + 1)), part, 0.0)
    return total


def attend_ends(g, kv_ref, q_ref, p_ref, ho_ref):
    rows = slice(g * TP, (g + 1) * TP)
    ends = slice(g * ENDS, (g + 1) * ENDS)
    key_mask = jnp.where(lax.broadcasted_iota(jnp.int32, (1, TP), 1) < TOK, 0.0, -1e30).astype(f32)
    scores = mm(spread_heads(q_ref[ends]), kv_ref[rows, :D], ABT) + key_mask
    exps = jnp.exp(scores - jnp.max(scores, -1, keepdims=True))
    probs = (exps * (1.0 / jnp.sum(exps, -1, keepdims=True))).astype(bf16)
    p_ref[g] = probs
    ho_ref[ends] = gather_heads(mm(probs, kv_ref[rows, D:])).astype(bf16)


def forward_kernel(partner_ref, mix_ref, own_ref, far_ref, t_ref, w_ref, sb_ref, *refs):
    x_ref, mid_ref, qkv_ref, p_ref, ho_ref, hid_ref, gp_ref = refs[:7]
    x1_ref, kv_ref, q1_ref, p1_ref, ho1_ref, mid1_ref, tok_ref = refs[7:14]
    qkv_w, out_w, nbuf, up_s, bias_ref = refs[14:]
    step = pl.program_id(0)

    @pl.when(step == 0)
    def _():
        tok_ref[...] = split_tokens(t_ref, 0)
        for layer in range(LAYERS):
            attn_tiles(w_ref.at[layer], qkv_w.at[layer], out_w.at[layer])
            pieces = [
                sb_ref[h // 3, layer : layer + 1, 128 * (h % 3) + HD * t : 128 * (h % 3) + HD * (t + 1)]
                for t in range(2)
                for h in PAIRS
            ]
            bias_ref[layer : layer + 1] = rounded(jnp.concatenate(pieces, 1))

    def row(layer, i):
        return token_row(tok_ref, layer, i)

    for g in range(F_GRP):
        w = mix_ref[partner_place(partner_ref, step * F_GRP + g)]
        x_ref[g * TP : g * TP + PATCHES] = (
            w * own_ref[g] + (1.0 - w) * far_ref[g, :PATCHES].astype(f32) + tok_ref[:PATCHES]
        )
        x_ref[g * TP + PATCHES : (g + 1) * TP] = tok_ref[PATCHES:TP]
    norm_rows(x_ref, row(0, 0), row(0, 1), nbuf)
    qkv = mm(nbuf[...], qkv_w[0])
    q = qkv[:, :D] + bias_ref[0:1, :D]
    qkv_ref[:, :D] = (q.astype(bf16).astype(f32) * 0.125).astype(bf16)
    qkv_ref[:, D : 2 * D] = qkv[:, D : 2 * D].astype(bf16)
    qkv_ref[:, 2 * D :] = (qkv[:, 2 * D :] + bias_ref[0:1, D : 2 * D]).astype(bf16)
    for g in range(F_GRP):
        attend(g, qkv_ref, p_ref, ho_ref)
    mid_ref[...] = x_ref[...] + mm(ho_ref[...], out_w[0], ABT) + row(0, 4)
    norm_rows(mid_ref, row(0, 2), row(0, 3), nbuf)
    up_w, down_w = w_ref.at[LAYERS], w_ref.at[LAYERS + 1]
    for m in range(2):
        cols = slice(HALF * m, HALF * (m + 1))
        up_s[...] = mm(nbuf[...], up_w[m]) + rounded(sb_ref[m, 0:1, D:])

        def body(rs):
            hid, gp = gelu_pair(up_s[rs])
            hid_ref[rs, cols] = hid.astype(bf16)
            gp_ref[rs, cols] = gp.astype(bf16)

        row_loop(F_GRP * TP, GELU_ROWS, body)
    out = mid_ref[...] + row(0, 5)
    for m in range(2):
        cols = slice(HALF * m, HALF * (m + 1))
        out = out + mm(hid_ref[:, cols], down_w[m], ABT)
    x1_ref[...] = out
    norm_rows(x1_ref, row(1, 0), row(1, 1), nbuf)
    kv = mm(nbuf[...], qkv_w[1, :, D:])
    kv_ref[:, :D] = kv[:, :D].astype(bf16)
    kv_ref[:, D:] = (kv[:, D:] + bias_ref[1:2, D : 2 * D]).astype(bf16)
    ends = jnp.concatenate([nbuf[(g + 1) * TP - ENDS : (g + 1) * TP] for g in range(F_GRP)], 0)
    q = mm(ends, qkv_w[1, :, :D]) + bias_ref[1:2, :D]
    q1_ref[...] = (q.astype(bf16).astype(f32) * 0.125).astype(bf16)
    for g in range(F_GRP):
        attend_ends(g, kv_ref, q1_ref, p1_ref, ho1_ref)
    x_ends = jnp.concatenate([x1_ref[(g + 1) * TP - ENDS : (g + 1) * TP] for g in range(F_GRP)], 0)
    mid1_ref[...] = x_ends + mm(ho1_ref[...], out_w[1], ABT) + row(1, 4)


def kept_shapes(count):
    n = count * TP
    return [
        ((n, D), f32),
        ((n, D), f32),
        ((n, 3 * D), bf16),
        ((count * HEADS, TP, TP), bf16),
        ((n, D), bf16),
        ((n, FF), bf16),
        ((n, FF), bf16),
        ((n, D), f32),
        ((n, 2 * D), bf16),
        ((count * ENDS, D), bf16),
        ((count, HEADS * ENDS, TP), bf16),
        ((count * ENDS, D), bf16),
        ((count * ENDS, D), f32),
    ]


def block_of(shape, steps):
    block = (shape[0] // steps,) + tuple(shape[1:])
    return pl.BlockSpec(block, lambda i: (i,) + (0,) * (len(block) - 1))


def forward(partner, mix, own, far, seg, weights, sb):
    count = own.shape[0]
    steps = count // F_GRP
    outs = kept_shapes(count)
    shapes = [jax.ShapeDtypeStruct(s, t) for s, t in outs] + [jax.ShapeDtypeStruct((256, D), f32)]
    specs = [block_of(s, steps) for s, _ in outs] + [full_spec((256, D))]
    return pl.pallas_call(
        forward_kernel,
        grid=(steps,),
        in_specs=[
            pl.BlockSpec(memory_space=pltpu.SMEM),
            pl.BlockSpec(memory_space=pltpu.SMEM),
            block_of(own.shape, steps),
            block_of(far.shape, steps),
            full_spec(seg.shape),
            pl.BlockSpec((4, 2, D, 768), lambda i: (0, 0, 0, 0), pipeline_mode=pl.Buffered(1)),
            full_spec(sb.shape),
        ],
        out_specs=specs,
        out_shape=shapes,
        scratch_shapes=[
            pltpu.VMEM((LAYERS, D, 3 * D), bf16),
            pltpu.VMEM((LAYERS, D, D), bf16),
            pltpu.VMEM((F_GRP * TP, D), bf16),
            pltpu.VMEM((F_GRP * TP, HALF), f32),
            pltpu.VMEM((LAYERS, 2 * D), f32),
        ],
        compiler_params=pltpu.CompilerParams(vmem_limit_bytes=60 * MIB),
        name="forward_layers",
    )(partner, mix, own, far, seg, weights, sb)


def norm_back(dy, xhat, scale, gain):
    dyg = dy * gain
    c1 = jnp.mean(dyg, -1, keepdims=True)
    c2 = jnp.mean(dyg * xhat, -1, keepdims=True)
    return scale * (dyg - c1 - xhat * c2)


def share(part, own_ref, mate_ref, mp):
    own_ref[...] = part[mp]
    mate_ref[...] = part[1 - mp].astype(bf16)


def head_kernel(
    partner_ref,
    mix_ref,
    label_ref,
    teacher_ref,
    mid_ref,
    wf_ref,
    w_ref,
    sb_ref,
    hb_ref,
    cw_ref,
    tok_ref,
    uo_ref,
    um_ref,
    do_ref,
    dm_ref,
    ho_ref,
    hm_ref,
    dz_ref,
    gv_ref,
    gu_ref,
    dhb_ref,
    stat_ref,
    lanes,
    g_ffw,
    g_head,
):
    mp = lax.axis_index("mp")
    gain2, shift2, bias_f = (token_row(tok_ref, 1, i) for i in (2, 3, 5))
    gain, shift = (token_row(tok_ref, 2, i) for i in range(2))
    count = mid_ref.shape[0] // ENDS
    images = partner_ref.shape[0]
    n_data = lax.axis_size("dp")
    dp = lax.axis_index("dp")
    far_base = lax.rem(dp + n_data // 2, n_data) * images + mp * count
    marks = []
    for k in range(count):
        place = partner_place(partner_ref, k)
        marks.append(
            (
                label_ref[dp * images + place],
                label_ref[far_base + k],
                teacher_ref[place],
                mix_ref[place],
            )
        )
    for j in range(3):
        lanes[j, : mid_ref.shape[0]] = mid_ref[:, 128 * j : 128 * (j + 1)]
    mid = jnp.concatenate(
        [
            jnp.concatenate(
                [lanes[j, pl.ds(END_AT + h, count, stride=ENDS), :] for j in range(3)], 1
            )
            for h in range(2)
        ],
        0,
    )
    xhat2, scale2 = center(mid)
    normed = (xhat2 * gain2 + shift2).astype(bf16)
    out = mid + bias_f
    hids, gps = [], []
    for m in range(2):
        up = mm(normed, wf_ref[0, m]) + rounded(sb_ref[m, 1:2, D:])
        hid, gp = gelu_pair(up)
        hids.append(hid.astype(bf16))
        gps.append(gp)
        out = out + mm(hids[m], wf_ref[1, m], ABT)
    xhat, scale = center(out)
    final = (xhat * gain + shift).astype(bf16)
    loss = jnp.zeros((1, 1), f32)
    weight = jnp.zeros((1, 1), f32)
    dfinals = []
    for h in range(2):
        mine = final[count * h : count * (h + 1)]
        halves = []
        for m in range(2):
            wh = w_ref[m, :, 512 * h : 512 * (h + 1)]
            at = 1024 * h + 512 * m
            logits = mm(mine, wh) + hb_ref[0:1, at : at + 512]
            ids = lax.broadcasted_iota(jnp.int32, (1, 512), 1) + 512 * m
            shares = []
            for k in range(count):
                first, second, teach, mix = marks[k]
                if h == 0:
                    both = jnp.where(ids == first, mix, 0.0) + jnp.where(ids == second, 1.0 - mix, 0.0)
                    shares.append(both)
                else:
                    shares.append(jnp.where(ids == teach, 1.0, 0.0))
            coef = jnp.concatenate(shares, 0) * cw_ref[0:1, 512 * m : 512 * (m + 1)]
            halves.append((wh, logits, coef))
        top = jnp.maximum(*[jnp.max(x[1], -1, keepdims=True) for x in halves])
        exps = [jnp.exp(x[1] - top) for x in halves]
        total = sum(jnp.sum(x, -1, keepdims=True) for x in exps)
        lse = top + jnp.log(total)
        csum = sum(jnp.sum(x[2], -1, keepdims=True) for x in halves)
        dfinal = jnp.zeros((count, D), f32)
        for m in range(2):
            wh, logits, coef = halves[m]
            loss = loss + jnp.sum(jnp.sum(coef * (lse - logits), -1, keepdims=True), 0, keepdims=True)
            dl = csum * (exps[m] / total) - coef
            at = 1024 * h + 512 * m
            dhb_ref[0:1, at : at + 512] = jnp.sum(dl, 0, keepdims=True)
            low = dl.astype(bf16)
            g_head[m, :, 512 * h : 512 * (h + 1)] = mm(mine, low, ATB)
            dfinal = dfinal + mm(low, wh, ABT)
        weight = weight + jnp.sum(csum, 0, keepdims=True)
        dfinals.append(dfinal)
    dfinal = jnp.concatenate(dfinals, 0)
    dz = norm_back(dfinal, xhat, scale, gain)
    low = dz.astype(bf16)
    dn = jnp.zeros_like(dz)
    for m in range(2):
        dh = mm(low, wf_ref[1, m])
        du = (dh.astype(bf16).astype(f32) * gps[m]).astype(bf16)
        gu_ref[0:1, HALF * m : HALF * (m + 1)] = jnp.sum(du.astype(f32), 0, keepdims=True)
        g_ffw[0, m] = mm(normed, du, ATB)
        g_ffw[1, m] = mm(low, hids[m], ATB)
        dn = dn + mm(du, wf_ref[0, m], ABT)
    dmid = dz + norm_back(dn, xhat2, scale2, gain2)
    gv_ref[...] = jnp.zeros_like(gv_ref)
    sums = [dn * xhat2, dn, dmid, dz, dfinal * xhat, dfinal]
    for i, item in enumerate(sums):
        gv_ref[i + 2 : i + 3] = jnp.sum(item, 0, keepdims=True)
    lanes[...] = jnp.zeros_like(lanes)
    for j in range(3):
        for h in range(2):
            lanes[j, pl.ds(END_AT + h, count, stride=ENDS), :] = dmid[
                count * h : count * (h + 1), 128 * j : 128 * (j + 1)
            ]
        dz_ref[:, 128 * j : 128 * (j + 1)] = lanes[j, : dz_ref.shape[0]]
    which = lax.broadcasted_iota(jnp.int32, stat_ref.shape, 1)
    stat_ref[...] = jnp.where(which == 0, loss, jnp.where(which == 1, weight, 0.0))
    share(g_ffw.at[0], uo_ref, um_ref, mp)
    share(g_ffw.at[1], do_ref, dm_ref, mp)
    share(g_head, ho_ref, hm_ref, mp)


def pair_shapes(shapes):
    return [jax.ShapeDtypeStruct(s, t) for s in shapes for t in (f32, bf16)]


def head(partner, mix, labels, teacher, mid, weights, w_heads, sb, hb, cw, tok):
    outs = pair_shapes([(D, 768), (D, 768), (D, 1024)]) + [
        jax.ShapeDtypeStruct(s, f32)
        for s in (mid.shape, (8, D), (1, FF), (1, 2048), (1, 128))
    ]
    return pl.pallas_call(
        head_kernel,
        grid=(1,),
        in_specs=[pl.BlockSpec(memory_space=pltpu.SMEM)] * 4
        + [
            full_spec(mid.shape),
            pl.BlockSpec((2, 2, D, 768), lambda i: (2, 0, 0, 0), pipeline_mode=pl.Buffered(1)),
        ]
        + [full_spec(x.shape) for x in (w_heads, sb, hb, cw, tok)],
        out_specs=[full_spec(x.shape) for x in outs],
        out_shape=outs,
        scratch_shapes=[
            pltpu.VMEM((3, mid.shape[0] + 2 * ENDS, 128), f32),
            pltpu.VMEM((2, 2, D, 768), f32),
            pltpu.VMEM((2, D, 1024), f32),
        ],
        compiler_params=pltpu.CompilerParams(vmem_limit_bytes=60 * MIB),
        name="loss_heads",
    )(partner, mix, labels, teacher, mid, weights, w_heads, sb, hb, cw, tok)


def attend_back(g, dho, qkv_ref, p_ref, dproj):
    rows = slice(g * TP, (g + 1) * TP)
    lane = lax.broadcasted_iota(jnp.int32, (TP, 128), 1)
    for j in range(3):
        q = qkv_ref[rows, 128 * j : 128 * (j + 1)]
        k = qkv_ref[rows, D + 128 * j : D + 128 * (j + 1)]
        v = qkv_ref[rows, 2 * D + 128 * j : 2 * D + 128 * (j + 1)]
        do = dho[rows, 128 * j : 128 * (j + 1)]
        qt, kt, dot_ = (jnp.transpose(a, (1, 0)) for a in (q, k, do))
        for s in range(2):
            mine = (lane < 64) if s == 0 else (lane >= 64)
            sub = slice(64 * s, 64 * (s + 1))
            at = 128 * j + 64 * s
            probs = p_ref[6 * g + 2 * j + s]
            dproj[g, 2 * D + at : 2 * D + at + 64] = mm(dot_[sub], probs).astype(bf16)
            dprob = mm(jnp.where(mine, do, jnp.zeros_like(do)), v, ABT)
            p32 = probs.astype(f32)
            delta = jnp.sum(dprob * p32, -1, keepdims=True)
            ds = (p32 * (dprob - delta)).astype(bf16)
            dproj[g, at : at + 64] = (mm(kt[sub], ds, ABT) * 0.125).astype(bf16)
            dproj[g, D + at : D + at + 64] = mm(qt[sub], ds).astype(bf16)


def ends_back(g, dho, kv_ref, q_ref, p_ref, dq, dproj):
    rows = slice(g * TP, (g + 1) * TP)
    ends = slice(g * ENDS, (g + 1) * ENDS)
    q = spread_heads(q_ref[ends])
    do = spread_heads(dho[ends])
    probs = p_ref[g]
    dprob = mm(do, kv_ref[rows, D:], ABT)
    p32 = probs.astype(f32)
    delta = jnp.sum(dprob * p32, -1, keepdims=True)
    ds = (p32 * (dprob - delta)).astype(bf16)
    dq[ends] = (gather_heads(mm(ds, kv_ref[rows, :D])) * 0.125).astype(bf16)
    dproj[g, :D] = mm(q, ds, ATB).astype(bf16)
    dproj[g, D : 2 * D] = mm(do, probs, ATB).astype(bf16)


def backward_kernel(
    dz_ref,
    x_ref,
    mid_ref,
    qkv_ref,
    p_ref,
    ho_ref,
    hid_ref,
    gp_ref,
    x1_ref,
    kv_ref,
    q1_ref,
    p1_ref,
    ho1_ref,
    wa_ref,
    wf_ref,
    tok_ref,
    dzo_ref,
    a0o_ref,
    a0m_ref,
    a1o_ref,
    a1m_ref,
    uo_ref,
    um_ref,
    do_ref,
    dm_ref,
    gv_ref,
    gb_ref,
    gu_ref,
    qkv_w,
    out_w,
    dqkv,
    dkv,
    dq1,
    dout,
    g_ffw,
    g_att,
    nbuf,
    dz,
    dn,
    du,
    dq,
    dproj,
):
    step = pl.program_id(0)
    mp = lax.axis_index("mp")

    def row(layer, i):
        return token_row(tok_ref, layer, i)

    @pl.when(step == 0)
    def _():
        for ref in (gv_ref, gb_ref, gu_ref, g_ffw, dqkv, dkv, dq1, dout):
            ref[...] = jnp.zeros_like(ref)
        nbuf[:, D:] = jnp.ones((ROWS, 128), bf16)
        for layer in range(LAYERS):
            attn_tiles(wa_ref.at[layer], qkv_w.at[layer], out_w.at[layer])

    def pull(src, gain, dz_out, at):
        xhat, scale = center(src[...])
        dy = dn[...]
        new = dz[...] + norm_back(dy, xhat, scale, gain)
        dz_out[...] = new
        gv_ref[at : at + 1] += jnp.sum(dy * xhat, 0, keepdims=True)
        gv_ref[at + 1 : at + 2] += jnp.sum(dy, 0, keepdims=True)

    normed = nbuf.at[:, :D]
    low = dz_ref[...].astype(bf16)
    dout[1] += mm(low, ho1_ref[...], ATB)
    dho = mm(low, out_w[1]).astype(bf16)
    norm_rows(x1_ref, row(1, 0), row(1, 1), normed)
    dz[...] = jnp.zeros_like(dz)
    for g in range(GRP):
        rows = slice(g * TP, (g + 1) * TP)
        ends_back(g, dho, kv_ref, q1_ref, p1_ref, dq, dproj)
        dkv[...] += mm(dproj[g, : 2 * D], nbuf[rows])
        dn[rows] = jnp.transpose(mm(qkv_w[1, :, D:], dproj[g, : 2 * D]), (1, 0))
    dq_all = dq[...]
    ends = jnp.concatenate([nbuf[(g + 1) * TP - ENDS : (g + 1) * TP, :D] for g in range(GRP)], 0)
    dq1[...] += mm(ends, dq_all, ATB)
    gb_ref[1:2, :D] += jnp.sum(dq_all.astype(f32), 0, keepdims=True)
    more = mm(dq_all, qkv_w[1, :, :D], ABT)
    for g in range(GRP):
        last = slice((g + 1) * TP - ENDS, (g + 1) * TP)
        part = slice(g * ENDS, (g + 1) * ENDS)
        dn[last] += more[part]
        dz[last] = dz_ref[part]
    pull(x1_ref, row(1, 0), dz, 6)

    norm_rows(mid_ref, row(0, 2), row(0, 3), normed)
    gv_ref[5:6] += jnp.sum(dz[...], 0, keepdims=True)
    rz = dz[...].astype(bf16)
    rzt = jnp.transpose(rz, (1, 0))
    nt = jnp.transpose(nbuf[:, :D], (1, 0))
    for m in range(2):
        cols = slice(HALF * m, HALF * (m + 1))
        dh = mm(rz, wf_ref[1, m])
        du[...] = (dh.astype(bf16).astype(f32) * gp_ref[:, cols].astype(f32)).astype(bf16)
        gu_ref[0:1, cols] += jnp.sum(du[...].astype(f32), 0, keepdims=True)
        g_ffw[1, m] += mm(rzt, hid_ref[:, cols])
        g_ffw[0, m] += mm(nt, du[...])
        part = mm(du[...], wf_ref[0, m], ABT)
        dn[...] = part if m == 0 else dn[...] + part
    pull(mid_ref, row(0, 2), dz, 2)
    gv_ref[4:5] += jnp.sum(dz[...], 0, keepdims=True)
    rz2 = dz[...].astype(bf16)
    dout[0] += mm(jnp.transpose(rz2, (1, 0)), ho_ref[...])
    dho = mm(rz2, out_w[0]).astype(bf16)
    norm_rows(x_ref, row(0, 0), row(0, 1), normed)
    for g in range(GRP):
        rows = slice(g * TP, (g + 1) * TP)
        attend_back(g, dho, qkv_ref, p_ref, dproj)
        dqkv[...] += mm(dproj[g], nbuf[rows])
        dn[rows] = jnp.transpose(mm(qkv_w[0], dproj[g]), (1, 0))
    pull(x_ref, row(0, 0), dzo_ref, 0)

    @pl.when(step == pl.num_programs(0) - 1)
    def _():
        for layer in range(LAYERS):
            for t in range(4):
                for j in range(3):
                    at = D * t + 128 * j
                    if t == 3:
                        tile = dout[layer, :, 128 * j : 128 * (j + 1)]
                    elif layer == 0:
                        tile = jnp.transpose(dqkv[at : at + 128, :D], (1, 0))
                    elif t == 0:
                        tile = dq1[:, 128 * j : 128 * (j + 1)]
                    else:
                        tile = jnp.transpose(dkv[at - D : at - D + 128, :D], (1, 0))
                    if j < 2:
                        g_att[layer, j, :, 128 * t : 128 * (t + 1)] = tile
                    else:
                        for m in range(2):
                            lo = 512 + 64 * t
                            g_att[layer, m, :, lo : lo + 64] = tile[:, 64 * m : 64 * (m + 1)]
        share(g_att.at[0], a0o_ref, a0m_ref, mp)
        share(g_att.at[1], a1o_ref, a1m_ref, mp)
        share(g_ffw.at[0], uo_ref, um_ref, mp)
        share(g_ffw.at[1], do_ref, dm_ref, mp)
        sums = jnp.transpose(dqkv[:, D:], (1, 0))[0:1]
        gb_ref[0:1, :D] = sums[:, :D]
        gb_ref[0:1, D:] = sums[:, 2 * D :]
        gb_ref[1:2, D:] = jnp.transpose(dkv[:, D:], (1, 0))[0:1, D:]


def attn_tiles(w_ref, qkv_w, out_w):
    for t in range(4):
        cols = 128 * t
        pieces = [w_ref[0, :, cols : cols + 128], w_ref[1, :, cols : cols + 128]]
        tile = 512 + 128 * (t // 2)
        lane = 64 * (t % 2)
        pieces.append(
            jnp.concatenate(
                [w_ref[m, :, tile : tile + 128][:, lane : lane + 64] for m in range(2)], 1
            )
        )
        for j in range(3):
            if t < 3:
                at = D * t + 128 * j
                qkv_w[:, at : at + 128] = pieces[j]
            else:
                out_w[:, 128 * j : 128 * (j + 1)] = pieces[j]


def backward(dz, kept, weights, tok):
    steps = dz.shape[0] // (GRP * ENDS)
    x_shape = kept[0].shape
    shares = pair_shapes([(D, 768)] * 4)
    extra = [jax.ShapeDtypeStruct(s, f32) for s in ((8, D), (2, 2 * D), (1, FF))]
    return pl.pallas_call(
        backward_kernel,
        grid=(steps,),
        in_specs=[block_of(a.shape, steps) for a in (dz,) + tuple(kept)]
        + [
            pl.BlockSpec((2, 2, D, 768), lambda i: (0, 0, 0, 0), pipeline_mode=pl.Buffered(1)),
            pl.BlockSpec((2, 2, D, 768), lambda i: (1, 0, 0, 0), pipeline_mode=pl.Buffered(1)),
            full_spec(tok.shape),
        ],
        out_specs=[block_of(x_shape, steps)] + [full_spec(x.shape) for x in shares + extra],
        out_shape=[jax.ShapeDtypeStruct(x_shape, f32)] + shares + extra,
        scratch_shapes=[
            pltpu.VMEM((LAYERS, D, 3 * D), bf16),
            pltpu.VMEM((LAYERS, D, D), bf16),
            pltpu.VMEM((3 * D, 512), f32),
            pltpu.VMEM((2 * D, 512), f32),
            pltpu.VMEM((D, D), f32),
            pltpu.VMEM((LAYERS, D, D), f32),
            pltpu.VMEM((2, 2, D, 768), f32),
            pltpu.VMEM((LAYERS, 2, D, 768), f32),
            pltpu.VMEM((ROWS, D + 128), bf16),
            pltpu.VMEM((ROWS, D), f32),
            pltpu.VMEM((ROWS, D), f32),
            pltpu.VMEM((ROWS, HALF), bf16),
            pltpu.VMEM((GRP * ENDS, D), bf16),
            pltpu.VMEM((GRP, 3 * D, TP), bf16),
        ],
        compiler_params=pltpu.CompilerParams(vmem_limit_bytes=62 * MIB),
        name="backward_layers",
    )(dz, *kept, weights, weights, tok)


def patch_grad_kernel(
    partner_ref,
    mix_ref,
    dz_ref,
    own_ref,
    far_ref,
    gvb_ref,
    gvh_ref,
    po_ref,
    pm_ref,
    eo_ref,
    em_ref,
    dzo,
    dzf,
    tok,
    g_patch,
    g_seg,
):
    mp = lax.axis_index("mp")
    count = far_ref.shape[0] // PATCHES
    both = own_ref.shape[0] // PATCHES
    dzo[...] = jnp.zeros_like(dzo)
    total = jnp.zeros((TP, D), f32)
    for k in range(count):
        place = partner_place(partner_ref, k)
        w = mix_ref[place]
        for j in range(3):
            part = dz_ref[k * TP : k * TP + PATCHES, 128 * j : 128 * (j + 1)]
            dzo[j, pl.ds(place, PATCHES, stride=both), :] = w * part
            dzf[j, pl.ds(k, PATCHES, stride=count), :] = (1.0 - w) * part
        total = total + dz_ref[k * TP : (k + 1) * TP]
    tok[...] = jnp.zeros_like(tok)
    tok[:TP] = total
    tok[TP : TP + 8] = gvb_ref[...]
    tok[TP + 8 : TP + 14] = gvh_ref[2:8]
    turned = jnp.transpose(tok[...], (1, 0))
    for m in range(2):
        g_seg[m] = turned[:, 128 * m : 128 * (m + 1)]
    lo, lf = (
        jnp.concatenate([jnp.transpose(ref[j, :rows].astype(bf16), (1, 0)) for j in range(3)], 0)
        for ref, rows in ((dzo, own_ref.shape[0]), (dzf, far_ref.shape[0]))
    )
    for m in range(2):
        cols = slice(D * m, D * (m + 1))
        g_patch[m] = mm(lo, own_ref[:, cols]) + mm(lf, far_ref[:, cols])
    share(g_patch, po_ref, pm_ref, mp)
    share(g_seg, eo_ref, em_ref, mp)


def patch_grad(partner, mix, dz, own, far, gvb, gvh):
    outs = pair_shapes([(D, D), (D, 128)])
    return pl.pallas_call(
        patch_grad_kernel,
        grid=(1,),
        in_specs=[pl.BlockSpec(memory_space=pltpu.SMEM)] * 2
        + [full_spec(a.shape) for a in (dz, own, far, gvb, gvh)],
        out_specs=[full_spec(x.shape) for x in outs],
        out_shape=outs,
        scratch_shapes=[
            pltpu.VMEM((3, own.shape[0] // PATCHES * TP, 128), f32),
            pltpu.VMEM((3, far.shape[0] // PATCHES * TP, 128), f32),
            pltpu.VMEM((256, D), f32),
            pltpu.VMEM((2, D, D), f32),
            pltpu.VMEM((2, D, 128), f32),
        ],
        compiler_params=pltpu.CompilerParams(vmem_limit_bytes=56 * MIB),
        name="patch_gradient",
    )(partner, mix, dz, own, far, gvb, gvh)


def link_orders(bits):
    far = [b for b in (range(1, bits, 2) if bits == 6 else [3]) if b < bits]
    near = [b for b in range(bits) if b not in far]
    return [near[i:] + near[:i] for i in range(len(near))], far


def gather_plan(bits, turns):
    near, far = link_orders(bits)
    deep = far + [near[0][-1]]
    flat = near[0][:-1]
    return [flat[t:] + flat[:t] for t in turns], deep


def chunk_plan(bits, cuts):
    near, far = link_orders(bits)
    return [
        (cuts[i], cuts[i + 1] - cuts[i], near[i % len(near)], far) for i in range(len(cuts) - 1)
    ]


def mesh_place():
    return lax.axis_index("dp"), lax.axis_index("mp")


def bit_of(value, bit):
    return (value // 2**bit) % 2


def flipped(value, bit):
    return value + 2**bit * (1 - 2 * bit_of(value, bit))


def meet(bits):
    dp, mp = mesh_place()
    barrier = pltpu.get_barrier_semaphore()
    for peer in [(dp, 1 - mp)] + [(flipped(dp, b), mp) for b in range(bits)]:
        pl.semaphore_signal(barrier, inc=1, device_id=peer, device_id_type=MESH)
    pl.semaphore_wait(barrier, bits + 1)


def push(src, dst, send, recv, peer):
    copy = pltpu.make_async_remote_copy(
        src_ref=src, dst_ref=dst, send_sem=send, recv_sem=recv, device_id=peer, device_id_type=MESH
    )
    copy.start()
    return copy


def held_part(ref, bits, lead, dp, done=(), flip=None):
    idx = list(lead)
    for b in reversed(bits):
        mine = bit_of(dp, b)
        idx.append(pl.ds(0, 2) if b in done else (1 - mine if b == flip else mine))
    return ref.at[tuple(idx)]


def gather_front_kernel(bits, tab_ref, main_ref, sb_ref, *refs):
    w_refs = refs[:2]
    far_refs = refs[2:4]
    sbo_ref, tabr, stage_p, stage_e, stage_h, s_loc, s_tab = refs[4:11]
    s_send, s_recv, f_send, f_recv, m_send, m_recv = refs[11:]
    dp, mp = mesh_place()
    mate = (dp, 1 - mp)
    turns, deep = gather_plan(bits, FRONT_TURNS)
    every = list(range(bits))

    far = deep[:-1]
    wide = {}

    def part(c, *args):
        return held_part(w_refs[c], every, (mp,), dp, *args)

    def main(c, *args):
        return held_part(far_refs[c], far, (), dp, *args)

    meet(bits)
    c_tab = push(tab_ref.at[1 - mp], tabr, s_tab.at[0], s_tab.at[1], mate)
    c_sb = push(sb_ref, sbo_ref.at[mp], s_tab.at[2], s_tab.at[3], mate)
    local = [pltpu.make_async_copy(sb_ref, sbo_ref.at[mp], s_loc.at[0])]
    local[0].start()
    c_tab.wait()
    mine = tab_ref[mp].astype(f32)
    other = tabr[...].astype(f32)
    first = jnp.where(mp == 0, mine, other)
    second = jnp.where(mp == 0, other, mine)
    table = jnp.concatenate([first, second], 0).astype(bf16)
    stage_p[...] = table[:, :D]
    stage_e[...] = table[:, D:F_COLS]
    stage_h[...] = table[:, F_COLS:]
    stages = (stage_p, stage_e)
    wides = (main_ref, stage_h)
    copies = {}
    forwards = []
    for s in range(bits + 1):
        for c in range(2):
            order = deep + turns[c]
            if s:
                copies[c, s - 1].wait_recv()
            if s < bits:
                held = part(c, order[:s])
                copies[c, s] = push(
                    held if s else stages[c],
                    held,
                    s_send.at[c, s],
                    s_recv.at[c, s],
                    (flipped(dp, order[s]), mp),
                )
            got = part(c, order[: s - 1], order[s - 1]) if s else part(c)
            forwards.append(
                push(got if s else stages[c], got, f_send.at[c, s], f_recv.at[c, s], mate)
            )
        if s == 0:
            for c in range(2):
                local.append(pltpu.make_async_copy(stages[c], part(c), s_loc.at[c + 1]))
                local[-1].start()
                local.append(pltpu.make_async_copy(wides[c], main(c), s_loc.at[c + 3]))
                local[-1].start()
            for copy in local:
                copy.wait()
        at = s - len(deep) + 1
        if 0 <= at < len(far):
            for c in range(2):
                if at:
                    wide[c, at - 1].wait_recv()
                dst = main(c, far[:at])
                wide[c, at] = push(
                    dst if at else wides[c],
                    dst,
                    m_send.at[c, at],
                    m_recv.at[c, at],
                    (flipped(dp, far[at]), mp),
                )
    for copy in forwards:
        copy.wait()
    for copy in copies.values():
        copy.wait_send()
    for copy in wide.values():
        copy.wait_send()
    for c in range(2):
        wide[c, len(far) - 1].wait_recv()
    c_sb.wait()


def gather_front(tab, shard, sb, n_data):
    bits = n_data.bit_length() - 1
    rows = D // n_data
    _, far = link_orders(bits)
    deep_shape = (2,) * len(far)
    sems = pltpu.SemaphoreType.DMA
    anywhere = pl.BlockSpec(memory_space=pl.ANY)
    inside = pl.BlockSpec(memory_space=pltpu.VMEM)
    return pl.pallas_call(
        functools.partial(gather_front_kernel, bits),
        in_specs=[inside] * 3,
        out_specs=[anywhere] * 4 + [inside],
        out_shape=[
            jax.ShapeDtypeStruct((2,) * (bits + 1) + (rows, w), bf16) for w in FRONT_WIDTHS
        ]
        + [
            jax.ShapeDtypeStruct(deep_shape + shard.shape, bf16),
            jax.ShapeDtypeStruct(deep_shape + (rows, T_COLS - F_COLS), bf16),
            jax.ShapeDtypeStruct((2,) + sb.shape, f32),
        ],
        scratch_shapes=[
            pltpu.VMEM(tab.shape[1:], bf16),
            pltpu.VMEM((rows, FRONT_WIDTHS[0]), bf16),
            pltpu.VMEM((rows, FRONT_WIDTHS[1]), bf16),
            pltpu.VMEM((rows, T_COLS - F_COLS), bf16),
            sems((5,)),
            sems((4,)),
            sems((2, bits)),
            sems((2, bits)),
            sems((2, bits + 1)),
            sems((2, bits + 1)),
            sems((2, len(far))),
            sems((2, len(far))),
        ],
        compiler_params=pltpu.CompilerParams(
            collective_id=2, has_side_effects=True, vmem_limit_bytes=60 * MIB
        ),
        name="gather_front",
    )(tab, shard, sb)


def gather_main_kernel(bits, *refs):
    turns, deep = gather_plan(bits, MAIN_TURNS)
    far, last = deep[:-1], deep[-1]
    mains, heads, pix_ref = refs[:2], refs[2:4], refs[4]
    w_ref, h_ref, mine_ref = refs[5:8]
    pix, s_pix, s_loc, s_send, s_recv, f_send, f_recv = refs[8:]
    dp, mp = mesh_place()
    mate = (dp, 1 - mp)
    every = list(range(bits))
    steps = bits - len(deep)
    chunks = len(MAIN_WIDTHS)

    def lead(c):
        return (w_ref, (c, mp)) if c < chunks - 1 else (h_ref, (mp,))

    def part(c, *args):
        return held_part(lead(c)[0], every, lead(c)[1], dp, *args)

    meet(bits)
    pix_in = pltpu.make_async_copy(pix_ref.at[:, mp], pix, s_pix.at[0])
    pix_in.start()
    copies = {}
    forwards = []
    local = []
    for c in range(chunks):
        for i, dst in enumerate((part(c, far), part(c, far, last))):
            lead_cut = (slice(None),) * len(far) + (c,)
            src = mains[i].at[lead_cut] if c < chunks - 1 else heads[i]
            local.append(pltpu.make_async_copy(src, dst, s_loc.at[c, i]))
            local[-1].start()
    pix_in.wait()
    pix_out = pltpu.make_async_copy(pix, mine_ref, s_pix.at[1])
    pix_out.start()
    for s in range(steps + 1):
        for c in range(chunks):
            order = turns[c]
            if s:
                copies[c, s - 1].wait_recv()
            else:
                for copy in local[2 * c : 2 * c + 2]:
                    copy.wait()
            done = deep + order[:s]
            if s < steps:
                held = part(c, done)
                copies[c, s] = push(
                    held, held, s_send.at[c, s], s_recv.at[c, s], (flipped(dp, order[s]), mp)
                )
            got = part(c, done[:-1], done[-1]) if s else part(c, done)
            forwards.append(push(got, got, f_send.at[c, s], f_recv.at[c, s], mate))
    for copy in forwards:
        copy.wait()
    for copy in copies.values():
        copy.wait_send()
    pix_out.wait()


def gather_main(mains, heads, pix, n_data):
    bits = n_data.bit_length() - 1
    rows = D // n_data
    near, _ = link_orders(bits)
    steps = len(near[0]) - 1
    chunks = len(MAIN_WIDTHS)
    sems = pltpu.SemaphoreType.DMA
    anywhere = pl.BlockSpec(memory_space=pl.ANY)
    inside = pl.BlockSpec(memory_space=pltpu.VMEM)
    places = (2,) * (bits + 1) + (rows,)
    mine = pix.shape[:1] + pix.shape[2:]
    main, head_w, pix_mine = pl.pallas_call(
        functools.partial(gather_main_kernel, bits),
        in_specs=[inside] * (2 * len(mains)) + [anywhere],
        out_specs=[anywhere] * 3,
        out_shape=[
            jax.ShapeDtypeStruct((chunks - 1,) + places + (768,), bf16),
            jax.ShapeDtypeStruct(places + (1024,), bf16),
            jax.ShapeDtypeStruct(mine, bf16),
        ],
        scratch_shapes=[
            pltpu.VMEM(mine, bf16),
            sems((2,)),
            sems((chunks, len(mains))),
            sems((chunks, steps)),
            sems((chunks, steps)),
            sems((chunks, steps + 1)),
            sems((chunks, steps + 1)),
        ],
        compiler_params=pltpu.CompilerParams(
            collective_id=0, has_side_effects=True, vmem_limit_bytes=60 * MIB
        ),
        cost_estimate=pl.CostEstimate(flops=0, bytes_accessed=150 * MIB, transcendentals=0),
        name="gather_main",
    )(*mains, *heads, pix)
    return main.reshape(chunks - 1, 2, D, 768), head_w.reshape(2, D, 1024), pix_mine


def reduce_plan(bits, turns):
    near, far = link_orders(bits)
    return [near[t % len(near)] + far for t in turns]


def block_index(free, fixed):
    def index(t):
        total = fixed
        for j, b in enumerate(free):
            total = total + ((t // 2**j) % 2) * 2**b
        return total

    return index


def reduce_kernel(bits, widths, turns, *refs):
    n = len(widths)
    own, mate_src = refs[:n], refs[n : 2 * n]
    smalls = refs[2 * n : 2 * n + 5]
    outs = refs[2 * n + 5 : 3 * n + 5]
    obun_ref, info_ref = refs[3 * n + 5 : 3 * n + 7]
    refs = refs[3 * n + 7 :]
    mrecv, acc, held = refs[:n], refs[n : 2 * n], refs[2 * n : 3 * n]
    refs = refs[3 * n :]
    sbufs, rbufs = refs[: n * bits], refs[n * bits : 2 * n * bits]
    bun, bunr, tsend, sq, sqr, o_sem, m_sem, s_sem, r_sem, b_sem, q_sem, t_sem = refs[2 * n * bits :]
    dp, mp = mesh_place()
    mate = (dp, 1 - mp)
    orders = reduce_plan(bits, turns)
    rows = D // 2**bits
    group = max(rows, 48)
    per = group // rows
    small = rows // 2

    loads = {}
    for c in REDUCE_ORDER:
        loads[c] = pltpu.make_async_copy(own[c], held[c], o_sem.at[c])
        loads[c].start()
    at = 0
    for ref in smalls:
        for i in range(ref.shape[0]):
            bun[:, at : at + ref.shape[1]] = ref[i : i + 1]
            at += ref.shape[1]
    meet(bits)
    mcopies = {
        c: push(mate_src[c], mrecv[c], m_sem.at[c, 0], m_sem.at[c, 1], mate) for c in REDUCE_ORDER
    }
    bcopies = [push(bun, bunr.at[0], b_sem.at[0, 0], b_sem.at[0, 1], mate)]

    def loop(total, body):
        def step(t, carry):
            body(t)
            return carry

        lax.fori_loop(0, total, step, 0)

    copies = {}

    def split(order, s, sent):
        free = [b for b in range(bits) if b not in order[: s + 1]]
        fixed = sum((bit_of(dp, b) * 2**b for b in order[:s]), 0)
        last = bit_of(dp, order[s])
        fixed = fixed + (1 - last if sent else last) * 2 ** order[s]
        return 2 ** len(free), block_index(free, fixed)

    def send_stage(c, s):
        total, index = split(orders[c], s, True)
        sbuf = sbufs[c * bits + s]

        def body(t):
            sbuf[t] = acc[c][index(t)].astype(bf16)

        loop(total, body)
        copies[c, s] = push(
            sbuf,
            rbufs[c * bits + s],
            s_sem.at[c, s],
            r_sem.at[c, s],
            (flipped(dp, orders[c][s]), mp),
        )

    def take_stage(c, s):
        copies[c, s].wait_recv()
        total, index = split(orders[c], s, False)
        rbuf = rbufs[c * bits + s]

        def body(t):
            acc[c][index(t)] += rbuf[t].astype(f32)

        loop(total, body)

    for c in REDUCE_ORDER:
        loads[c].wait()
        mcopies[c].wait_recv()

        def body(b):
            rs = pl.ds(pl.multiple_of(b * group, group), group)
            got = held[c][rs] + mrecv[c][rs].astype(f32)
            for i in range(per):
                acc[c][b * per + i] = got[rows * i : rows * (i + 1)]

        loop(D // group, body)
        send_stage(c, 0)
    for s in range(1, bits + 1):
        for c in REDUCE_ORDER:
            take_stage(c, s - 1)
            if s < bits:
                send_stage(c, s)
        bcopies[-1].wait()
        bun[...] = bun[...] + bunr[s - 1]
        bcopies.append(
            push(bun, bunr.at[s], b_sem.at[s, 0], b_sem.at[s, 1], (flipped(dp, s - 1), mp))
        )
    tails = []
    total = jnp.zeros((1, 1), f32)
    for c in range(n):
        mine = acc[c][dp]
        total = total + jnp.sum(mine * mine, keepdims=True)
        if c in TABLE_CHUNKS:
            k = TABLE_CHUNKS.index(c)
            send, recv = tsend[2 * k], tsend[2 * k + 1]
            send[...] = jnp.where(mp == 0, mine[small:], mine[:small])
            outs[c][mp] = jnp.where(mp == 0, mine[:small], mine[small:])
            tails.append((c, recv, push(send, recv, t_sem.at[k, 0], t_sem.at[k, 1], mate)))
        else:
            outs[c][...] = mine
    sq[0] = jnp.broadcast_to(total, (8, 128))
    bcopies[-1].wait()
    final = bun[...] + bunr[bits]
    obun_ref[...] = final
    shared = jnp.sum(final[:, 128:] * final[:, 128:], keepdims=True)
    for s in range(bits + 1):
        peer = mate if s == 0 else (flipped(dp, s - 1), mp)
        copy = push(sq.at[s], sqr.at[s], q_sem.at[s, 0], q_sem.at[s, 1], peer)
        copy.wait()
        sq[s + 1] = sq[s] + sqr[s]
    for c, recv, copy in tails:
        copy.wait()
        outs[c][1 - mp] = recv[...]
    squares = sq[bits + 1] + shared
    loss, weight = final[:, 0:1], final[:, 1:2]
    norm = jnp.sqrt(squares) / weight
    factor = jnp.minimum(1.0, clip_limit / norm) / weight
    which = lax.broadcasted_iota(jnp.int32, (8, 128), 1)
    info = jnp.where(which == 0, loss, jnp.where(which == 1, weight, norm))
    info_ref[...] = jnp.where(which == 3, factor, info)
    for copy in mcopies.values():
        copy.wait_send()
    for copy in copies.values():
        copy.wait_send()


def reduce_all(own, mates, smalls, turns, n_data):
    bits = n_data.bit_length() - 1
    rows = D // n_data
    widths = [x.shape[1] for x in own]
    n = len(widths)
    sems = pltpu.SemaphoreType.DMA
    inside = pl.BlockSpec(memory_space=pltpu.VMEM)
    anywhere = pl.BlockSpec(memory_space=pl.ANY)
    bufs = [
        pltpu.VMEM((2 ** (bits - 1 - s), rows, w), bf16) for w in widths for s in range(bits)
    ]
    length = sum(x.shape[0] * x.shape[1] for x in smalls)
    outs = [
        jax.ShapeDtypeStruct((2, rows // 2, w) if c in TABLE_CHUNKS else (rows, w), f32)
        for c, w in enumerate(widths)
    ]
    tails = [
        pltpu.VMEM((rows // 2, widths[c]), f32) for c in TABLE_CHUNKS for _ in range(2)
    ]

    def kernel(*refs):
        cut = len(refs) - 11 - len(tails)
        head, rest = refs[:cut], refs[cut:]
        tsend, rest = rest[: len(tails)], rest[len(tails) :]
        reduce_kernel(bits, widths, turns, *head, rest[0], rest[1], tsend, *rest[2:])

    return pl.pallas_call(
        kernel,
        in_specs=[anywhere] * (2 * n) + [inside] * len(smalls),
        out_specs=[inside] * (n + 2),
        out_shape=outs
        + [
            jax.ShapeDtypeStruct((1, length), f32),
            jax.ShapeDtypeStruct((8, 128), f32),
        ],
        scratch_shapes=[pltpu.VMEM((D, w), bf16) for w in widths]
        + [pltpu.VMEM((n_data, rows, w), f32) for w in widths]
        + [pltpu.VMEM((D, w), f32) for w in widths]
        + bufs
        + bufs
        + tails
        + [
            pltpu.VMEM((1, length), f32),
            pltpu.VMEM((bits + 1, 1, length), f32),
            pltpu.VMEM((bits + 2, 8, 128), f32),
            pltpu.VMEM((bits + 1, 8, 128), f32),
            sems((n,)),
            sems((n, 2)),
            sems((n, bits)),
            sems((n, bits)),
            sems((bits + 1, 2)),
            sems((bits + 1, 2)),
            sems((len(TABLE_CHUNKS), 2)),
        ],
        compiler_params=pltpu.CompilerParams(
            collective_id=1, has_side_effects=True, vmem_limit_bytes=62 * MIB
        ),
        name="reduce_gradients",
    )(*own, *mates, *smalls)


def adamw(master, first, second, gradient, rate, decay):
    first = beta_one * first + (1.0 - beta_one) * gradient
    second = beta_two * second + (1.0 - beta_two) * gradient * gradient
    first_hat = first / (1.0 - beta_one**STEP)
    second_hat = second / (1.0 - beta_two**STEP)
    master = master - rate * (first_hat / (jnp.sqrt(second_hat) + adam_eps) + decay * master)
    return (master, first, second)


def local_split(flat, layer):
    mp = lax.axis_index("mp")
    rows = []
    for m in range(2):
        pieces = []
        for h in range(3):
            at = 128 + 2 * D * layer + (128 * m + HD * h if h < 2 else 256 + HD * m)
            pieces += [flat[:, at : at + HD], flat[:, at + D : at + D + HD]]
        at = 128 + 2 * D * LAYERS + FF * layer + HALF * m
        rows.append(jnp.concatenate(pieces + [flat[:, at : at + HALF]], 1))
    return jnp.where(mp == 0, rows[0], rows[1])


def update_kernel(info_ref, *refs):
    g = refs[:9]
    flat_ref = refs[9]
    params = refs[10:25]
    outs = refs[25:]
    factor = info_ref[0, 3]

    def write(grad, item, rate, decay, at, outs, low):
        new, one, two = adamw(
            item[0][at], item[1][at], item[2][at], grad * factor, rate, decay
        )
        outs[0][at], outs[1][at], outs[2][at] = new, one, two
        if low:
            outs[3][at] = new.astype(bf16)

    everything = (slice(None), slice(None))
    heads = [
        jnp.concatenate([g[6][m, :, 512 * h : 512 * (h + 1)] for m in range(2)], 1)[:, :CLS]
        for h in range(2)
    ]
    token = jnp.concatenate([g[8][0], g[8][1]], 1)
    table = jnp.concatenate(
        [g[7][0], g[7][1], token[:, PATCHES:TOK], token[:, :PATCHES]] + heads, 1
    )
    write(table, params[0:3], matrix_rate, matrix_decay, everything, outs[0:4], True)
    vec = jnp.transpose(token, (1, 0))[TP : TP + 6 * LAYERS + 2]
    write(vec, params[3:6], vector_rate, 0.0, everything, outs[4:7], False)
    for layer in range(LAYERS):
        packed = g[layer][...]
        pieces = []
        for h in range(3):
            for t in range(4):
                lo = 128 * t + HD * h if h < 2 else 512 + HD * t
                pieces.append(packed[:, lo : lo + HD])
        grad = jnp.concatenate(pieces, 1)
        write(grad, params[6:9], matrix_rate, matrix_decay, layer, outs[7:11], True)
        for half in range(2):
            write(
                g[LAYERS + 2 * layer + half][...],
                params[9:12],
                matrix_rate,
                matrix_decay,
                (layer, slice(None), half),
                outs[11:15],
                True,
            )
    flat = flat_ref[...]
    for layer in range(LAYERS):
        grad = local_split(flat, layer)
        write(grad, params[12:15], vector_rate, 0.0, slice(layer, layer + 1), outs[15:18], False)


def update(info, grads, split, params):
    outs = []
    for i in range(5):
        low = i in (0, 2, 3)
        shape = params[3 * i].shape
        outs += [jax.ShapeDtypeStruct(shape, f32)] * 3
        outs += [jax.ShapeDtypeStruct(shape, bf16)] if low else []
    ins = list(grads) + [split] + list(params)
    return pl.pallas_call(
        update_kernel,
        grid=(1,),
        in_specs=[pl.BlockSpec(memory_space=pltpu.SMEM)] + [full_spec(x.shape) for x in ins],
        out_specs=[full_spec(x.shape) for x in outs],
        out_shape=outs,
        compiler_params=pltpu.CompilerParams(vmem_limit_bytes=60 * MIB),
        name="update_weights",
    )(info, *ins)


def pack_kernel(t_ref, v_ref, a_ref, f_ref, tab_ref, main_ref):
    small = t_ref.shape[0]
    table = t_ref[...]

    def zeros(n):
        return jnp.zeros((small, n), f32)

    turned = jnp.transpose(v_ref[...], (1, 0))
    low = PD + 2
    seg = jnp.concatenate(
        [
            table[:, low : low + PATCHES],
            table[:, PD:low],
            zeros(TP - TOK),
            turned,
            zeros(256 - TP - turned.shape[1]),
        ],
        1,
    )
    heads = [
        jnp.concatenate(
            [table[:, PD + TOK + CLS * h : PD + TOK + CLS * (h + 1)], zeros(1024 - CLS)], 1
        )
        for h in range(2)
    ]
    parts = [table[:, :PD], seg] + heads
    for m in range(2):
        at = 0
        for x in parts:
            half = x.shape[1] // 2
            tab_ref[m, :, at : at + half] = x[:, half * m : half * (m + 1)].astype(bf16)
            at += half
    for layer in range(LAYERS):
        a = a_ref[layer]
        for t in range(4):
            pair = jnp.concatenate(
                [a[:, 256 * h + HD * t : 256 * h + HD * (t + 1)] for h in range(2)], 1
            )
            main_ref[layer, :, 128 * t : 128 * (t + 1)] = pair.astype(bf16)
        main_ref[layer, :, 512:] = a[:, 512:].astype(bf16)
        for half in range(2):
            main_ref[LAYERS + 2 * layer + half] = f_ref[layer, :, half].astype(bf16)


def pack(tab, vec, attn, ffw):
    layers, rows, _ = attn.shape
    ins = [tab, vec, attn, ffw]
    shapes = [(2, tab.shape[0], T_COLS), (3 * layers, rows, HALF)]
    return pl.pallas_call(
        pack_kernel,
        grid=(1,),
        in_specs=[full_spec(x.shape) for x in ins],
        out_specs=[full_spec(x) for x in shapes],
        out_shape=[jax.ShapeDtypeStruct(x, bf16) for x in shapes],
        compiler_params=pltpu.CompilerParams(vmem_limit_bytes=60 * MIB),
        name="pack_shards",
    )(*ins)


def shards(
    pixels,
    labels,
    teacher,
    partner,
    mix_weight,
    class_weight,
    tables,
    tables_first,
    tables_second,
    vectors,
    vectors_first,
    vectors_second,
    attention,
    attention_first,
    attention_second,
    feedforward,
    feedforward_first,
    feedforward_second,
    split_bias,
    split_bias_first,
    split_bias_second,
    head_bias,
    head_bias_first,
    head_bias_second,
):
    n_data = lax.axis_size("dp")
    dp, mp = mesh_place()
    images_here = pixels.shape[0]
    count = images_here // 2
    rows = D // n_data
    far_pairs = [(i, (i + n_data // 2) % n_data) for i in range(n_data)]
    pix = pixels.transpose(1, 0, 2)
    tab, shard = pack(tables.T, vectors, attention, feedforward)
    deep = gather_plan(n_data.bit_length() - 1, MAIN_TURNS)[1]
    front, seg, *heights, sb = gather_front(tab, shard, split_bias, n_data)
    front = front.reshape(2, D, FRONT_WIDTHS[0])
    seg = seg.reshape(2, D, FRONT_WIDTHS[1])
    near_pairs = [(i, i ^ (1 << deep[-1])) for i in range(n_data)]
    mains, heads = ([x, lax.ppermute(x, "dp", near_pairs)] for x in heights)
    pix_halves = pix.reshape(PATCHES, 2, count, PD)
    send = embed_send(pix_halves, front)
    mains, heads, send = lax.optimization_barrier((mains, heads, send))
    far = lax.ppermute(send, "dp", far_pairs)
    weights, w_heads, pix_mine = gather_main(mains, heads, pix_halves, n_data)
    hb = jnp.pad(
        head_bias.astype(bf16).astype(f32).reshape(2, CLS),
        ((0, 0), (0, 1024 - CLS)),
        constant_values=-1e30,
    ).reshape(1, -1)
    cw = jnp.pad(class_weight, (0, 1024 - CLS)).reshape(1, -1)
    front, hb, cw, weights = lax.optimization_barrier((front, hb, cw, weights))
    own = embed_own(partner, pix, front)
    pix_mine, far, own = lax.optimization_barrier((pix_mine, far, own))
    pix_far = lax.ppermute(pix_mine, "dp", far_pairs)
    *kept, mid, tok = forward(
        partner, mix_weight, own, far, seg, weights, sb
    )
    u1o, u1m, d1o, d1m, ho, hm, dz, gvh, gu1, dhb, stat = head(
        partner, mix_weight, labels, teacher, mid, weights, w_heads, sb, hb, cw, tok
    )
    dz0, a0o, a0m, a1o, a1m, u0o, u0m, d0o, d0m, gvb, gb, gu0 = backward(dz, kept, weights, tok)
    po, pm, eo, em = patch_grad(
        partner,
        mix_weight,
        dz0,
        pix.reshape(PATCHES * images_here, PD),
        pix_far.reshape(PATCHES * count, PD),
        gvb,
        gvh,
    )
    own_parts = [a0o, a1o, u0o, d0o, u1o, d1o, ho, po, eo]
    mate_parts = [a0m, a1m, u0m, d0m, u1m, d1m, hm, pm, em]
    *g, flat, info = reduce_all(
        own_parts, mate_parts, [stat, gb, gu0, gu1, dhb], REDUCE_TURNS, n_data
    )
    loss_sum, weight_sum, grad_norm, factor = (info[0, i] for i in range(4))
    at = 128 + 2 * D * LAYERS + FF * LAYERS
    g_head = flat[0, at : at + 2048].reshape(2, 1024)[:, :CLS].reshape(-1)
    fresh = update(
        info,
        g,
        flat,
        [
            tables.T,
            tables_first.T,
            tables_second.T,
            vectors,
            vectors_first,
            vectors_second,
            attention,
            attention_first,
            attention_second,
            feedforward,
            feedforward_first,
            feedforward_second,
            split_bias,
            split_bias_first,
            split_bias_second,
        ],
    )
    fresh = [x.T for x in fresh[:4]] + list(fresh[4:])
    h_new, h_one, h_two = adamw(
        head_bias, head_bias_first, head_bias_second, g_head * factor, vector_rate, 0.0
    )
    return (loss_sum, weight_sum, grad_norm, *fresh, h_new, h_one, h_two)


def solution(mesh):
    table = P(None, ("dp", "mp"))
    attn = P(None, "dp", "mp")
    ffw = P(None, "dp", None, "mp")
    split = P(None, "mp")
    return jax.shard_map(
        shards,
        mesh=mesh,
        in_specs=(P("dp", None, None), P(), P("dp"), P("dp"), P("dp"), P())
        + (table,) * 6
        + (attn,) * 3
        + (ffw,) * 3
        + (split,) * 3
        + (P(),) * 3,
        out_specs=(P(),) * 3
        + (table,) * 7
        + (attn,) * 4
        + (ffw,) * 4
        + (split,) * 3
        + (P(),) * 3,
        check_vma=False,
    )
```

```python
import functools

import jax
import jax.numpy as jnp
from jax import lax
from jax.experimental import pallas as pl
from jax.experimental.pallas import tpu as pltpu
from jax.sharding import PartitionSpec as P

D = 384
HEADS = 6
HD = 64
FF = 1536
CLS = 1000
PD = 768
PATCHES = 196
LAYERS = 2
STEP = 10
TOK = 198
TP = 208
GRP = 2
F_GRP = 4
ENDS = 16
END_AT = 4
SENT = 200
ROWS = GRP * TP
HALF = FF // 2
COLS = 6144
T_COLS = 1536
F_COLS = 512
TABLE_CHUNKS = (6, 7, 8)
REDUCE_ORDER = (0, 2, 4, 1, 3, 6, 5, 7, 8)
REDUCE_TURNS = (0, 0, 1, 1, 2, 1, 2, 0, 0)
MAIN_WIDTHS = (768, 768, 768, 768, 768, 768, 1024)
MAIN_TURNS = (0, 0, 0, 1, 0, 1, 1)
FRONT_WIDTHS = (384, 128)
FRONT_TURNS = (0, 1)
M_COLS = 4608
MIB = 1 << 20
NORM_ROWS = ROWS
GELU_ROWS = 32

norm_eps = 1e-06
clip_limit = 0.02
beta_one = 0.9
beta_two = 0.999
adam_eps = 1e-08
matrix_rate = 0.08
vector_rate = 0.5
matrix_decay = 0.05

f32 = jnp.float32
bf16 = jnp.bfloat16
MESH = pl.DeviceIdType.MESH
AB = ((1,), (0,))
ABT = ((1,), (1,))
ATB = ((0,), (0,))


def mm(left, right, dims=AB):
    return lax.dot_general(left, right, (dims, ((), ())), preferred_element_type=f32)


def full_spec(shape):
    return pl.BlockSpec(shape, lambda *_: (0,) * len(shape), pipeline_mode=pl.Buffered(1))


def row_loop(total, chunk, body):
    def step(index, carry):
        body(pl.ds(pl.multiple_of(index * chunk, chunk), chunk))
        return carry

    if total == chunk:
        body(slice(0, total))
    else:
        lax.fori_loop(0, total // chunk, step, 0)


def center(x):
    mean = jnp.mean(x, -1, keepdims=True)
    xc = x - mean
    scale = lax.rsqrt(jnp.mean(xc * xc, -1, keepdims=True) + norm_eps)
    return xc * scale, scale


def gelu_pair(x):
    e = jnp.exp2((x * x) * -0.7213475204444817)
    den = 1.0 + 0.23164189 * jnp.abs(x)
    r = pl.reciprocal(den, approx=True)
    r = r * (2.0 - den * r)
    poly = r * (
        0.127414796
        + r * (-0.142248368 + r * (0.7107068705 + r * (-0.7265760135 + r * 0.5307027145)))
    )
    tail = poly * e
    cdf = jnp.where(x > 0.0, 1.0 - tail, tail)
    return x * cdf, cdf + x * (e * 0.3989422804014327)


def partner_place(partner_ref, k):
    images = partner_ref.shape[0]
    n_data = lax.axis_size("dp")
    far = lax.rem(lax.axis_index("dp") + n_data // 2, n_data)
    wanted = far * images + lax.axis_index("mp") * (images // 2) + k
    place = jnp.int32(0)
    for i in range(images):
        place = place + jnp.where(partner_ref[i] == wanted, i, 0)
    return place


def project(pix, w_ref):
    return mm(pix[:, :D], w_ref[0], ABT) + mm(pix[:, D:], w_ref[1], ABT)


def embed_send_kernel(pix_ref, w_ref, send_ref, flat):
    mp = lax.axis_index("mp")
    patches, _, images, _ = pix_ref.shape
    part = patches // 7
    for c in range(7):
        out = project(pix_ref[c * part : (c + 1) * part, mp].reshape(part * images, PD), w_ref)
        for j in range(3):
            flat[j, c * part * images : (c + 1) * part * images] = out[:, 128 * j : 128 * (j + 1)]
    for k in range(images):
        for j in range(3):
            cols = slice(128 * j, 128 * (j + 1))
            send_ref[k, :patches, cols] = flat[j, pl.ds(k, patches, stride=images), :].astype(bf16)
        send_ref[k, patches:] = jnp.zeros((SENT - patches, D), bf16)


def embed_own_kernel(partner_ref, pix_ref, w_ref, own_ref, flat):
    count = partner_ref.shape[0]
    patches = pix_ref.shape[0]
    part = patches // 7
    for c in range(7):
        out = project(pix_ref[c * part : (c + 1) * part].reshape(part * count, PD), w_ref)
        for j in range(3):
            flat[j, c * part * count : (c + 1) * part * count] = out[:, 128 * j : 128 * (j + 1)]
    for k in range(count // 2):
        place = partner_place(partner_ref, k)
        for j in range(3):
            cols = slice(128 * j, 128 * (j + 1))
            own_ref[k, :, cols] = flat[j, pl.ds(place, patches, stride=count), :]


def embed_call(kernel, prefix, pix, weights, shape, dtype, rows, name):
    return pl.pallas_call(
        kernel,
        grid=(1,),
        in_specs=[pl.BlockSpec(memory_space=pltpu.SMEM)] * len(prefix)
        + [full_spec(pix.shape), full_spec(weights.shape)],
        out_specs=full_spec(shape),
        out_shape=jax.ShapeDtypeStruct(shape, dtype),
        scratch_shapes=[pltpu.VMEM((3, rows, 128), f32)],
        compiler_params=pltpu.CompilerParams(vmem_limit_bytes=60 * MIB),
        name=name,
    )(*prefix, pix, weights)


def embed_send(pix, weights):
    images = pix.shape[2]
    shape = (images, SENT, D)
    rows = TP * images
    return embed_call(embed_send_kernel, [], pix, weights, shape, bf16, rows, "embed_sent_images")


def embed_own(partner, pix, weights):
    images = pix.shape[1]
    shape = (images // 2, PATCHES, D)
    rows = TP * images
    return embed_call(
        embed_own_kernel, [partner], pix, weights, shape, f32, rows, "embed_own_images"
    )


def split_tokens(w_ref, col):
    seg = jnp.concatenate([w_ref[0, :, col : col + 128], w_ref[1, :, col : col + 128]], 1)
    return jnp.transpose(seg.astype(f32), (1, 0))


def attend(g, qkv_ref, p_ref, ho_ref):
    rows = slice(g * TP, (g + 1) * TP)
    lane = lax.broadcasted_iota(jnp.int32, (TP, 128), 1)
    key_mask = jnp.where(lax.broadcasted_iota(jnp.int32, (1, TP), 1) < TOK, 0.0, -1e30).astype(f32)
    for j in range(3):
        q = qkv_ref[rows, 128 * j : 128 * (j + 1)]
        k = qkv_ref[rows, D + 128 * j : D + 128 * (j + 1)]
        v = qkv_ref[rows, 2 * D + 128 * j : 2 * D + 128 * (j + 1)]
        outs = []
        for s in range(2):
            mine = (lane < 64) if s == 0 else (lane >= 64)
            scores = mm(jnp.where(mine, q, jnp.zeros_like(q)), k, ABT) + key_mask
            exps = jnp.exp(scores - jnp.max(scores, -1, keepdims=True))
            probs = (exps * (1.0 / jnp.sum(exps, -1, keepdims=True))).astype(bf16)
            p_ref[6 * g + 2 * j + s] = probs
            outs.append(mm(probs, v))
        ho_ref[rows, 128 * j : 128 * (j + 1)] = jnp.where(lane < 64, outs[0], outs[1]).astype(bf16)


PAIRS = (0, 1, 3, 4, 2, 5)


def rounded(x):
    return x.astype(bf16).astype(f32)


def norm_rows(src, gain, shift, dst):
    dst[...] = (center(src[...])[0] * gain + shift).astype(bf16)


def token_row(tok_ref, layer, i):
    at = TP + 6 * layer + i
    return tok_ref[at : at + 1]


def spread_heads(x):
    lane = lax.broadcasted_iota(jnp.int32, x.shape, 1)
    zero = jnp.zeros_like(x)
    return jnp.concatenate(
        [jnp.where((lane >= HD * h) & (lane < HD * (h + 1)), x, zero) for h in range(HEADS)], 0
    )


def gather_heads(x):
    lane = lax.broadcasted_iota(jnp.int32, (ENDS, D), 1)
    total = jnp.zeros((ENDS, D), f32)
    for h in range(HEADS):
        part = x[ENDS * h : ENDS * (h + 1)]
        total = total + jnp.where((lane >= HD * h) & (lane < HD * (h + 1)), part, 0.0)
    return total


def attend_ends(g, kv_ref, q_ref, p_ref, ho_ref):
    rows = slice(g * TP, (g + 1) * TP)
    ends = slice(g * ENDS, (g + 1) * ENDS)
    key_mask = jnp.where(lax.broadcasted_iota(jnp.int32, (1, TP), 1) < TOK, 0.0, -1e30).astype(f32)
    scores = mm(spread_heads(q_ref[ends]), kv_ref[rows, :D], ABT) + key_mask
    exps = jnp.exp(scores - jnp.max(scores, -1, keepdims=True))
    probs = (exps * (1.0 / jnp.sum(exps, -1, keepdims=True))).astype(bf16)
    p_ref[g] = probs
    ho_ref[ends] = gather_heads(mm(probs, kv_ref[rows, D:])).astype(bf16)


def forward_kernel(partner_ref, mix_ref, own_ref, far_ref, t_ref, w_ref, sb_ref, *refs):
    x_ref, mid_ref, qkv_ref, p_ref, ho_ref, hid_ref, gp_ref = refs[:7]
    x1_ref, kv_ref, q1_ref, p1_ref, ho1_ref, mid1_ref, tok_ref = refs[7:14]
    qkv_w, out_w, nbuf, up_s, bias_ref = refs[14:]
    step = pl.program_id(0)

    @pl.when(step == 0)
    def _():
        tok_ref[...] = split_tokens(t_ref, 0)
        for layer in range(LAYERS):
            attn_tiles(w_ref.at[layer], qkv_w.at[layer], out_w.at[layer])
            pieces = [
                sb_ref[h // 3, layer : layer + 1, 128 * (h % 3) + HD * t : 128 * (h % 3) + HD * (t + 1)]
                for t in range(2)
                for h in PAIRS
            ]
            bias_ref[layer : layer + 1] = rounded(jnp.concatenate(pieces, 1))

    def row(layer, i):
        return token_row(tok_ref, layer, i)

    for g in range(F_GRP):
        w = mix_ref[partner_place(partner_ref, step * F_GRP + g)]
        x_ref[g * TP : g * TP + PATCHES] = (
            w * own_ref[g] + (1.0 - w) * far_ref[g, :PATCHES].astype(f32) + tok_ref[:PATCHES]
        )
        x_ref[g * TP + PATCHES : (g + 1) * TP] = tok_ref[PATCHES:TP]
    norm_rows(x_ref, row(0, 0), row(0, 1), nbuf)
    qkv = mm(nbuf[...], qkv_w[0])
    q = qkv[:, :D] + bias_ref[0:1, :D]
    qkv_ref[:, :D] = (q.astype(bf16).astype(f32) * 0.125).astype(bf16)
    qkv_ref[:, D : 2 * D] = qkv[:, D : 2 * D].astype(bf16)
    qkv_ref[:, 2 * D :] = (qkv[:, 2 * D :] + bias_ref[0:1, D : 2 * D]).astype(bf16)
    for g in range(F_GRP):
        attend(g, qkv_ref, p_ref, ho_ref)
    mid_ref[...] = x_ref[...] + mm(ho_ref[...], out_w[0], ABT) + row(0, 4)
    norm_rows(mid_ref, row(0, 2), row(0, 3), nbuf)
    up_w, down_w = w_ref.at[LAYERS], w_ref.at[LAYERS + 1]
    for m in range(2):
        cols = slice(HALF * m, HALF * (m + 1))
        up_s[...] = mm(nbuf[...], up_w[m]) + rounded(sb_ref[m, 0:1, D:])

        def body(rs):
            hid, gp = gelu_pair(up_s[rs])
            hid_ref[rs, cols] = hid.astype(bf16)
            gp_ref[rs, cols] = gp.astype(bf16)

        row_loop(F_GRP * TP, GELU_ROWS, body)
    out = mid_ref[...] + row(0, 5)
    for m in range(2):
        cols = slice(HALF * m, HALF * (m + 1))
        out = out + mm(hid_ref[:, cols], down_w[m], ABT)
    x1_ref[...] = out
    norm_rows(x1_ref, row(1, 0), row(1, 1), nbuf)
    kv = mm(nbuf[...], qkv_w[1, :, D:])
    kv_ref[:, :D] = kv[:, :D].astype(bf16)
    kv_ref[:, D:] = (kv[:, D:] + bias_ref[1:2, D : 2 * D]).astype(bf16)
    ends = jnp.concatenate([nbuf[(g + 1) * TP - ENDS : (g + 1) * TP] for g in range(F_GRP)], 0)
    q = mm(ends, qkv_w[1, :, :D]) + bias_ref[1:2, :D]
    q1_ref[...] = (q.astype(bf16).astype(f32) * 0.125).astype(bf16)
    for g in range(F_GRP):
        attend_ends(g, kv_ref, q1_ref, p1_ref, ho1_ref)
    x_ends = jnp.concatenate([x1_ref[(g + 1) * TP - ENDS : (g + 1) * TP] for g in range(F_GRP)], 0)
    mid1_ref[...] = x_ends + mm(ho1_ref[...], out_w[1], ABT) + row(1, 4)


def kept_shapes(count):
    n = count * TP
    return [
        ((n, D), f32),
        ((n, D), f32),
        ((n, 3 * D), bf16),
        ((count * HEADS, TP, TP), bf16),
        ((n, D), bf16),
        ((n, FF), bf16),
        ((n, FF), bf16),
        ((n, D), f32),
        ((n, 2 * D), bf16),
        ((count * ENDS, D), bf16),
        ((count, HEADS * ENDS, TP), bf16),
        ((count * ENDS, D), bf16),
        ((count * ENDS, D), f32),
    ]


def block_of(shape, steps):
    block = (shape[0] // steps,) + tuple(shape[1:])
    return pl.BlockSpec(block, lambda i: (i,) + (0,) * (len(block) - 1))


def forward(partner, mix, own, far, seg, weights, sb):
    count = own.shape[0]
    steps = count // F_GRP
    outs = kept_shapes(count)
    shapes = [jax.ShapeDtypeStruct(s, t) for s, t in outs] + [jax.ShapeDtypeStruct((256, D), f32)]
    specs = [block_of(s, steps) for s, _ in outs] + [full_spec((256, D))]
    return pl.pallas_call(
        forward_kernel,
        grid=(steps,),
        in_specs=[
            pl.BlockSpec(memory_space=pltpu.SMEM),
            pl.BlockSpec(memory_space=pltpu.SMEM),
            block_of(own.shape, steps),
            block_of(far.shape, steps),
            full_spec(seg.shape),
            pl.BlockSpec((4, 2, D, 768), lambda i: (0, 0, 0, 0), pipeline_mode=pl.Buffered(1)),
            full_spec(sb.shape),
        ],
        out_specs=specs,
        out_shape=shapes,
        scratch_shapes=[
            pltpu.VMEM((LAYERS, D, 3 * D), bf16),
            pltpu.VMEM((LAYERS, D, D), bf16),
            pltpu.VMEM((F_GRP * TP, D), bf16),
            pltpu.VMEM((F_GRP * TP, HALF), f32),
            pltpu.VMEM((LAYERS, 2 * D), f32),
        ],
        compiler_params=pltpu.CompilerParams(vmem_limit_bytes=60 * MIB),
        name="forward_layers",
    )(partner, mix, own, far, seg, weights, sb)


def norm_back(dy, xhat, scale, gain):
    dyg = dy * gain
    c1 = jnp.mean(dyg, -1, keepdims=True)
    c2 = jnp.mean(dyg * xhat, -1, keepdims=True)
    return scale * (dyg - c1 - xhat * c2)


def share(part, own_ref, mate_ref, mp):
    own_ref[...] = part[mp]
    mate_ref[...] = part[1 - mp].astype(bf16)


def head_kernel(
    partner_ref,
    mix_ref,
    label_ref,
    teacher_ref,
    mid_ref,
    wf_ref,
    w_ref,
    sb_ref,
    hb_ref,
    cw_ref,
    tok_ref,
    uo_ref,
    um_ref,
    do_ref,
    dm_ref,
    ho_ref,
    hm_ref,
    dz_ref,
    gv_ref,
    gu_ref,
    dhb_ref,
    stat_ref,
    lanes,
    g_ffw,
    g_head,
):
    mp = lax.axis_index("mp")
    gain2, shift2, bias_f = (token_row(tok_ref, 1, i) for i in (2, 3, 5))
    gain, shift = (token_row(tok_ref, 2, i) for i in range(2))
    count = mid_ref.shape[0] // ENDS
    images = partner_ref.shape[0]
    n_data = lax.axis_size("dp")
    dp = lax.axis_index("dp")
    far_base = lax.rem(dp + n_data // 2, n_data) * images + mp * count
    marks = []
    for k in range(count):
        place = partner_place(partner_ref, k)
        marks.append(
            (
                label_ref[dp * images + place],
                label_ref[far_base + k],
                teacher_ref[place],
                mix_ref[place],
            )
        )
    for j in range(3):
        lanes[j, : mid_ref.shape[0]] = mid_ref[:, 128 * j : 128 * (j + 1)]
    mid = jnp.concatenate(
        [
            jnp.concatenate(
                [lanes[j, pl.ds(END_AT + h, count, stride=ENDS), :] for j in range(3)], 1
            )
            for h in range(2)
        ],
        0,
    )
    xhat2, scale2 = center(mid)
    normed = (xhat2 * gain2 + shift2).astype(bf16)
    out = mid + bias_f
    hids, gps = [], []
    for m in range(2):
        up = mm(normed, wf_ref[0, m]) + rounded(sb_ref[m, 1:2, D:])
        hid, gp = gelu_pair(up)
        hids.append(hid.astype(bf16))
        gps.append(gp)
        out = out + mm(hids[m], wf_ref[1, m], ABT)
    xhat, scale = center(out)
    final = (xhat * gain + shift).astype(bf16)
    loss = jnp.zeros((1, 1), f32)
    weight = jnp.zeros((1, 1), f32)
    dfinals = []
    for h in range(2):
        mine = final[count * h : count * (h + 1)]
        halves = []
        for m in range(2):
            wh = w_ref[m, :, 512 * h : 512 * (h + 1)]
            at = 1024 * h + 512 * m
            logits = mm(mine, wh) + hb_ref[0:1, at : at + 512]
            ids = lax.broadcasted_iota(jnp.int32, (1, 512), 1) + 512 * m
            shares = []
            for k in range(count):
                first, second, teach, mix = marks[k]
                if h == 0:
                    both = jnp.where(ids == first, mix, 0.0) + jnp.where(ids == second, 1.0 - mix, 0.0)
                    shares.append(both)
                else:
                    shares.append(jnp.where(ids == teach, 1.0, 0.0))
            coef = jnp.concatenate(shares, 0) * cw_ref[0:1, 512 * m : 512 * (m + 1)]
            halves.append((wh, logits, coef))
        top = jnp.maximum(*[jnp.max(x[1], -1, keepdims=True) for x in halves])
        exps = [jnp.exp(x[1] - top) for x in halves]
        total = sum(jnp.sum(x, -1, keepdims=True) for x in exps)
        lse = top + jnp.log(total)
        csum = sum(jnp.sum(x[2], -1, keepdims=True) for x in halves)
        dfinal = jnp.zeros((count, D), f32)
        for m in range(2):
            wh, logits, coef = halves[m]
            loss = loss + jnp.sum(jnp.sum(coef * (lse - logits), -1, keepdims=True), 0, keepdims=True)
            dl = csum * (exps[m] / total) - coef
            at = 1024 * h + 512 * m
            dhb_ref[0:1, at : at + 512] = jnp.sum(dl, 0, keepdims=True)
            low = dl.astype(bf16)
            g_head[m, :, 512 * h : 512 * (h + 1)] = mm(mine, low, ATB)
            dfinal = dfinal + mm(low, wh, ABT)
        weight = weight + jnp.sum(csum, 0, keepdims=True)
        dfinals.append(dfinal)
    dfinal = jnp.concatenate(dfinals, 0)
    dz = norm_back(dfinal, xhat, scale, gain)
    low = dz.astype(bf16)
    dn = jnp.zeros_like(dz)
    for m in range(2):
        dh = mm(low, wf_ref[1, m])
        du = (dh.astype(bf16).astype(f32) * gps[m]).astype(bf16)
        gu_ref[0:1, HALF * m : HALF * (m + 1)] = jnp.sum(du.astype(f32), 0, keepdims=True)
        g_ffw[0, m] = mm(normed, du, ATB)
        g_ffw[1, m] = mm(low, hids[m], ATB)
        dn = dn + mm(du, wf_ref[0, m], ABT)
    dmid = dz + norm_back(dn, xhat2, scale2, gain2)
    gv_ref[...] = jnp.zeros_like(gv_ref)
    sums = [dn * xhat2, dn, dmid, dz, dfinal * xhat, dfinal]
    for i, item in enumerate(sums):
        gv_ref[i + 2 : i + 3] = jnp.sum(item, 0, keepdims=True)
    lanes[...] = jnp.zeros_like(lanes)
    for j in range(3):
        for h in range(2):
            lanes[j, pl.ds(END_AT + h, count, stride=ENDS), :] = dmid[
                count * h : count * (h + 1), 128 * j : 128 * (j + 1)
            ]
        dz_ref[:, 128 * j : 128 * (j + 1)] = lanes[j, : dz_ref.shape[0]]
    which = lax.broadcasted_iota(jnp.int32, stat_ref.shape, 1)
    stat_ref[...] = jnp.where(which == 0, loss, jnp.where(which == 1, weight, 0.0))
    share(g_ffw.at[0], uo_ref, um_ref, mp)
    share(g_ffw.at[1], do_ref, dm_ref, mp)
    share(g_head, ho_ref, hm_ref, mp)


def pair_shapes(shapes):
    return [jax.ShapeDtypeStruct(s, t) for s in shapes for t in (f32, bf16)]


def head(partner, mix, labels, teacher, mid, weights, w_heads, sb, hb, cw, tok):
    outs = pair_shapes([(D, 768), (D, 768), (D, 1024)]) + [
        jax.ShapeDtypeStruct(s, f32)
        for s in (mid.shape, (8, D), (1, FF), (1, 2048), (1, 128))
    ]
    return pl.pallas_call(
        head_kernel,
        grid=(1,),
        in_specs=[pl.BlockSpec(memory_space=pltpu.SMEM)] * 4
        + [
            full_spec(mid.shape),
            pl.BlockSpec((2, 2, D, 768), lambda i: (2, 0, 0, 0), pipeline_mode=pl.Buffered(1)),
        ]
        + [full_spec(x.shape) for x in (w_heads, sb, hb, cw, tok)],
        out_specs=[full_spec(x.shape) for x in outs],
        out_shape=outs,
        scratch_shapes=[
            pltpu.VMEM((3, mid.shape[0] + 2 * ENDS, 128), f32),
            pltpu.VMEM((2, 2, D, 768), f32),
            pltpu.VMEM((2, D, 1024), f32),
        ],
        compiler_params=pltpu.CompilerParams(vmem_limit_bytes=60 * MIB),
        name="loss_heads",
    )(partner, mix, labels, teacher, mid, weights, w_heads, sb, hb, cw, tok)


def attend_back(g, dho, qkv_ref, p_ref, dproj):
    rows = slice(g * TP, (g + 1) * TP)
    lane = lax.broadcasted_iota(jnp.int32, (TP, 128), 1)
    for j in range(3):
        q = qkv_ref[rows, 128 * j : 128 * (j + 1)]
        k = qkv_ref[rows, D + 128 * j : D + 128 * (j + 1)]
        v = qkv_ref[rows, 2 * D + 128 * j : 2 * D + 128 * (j + 1)]
        do = dho[rows, 128 * j : 128 * (j + 1)]
        qt, kt, dot_ = (jnp.transpose(a, (1, 0)) for a in (q, k, do))
        for s in range(2):
            mine = (lane < 64) if s == 0 else (lane >= 64)
            sub = slice(64 * s, 64 * (s + 1))
            at = 128 * j + 64 * s
            probs = p_ref[6 * g + 2 * j + s]
            dproj[g, 2 * D + at : 2 * D + at + 64] = mm(dot_[sub], probs).astype(bf16)
            dprob = mm(jnp.where(mine, do, jnp.zeros_like(do)), v, ABT)
            p32 = probs.astype(f32)
            delta = jnp.sum(dprob * p32, -1, keepdims=True)
            ds = (p32 * (dprob - delta)).astype(bf16)
            dproj[g, at : at + 64] = (mm(kt[sub], ds, ABT) * 0.125).astype(bf16)
            dproj[g, D + at : D + at + 64] = mm(qt[sub], ds).astype(bf16)


def ends_back(g, dho, kv_ref, q_ref, p_ref, dq, dproj):
    rows = slice(g * TP, (g + 1) * TP)
    ends = slice(g * ENDS, (g + 1) * ENDS)
    q = spread_heads(q_ref[ends])
    do = spread_heads(dho[ends])
    probs = p_ref[g]
    dprob = mm(do, kv_ref[rows, D:], ABT)
    p32 = probs.astype(f32)
    delta = jnp.sum(dprob * p32, -1, keepdims=True)
    ds = (p32 * (dprob - delta)).astype(bf16)
    dq[ends] = (gather_heads(mm(ds, kv_ref[rows, :D])) * 0.125).astype(bf16)
    dproj[g, :D] = mm(q, ds, ATB).astype(bf16)
    dproj[g, D : 2 * D] = mm(do, probs, ATB).astype(bf16)


def backward_kernel(
    dz_ref,
    x_ref,
    mid_ref,
    qkv_ref,
    p_ref,
    ho_ref,
    hid_ref,
    gp_ref,
    x1_ref,
    kv_ref,
    q1_ref,
    p1_ref,
    ho1_ref,
    wa_ref,
    wf_ref,
    tok_ref,
    dzo_ref,
    a0o_ref,
    a0m_ref,
    a1o_ref,
    a1m_ref,
    uo_ref,
    um_ref,
    do_ref,
    dm_ref,
    gv_ref,
    gb_ref,
    gu_ref,
    qkv_w,
    out_w,
    dqkv,
    dkv,
    dq1,
    dout,
    g_ffw,
    g_att,
    nbuf,
    dz,
    dn,
    du,
    dq,
    dproj,
):
    step = pl.program_id(0)
    mp = lax.axis_index("mp")

    def row(layer, i):
        return token_row(tok_ref, layer, i)

    @pl.when(step == 0)
    def _():
        for ref in (gv_ref, gb_ref, gu_ref, g_ffw, dqkv, dkv, dq1, dout):
            ref[...] = jnp.zeros_like(ref)
        nbuf[:, D:] = jnp.ones((ROWS, 128), bf16)
        for layer in range(LAYERS):
            attn_tiles(wa_ref.at[layer], qkv_w.at[layer], out_w.at[layer])

    def pull(src, gain, dz_out, at):
        xhat, scale = center(src[...])
        dy = dn[...]
        new = dz[...] + norm_back(dy, xhat, scale, gain)
        dz_out[...] = new
        gv_ref[at : at + 1] += jnp.sum(dy * xhat, 0, keepdims=True)
        gv_ref[at + 1 : at + 2] += jnp.sum(dy, 0, keepdims=True)

    normed = nbuf.at[:, :D]
    low = dz_ref[...].astype(bf16)
    dout[1] += mm(low, ho1_ref[...], ATB)
    dho = mm(low, out_w[1]).astype(bf16)
    norm_rows(x1_ref, row(1, 0), row(1, 1), normed)
    dz[...] = jnp.zeros_like(dz)
    for g in range(GRP):
        rows = slice(g * TP, (g + 1) * TP)
        ends_back(g, dho, kv_ref, q1_ref, p1_ref, dq, dproj)
        dkv[...] += mm(dproj[g, : 2 * D], nbuf[rows])
        dn[rows] = jnp.transpose(mm(qkv_w[1, :, D:], dproj[g, : 2 * D]), (1, 0))
    dq_all = dq[...]
    ends = jnp.concatenate([nbuf[(g + 1) * TP - ENDS : (g + 1) * TP, :D] for g in range(GRP)], 0)
    dq1[...] += mm(ends, dq_all, ATB)
    gb_ref[1:2, :D] += jnp.sum(dq_all.astype(f32), 0, keepdims=True)
    more = mm(dq_all, qkv_w[1, :, :D], ABT)
    for g in range(GRP):
        last = slice((g + 1) * TP - ENDS, (g + 1) * TP)
        part = slice(g * ENDS, (g + 1) * ENDS)
        dn[last] += more[part]
        dz[last] = dz_ref[part]
    pull(x1_ref, row(1, 0), dz, 6)

    norm_rows(mid_ref, row(0, 2), row(0, 3), normed)
    gv_ref[5:6] += jnp.sum(dz[...], 0, keepdims=True)
    rz = dz[...].astype(bf16)
    rzt = jnp.transpose(rz, (1, 0))
    nt = jnp.transpose(nbuf[:, :D], (1, 0))
    for m in range(2):
        cols = slice(HALF * m, HALF * (m + 1))
        dh = mm(rz, wf_ref[1, m])
        du[...] = (dh.astype(bf16).astype(f32) * gp_ref[:, cols].astype(f32)).astype(bf16)
        gu_ref[0:1, cols] += jnp.sum(du[...].astype(f32), 0, keepdims=True)
        g_ffw[1, m] += mm(rzt, hid_ref[:, cols])
        g_ffw[0, m] += mm(nt, du[...])
        part = mm(du[...], wf_ref[0, m], ABT)
        dn[...] = part if m == 0 else dn[...] + part
    pull(mid_ref, row(0, 2), dz, 2)
    gv_ref[4:5] += jnp.sum(dz[...], 0, keepdims=True)
    rz2 = dz[...].astype(bf16)
    dout[0] += mm(jnp.transpose(rz2, (1, 0)), ho_ref[...])
    dho = mm(rz2, out_w[0]).astype(bf16)
    norm_rows(x_ref, row(0, 0), row(0, 1), normed)
    for g in range(GRP):
        rows = slice(g * TP, (g + 1) * TP)
        attend_back(g, dho, qkv_ref, p_ref, dproj)
        dqkv[...] += mm(dproj[g], nbuf[rows])
        dn[rows] = jnp.transpose(mm(qkv_w[0], dproj[g]), (1, 0))
    pull(x_ref, row(0, 0), dzo_ref, 0)

    @pl.when(step == pl.num_programs(0) - 1)
    def _():
        for layer in range(LAYERS):
            for t in range(4):
                for j in range(3):
                    at = D * t + 128 * j
                    if t == 3:
                        tile = dout[layer, :, 128 * j : 128 * (j + 1)]
                    elif layer == 0:
                        tile = jnp.transpose(dqkv[at : at + 128, :D], (1, 0))
                    elif t == 0:
                        tile = dq1[:, 128 * j : 128 * (j + 1)]
                    else:
                        tile = jnp.transpose(dkv[at - D : at - D + 128, :D], (1, 0))
                    if j < 2:
                        g_att[layer, j, :, 128 * t : 128 * (t + 1)] = tile
                    else:
                        for m in range(2):
                            lo = 512 + 64 * t
                            g_att[layer, m, :, lo : lo + 64] = tile[:, 64 * m : 64 * (m + 1)]
        share(g_att.at[0], a0o_ref, a0m_ref, mp)
        share(g_att.at[1], a1o_ref, a1m_ref, mp)
        share(g_ffw.at[0], uo_ref, um_ref, mp)
        share(g_ffw.at[1], do_ref, dm_ref, mp)
        sums = jnp.transpose(dqkv[:, D:], (1, 0))[0:1]
        gb_ref[0:1, :D] = sums[:, :D]
        gb_ref[0:1, D:] = sums[:, 2 * D :]
        gb_ref[1:2, D:] = jnp.transpose(dkv[:, D:], (1, 0))[0:1, D:]


def attn_tiles(w_ref, qkv_w, out_w):
    for t in range(4):
        cols = 128 * t
        pieces = [w_ref[0, :, cols : cols + 128], w_ref[1, :, cols : cols + 128]]
        tile = 512 + 128 * (t // 2)
        lane = 64 * (t % 2)
        pieces.append(
            jnp.concatenate(
                [w_ref[m, :, tile : tile + 128][:, lane : lane + 64] for m in range(2)], 1
            )
        )
        for j in range(3):
            if t < 3:
                at = D * t + 128 * j
                qkv_w[:, at : at + 128] = pieces[j]
            else:
                out_w[:, 128 * j : 128 * (j + 1)] = pieces[j]


def backward(dz, kept, weights, tok):
    steps = dz.shape[0] // (GRP * ENDS)
    x_shape = kept[0].shape
    shares = pair_shapes([(D, 768)] * 4)
    extra = [jax.ShapeDtypeStruct(s, f32) for s in ((8, D), (2, 2 * D), (1, FF))]
    return pl.pallas_call(
        backward_kernel,
        grid=(steps,),
        in_specs=[block_of(a.shape, steps) for a in (dz,) + tuple(kept)]
        + [
            pl.BlockSpec((2, 2, D, 768), lambda i: (0, 0, 0, 0), pipeline_mode=pl.Buffered(1)),
            pl.BlockSpec((2, 2, D, 768), lambda i: (1, 0, 0, 0), pipeline_mode=pl.Buffered(1)),
            full_spec(tok.shape),
        ],
        out_specs=[block_of(x_shape, steps)] + [full_spec(x.shape) for x in shares + extra],
        out_shape=[jax.ShapeDtypeStruct(x_shape, f32)] + shares + extra,
        scratch_shapes=[
            pltpu.VMEM((LAYERS, D, 3 * D), bf16),
            pltpu.VMEM((LAYERS, D, D), bf16),
            pltpu.VMEM((3 * D, 512), f32),
            pltpu.VMEM((2 * D, 512), f32),
            pltpu.VMEM((D, D), f32),
            pltpu.VMEM((LAYERS, D, D), f32),
            pltpu.VMEM((2, 2, D, 768), f32),
            pltpu.VMEM((LAYERS, 2, D, 768), f32),
            pltpu.VMEM((ROWS, D + 128), bf16),
            pltpu.VMEM((ROWS, D), f32),
            pltpu.VMEM((ROWS, D), f32),
            pltpu.VMEM((ROWS, HALF), bf16),
            pltpu.VMEM((GRP * ENDS, D), bf16),
            pltpu.VMEM((GRP, 3 * D, TP), bf16),
        ],
        compiler_params=pltpu.CompilerParams(vmem_limit_bytes=62 * MIB),
        name="backward_layers",
    )(dz, *kept, weights, weights, tok)


def patch_grad_kernel(
    partner_ref,
    mix_ref,
    dz_ref,
    own_ref,
    far_ref,
    gvb_ref,
    gvh_ref,
    po_ref,
    pm_ref,
    eo_ref,
    em_ref,
    dzo,
    dzf,
    tok,
    g_patch,
    g_seg,
):
    mp = lax.axis_index("mp")
    count = far_ref.shape[0] // PATCHES
    both = own_ref.shape[0] // PATCHES
    dzo[...] = jnp.zeros_like(dzo)
    total = jnp.zeros((TP, D), f32)
    for k in range(count):
        place = partner_place(partner_ref, k)
        w = mix_ref[place]
        for j in range(3):
            part = dz_ref[k * TP : k * TP + PATCHES, 128 * j : 128 * (j + 1)]
            dzo[j, pl.ds(place, PATCHES, stride=both), :] = w * part
            dzf[j, pl.ds(k, PATCHES, stride=count), :] = (1.0 - w) * part
        total = total + dz_ref[k * TP : (k + 1) * TP]
    tok[...] = jnp.zeros_like(tok)
    tok[:TP] = total
    tok[TP : TP + 8] = gvb_ref[...]
    tok[TP + 8 : TP + 14] = gvh_ref[2:8]
    turned = jnp.transpose(tok[...], (1, 0))
    for m in range(2):
        g_seg[m] = turned[:, 128 * m : 128 * (m + 1)]
    lo, lf = (
        jnp.concatenate([jnp.transpose(ref[j, :rows].astype(bf16), (1, 0)) for j in range(3)], 0)
        for ref, rows in ((dzo, own_ref.shape[0]), (dzf, far_ref.shape[0]))
    )
    for m in range(2):
        cols = slice(D * m, D * (m + 1))
        g_patch[m] = mm(lo, own_ref[:, cols]) + mm(lf, far_ref[:, cols])
    share(g_patch, po_ref, pm_ref, mp)
    share(g_seg, eo_ref, em_ref, mp)


def patch_grad(partner, mix, dz, own, far, gvb, gvh):
    outs = pair_shapes([(D, D), (D, 128)])
    return pl.pallas_call(
        patch_grad_kernel,
        grid=(1,),
        in_specs=[pl.BlockSpec(memory_space=pltpu.SMEM)] * 2
        + [full_spec(a.shape) for a in (dz, own, far, gvb, gvh)],
        out_specs=[full_spec(x.shape) for x in outs],
        out_shape=outs,
        scratch_shapes=[
            pltpu.VMEM((3, own.shape[0] // PATCHES * TP, 128), f32),
            pltpu.VMEM((3, far.shape[0] // PATCHES * TP, 128), f32),
            pltpu.VMEM((256, D), f32),
            pltpu.VMEM((2, D, D), f32),
            pltpu.VMEM((2, D, 128), f32),
        ],
        compiler_params=pltpu.CompilerParams(vmem_limit_bytes=56 * MIB),
        name="patch_gradient",
    )(partner, mix, dz, own, far, gvb, gvh)


def link_orders(bits):
    far = [b for b in (range(1, bits, 2) if bits == 6 else [3]) if b < bits]
    near = [b for b in range(bits) if b not in far]
    return [near[i:] + near[:i] for i in range(len(near))], far


def gather_plan(bits, turns):
    near, far = link_orders(bits)
    deep = far + [near[0][-1]]
    flat = near[0][:-1]
    return [flat[t:] + flat[:t] for t in turns], deep


def chunk_plan(bits, cuts):
    near, far = link_orders(bits)
    return [
        (cuts[i], cuts[i + 1] - cuts[i], near[i % len(near)], far) for i in range(len(cuts) - 1)
    ]


def mesh_place():
    return lax.axis_index("dp"), lax.axis_index("mp")


def bit_of(value, bit):
    return (value // 2**bit) % 2


def flipped(value, bit):
    return value + 2**bit * (1 - 2 * bit_of(value, bit))


def meet(bits, pairs=()):
    dp, mp = mesh_place()
    barrier = pltpu.get_barrier_semaphore()
    peers = [(dp, 1 - mp)] + [(flipped(dp, b), mp) for b in range(bits)]
    peers += [(flipped(flipped(dp, b), b + 1), mp) for b in pairs]
    for peer in peers:
        pl.semaphore_signal(barrier, inc=1, device_id=peer, device_id_type=MESH)
    pl.semaphore_wait(barrier, len(peers))


def push(src, dst, send, recv, peer):
    copy = pltpu.make_async_remote_copy(
        src_ref=src, dst_ref=dst, send_sem=send, recv_sem=recv, device_id=peer, device_id_type=MESH
    )
    copy.start()
    return copy


def held_part(ref, bits, lead, dp, done=(), flip=None):
    idx = list(lead)
    for b in reversed(bits):
        mine = bit_of(dp, b)
        idx.append(pl.ds(0, 2) if b in done else (1 - mine if b == flip else mine))
    return ref.at[tuple(idx)]


def gather_front_kernel(bits, tab_ref, main_ref, sb_ref, *refs):
    w_refs = refs[:2]
    far_refs = refs[2:4]
    sbo_ref, tabr, stage_p, stage_e, stage_h, s_loc, s_tab = refs[4:11]
    s_send, s_recv, f_send, f_recv, m_send, m_recv = refs[11:]
    dp, mp = mesh_place()
    mate = (dp, 1 - mp)
    turns, deep = gather_plan(bits, FRONT_TURNS)
    every = list(range(bits))

    far = deep[:-1]
    wide = {}

    def part(c, *args):
        return held_part(w_refs[c], every, (mp,), dp, *args)

    def main(c, *args):
        return held_part(far_refs[c], far, (), dp, *args)

    meet(bits)
    c_tab = push(tab_ref.at[1 - mp], tabr, s_tab.at[0], s_tab.at[1], mate)
    c_sb = push(sb_ref, sbo_ref.at[mp], s_tab.at[2], s_tab.at[3], mate)
    local = [pltpu.make_async_copy(sb_ref, sbo_ref.at[mp], s_loc.at[0])]
    local[0].start()
    c_tab.wait()
    mine = tab_ref[mp].astype(f32)
    other = tabr[...].astype(f32)
    first = jnp.where(mp == 0, mine, other)
    second = jnp.where(mp == 0, other, mine)
    table = jnp.concatenate([first, second], 0).astype(bf16)
    stage_p[...] = table[:, :D]
    stage_e[...] = table[:, D:F_COLS]
    stage_h[...] = table[:, F_COLS:]
    stages = (stage_p, stage_e)
    wides = (main_ref, stage_h)
    copies = {}
    forwards = []
    for s in range(bits + 1):
        for c in range(2):
            order = deep + turns[c]
            if s:
                copies[c, s - 1].wait_recv()
            if s < bits:
                held = part(c, order[:s])
                copies[c, s] = push(
                    held if s else stages[c],
                    held,
                    s_send.at[c, s],
                    s_recv.at[c, s],
                    (flipped(dp, order[s]), mp),
                )
            got = part(c, order[: s - 1], order[s - 1]) if s else part(c)
            forwards.append(
                push(got if s else stages[c], got, f_send.at[c, s], f_recv.at[c, s], mate)
            )
        if s == 0:
            for c in range(2):
                local.append(pltpu.make_async_copy(stages[c], part(c), s_loc.at[c + 1]))
                local[-1].start()
                local.append(pltpu.make_async_copy(wides[c], main(c), s_loc.at[c + 3]))
                local[-1].start()
            for copy in local:
                copy.wait()
        at = s - len(deep) + 1
        if 0 <= at < len(far):
            for c in range(2):
                if at:
                    wide[c, at - 1].wait_recv()
                dst = main(c, far[:at])
                wide[c, at] = push(
                    dst if at else wides[c],
                    dst,
                    m_send.at[c, at],
                    m_recv.at[c, at],
                    (flipped(dp, far[at]), mp),
                )
    for copy in forwards:
        copy.wait()
    for copy in copies.values():
        copy.wait_send()
    for copy in wide.values():
        copy.wait_send()
    for c in range(2):
        wide[c, len(far) - 1].wait_recv()
    c_sb.wait()


def gather_front(tab, shard, sb, n_data):
    bits = n_data.bit_length() - 1
    rows = D // n_data
    _, far = link_orders(bits)
    deep_shape = (2,) * len(far)
    sems = pltpu.SemaphoreType.DMA
    anywhere = pl.BlockSpec(memory_space=pl.ANY)
    inside = pl.BlockSpec(memory_space=pltpu.VMEM)
    return pl.pallas_call(
        functools.partial(gather_front_kernel, bits),
        in_specs=[inside] * 3,
        out_specs=[anywhere] * 4 + [inside],
        out_shape=[
            jax.ShapeDtypeStruct((2,) * (bits + 1) + (rows, w), bf16) for w in FRONT_WIDTHS
        ]
        + [
            jax.ShapeDtypeStruct(deep_shape + shard.shape, bf16),
            jax.ShapeDtypeStruct(deep_shape + (rows, T_COLS - F_COLS), bf16),
            jax.ShapeDtypeStruct((2,) + sb.shape, f32),
        ],
        scratch_shapes=[
            pltpu.VMEM(tab.shape[1:], bf16),
            pltpu.VMEM((rows, FRONT_WIDTHS[0]), bf16),
            pltpu.VMEM((rows, FRONT_WIDTHS[1]), bf16),
            pltpu.VMEM((rows, T_COLS - F_COLS), bf16),
            sems((5,)),
            sems((4,)),
            sems((2, bits)),
            sems((2, bits)),
            sems((2, bits + 1)),
            sems((2, bits + 1)),
            sems((2, len(far))),
            sems((2, len(far))),
        ],
        compiler_params=pltpu.CompilerParams(
            collective_id=2, has_side_effects=True, vmem_limit_bytes=60 * MIB
        ),
        name="gather_front",
    )(tab, shard, sb)


def gather_main_kernel(bits, *refs):
    turns, deep = gather_plan(bits, MAIN_TURNS)
    far, last = deep[:-1], deep[-1]
    mains, heads, pix_ref = refs[:2], refs[2:4], refs[4]
    w_ref, h_ref, mine_ref = refs[5:8]
    pix, s_pix, s_loc, s_send, s_recv, f_send, f_recv = refs[8:]
    dp, mp = mesh_place()
    mate = (dp, 1 - mp)
    every = list(range(bits))
    steps = bits - len(deep)
    chunks = len(MAIN_WIDTHS)

    def lead(c):
        return (w_ref, (c, mp)) if c < chunks - 1 else (h_ref, (mp,))

    def part(c, *args):
        return held_part(lead(c)[0], every, lead(c)[1], dp, *args)

    meet(bits)
    pix_in = pltpu.make_async_copy(pix_ref.at[:, mp], pix, s_pix.at[0])
    pix_in.start()
    copies = {}
    forwards = []
    local = []
    for c in range(chunks):
        for i, dst in enumerate((part(c, far), part(c, far, last))):
            lead_cut = (slice(None),) * len(far) + (c,)
            src = mains[i].at[lead_cut] if c < chunks - 1 else heads[i]
            local.append(pltpu.make_async_copy(src, dst, s_loc.at[c, i]))
            local[-1].start()
    pix_in.wait()
    pix_out = pltpu.make_async_copy(pix, mine_ref, s_pix.at[1])
    pix_out.start()
    for s in range(steps + 1):
        for c in range(chunks):
            order = turns[c]
            if s:
                copies[c, s - 1].wait_recv()
            else:
                for copy in local[2 * c : 2 * c + 2]:
                    copy.wait()
            done = deep + order[:s]
            if s < steps:
                held = part(c, done)
                copies[c, s] = push(
                    held, held, s_send.at[c, s], s_recv.at[c, s], (flipped(dp, order[s]), mp)
                )
            got = part(c, done[:-1], done[-1]) if s else part(c, done)
            forwards.append(push(got, got, f_send.at[c, s], f_recv.at[c, s], mate))
    for copy in forwards:
        copy.wait()
    for copy in copies.values():
        copy.wait_send()
    pix_out.wait()


def gather_main(mains, heads, pix, n_data):
    bits = n_data.bit_length() - 1
    rows = D // n_data
    near, _ = link_orders(bits)
    steps = len(near[0]) - 1
    chunks = len(MAIN_WIDTHS)
    sems = pltpu.SemaphoreType.DMA
    anywhere = pl.BlockSpec(memory_space=pl.ANY)
    inside = pl.BlockSpec(memory_space=pltpu.VMEM)
    places = (2,) * (bits + 1) + (rows,)
    mine = pix.shape[:1] + pix.shape[2:]
    main, head_w, pix_mine = pl.pallas_call(
        functools.partial(gather_main_kernel, bits),
        in_specs=[inside] * (2 * len(mains)) + [anywhere],
        out_specs=[anywhere] * 3,
        out_shape=[
            jax.ShapeDtypeStruct((chunks - 1,) + places + (768,), bf16),
            jax.ShapeDtypeStruct(places + (1024,), bf16),
            jax.ShapeDtypeStruct(mine, bf16),
        ],
        scratch_shapes=[
            pltpu.VMEM(mine, bf16),
            sems((2,)),
            sems((chunks, len(mains))),
            sems((chunks, steps)),
            sems((chunks, steps)),
            sems((chunks, steps + 1)),
            sems((chunks, steps + 1)),
        ],
        compiler_params=pltpu.CompilerParams(
            collective_id=0, has_side_effects=True, vmem_limit_bytes=60 * MIB
        ),
        cost_estimate=pl.CostEstimate(flops=0, bytes_accessed=150 * MIB, transcendentals=0),
        name="gather_main",
    )(*mains, *heads, pix)
    return main.reshape(chunks - 1, 2, D, 768), head_w.reshape(2, D, 1024), pix_mine


def reduce_plan(bits, turns):
    near, far = link_orders(bits)
    return [near[t % len(near)] + far for t in turns]


def block_index(free, fixed):
    def index(t):
        total = fixed
        for j, b in enumerate(free):
            total = total + ((t // 2**j) % 2) * 2**b
        return total

    return index


def reduce_kernel(bits, widths, turns, *refs):
    n = len(widths)
    own, mate_src = refs[:n], refs[n : 2 * n]
    smalls = refs[2 * n : 2 * n + 5]
    outs = refs[2 * n + 5 : 3 * n + 5]
    obun_ref, info_ref = refs[3 * n + 5 : 3 * n + 7]
    refs = refs[3 * n + 7 :]
    mrecv, acc, held = refs[:n], refs[n : 2 * n], refs[2 * n : 3 * n]
    refs = refs[3 * n :]
    sbufs, rbufs = refs[: n * bits], refs[n * bits : 2 * n * bits]
    bun, bunr, tsend, sq, sqr, o_sem, m_sem, s_sem, r_sem, b_sem, q_sem, t_sem = refs[2 * n * bits :]
    dp, mp = mesh_place()
    mate = (dp, 1 - mp)
    orders = reduce_plan(bits, turns)
    rows = D // 2**bits
    group = max(rows, 48)
    per = group // rows
    small = rows // 2

    loads = {}
    for c in REDUCE_ORDER:
        loads[c] = pltpu.make_async_copy(own[c], held[c], o_sem.at[c])
        loads[c].start()
    at = 0
    for ref in smalls:
        for i in range(ref.shape[0]):
            bun[:, at : at + ref.shape[1]] = ref[i : i + 1]
            at += ref.shape[1]
    pairs = range(0, bits, 2)
    meet(bits, pairs)
    mcopies = {
        c: push(mate_src[c], mrecv[c], m_sem.at[c, 0], m_sem.at[c, 1], mate) for c in REDUCE_ORDER
    }
    bcopies = [push(bun, bunr.at[0], b_sem.at[0, 0], b_sem.at[0, 1], mate)]

    def loop(total, body):
        def step(t, carry):
            body(t)
            return carry

        lax.fori_loop(0, total, step, 0)

    copies = {}

    def split(order, s, sent):
        free = [b for b in range(bits) if b not in order[: s + 1]]
        fixed = sum((bit_of(dp, b) * 2**b for b in order[:s]), 0)
        last = bit_of(dp, order[s])
        fixed = fixed + (1 - last if sent else last) * 2 ** order[s]
        return 2 ** len(free), block_index(free, fixed)

    def send_stage(c, s):
        total, index = split(orders[c], s, True)
        sbuf = sbufs[c * bits + s]

        def body(t):
            sbuf[t] = acc[c][index(t)].astype(bf16)

        loop(total, body)
        copies[c, s] = push(
            sbuf,
            rbufs[c * bits + s],
            s_sem.at[c, s],
            r_sem.at[c, s],
            (flipped(dp, orders[c][s]), mp),
        )

    def take_stage(c, s):
        copies[c, s].wait_recv()
        total, index = split(orders[c], s, False)
        rbuf = rbufs[c * bits + s]

        def body(t):
            acc[c][index(t)] += rbuf[t].astype(f32)

        loop(total, body)

    for c in REDUCE_ORDER:
        loads[c].wait()
        mcopies[c].wait_recv()

        def body(b):
            rs = pl.ds(pl.multiple_of(b * group, group), group)
            got = held[c][rs] + mrecv[c][rs].astype(f32)
            for i in range(per):
                acc[c][b * per + i] = got[rows * i : rows * (i + 1)]

        loop(D // group, body)
        send_stage(c, 0)
    for s in range(1, bits + 1):
        for c in REDUCE_ORDER:
            take_stage(c, s - 1)
            if s < bits:
                send_stage(c, s)
        bcopies[-1].wait()
        bun[...] = bun[...] + bunr[s - 1]
        bcopies.append(
            push(bun, bunr.at[s], b_sem.at[s, 0], b_sem.at[s, 1], (flipped(dp, s - 1), mp))
        )
    tails = []
    total = jnp.zeros((1, 1), f32)
    for c in range(n):
        mine = acc[c][dp]
        total = total + jnp.sum(mine * mine, keepdims=True)
        if c in TABLE_CHUNKS:
            k = TABLE_CHUNKS.index(c)
            send, recv = tsend[2 * k], tsend[2 * k + 1]
            send[...] = jnp.where(mp == 0, mine[small:], mine[:small])
            outs[c][mp] = jnp.where(mp == 0, mine[:small], mine[small:])
            tails.append((c, recv, push(send, recv, t_sem.at[k, 0], t_sem.at[k, 1], mate)))
        else:
            outs[c][...] = mine
    sq[0] = jnp.broadcast_to(total, (8, 128))
    bcopies[-1].wait()
    final = bun[...] + bunr[bits]
    obun_ref[...] = final
    shared = jnp.sum(final[:, 128:] * final[:, 128:], keepdims=True)
    push(sq.at[0], sqr.at[0], q_sem.at[0, 0], q_sem.at[0, 1], mate).wait()
    sq[1] = sq[0] + sqr[0]
    for i, b in enumerate(pairs):
        one, two = flipped(dp, b), flipped(dp, b + 1)
        around = [
            push(sq.at[i + 1], sqr.at[at], q_sem.at[at, 0], q_sem.at[at, 1], (peer, mp))
            for at, peer in enumerate((one, two, flipped(one, b + 1)), 3 * i + 1)
        ]
        for copy in around:
            copy.wait()
        at = 3 * i + 1
        sq[i + 2] = (sq[i + 1] + sqr[at]) + (sqr[at + 1] + sqr[at + 2])
    for c, recv, copy in tails:
        copy.wait()
        outs[c][1 - mp] = recv[...]
    squares = sq[len(pairs) + 1] + shared
    loss, weight = final[:, 0:1], final[:, 1:2]
    norm = jnp.sqrt(squares) / weight
    factor = jnp.minimum(1.0, clip_limit / norm) / weight
    which = lax.broadcasted_iota(jnp.int32, (8, 128), 1)
    info = jnp.where(which == 0, loss, jnp.where(which == 1, weight, norm))
    info_ref[...] = jnp.where(which == 3, factor, info)
    for copy in mcopies.values():
        copy.wait_send()
    for copy in copies.values():
        copy.wait_send()


def reduce_all(own, mates, smalls, turns, n_data):
    bits = n_data.bit_length() - 1
    rows = D // n_data
    widths = [x.shape[1] for x in own]
    n = len(widths)
    sems = pltpu.SemaphoreType.DMA
    inside = pl.BlockSpec(memory_space=pltpu.VMEM)
    anywhere = pl.BlockSpec(memory_space=pl.ANY)
    bufs = [
        pltpu.VMEM((2 ** (bits - 1 - s), rows, w), bf16) for w in widths for s in range(bits)
    ]
    length = sum(x.shape[0] * x.shape[1] for x in smalls)
    outs = [
        jax.ShapeDtypeStruct((2, rows // 2, w) if c in TABLE_CHUNKS else (rows, w), f32)
        for c, w in enumerate(widths)
    ]
    tails = [
        pltpu.VMEM((rows // 2, widths[c]), f32) for c in TABLE_CHUNKS for _ in range(2)
    ]

    def kernel(*refs):
        cut = len(refs) - 11 - len(tails)
        head, rest = refs[:cut], refs[cut:]
        tsend, rest = rest[: len(tails)], rest[len(tails) :]
        reduce_kernel(bits, widths, turns, *head, rest[0], rest[1], tsend, *rest[2:])

    return pl.pallas_call(
        kernel,
        in_specs=[anywhere] * (2 * n) + [inside] * len(smalls),
        out_specs=[inside] * (n + 2),
        out_shape=outs
        + [
            jax.ShapeDtypeStruct((1, length), f32),
            jax.ShapeDtypeStruct((8, 128), f32),
        ],
        scratch_shapes=[pltpu.VMEM((D, w), bf16) for w in widths]
        + [pltpu.VMEM((n_data, rows, w), f32) for w in widths]
        + [pltpu.VMEM((D, w), f32) for w in widths]
        + bufs
        + bufs
        + tails
        + [
            pltpu.VMEM((1, length), f32),
            pltpu.VMEM((bits + 1, 1, length), f32),
            pltpu.VMEM((bits // 2 + 2, 8, 128), f32),
            pltpu.VMEM((3 * (bits // 2) + 1, 8, 128), f32),
            sems((n,)),
            sems((n, 2)),
            sems((n, bits)),
            sems((n, bits)),
            sems((bits + 1, 2)),
            sems((3 * (bits // 2) + 1, 2)),
            sems((len(TABLE_CHUNKS), 2)),
        ],
        compiler_params=pltpu.CompilerParams(
            collective_id=1, has_side_effects=True, vmem_limit_bytes=62 * MIB
        ),
        name="reduce_gradients",
    )(*own, *mates, *smalls)


def adamw(master, first, second, gradient, rate, decay):
    first = beta_one * first + (1.0 - beta_one) * gradient
    second = beta_two * second + (1.0 - beta_two) * gradient * gradient
    first_hat = first / (1.0 - beta_one**STEP)
    second_hat = second / (1.0 - beta_two**STEP)
    master = master - rate * (first_hat / (jnp.sqrt(second_hat) + adam_eps) + decay * master)
    return (master, first, second)


def local_split(flat, layer):
    mp = lax.axis_index("mp")
    rows = []
    for m in range(2):
        pieces = []
        for h in range(3):
            at = 128 + 2 * D * layer + (128 * m + HD * h if h < 2 else 256 + HD * m)
            pieces += [flat[:, at : at + HD], flat[:, at + D : at + D + HD]]
        at = 128 + 2 * D * LAYERS + FF * layer + HALF * m
        rows.append(jnp.concatenate(pieces + [flat[:, at : at + HALF]], 1))
    return jnp.where(mp == 0, rows[0], rows[1])


def update_kernel(info_ref, *refs):
    g = refs[:9]
    flat_ref = refs[9]
    params = refs[10:25]
    outs = refs[25:]
    factor = info_ref[0, 3]

    def write(grad, item, rate, decay, at, outs, low):
        new, one, two = adamw(
            item[0][at], item[1][at], item[2][at], grad * factor, rate, decay
        )
        outs[0][at], outs[1][at], outs[2][at] = new, one, two
        if low:
            outs[3][at] = new.astype(bf16)

    everything = (slice(None), slice(None))
    heads = [
        jnp.concatenate([g[6][m, :, 512 * h : 512 * (h + 1)] for m in range(2)], 1)[:, :CLS]
        for h in range(2)
    ]
    token = jnp.concatenate([g[8][0], g[8][1]], 1)
    table = jnp.concatenate(
        [g[7][0], g[7][1], token[:, PATCHES:TOK], token[:, :PATCHES]] + heads, 1
    )
    write(table, params[0:3], matrix_rate, matrix_decay, everything, outs[0:4], True)
    vec = jnp.transpose(token, (1, 0))[TP : TP + 6 * LAYERS + 2]
    write(vec, params[3:6], vector_rate, 0.0, everything, outs[4:7], False)
    for layer in range(LAYERS):
        packed = g[layer][...]
        pieces = []
        for h in range(3):
            for t in range(4):
                lo = 128 * t + HD * h if h < 2 else 512 + HD * t
                pieces.append(packed[:, lo : lo + HD])
        grad = jnp.concatenate(pieces, 1)
        write(grad, params[6:9], matrix_rate, matrix_decay, layer, outs[7:11], True)
        for half in range(2):
            write(
                g[LAYERS + 2 * layer + half][...],
                params[9:12],
                matrix_rate,
                matrix_decay,
                (layer, slice(None), half),
                outs[11:15],
                True,
            )
    flat = flat_ref[...]
    for layer in range(LAYERS):
        grad = local_split(flat, layer)
        write(grad, params[12:15], vector_rate, 0.0, slice(layer, layer + 1), outs[15:18], False)


def update(info, grads, split, params):
    outs = []
    for i in range(5):
        low = i in (0, 2, 3)
        shape = params[3 * i].shape
        outs += [jax.ShapeDtypeStruct(shape, f32)] * 3
        outs += [jax.ShapeDtypeStruct(shape, bf16)] if low else []
    ins = list(grads) + [split] + list(params)
    return pl.pallas_call(
        update_kernel,
        grid=(1,),
        in_specs=[pl.BlockSpec(memory_space=pltpu.SMEM)] + [full_spec(x.shape) for x in ins],
        out_specs=[full_spec(x.shape) for x in outs],
        out_shape=outs,
        compiler_params=pltpu.CompilerParams(vmem_limit_bytes=60 * MIB),
        name="update_weights",
    )(info, *ins)


def pack_kernel(t_ref, v_ref, a_ref, f_ref, tab_ref, main_ref):
    small = t_ref.shape[0]
    table = t_ref[...]

    def zeros(n):
        return jnp.zeros((small, n), f32)

    turned = jnp.transpose(v_ref[...], (1, 0))
    low = PD + 2
    seg = jnp.concatenate(
        [
            table[:, low : low + PATCHES],
            table[:, PD:low],
            zeros(TP - TOK),
            turned,
            zeros(256 - TP - turned.shape[1]),
        ],
        1,
    )
    heads = [
        jnp.concatenate(
            [table[:, PD + TOK + CLS * h : PD + TOK + CLS * (h + 1)], zeros(1024 - CLS)], 1
        )
        for h in range(2)
    ]
    parts = [table[:, :PD], seg] + heads
    for m in range(2):
        at = 0
        for x in parts:
            half = x.shape[1] // 2
            tab_ref[m, :, at : at + half] = x[:, half * m : half * (m + 1)].astype(bf16)
            at += half
    for layer in range(LAYERS):
        a = a_ref[layer]
        for t in range(4):
            pair = jnp.concatenate(
                [a[:, 256 * h + HD * t : 256 * h + HD * (t + 1)] for h in range(2)], 1
            )
            main_ref[layer, :, 128 * t : 128 * (t + 1)] = pair.astype(bf16)
        main_ref[layer, :, 512:] = a[:, 512:].astype(bf16)
        for half in range(2):
            main_ref[LAYERS + 2 * layer + half] = f_ref[layer, :, half].astype(bf16)


def pack(tab, vec, attn, ffw):
    layers, rows, _ = attn.shape
    ins = [tab, vec, attn, ffw]
    shapes = [(2, tab.shape[0], T_COLS), (3 * layers, rows, HALF)]
    return pl.pallas_call(
        pack_kernel,
        grid=(1,),
        in_specs=[full_spec(x.shape) for x in ins],
        out_specs=[full_spec(x) for x in shapes],
        out_shape=[jax.ShapeDtypeStruct(x, bf16) for x in shapes],
        compiler_params=pltpu.CompilerParams(vmem_limit_bytes=60 * MIB),
        name="pack_shards",
    )(*ins)


def shards(
    pixels,
    labels,
    teacher,
    partner,
    mix_weight,
    class_weight,
    tables,
    tables_first,
    tables_second,
    vectors,
    vectors_first,
    vectors_second,
    attention,
    attention_first,
    attention_second,
    feedforward,
    feedforward_first,
    feedforward_second,
    split_bias,
    split_bias_first,
    split_bias_second,
    head_bias,
    head_bias_first,
    head_bias_second,
):
    n_data = lax.axis_size("dp")
    dp, mp = mesh_place()
    images_here = pixels.shape[0]
    count = images_here // 2
    rows = D // n_data
    far_pairs = [(i, (i + n_data // 2) % n_data) for i in range(n_data)]
    pix = pixels.transpose(1, 0, 2)
    tab, shard = pack(tables.T, vectors, attention, feedforward)
    deep = gather_plan(n_data.bit_length() - 1, MAIN_TURNS)[1]
    front, seg, *heights, sb = gather_front(tab, shard, split_bias, n_data)
    front = front.reshape(2, D, FRONT_WIDTHS[0])
    seg = seg.reshape(2, D, FRONT_WIDTHS[1])
    near_pairs = [(i, i ^ (1 << deep[-1])) for i in range(n_data)]
    mains, heads = ([x, lax.ppermute(x, "dp", near_pairs)] for x in heights)
    pix_halves = pix.reshape(PATCHES, 2, count, PD)
    send = embed_send(pix_halves, front)
    mains, heads, send = lax.optimization_barrier((mains, heads, send))
    far = lax.ppermute(send, "dp", far_pairs)
    weights, w_heads, pix_mine = gather_main(mains, heads, pix_halves, n_data)
    hb = jnp.pad(
        head_bias.astype(bf16).astype(f32).reshape(2, CLS),
        ((0, 0), (0, 1024 - CLS)),
        constant_values=-1e30,
    ).reshape(1, -1)
    cw = jnp.pad(class_weight, (0, 1024 - CLS)).reshape(1, -1)
    front, hb, cw, weights = lax.optimization_barrier((front, hb, cw, weights))
    own = embed_own(partner, pix, front)
    pix_mine, far, own = lax.optimization_barrier((pix_mine, far, own))
    pix_far = lax.ppermute(pix_mine, "dp", far_pairs)
    *kept, mid, tok = forward(
        partner, mix_weight, own, far, seg, weights, sb
    )
    u1o, u1m, d1o, d1m, ho, hm, dz, gvh, gu1, dhb, stat = head(
        partner, mix_weight, labels, teacher, mid, weights, w_heads, sb, hb, cw, tok
    )
    dz0, a0o, a0m, a1o, a1m, u0o, u0m, d0o, d0m, gvb, gb, gu0 = backward(dz, kept, weights, tok)
    po, pm, eo, em = patch_grad(
        partner,
        mix_weight,
        dz0,
        pix.reshape(PATCHES * images_here, PD),
        pix_far.reshape(PATCHES * count, PD),
        gvb,
        gvh,
    )
    own_parts = [a0o, a1o, u0o, d0o, u1o, d1o, ho, po, eo]
    mate_parts = [a0m, a1m, u0m, d0m, u1m, d1m, hm, pm, em]
    *g, flat, info = reduce_all(
        own_parts, mate_parts, [stat, gb, gu0, gu1, dhb], REDUCE_TURNS, n_data
    )
    loss_sum, weight_sum, grad_norm, factor = (info[0, i] for i in range(4))
    at = 128 + 2 * D * LAYERS + FF * LAYERS
    g_head = flat[0, at : at + 2048].reshape(2, 1024)[:, :CLS].reshape(-1)
    fresh = update(
        info,
        g,
        flat,
        [
            tables.T,
            tables_first.T,
            tables_second.T,
            vectors,
            vectors_first,
            vectors_second,
            attention,
            attention_first,
            attention_second,
            feedforward,
            feedforward_first,
            feedforward_second,
            split_bias,
            split_bias_first,
            split_bias_second,
        ],
    )
    fresh = [x.T for x in fresh[:4]] + list(fresh[4:])
    h_new, h_one, h_two = adamw(
        head_bias, head_bias_first, head_bias_second, g_head * factor, vector_rate, 0.0
    )
    return (loss_sum, weight_sum, grad_norm, *fresh, h_new, h_one, h_two)


def solution(mesh):
    table = P(None, ("dp", "mp"))
    attn = P(None, "dp", "mp")
    ffw = P(None, "dp", None, "mp")
    split = P(None, "mp")
    return jax.shard_map(
        shards,
        mesh=mesh,
        in_specs=(P("dp", None, None), P(), P("dp"), P("dp"), P("dp"), P())
        + (table,) * 6
        + (attn,) * 3
        + (ffw,) * 3
        + (split,) * 3
        + (P(),) * 3,
        out_specs=(P(),) * 3
        + (table,) * 7
        + (attn,) * 4
        + (ffw,) * 4
        + (split,) * 3
        + (P(),) * 3,
        check_vma=False,
    )
```
